32 devices in a mesh: dp: 8 (over z, y), sp: 4 (over x, core).
Axes of the slice: x: 2, y: 2, z: 4, core: 2. Of those that a mesh axis runs over, the one named last changes fastest.
Arguments:
- inputs: bfloat16 [16, 2048, 1024], P('dp', 'sp'), may hold values from -6 to 6
- cotangent: bfloat16 [16, 2048, 1024], P('dp', 'sp'), may hold values from -6 to 6
- group_ids: int32 [16], P('dp'), may hold values from 0 to 7
- group_scale: float32 [8], replicated, may hold values from 0.3 to 3
- norm_gain: bfloat16 [1024], P(('dp', 'sp')), may hold values from 0.5 to 1.5
- w_query: bfloat16 [1024, 1024], P(('dp', 'sp')), may hold values from -0.1875 to 0.1875
- w_latent: bfloat16 [1024, 512], P(('dp', 'sp')), may hold values from -0.1875 to 0.1875
- expansion_weight: bfloat16 [2, 256, 1024], P(None, ('dp', 'sp')), may hold values from -0.375 to 0.375
- w_output: bfloat16 [1024, 1024], P(('dp', 'sp')), may hold values from -3 to 3
- ffn_gain: bfloat16 [1024], P(('dp', 'sp')), may hold values from 0.5 to 1.5
- w_gate: bfloat16 [1024, 2816], P(('dp', 'sp')), may hold values from -0.1875 to 0.1875
- w_up: bfloat16 [1024, 2816], P(('dp', 'sp')), may hold values from -0.1875 to 0.1875
- w_down: bfloat16 [2816, 1024], P(('dp', 'sp')), may hold values from -0.109375 to 0.109375
Outputs:
- output: bfloat16 [16, 2048, 1024], P('dp', 'sp')
- input_grad: bfloat16 [16, 2048, 1024], P('dp', 'sp')
- norm_gain_grad: float32 [1024], P(('dp', 'sp'))
- query_grad: float32 [1024, 1024], P(('dp', 'sp'))
- latent_grad: float32 [1024, 512], P(('dp', 'sp'))
- expand_grad: float32 [2, 256, 1024], P(None, ('dp', 'sp'))
- output_grad: float32 [1024, 1024], P(('dp', 'sp'))
- ffn_gain_grad: float32 [1024], P(('dp', 'sp'))
- gate_grad: float32 [1024, 2816], P(('dp', 'sp'))
- up_grad: float32 [1024, 2816], P(('dp', 'sp'))
- down_grad: float32 [2816, 1024], P(('dp', 'sp'))
The draws below stay inside these ranges and needn't reach their ends.
All inputs are finite; a program needn't handle non-finite values.
Results may differ from the reference program's by a relative error of at most 0.02.
Values may be sent and summed in bfloat16 or wider, within the bound.
A program may use at most 192 MiB of HBM per device.

```python
import math
import jax
import jax.numpy as jnp
from jax import lax

D = 1024
FF = 2816
HEADS = 16
DH = 64
KVH = 2
LATD = 256
HG = 8
CTX = 2048
GROUPS = 8
SEQS = 16


def place_ends(values, own_key, least, largest):
    dims = values.shape
    index_at = [jax.random.randint(jax.random.fold_in(own_key, axis), (), 0, dims[axis]) for axis in range(len(dims))]
    values = values.at[tuple(index_at)].set(least)
    longest = dims.index(max(dims))
    index_at[longest] = (index_at[longest] + 1) % dims[longest]
    return values.at[tuple(index_at)].set(largest)


def levels(rng, shape, pieces, smallest, top_value):
    def one(axis_at, parts):
        draws = jax.random.uniform(jax.random.fold_in(jax.random.fold_in(rng, 6), axis_at), (parts,), jnp.float32, smallest / len(pieces), top_value / len(pieces))
        return jnp.repeat(jnp.exp(draws), shape[axis_at] // parts).reshape((-1,) + (1,) * (len(shape) - axis_at - 1))

    loudness = one(*pieces[0])
    for cut in pieces[1:]:
        loudness = loudness * one(*cut)
    return loudness


def normal_values(own_key, shape, width, bound, cuts=(), kind=jnp.bfloat16):
    values = jax.random.normal(own_key, shape, jnp.float32) * width
    if len(cuts) > 0:
        values = levels(own_key, shape, cuts, -0.22, 0.18) * values
    return jnp.clip(values, min=-bound, max=bound).astype(kind)


def setup_inputs(seed: int = 0) -> dict:
    key_list = jax.random.split(jax.random.key(seed), 14)
    inputs = normal_values(key_list[0], (SEQS, CTX, D), 1.0, 6.0, ((0, 8), (1, 4)))
    cotangent = normal_values(key_list[1], (SEQS, CTX, D), 1.0, 6.0, ((0, 8), (1, 4)))
    group_ids = place_ends(jax.random.randint(key_list[2], (SEQS,), 0, GROUPS), jax.random.fold_in(key_list[2], 1), 0, GROUPS - 1).astype(jnp.int32)
    group_scale = jnp.clip(jnp.exp(jax.random.uniform(key_list[3], (GROUPS,), jnp.float32, math.log(0.3), math.log(3.0))), 0.3, 3.0)
    norm_gain = jnp.clip(1.0 + 0.1 * jax.random.normal(key_list[4], (D,), jnp.float32), 0.5, 1.5).astype(jnp.bfloat16)
    w_query = normal_values(key_list[5], (D, HEADS * DH), D ** -0.5, 0.1875, ((0, 32),))
    w_latent = normal_values(key_list[6], (D, KVH * LATD), D ** -0.5, 0.1875, ((0, 32),))
    expansion_weight = normal_values(key_list[7], (KVH, LATD, HG * 2 * DH), LATD ** -0.5, 0.375, ((1, 32),))
    w_output = normal_values(key_list[8], (HEADS * DH, D), 4 ** -0.5, 3.0, ((0, 32),))
    ffn_gain = jnp.clip(1.0 + 0.1 * jax.random.normal(key_list[9], (D,), jnp.float32), 0.5, 1.5).astype(jnp.bfloat16)
    w_gate = normal_values(key_list[10], (D, FF), D ** -0.5, 0.1875, ((0, 32),))
    w_up = normal_values(key_list[11], (D, FF), D ** -0.5, 0.1875, ((0, 32),))
    w_down = normal_values(key_list[12], (FF, D), FF ** -0.5, 0.109375, ((0, 32),))
    return dict(inputs=inputs, cotangent=cotangent, group_ids=group_ids, group_scale=group_scale, norm_gain=norm_gain, w_query=w_query, w_latent=w_latent, expansion_weight=expansion_weight, w_output=w_output, ffn_gain=ffn_gain, w_gate=w_gate, w_up=w_up, w_down=w_down)


@jax.custom_vjp
def reduced_precision(v):
    return lax.optimization_barrier(v.astype(jnp.bfloat16)).astype(jnp.float32)

@jax.custom_vjp
def reduced_precision_backward(v):
    return v

def low_keep(v):
    return (reduced_precision(v), None)

def low_pass(kept, grad):
    return (grad,)

def back_keep(v):
    return (v, None)

def back_low(kept, grad):
    return (reduced_precision(grad),)
reduced_precision.defvjp(low_keep, low_pass)
reduced_precision_backward.defvjp(back_keep, back_low)

def precise_dot(left, right):
    return jnp.dot(left, right, precision=lax.Precision.HIGHEST)

def rms_norm(values, gain):
    return values * lax.rsqrt(lax.optimization_barrier(jnp.mean(values * values, axis=-1, keepdims=True)) + 1e-05) * gain

def attend(queries, key_heads, value_heads):
    seq_length = queries.shape[0]
    block_rows = min(512, seq_length)
    block_count = seq_length // block_rows
    blocks = queries.reshape(block_count, block_rows, HEADS, DH)
    starts = (jnp.arange(block_count) * block_rows).astype(jnp.int32)
    positions = jnp.arange(seq_length)

    @jax.checkpoint
    def one_block(block_item):
        query_block, block_start = block_item
        scores = jnp.einsum('qhd,khd->hqk', query_block, key_heads, precision=lax.Precision.HIGHEST) * DH ** (-0.5)
        scores = reduced_precision_backward(scores)
        row_index = block_start + jnp.arange(block_rows)
        scores = jnp.where(row_index[None, :, None] >= positions[None, None, :], scores, -1e+30)
        probabilities = reduced_precision(jax.nn.softmax(scores, axis=-1))
        return jnp.einsum('hqk,khd->qhd', probabilities, value_heads, precision=lax.Precision.HIGHEST)
    return lax.map(one_block, (blocks, starts)).reshape(seq_length, HEADS, DH)

def block_forward(inputs, norm_gain, w_query, w_latent, expansion_weight, w_output, ffn_gain, w_gate, w_up, w_down):
    batch_size = inputs.shape[0]
    token_rows = inputs.reshape(batch_size * CTX, D)
    normed = reduced_precision(rms_norm(token_rows, norm_gain))
    queries = reduced_precision_backward(reduced_precision(precise_dot(normed, w_query)))
    latent_state = reduced_precision_backward(reduced_precision(precise_dot(normed, w_latent))).reshape(batch_size * CTX, KVH, LATD)
    paired_rows = reduced_precision_backward(reduced_precision(jnp.einsum('fku,kuy->fky', latent_state, expansion_weight, precision=lax.Precision.HIGHEST)))
    paired_rows = paired_rows.reshape(batch_size, CTX, HEADS, 2, DH)
    head_view = queries.reshape(batch_size, CTX, HEADS, DH)
    mixed = jax.vmap(attend)(head_view, paired_rows[:, :, :, 0], paired_rows[:, :, :, 1])
    mixed = reduced_precision_backward(reduced_precision(mixed.reshape(batch_size * CTX, HEADS * DH)))
    branch = reduced_precision_backward(precise_dot(mixed, w_output))
    middle = token_rows + branch
    normed_two = reduced_precision(rms_norm(middle, ffn_gain))
    gate_pre = reduced_precision_backward(precise_dot(normed_two, w_gate))
    upward = reduced_precision_backward(precise_dot(normed_two, w_up))
    hidden = reduced_precision(jax.nn.silu(gate_pre) * upward)
    result = middle + reduced_precision_backward(precise_dot(hidden, w_down))
    return result.reshape(batch_size, CTX, D)

def reference(inputs, cotangent, group_ids, group_scale, norm_gain, w_query, w_latent, expansion_weight, w_output, ffn_gain, w_gate, w_up, w_down):
    weights = tuple((w.astype(jnp.float32) for w in (norm_gain, w_query, w_latent, expansion_weight, w_output, ffn_gain, w_gate, w_up, w_down)))
    seq_scale = group_scale.astype(jnp.float32)[group_ids]
    grad_out = cotangent.astype(jnp.float32) * seq_scale[:, None, None]
    pair_count = SEQS // 2
    input_pairs = inputs.astype(jnp.float32).reshape(pair_count, 2, CTX, D)
    grad_pairs = grad_out.reshape(pair_count, 2, CTX, D)
    zero_grads = tuple((jnp.zeros(w.shape, jnp.float32) for w in weights))

    def paired_step(totals, pair_item):
        part_in, part_grad = pair_item
        result, pullback = jax.vjp(block_forward, part_in, *weights)
        grads = pullback(part_grad)
        totals = tuple((total + grad for total, grad in zip(totals, grads[1:])))
        return (totals, (result, grads[0]))
    totals, (results, input_grads) = lax.scan(paired_step, zero_grads, (input_pairs, grad_pairs))
    output = results.reshape(SEQS, CTX, D).astype(jnp.bfloat16)
    input_grad = input_grads.reshape(SEQS, CTX, D).astype(jnp.bfloat16)
    return (output, input_grad, totals[0], totals[1], totals[2], totals[3], totals[4], totals[5], totals[6], totals[7], totals[8])
```

```python
import functools
import jax
import jax.numpy as jnp
from jax import lax
from jax.sharding import Mesh
from jax.sharding import PartitionSpec as P
from jax.experimental import pallas as pl
from jax.experimental.pallas import tpu as pltpu

DH = 64
F32 = jnp.float32
BF = jnp.bfloat16


def low_half(x):
    return jnp.concatenate([x[:, :DH], jnp.zeros((x.shape[0], DH), x.dtype)], axis=1)


def dot_nt(a, b):
    return lax.dot_general(a, b, (((1,), (1,)), ((), ())), preferred_element_type=F32)


def dot_nn(a, b):
    return lax.dot_general(a, b, (((1,), (0,)), ((), ())), preferred_element_type=F32)


def causal(s, first_key, first_query):
    keys = first_key + lax.broadcasted_iota(jnp.int32, s.shape, 0)
    rows = first_query + lax.broadcasted_iota(jnp.int32, s.shape, 1)
    return jnp.where(rows >= keys, s, -1e30)


def forward_kernel(q_ref, kv_ref, o_ref, lse_ref, vt_s):
    groups, chunks, rows, _ = q_ref.shape
    seq = kv_ref.shape[0]
    for h in range(2):
        vt_s[h] = kv_ref[:, h * 128 : (h + 1) * 128].astype(F32).T[DH:].astype(BF)
    for i in range(groups * chunks):
        q = q_ref[i % groups, i // groups].astype(F32) * 0.125
        outs = []
        for h in range(2):
            qh = q[:, h * DH : (h + 1) * DH]
            qp = jnp.concatenate([qh, jnp.zeros_like(qh)], axis=1).astype(BF)
            width = (i + 1) * rows
            s = dot_nt(kv_ref[0:width, h * 128 : (h + 1) * 128], qp)
            tail = causal(s[i * rows :], 0, 0)
            if i > 0:
                head = s[: i * rows]
                top = jnp.maximum(
                    jnp.max(head, axis=0, keepdims=True), jnp.max(tail, axis=0, keepdims=True)
                )
                ph = jnp.exp(head - top)
                pt = jnp.exp(tail - top)
                total = jnp.sum(ph, axis=0, keepdims=True) + jnp.sum(pt, axis=0, keepdims=True)
                o = dot_nn(vt_s[h, :, 0 : i * rows], ph.astype(BF)) + dot_nn(
                    vt_s[h, :, i * rows : width], pt.astype(BF)
                )
            else:
                top = jnp.max(tail, axis=0, keepdims=True)
                pt = jnp.exp(tail - top)
                total = jnp.sum(pt, axis=0, keepdims=True)
                o = dot_nn(vt_s[h, :, 0:width], pt.astype(BF))
            outs.append(o / total)
            lse_ref[h, i * rows : (i + 1) * rows] = (top + jnp.log(total))[0]
        o_ref[i % groups, i // groups] = jnp.concatenate(outs, axis=0).T.astype(BF)


def attention_forward(q, kv):
    groups, chunks, rows, cols = q.shape
    seq = kv.shape[0]
    pairs = cols // 128
    return pl.pallas_call(
        forward_kernel,
        grid=(pairs,),
        in_specs=[
            pl.BlockSpec((groups, chunks, rows, 128), lambda p: (0, 0, 0, p)),
            pl.BlockSpec((seq, 256), lambda p: (0, p)),
        ],
        out_specs=[
            pl.BlockSpec((groups, chunks, rows, 128), lambda p: (0, 0, 0, p)),
            pl.BlockSpec((None, 2, seq), lambda p: (p, 0, 0)),
        ],
        out_shape=[
            jax.ShapeDtypeStruct(q.shape, BF),
            jax.ShapeDtypeStruct((pairs, 2, seq), F32),
        ],
        scratch_shapes=[pltpu.VMEM((2, DH, seq), BF)],
        compiler_params=pltpu.CompilerParams(vmem_limit_bytes=56 * 2**20),
    )(q, kv)


def backward_kernel(blk, q_ref, kv_ref, do_ref, o_ref, lse_ref, dq_ref, dkv_ref,
                    kt_s, acc_s, dqt_s, qp_s, dop_s, delta_s):
    groups, chunks, rows, _ = q_ref.shape
    seq = kv_ref.shape[0]
    n = groups * chunks
    for h in range(2):
        kt_s[h] = kv_ref[:, h * 128 : (h + 1) * 128].astype(F32).T[:DH].astype(BF)
    acc_s[...] = jnp.zeros_like(acc_s)
    for i in range(n):
        at = pl.ds(i * rows, rows)
        q = q_ref[i % groups, i // groups].astype(F32) * 0.125
        do = do_ref[i % groups, i // groups].astype(F32)
        o = o_ref[i % groups, i // groups].astype(F32)
        prod = (do * o).T
        zero = jnp.zeros((rows, DH), F32)
        for h in range(2):
            cut = slice(h * DH, (h + 1) * DH)
            qp_s[h, at] = jnp.concatenate([q[:, cut], zero], axis=1).astype(BF)
            dop_s[h, at] = jnp.concatenate([zero, do[:, cut]], axis=1).astype(BF)
            delta_s[h, at] = jnp.sum(prod[cut], axis=0)

    def block(i, j, masked):
        qat = pl.ds(pl.multiple_of(i * blk, blk), blk)
        kat = pl.ds(pl.multiple_of(j * blk, blk), blk)
        for h in range(2):
            kv = kv_ref[kat, h * 128 : (h + 1) * 128]
            qp = qp_s[h, qat]
            dop = dop_s[h, qat]
            s = dot_nt(kv, qp)
            dp = dot_nt(kv, dop)
            if masked:
                s = causal(s, 0, 0)
            p = jnp.exp(s - lse_ref[h : h + 1, qat])
            ds = (p * (dp - delta_s[h : h + 1, qat])).astype(BF)
            acc_s[h, kat] += dot_nn(p.astype(BF), dop) + dot_nn(ds, qp)
            part = dot_nn(kt_s[h, :, kat], ds)
            if masked:
                dqt_s[h * DH : (h + 1) * DH, qat] = part
            else:
                dqt_s[h * DH : (h + 1) * DH, qat] += part

    m = seq // blk

    def outer(i, _):
        block(i, i, True)

        def inner(j, _):
            block(i, j, False)
            return 0

        lax.fori_loop(0, i, inner, 0)
        return 0

    lax.fori_loop(0, m, outer, 0)
    for i in range(n):
        at = pl.ds(i * rows, rows)
        dq_ref[i % groups, i // groups] = (dqt_s[:, at].T * 0.125).astype(BF)
    for h in range(2):
        dkv_ref[:, h * 128 : (h + 1) * 128] = acc_s[h].astype(BF)


def attention_backward(q, kv, do, o, lse, blk=512):
    groups, chunks, rows, cols = q.shape
    seq = kv.shape[0]
    pairs = cols // 128
    tok = pl.BlockSpec((groups, chunks, rows, 128), lambda p: (0, 0, 0, p))
    return pl.pallas_call(
        functools.partial(backward_kernel, blk),
        grid=(pairs,),
        in_specs=[tok, pl.BlockSpec((seq, 256), lambda p: (0, p)), tok, tok,
                  pl.BlockSpec((None, 2, seq), lambda p: (p, 0, 0))],
        out_specs=[tok, pl.BlockSpec((seq, 256), lambda p: (0, p))],
        out_shape=[jax.ShapeDtypeStruct(q.shape, BF), jax.ShapeDtypeStruct(kv.shape, BF)],
        scratch_shapes=[
            pltpu.VMEM((2, DH, seq), BF),
            pltpu.VMEM((2, seq, 128), F32),
            pltpu.VMEM((128, seq), F32),
            pltpu.VMEM((2, seq, 128), BF),
            pltpu.VMEM((2, seq, 128), BF),
            pltpu.VMEM((2, seq), F32),
        ],
        compiler_params=pltpu.CompilerParams(vmem_limit_bytes=56 * 2**20),
    )(q, kv, do, o, lse)


HEADS = 16
KVH = 2
LATD = 256
HG = 8
GROUPS = 8
EPSILON = 1e-05
ALL = ("dp", "seq", "grp")


def norm_parts(values, gain):
    inverse = lax.rsqrt(jnp.mean(values * values, axis=-1, keepdims=True) + EPSILON)
    return (values * inverse * gain, inverse)


def norm_back(values, inverse, gain, upstream):
    scaled = upstream * gain
    gain_grad = jnp.sum(upstream * values * inverse, axis=0)
    input_part = inverse * scaled - values * inverse**3 * jnp.mean(
        scaled * values, axis=-1, keepdims=True
    )
    return (input_part, gain_grad)


def dot_tn(a, b):
    return lax.dot_general(a, b, (((0,), (0,)), ((), ())), preferred_element_type=F32)


def swap_sequences(blocks, count):
    if count == 2:
        me = lax.axis_index("seq")
        sent = lax.ppermute(blocks[1 - me], "seq", [(0, 1), (1, 0)])
        kept = blocks[me]
        first = me == 0
        return jnp.stack([jnp.where(first, kept, sent), jnp.where(first, sent, kept)])
    return lax.all_to_all(blocks, "seq", 0, 0, tiled=True)


def swap_group(blocks):
    return lax.all_to_all(blocks, "grp", 0, 0, tiled=True)


def local(
    inputs,
    cotangent,
    group_ids,
    group_scale,
    norm_gain,
    w_query,
    w_latent,
    expansion_weight,
    w_output,
    ffn_gain,
    w_gate,
    w_up,
    w_down,
):
    devices = lax.axis_size("dp") * lax.axis_size("seq") * lax.axis_size("grp")
    groups = lax.axis_size("grp")
    me = lax.axis_index("grp")
    seqs, rows, width = inputs.shape
    count = seqs * rows
    hidden_size = w_gate.shape[1]
    heads = HEADS // groups
    cols = heads * DH
    drows = width // devices

    gains = jnp.concatenate(
        [norm_gain[:, None], ffn_gain[:, None], jnp.zeros((drows, 126), BF)], axis=1
    )
    expand_rows = expansion_weight.reshape(drows, -1)
    attn_weights = jnp.concatenate([w_query, w_latent, w_output, expand_rows, gains], axis=1)
    attn_full = lax.all_gather(attn_weights, ALL, axis=0, tiled=True)
    ffn_full = lax.all_gather(jnp.concatenate([w_gate, w_up], axis=1), ALL, axis=0, tiled=True)
    down_full = lax.all_gather(w_down, ALL, axis=0, tiled=True)
    query_full = attn_full[:, :width]
    latent_full = attn_full[:, width : width + KVH * LATD]
    output_full = attn_full[:, width + KVH * LATD : 2 * width + KVH * LATD]
    ecols = expand_rows.shape[1]
    at = 2 * width + KVH * LATD
    expand_full = attn_full[:, at : at + ecols].reshape(devices, KVH, LATD // devices, -1)
    expand_full = expand_full.transpose(1, 0, 2, 3).reshape(KVH, LATD, -1)
    gain_one = attn_full[:, at + ecols].astype(F32)
    gain_two = attn_full[:, at + ecols + 1].astype(F32)
    gate_full = ffn_full[:, :hidden_size]
    up_full = ffn_full[:, hidden_size:]

    own_inputs = swap_sequences(inputs, seqs)
    own_cotangent = swap_sequences(cotangent, seqs)

    token_rows = own_inputs.astype(F32).reshape(count, width)
    normed, inverse_one = norm_parts(token_rows, gain_one)
    normed_low = normed.astype(BF)
    query_send = jnp.stack(
        [dot_nn(normed_low, query_full[:, j * cols : (j + 1) * cols]).astype(BF) for j in range(groups)]
    ).reshape(groups, seqs, rows, cols)
    latent_state = [
        dot_nn(normed_low, latent_full[:, g * LATD : (g + 1) * LATD]).astype(BF) for g in range(KVH)
    ]
    latent_send = jnp.stack([latent_state[j * heads // HG] for j in range(groups)]).reshape(
        groups, seqs, rows, LATD
    )
    head_queries = swap_group(query_send)
    head_latent = swap_group(latent_send).transpose(1, 0, 2, 3).reshape(-1, LATD)
    expand_local = lax.dynamic_slice(
        expand_full, (me * heads // HG, 0, me * heads % HG * 2 * DH), (1, LATD, heads * 2 * DH)
    )[0]
    head_pairs = dot_nn(head_latent, expand_local).astype(BF)
    attended, logsum = attention_forward(head_queries, head_pairs)
    token_attended = swap_group(attended).reshape(groups, count, cols)
    branch = sum(
        dot_nn(token_attended[j], output_full[j * cols : (j + 1) * cols]) for j in range(groups)
    )
    middle = token_rows + branch
    normed_two, inverse_two = norm_parts(middle, gain_two)
    normed_two_low = normed_two.astype(BF)
    gate_pre = dot_nn(normed_two_low, gate_full)
    upward = dot_nn(normed_two_low, up_full)
    sigmoid = jax.nn.sigmoid(gate_pre)
    activated = gate_pre * sigmoid
    hidden = (activated * upward).astype(BF)
    result = middle + dot_nn(hidden, down_full)
    output = swap_sequences(result.astype(BF).reshape(seqs, rows, width), seqs)

    seq_group = lax.dynamic_index_in_dim(group_ids, lax.axis_index("seq"), 0, keepdims=False)
    chosen = (seq_group == jnp.arange(GROUPS)).astype(F32)
    seq_scale = jnp.sum(chosen * group_scale)
    upstream = own_cotangent.astype(F32).reshape(count, width) * seq_scale
    upstream_low = upstream.astype(BF)
    down_grad = dot_tn(hidden, upstream_low)
    hidden_back = dot_nt(upstream_low, down_full)
    gate_back = (hidden_back * upward * sigmoid * (1.0 + gate_pre * (1.0 - sigmoid))).astype(BF)
    up_back = (hidden_back * activated).astype(BF)
    gate_grad = dot_tn(normed_two_low, gate_back)
    up_grad = dot_tn(normed_two_low, up_back)
    normed_two_back = dot_nt(gate_back, gate_full) + dot_nt(up_back, up_full)
    middle_part, gain_two_grad = norm_back(middle, inverse_two, gain_two, normed_two_back)
    middle_grad = upstream + middle_part
    ffn_share = lax.psum_scatter(
        jnp.concatenate([gate_grad.astype(BF), up_grad.astype(BF)], axis=1),
        ALL,
        scatter_dimension=0,
        tiled=True,
    ).astype(F32)
    down_share = lax.psum_scatter(
        down_grad.astype(BF), ALL, scatter_dimension=0, tiled=True
    ).astype(F32)

    branch_low = middle_grad.astype(BF)
    output_grad = jnp.concatenate(
        [dot_tn(token_attended[j], branch_low) for j in range(groups)], axis=0
    )
    back_send = jnp.stack(
        [
            dot_nt(branch_low, output_full[j * cols : (j + 1) * cols]).astype(BF)
            for j in range(groups)
        ]
    ).reshape(groups, seqs, rows, cols)
    head_upstream = swap_group(back_send)
    query_back, pair_back = attention_backward(
        head_queries, head_pairs, head_upstream, attended, logsum
    )
    latent_terms = dot_nt(pair_back, expand_local).astype(BF)
    expand_part = dot_tn(head_latent, pair_back)
    expand_grad = lax.dynamic_update_slice(
        jnp.zeros(expand_full.shape, F32),
        expand_part[None],
        (me * heads // HG, 0, me * heads % HG * 2 * DH),
    )
    query_token = swap_group(query_back).reshape(groups, count, cols)
    latent_token = swap_group(
        latent_terms.reshape(seqs, groups, rows, LATD).transpose(1, 0, 2, 3)
    ).reshape(KVH, groups // KVH, count, LATD)
    latent_token = jnp.sum(latent_token.astype(F32), axis=1).astype(BF)
    query_grad = jnp.concatenate([dot_tn(normed_low, query_token[j]) for j in range(groups)], axis=1)
    latent_grad = jnp.concatenate([dot_tn(normed_low, latent_token[g]) for g in range(KVH)], axis=1)
    normed_back = sum(
        dot_nt(query_token[j], query_full[:, j * cols : (j + 1) * cols]) for j in range(groups)
    ) + sum(
        dot_nt(latent_token[g], latent_full[:, g * LATD : (g + 1) * LATD]) for g in range(KVH)
    )
    input_part, gain_one_grad = norm_back(token_rows, inverse_one, gain_one, normed_back)
    input_grad = swap_sequences(
        (middle_grad + input_part).astype(BF).reshape(seqs, rows, width), seqs
    )
    expand_out = (
        expand_grad.astype(BF)
        .reshape(KVH, devices, LATD // devices, -1)
        .transpose(1, 0, 2, 3)
        .reshape(width, -1)
    )
    gain_grads = jnp.concatenate(
        [gain_one_grad[:, None], gain_two_grad[:, None], jnp.zeros((width, 126), F32)], axis=1
    )
    attn_share = lax.psum_scatter(
        jnp.concatenate(
            [
                query_grad.astype(BF),
                latent_grad.astype(BF),
                output_grad.astype(BF),
                expand_out,
                gain_grads.astype(BF),
            ],
            axis=1,
        ),
        ALL,
        scatter_dimension=0,
        tiled=True,
    ).astype(F32)
    return (
        output,
        input_grad,
        attn_share[:, at + ecols],
        attn_share[:, :width],
        attn_share[:, width : width + KVH * LATD],
        attn_share[:, at : at + ecols].reshape(expansion_weight.shape),
        attn_share[:, width + KVH * LATD : at],
        attn_share[:, at + ecols + 1],
        ffn_share[:, :hidden_size],
        ffn_share[:, hidden_size:],
        down_share,
    )


def solution(mesh):
    def run(*arrays):
        dp, sp = mesh.shape["dp"], mesh.shape["sp"]
        seqs = arrays[0].shape[0] // dp
        grid = Mesh(mesh.devices.reshape(dp, seqs, sp // seqs), ALL)
        tokens = P("dp", ("seq", "grp"), None)
        matrix = P(ALL, None)
        expand = P(None, ALL, None)
        return jax.shard_map(
            local,
            mesh=grid,
            in_specs=(
                tokens,
                tokens,
                P("dp"),
                P(),
                P(ALL),
                matrix,
                matrix,
                expand,
                matrix,
                P(ALL),
                matrix,
                matrix,
                matrix,
            ),
            out_specs=(
                tokens,
                tokens,
                P(ALL),
                matrix,
                matrix,
                expand,
                matrix,
                P(ALL),
                matrix,
                matrix,
                matrix,
            ),
            check_vma=False,
        )(*arrays)

    return run
```

```python
import functools
import jax
import jax.numpy as jnp
from jax import lax
from jax.sharding import Mesh
from jax.sharding import PartitionSpec as P
from jax.experimental import pallas as pl
from jax.experimental.pallas import tpu as pltpu

DH = 64
F32 = jnp.float32
BF = jnp.bfloat16


def cost(flops):
    return pl.CostEstimate(flops=flops, bytes_accessed=2**23, transcendentals=0)


def dot_nt(a, b):
    return lax.dot_general(a, b, (((1,), (1,)), ((), ())), preferred_element_type=F32)


def dot_nn(a, b):
    return lax.dot_general(a, b, (((1,), (0,)), ((), ())), preferred_element_type=F32)


def causal(s, first_key, first_query):
    keys = first_key + lax.broadcasted_iota(jnp.int32, s.shape, 0)
    rows = first_query + lax.broadcasted_iota(jnp.int32, s.shape, 1)
    return jnp.where(rows >= keys, s, -1e30)


def forward_kernel(q_ref, kv_ref, o_ref, lse_ref, vt_s):
    groups, chunks, rows, _ = q_ref.shape
    seq = kv_ref.shape[0]
    for h in range(2):
        vt_s[h] = kv_ref[:, h * 128 : (h + 1) * 128].astype(F32).T[DH:].astype(BF)
    for i in range(groups * chunks):
        q = q_ref[i % groups, i // groups].astype(F32) * 0.125
        outs = []
        for h in range(2):
            qh = q[:, h * DH : (h + 1) * DH]
            qp = jnp.concatenate([qh, jnp.zeros_like(qh)], axis=1).astype(BF)
            width = (i + 1) * rows
            s = dot_nt(kv_ref[0:width, h * 128 : (h + 1) * 128], qp)
            tail = causal(s[i * rows :], 0, 0)
            if i > 0:
                head = s[: i * rows]
                top = jnp.maximum(
                    jnp.max(head, axis=0, keepdims=True), jnp.max(tail, axis=0, keepdims=True)
                )
                ph = jnp.exp(head - top)
                pt = jnp.exp(tail - top)
                total = jnp.sum(ph, axis=0, keepdims=True) + jnp.sum(pt, axis=0, keepdims=True)
                o = dot_nn(vt_s[h, :, 0 : i * rows], ph.astype(BF)) + dot_nn(
                    vt_s[h, :, i * rows : width], pt.astype(BF)
                )
            else:
                top = jnp.max(tail, axis=0, keepdims=True)
                pt = jnp.exp(tail - top)
                total = jnp.sum(pt, axis=0, keepdims=True)
                o = dot_nn(vt_s[h, :, 0:width], pt.astype(BF))
            outs.append(o / total)
            lse_ref[h, i * rows : (i + 1) * rows] = (top + jnp.log(total))[0]
        o_ref[i % groups, i // groups] = jnp.concatenate(outs, axis=0).T.astype(BF)


def attention_forward(q, kv):
    groups, chunks, rows, cols = q.shape
    seq = kv.shape[0]
    pairs = cols // 128
    return pl.pallas_call(
        forward_kernel,
        grid=(pairs,),
        in_specs=[
            pl.BlockSpec((groups, chunks, rows, 128), lambda p: (0, 0, 0, p)),
            pl.BlockSpec((seq, 256), lambda p: (0, p)),
        ],
        out_specs=[
            pl.BlockSpec((groups, chunks, rows, 128), lambda p: (0, 0, 0, p)),
            pl.BlockSpec((None, 2, seq), lambda p: (p, 0, 0)),
        ],
        out_shape=[
            jax.ShapeDtypeStruct(q.shape, BF),
            jax.ShapeDtypeStruct((pairs, 2, seq), F32),
        ],
        scratch_shapes=[pltpu.VMEM((2, DH, seq), BF)],
        compiler_params=pltpu.CompilerParams(vmem_limit_bytes=56 * 2**20),
        cost_estimate=cost(8 * pairs * seq * seq * 128),
    )(q, kv)


def backward_kernel(blk, q_ref, kv_ref, do_ref, o_ref, lse_ref, dq_ref, dkv_ref,
                    kt_s, acc_s, dqt_s, qp_s, dop_s, delta_s):
    groups, chunks, rows, _ = q_ref.shape
    seq = kv_ref.shape[0]
    n = groups * chunks
    for h in range(2):
        kt_s[h] = kv_ref[:, h * 128 : (h + 1) * 128].astype(F32).T[:DH].astype(BF)
    acc_s[...] = jnp.zeros_like(acc_s)
    for i in range(n):
        at = pl.ds(i * rows, rows)
        q = q_ref[i % groups, i // groups].astype(F32) * 0.125
        do = do_ref[i % groups, i // groups].astype(F32)
        o = o_ref[i % groups, i // groups].astype(F32)
        prod = (do * o).T
        zero = jnp.zeros((rows, DH), F32)
        for h in range(2):
            cut = slice(h * DH, (h + 1) * DH)
            qp_s[h, at] = jnp.concatenate([q[:, cut], zero], axis=1).astype(BF)
            dop_s[h, at] = jnp.concatenate([zero, do[:, cut]], axis=1).astype(BF)
            delta_s[h, at] = jnp.sum(prod[cut], axis=0)

    def block(i, j, masked):
        qat = pl.ds(pl.multiple_of(i * blk, blk), blk)
        kat = pl.ds(pl.multiple_of(j * blk, blk), blk)
        for h in range(2):
            kv = kv_ref[kat, h * 128 : (h + 1) * 128]
            qp = qp_s[h, qat]
            dop = dop_s[h, qat]
            s = dot_nt(kv, qp)
            dp = dot_nt(kv, dop)
            if masked:
                s = causal(s, 0, 0)
            p = jnp.exp(s - lse_ref[h : h + 1, qat])
            ds = (p * (dp - delta_s[h : h + 1, qat])).astype(BF)
            acc_s[h, kat] += dot_nn(p.astype(BF), dop) + dot_nn(ds, qp)
            part = dot_nn(kt_s[h, :, kat], ds)
            if masked:
                dqt_s[h * DH : (h + 1) * DH, qat] = part
            else:
                dqt_s[h * DH : (h + 1) * DH, qat] += part

    m = seq // blk

    def outer(i, _):
        block(i, i, True)

        def inner(j, _):
            block(i, j, False)
            return 0

        lax.fori_loop(0, i, inner, 0)
        return 0

    lax.fori_loop(0, m, outer, 0)
    for i in range(n):
        at = pl.ds(i * rows, rows)
        dq_ref[i % groups, i // groups] = (dqt_s[:, at].T * 0.125).astype(BF)
    for h in range(2):
        dkv_ref[:, h * 128 : (h + 1) * 128] = acc_s[h].astype(BF)


def attention_backward(q, kv, do, o, lse, blk=512):
    groups, chunks, rows, cols = q.shape
    seq = kv.shape[0]
    pairs = cols // 128
    tok = pl.BlockSpec((groups, chunks, rows, 128), lambda p: (0, 0, 0, p))
    return pl.pallas_call(
        functools.partial(backward_kernel, blk),
        grid=(pairs,),
        in_specs=[tok, pl.BlockSpec((seq, 256), lambda p: (0, p)), tok, tok,
                  pl.BlockSpec((None, 2, seq), lambda p: (p, 0, 0))],
        out_specs=[tok, pl.BlockSpec((seq, 256), lambda p: (0, p))],
        out_shape=[jax.ShapeDtypeStruct(q.shape, BF), jax.ShapeDtypeStruct(kv.shape, BF)],
        scratch_shapes=[
            pltpu.VMEM((2, DH, seq), BF),
            pltpu.VMEM((2, seq, 128), F32),
            pltpu.VMEM((128, seq), F32),
            pltpu.VMEM((2, seq, 128), BF),
            pltpu.VMEM((2, seq, 128), BF),
            pltpu.VMEM((2, seq), F32),
        ],
        compiler_params=pltpu.CompilerParams(vmem_limit_bytes=56 * 2**20),
        cost_estimate=cost(16 * pairs * seq * seq * 128),
    )(q, kv, do, o, lse)


MESH = pl.DeviceIdType.MESH


def ring_place(dp, d, s):
    even = lax.rem(d, 2)
    p = d - even + lax.rem(even + lax.div(d, 2), 2)
    return p + s * (2 * dp - 1 - 2 * p)


def ring_device(dp, r):
    s = lax.div(r, dp)
    p = r + s * (2 * dp - 1 - 2 * r)
    even = lax.rem(p, 2)
    return p - even + lax.rem(even + lax.div(p, 2), 2), s


def greet(neighbours):
    barrier = pltpu.get_barrier_semaphore()
    for there in neighbours:
        pl.semaphore_signal(barrier, inc=1, device_id=there, device_id_type=MESH)
    pl.semaphore_wait(barrier, len(neighbours))


def remote(src, dst, send, recv, there):
    return pltpu.make_async_remote_copy(
        src_ref=src, dst_ref=dst, send_sem=send, recv_sem=recv, device_id=there, device_id_type=MESH
    )


def gather_kernel(dp, count, *refs):
    srcs, x_in = refs[:count], refs[count]
    outs, x_out = refs[count + 1 : 2 * count + 1], refs[2 * count + 1]
    ring_send, ring_recv, pair_send, pair_recv, own_sem, x_sem = refs[2 * count + 2 :]
    d, s, c = lax.axis_index("dp"), lax.axis_index("seq"), lax.axis_index("grp")
    n = 2 * dp
    r = ring_place(dp, d, s)
    right = (*ring_device(dp, lax.rem(r + 1, n)), c)
    left = (*ring_device(dp, lax.rem(r + n - 1, n)), c)
    pair = (d, s, 1 - c)
    across = (d, 1 - s, c)

    def place(at, core):
        dk, sk = ring_device(dp, lax.rem(at + n, n))
        return (dk * 2 + sk) * 2 + core

    greet((right, left, pair, across))
    swap = remote(x_in.at[1 - s], x_out.at[s], x_sem.at[0], x_sem.at[1], across)
    swap.start()
    mine = place(r, c)
    waits = []
    hops = (n // 2, n - 1 - n // 2)
    ways = (right, left)
    for a in range(count):
        for way in range(2):
            copy = remote(
                srcs[a], outs[a].at[mine], ring_send.at[way, 0, a], ring_recv.at[way, 0, a], ways[way]
            )
            copy.start()
            waits.append(copy)
        copy = remote(srcs[a], outs[a].at[mine], pair_send.at[0, a], pair_recv.at[0, a], pair)
        copy.start()
        waits.append(copy)
        kept = pltpu.make_async_copy(srcs[a], outs[a].at[mine], own_sem.at[a])
        kept.start()
        waits.append(kept)
    kept = pltpu.make_async_copy(x_in.at[s], x_out.at[s], x_sem.at[2])
    kept.start()
    slot = 1
    pairs_in = [(0, place(r, 1 - c))]
    for t in range(1, hops[0] + 1):
        for way in range(2):
            if t > hops[way]:
                continue
            at = place(r - t if way == 0 else r + t, c)
            other = place(r - t if way == 0 else r + t, 1 - c)
            for a in range(count):
                here = outs[a].at[at]
                remote(
                    here, here, ring_send.at[way, t - 1, a], ring_recv.at[way, t - 1, a], ways[way]
                ).wait_recv()
                if t < hops[way]:
                    copy = remote(
                        here, here, ring_send.at[way, t, a], ring_recv.at[way, t, a], ways[way]
                    )
                    copy.start()
                    waits.append(copy)
                copy = remote(here, here, pair_send.at[slot, a], pair_recv.at[slot, a], pair)
                copy.start()
                waits.append(copy)
            pairs_in.append((slot, other))
            slot += 1
    for number, other in pairs_in:
        for a in range(count):
            here = outs[a].at[other]
            remote(here, here, pair_send.at[number, a], pair_recv.at[number, a], pair).wait_recv()
    for copy in waits:
        if copy.is_remote:
            copy.wait_send()
        else:
            copy.wait()
    swap.wait()
    kept.wait()


def ring_gather(dp, shards, blocks):
    count = len(shards)
    n = 2 * dp
    anywhere = pl.BlockSpec(memory_space=pl.ANY)
    sem = pltpu.SemaphoreType.DMA
    out = pl.pallas_call(
        functools.partial(gather_kernel, dp, count),
        in_specs=[anywhere] * (count + 1),
        out_specs=[anywhere] * (count + 1),
        out_shape=[jax.ShapeDtypeStruct((2 * n, *w.shape), w.dtype) for w in shards]
        + [jax.ShapeDtypeStruct(blocks.shape, blocks.dtype)],
        scratch_shapes=[
            sem((2, n // 2, count)),
            sem((2, n // 2, count)),
            sem((n, count)),
            sem((n, count)),
            sem((count,)),
            sem((3,)),
        ],
        compiler_params=pltpu.CompilerParams(collective_id=0, has_side_effects=True),
    )(*shards, blocks)
    return out[:-1], out[-1]


def scatter_kernel(dp, ways_of, *refs):
    count = len(ways_of)
    terms, x_in = refs[:count], refs[count]
    outs, x_out = refs[count + 1 : 2 * count + 1], refs[2 * count + 1]
    rest = refs[2 * count + 2 :]
    pair_bufs, ring_bufs = rest[:count], rest[count : 2 * count]
    ring_send, ring_recv, pair_send, pair_recv, x_sem = rest[2 * count :]
    d, s, c = lax.axis_index("dp"), lax.axis_index("seq"), lax.axis_index("grp")
    n = 2 * dp
    r = ring_place(dp, d, s)
    right = (*ring_device(dp, lax.rem(r + 1, n)), c)
    left = (*ring_device(dp, lax.rem(r + n - 1, n)), c)
    pair = (d, s, 1 - c)
    across = (d, 1 - s, c)
    ways = (right, left)

    def place(t, way, core):
        at = r - 1 - t if way == 0 else r + 1 + t
        dk, sk = ring_device(dp, lax.rem(at + n, n))
        return (dk * 2 + sk) * 2 + core

    greet((right, left, pair, across))
    for t in range(n):
        for a in range(count):
            remote(
                terms[a].at[place(t, ways_of[a], 1 - c)],
                pair_bufs[a].at[t],
                pair_send.at[t, a],
                pair_recv.at[t, a],
                pair,
            ).start()
    swap = remote(x_in.at[1 - s], x_out.at[s], x_sem.at[0], x_sem.at[1], across)
    swap.start()
    kept = pltpu.make_async_copy(x_in.at[s], x_out.at[s], x_sem.at[2])
    kept.start()

    def pair_copy(t, a):
        return remote(
            terms[a].at[place(t, ways_of[a], 1 - c)],
            pair_bufs[a].at[t],
            pair_send.at[t, a],
            pair_recv.at[t, a],
            pair,
        )

    def ring_copy(t, a):
        src = pair_bufs[a].at[0] if t == 0 else ring_bufs[a].at[t - 1]
        return remote(
            src, ring_bufs[a].at[t], ring_send.at[t, a], ring_recv.at[t, a], ways[ways_of[a]]
        )

    for t in range(n):
        for a in range(count):
            pair_copy(t, a).wait_recv()
            total = terms[a][place(t, ways_of[a], c)].astype(F32) + pair_bufs[a][t].astype(F32)
            if t > 0:
                ring_copy(t - 1, a).wait_recv()
                total = total + ring_bufs[a][t - 1].astype(F32)
            if t == n - 1:
                outs[a][...] = total
            elif t == 0:
                pair_bufs[a][0] = total.astype(BF)
            else:
                ring_bufs[a][t - 1] = total.astype(BF)
            if t < n - 1:
                ring_copy(t, a).start()
    for t in range(n):
        for a in range(count):
            pair_copy(t, a).wait_send()
            if t < n - 1:
                ring_copy(t, a).wait_send()
    swap.wait()
    kept.wait()


def ring_scatter(dp, terms, ways_of, blocks):
    count = len(terms)
    n = 2 * dp
    anywhere = pl.BlockSpec(memory_space=pl.ANY)
    inside = pl.BlockSpec(memory_space=pltpu.VMEM)
    sem = pltpu.SemaphoreType.DMA
    out = pl.pallas_call(
        functools.partial(scatter_kernel, dp, ways_of),
        in_specs=[inside] * count + [anywhere],
        out_specs=[inside] * count + [anywhere],
        out_shape=[jax.ShapeDtypeStruct(w.shape[1:], F32) for w in terms]
        + [jax.ShapeDtypeStruct(blocks.shape, blocks.dtype)],
        scratch_shapes=[pltpu.VMEM((n, *w.shape[1:]), BF) for w in terms]
        + [pltpu.VMEM((n - 1, *w.shape[1:]), BF) for w in terms]
        + [sem((n - 1, count)), sem((n - 1, count)), sem((n, count)), sem((n, count)), sem((3,))],
        compiler_params=pltpu.CompilerParams(
            collective_id=1, has_side_effects=True, vmem_limit_bytes=48 * 2**20
        ),
    )(*terms, blocks)
    return out[:-1], out[-1]


HEADS = 16
KVH = 2
LATD = 256
HG = 8
GROUPS = 8
EPSILON = 1e-05
ALL = ("dp", "seq", "grp")


def norm_parts(values, gain):
    inverse = lax.rsqrt(jnp.mean(values * values, axis=-1, keepdims=True) + EPSILON)
    return (values * inverse * gain, inverse)


def norm_back(values, inverse, gain, upstream):
    scaled = upstream * gain
    gain_grad = jnp.sum(upstream * values * inverse, axis=0)
    input_part = inverse * scaled - values * inverse**3 * jnp.mean(
        scaled * values, axis=-1, keepdims=True
    )
    return (input_part, gain_grad)


def dot_tn(a, b):
    return lax.dot_general(a, b, (((0,), (0,)), ((), ())), preferred_element_type=F32)


def swap_sequences(blocks, count):
    if count == 2:
        me = lax.axis_index("seq")
        sent = lax.ppermute(blocks[1 - me], "seq", [(0, 1), (1, 0)])
        kept = blocks[me]
        first = me == 0
        return jnp.stack([jnp.where(first, kept, sent), jnp.where(first, sent, kept)])
    return lax.all_to_all(blocks, "seq", 0, 0, tiled=True)


def swap_group(blocks):
    return lax.all_to_all(blocks, "grp", 0, 0, tiled=True)


def local(
    inputs,
    cotangent,
    group_ids,
    group_scale,
    norm_gain,
    w_query,
    w_latent,
    expansion_weight,
    w_output,
    ffn_gain,
    w_gate,
    w_up,
    w_down,
):
    devices = lax.axis_size("dp") * lax.axis_size("seq") * lax.axis_size("grp")
    groups = lax.axis_size("grp")
    me = lax.axis_index("grp")
    seqs, rows, width = inputs.shape
    count = seqs * rows
    hidden_size = w_gate.shape[1]
    heads = HEADS // groups
    cols = heads * DH
    drows = width // devices

    dp = lax.axis_size("dp")
    ring = groups == 2 and seqs == 2 and dp % 2 == 0
    expand_rows = expansion_weight.reshape(-1, expansion_weight.shape[2])
    gains = jnp.pad(jnp.concatenate([norm_gain, ffn_gain])[None], ((0, 15), (0, 128 - 2 * drows)))
    shards = (w_query, w_latent, w_output, expand_rows, gains)
    if ring:
        full, own_inputs = ring_gather(dp, shards, inputs)
    else:
        full = [lax.all_gather(w, ALL, axis=0) for w in shards]
        own_inputs = swap_sequences(inputs, seqs)
    ffn_full = lax.all_gather(jnp.concatenate([w_gate, w_up], axis=1), ALL, axis=0, tiled=True)
    down_full = lax.all_gather(w_down, ALL, axis=0, tiled=True)
    query_full = full[0].reshape(width, -1)
    latent_full = full[1].reshape(width, -1)
    output_full = full[2].reshape(-1, width)
    expand_full = full[3].reshape(devices, KVH, LATD // devices, -1)
    gain_one = full[4][:, 0, :drows].reshape(width).astype(F32)
    gain_two = full[4][:, 0, drows : 2 * drows].reshape(width).astype(F32)
    gate_full = ffn_full[:, :hidden_size]
    up_full = ffn_full[:, hidden_size:]

    own_cotangent = swap_sequences(cotangent, seqs)

    token_rows = own_inputs.astype(F32).reshape(count, width)
    normed, inverse_one = norm_parts(token_rows, gain_one)
    normed_low = normed.astype(BF)
    query_send = jnp.stack(
        [dot_nn(normed_low, query_full[:, j * cols : (j + 1) * cols]).astype(BF) for j in range(groups)]
    ).reshape(groups, seqs, rows, cols)
    latent_state = [
        dot_nn(normed_low, latent_full[:, g * LATD : (g + 1) * LATD]).astype(BF) for g in range(KVH)
    ]
    latent_send = jnp.stack([latent_state[j * heads // HG] for j in range(groups)]).reshape(
        groups, seqs, rows, LATD
    )
    head_queries = swap_group(query_send)
    head_latent = swap_group(latent_send).transpose(1, 0, 2, 3).reshape(-1, LATD)
    expand_local = lax.dynamic_slice(
        expand_full,
        (0, me * heads // HG, 0, me * heads % HG * 2 * DH),
        (devices, 1, LATD // devices, heads * 2 * DH),
    ).reshape(LATD, -1)
    head_pairs = dot_nn(head_latent, expand_local).astype(BF)
    attended, logsum = attention_forward(head_queries, head_pairs)
    token_attended = swap_group(attended).reshape(groups, count, cols)
    branch = sum(
        dot_nn(token_attended[j], output_full[j * cols : (j + 1) * cols]) for j in range(groups)
    )
    middle = token_rows + branch
    normed_two, inverse_two = norm_parts(middle, gain_two)
    normed_two_low = normed_two.astype(BF)
    gate_pre = dot_nn(normed_two_low, gate_full)
    upward = dot_nn(normed_two_low, up_full)
    sigmoid = jax.nn.sigmoid(gate_pre)
    activated = gate_pre * sigmoid
    hidden = (activated * upward).astype(BF)
    result = middle + dot_nn(hidden, down_full)
    output = swap_sequences(result.astype(BF).reshape(seqs, rows, width), seqs)

    seq_group = lax.dynamic_index_in_dim(group_ids, lax.axis_index("seq"), 0, keepdims=False)
    chosen = (seq_group == jnp.arange(GROUPS)).astype(F32)
    seq_scale = jnp.sum(chosen * group_scale)
    upstream = own_cotangent.astype(F32).reshape(count, width) * seq_scale
    upstream_low = upstream.astype(BF)
    down_grad = dot_tn(hidden, upstream_low)
    hidden_back = dot_nt(upstream_low, down_full)
    gate_back = (hidden_back * upward * sigmoid * (1.0 + gate_pre * (1.0 - sigmoid))).astype(BF)
    up_back = (hidden_back * activated).astype(BF)
    gate_grad = dot_tn(normed_two_low, gate_back)
    up_grad = dot_tn(normed_two_low, up_back)
    normed_two_back = dot_nt(gate_back, gate_full) + dot_nt(up_back, up_full)
    middle_part, gain_two_grad = norm_back(middle, inverse_two, gain_two, normed_two_back)
    middle_grad = upstream + middle_part
    if ring:
        both = jnp.concatenate([gate_grad.astype(BF), up_grad.astype(BF)], axis=1).reshape(
            devices, drows, -1
        )
        whole = both.shape[2] // width * width
        half = drows // 2
        packed = jnp.concatenate(
            [both[:, :, a : a + width] for a in range(0, whole, width)]
            + [
                jnp.concatenate([both[:, :half, whole:], both[:, half:, whole:]], axis=2),
                down_grad.astype(BF).reshape(devices, -1, width),
            ],
            axis=1,
        )
        share = lax.psum_scatter(packed, ALL, scatter_dimension=0, tiled=True)[0].astype(F32)
        tall = whole // width * drows
        tail = share[tall : tall + half]
        ffn_share = jnp.concatenate(
            [share[a : a + drows] for a in range(0, tall, drows)]
            + [jnp.concatenate([tail[:, : width // 2], tail[:, width // 2 :]], axis=0)],
            axis=1,
        )
        down_share = share[tall + half :]
    else:
        ffn_share = lax.psum_scatter(
            jnp.concatenate([gate_grad.astype(BF), up_grad.astype(BF)], axis=1),
            ALL,
            scatter_dimension=0,
            tiled=True,
        ).astype(F32)
        down_share = lax.psum_scatter(
            down_grad.astype(BF), ALL, scatter_dimension=0, tiled=True
        ).astype(F32)

    branch_low = middle_grad.astype(BF)
    output_grad = jnp.concatenate(
        [dot_tn(token_attended[j], branch_low) for j in range(groups)], axis=0
    )
    back_send = jnp.stack(
        [
            dot_nt(branch_low, output_full[j * cols : (j + 1) * cols]).astype(BF)
            for j in range(groups)
        ]
    ).reshape(groups, seqs, rows, cols)
    head_upstream = swap_group(back_send)
    query_back, pair_back = attention_backward(
        head_queries, head_pairs, head_upstream, attended, logsum
    )
    latent_terms = dot_nt(pair_back, expand_local).astype(BF)
    expand_part = dot_tn(head_latent, pair_back)
    expand_grad = lax.dynamic_update_slice(
        jnp.zeros(expand_full.shape, BF),
        expand_part.astype(BF).reshape(devices, 1, LATD // devices, -1),
        (0, me * heads // HG, 0, me * heads % HG * 2 * DH),
    )
    query_token = swap_group(query_back).reshape(groups, count, cols)
    latent_token = swap_group(
        latent_terms.reshape(seqs, groups, rows, LATD).transpose(1, 0, 2, 3)
    ).reshape(KVH, groups // KVH, count, LATD)
    latent_token = jnp.sum(latent_token.astype(F32), axis=1).astype(BF)
    query_grad = jnp.concatenate([dot_tn(normed_low, query_token[j]) for j in range(groups)], axis=1)
    latent_grad = jnp.concatenate([dot_tn(normed_low, latent_token[g]) for g in range(KVH)], axis=1)
    normed_back = sum(
        dot_nt(query_token[j], query_full[:, j * cols : (j + 1) * cols]) for j in range(groups)
    ) + sum(
        dot_nt(latent_token[g], latent_full[:, g * LATD : (g + 1) * LATD]) for g in range(KVH)
    )
    input_part, gain_one_grad = norm_back(token_rows, inverse_one, gain_one, normed_back)
    own_input_grad = (middle_grad + input_part).astype(BF).reshape(seqs, rows, width)
    gain_grads = jnp.concatenate(
        [gain_one_grad.reshape(devices, 1, drows), gain_two_grad.reshape(devices, 1, drows)], axis=2
    ).astype(BF)
    gain_grads = jnp.pad(gain_grads, ((0, 0), (0, 15), (0, 128 - 2 * drows)))
    terms = (
        query_grad.astype(BF).reshape(devices, drows, -1),
        latent_grad.astype(BF).reshape(devices, drows, -1),
        output_grad.astype(BF).reshape(devices, drows, -1),
        expand_grad.reshape(devices, -1, expand_grad.shape[3]),
        gain_grads,
    )
    if ring:
        half = drows // 2
        sums, input_grad = ring_scatter(
            dp,
            (terms[0], terms[2][:, :half], terms[2][:, half:], terms[1], terms[3], terms[4]),
            (0, 0, 1, 1, 1, 1),
            own_input_grad,
        )
        sums = (sums[0], sums[3], jnp.concatenate(sums[1:3], axis=0), sums[4], sums[5])
    else:
        sums = [
            lax.psum_scatter(w, ALL, scatter_dimension=0, tiled=True)[0].astype(F32) for w in terms
        ]
        input_grad = swap_sequences(own_input_grad, seqs)
    return (
        output,
        input_grad,
        sums[4][0, :drows],
        sums[0],
        sums[1],
        sums[3].reshape(expansion_weight.shape),
        sums[2],
        sums[4][0, drows : 2 * drows],
        ffn_share[:, :hidden_size],
        ffn_share[:, hidden_size:],
        down_share,
    )


def solution(mesh):
    def run(*arrays):
        dp, sp = mesh.shape["dp"], mesh.shape["sp"]
        seqs = arrays[0].shape[0] // dp
        grid = Mesh(mesh.devices.reshape(dp, seqs, sp // seqs), ALL)
        tokens = P("dp", ("seq", "grp"), None)
        matrix = P(ALL, None)
        expand = P(None, ALL, None)
        return jax.shard_map(
            local,
            mesh=grid,
            in_specs=(
                tokens,
                tokens,
                P("dp"),
                P(),
                P(ALL),
                matrix,
                matrix,
                expand,
                matrix,
                P(ALL),
                matrix,
                matrix,
                matrix,
            ),
            out_specs=(
                tokens,
                tokens,
                P(ALL),
                matrix,
                matrix,
                expand,
                matrix,
                P(ALL),
                matrix,
                matrix,
                matrix,
            ),
            check_vma=False,
        )(*arrays)

    return run
```

```python
import functools
import jax
import jax.numpy as jnp
from jax import lax
from jax.sharding import Mesh
from jax.sharding import PartitionSpec as P
from jax.experimental import pallas as pl
from jax.experimental.pallas import tpu as pltpu

DH = 64
F32 = jnp.float32
BF = jnp.bfloat16


def cost(flops):
    return pl.CostEstimate(flops=flops, bytes_accessed=2**23, transcendentals=0)


MESH = pl.DeviceIdType.MESH


class Place:

    def __init__(self, dp):
        self.sizes = {"x": 2, "y": 2, "z": dp // 2}
        d = lax.axis_index("dp")
        self.at = {"x": lax.axis_index("seq"), "y": lax.rem(d, 2), "z": lax.div(d, 2)}
        self.core = lax.axis_index("grp")

    def coords(self, offset):
        at = {k: lax.rem(self.at[k] + o, self.sizes[k]) if o else self.at[k] for k, o in offset.items()}
        return at["z"] * 2 + at["y"], at["x"]

    def index(self, offset, other):
        d, s = self.coords(offset)
        core = 1 - self.core if other else self.core
        return (d * 2 + s) * 2 + core

    def device(self, offset):
        return (*self.coords(offset), self.core)

    def pair(self):
        return (*self.coords({"x": 0, "y": 0, "z": 0}), 1 - self.core)

    def greet(self):
        there = [self.pair()]
        for k in "xyz":
            for o in range(1, self.sizes[k]):
                there.append(self.device({"x": 0, "y": 0, "z": 0, k: o}))
        barrier = pltpu.get_barrier_semaphore()
        for device in there:
            pl.semaphore_signal(barrier, inc=1, device_id=device, device_id_type=MESH)
        pl.semaphore_wait(barrier, len(there))


def offsets_of(order, dp):
    sizes = {"x": 2, "y": 2, "z": dp // 2}
    a, b, c = (sizes[k] for k in order)
    return [(i, j, k) for i in range(a) for j in range(b) for k in range(c)]


def named(order, steps):
    return dict(zip(order, steps))


def remote(src, dst, send, recv, there):
    return pltpu.make_async_remote_copy(
        src_ref=src, dst_ref=dst, send_sem=send, recv_sem=recv, device_id=there, device_id_type=MESH
    )


class Gather:

    def __init__(self, place, dp, order, src, out, sems, number):
        self.place, self.order, self.src, self.out = place, order, src, out
        self.steps = offsets_of(order, dp)
        self.sems, self.number = sems, number

    def slot(self, steps, other=False):
        return self.out(self.place.index(named(self.order, steps), other))

    def source(self, steps):
        last = max(i for i in range(3) if steps[i])
        return tuple(0 if i == last else o for i, o in enumerate(steps))

    def hop(self, steps):
        last = max(i for i in range(3) if steps[i])
        source = self.source(steps)
        size = self.place.sizes[self.order[last]]
        back = tuple(size - o if i == last else 0 for i, o in enumerate(steps))
        number = self.steps.index(steps)
        here = self.slot(source)
        src = here if any(source) else self.src
        return remote(
            src,
            here,
            self.sems[0].at[self.number, number],
            self.sems[1].at[self.number, number],
            self.place.device(named(self.order, back)),
        )

    def across(self, steps):
        number = self.steps.index(steps)
        src = self.slot(steps) if any(steps) else self.src
        return remote(
            src,
            self.slot(steps),
            self.sems[2].at[self.number, number],
            self.sems[3].at[self.number, number],
            self.place.pair(),
        )

    def keep(self):
        return pltpu.make_async_copy(self.src, self.slot((0, 0, 0)), self.sems[4].at[self.number])

    def send_from(self, source):
        for steps in self.steps:
            if any(steps) and self.source(steps) == source:
                self.hop(steps).start()
        self.across(source).start()

    def start(self):
        self.send_from((0, 0, 0))
        self.keep().start()

    def arrivals(self):
        return sorted((s for s in self.steps if any(s)), key=lambda s: [o > 0 for o in s][::-1])

    def forward(self, steps):
        number = self.steps.index(steps)
        here = self.slot(steps)
        remote(
            here,
            here,
            self.sems[0].at[self.number, number],
            self.sems[1].at[self.number, number],
            self.place.pair(),
        ).wait_recv()
        self.send_from(steps)

    def finish(self):
        for steps in self.steps:
            number = self.steps.index(steps)
            here = self.slot(steps, True)
            remote(
                here,
                here,
                self.sems[2].at[self.number, number],
                self.sems[3].at[self.number, number],
                self.place.pair(),
            ).wait_recv()
            self.across(steps).wait_send()
            if any(steps):
                self.hop(steps).wait_send()
        self.keep().wait()


class Scatter:

    def __init__(self, place, dp, order, term, pair_buf, ring_buf, sems, number, own=None):
        self.place, self.order, self.term = place, order, term
        self.own_buf, self.own_sem = own if own else (None, None)
        self.steps = offsets_of(order, dp)
        self.pair_buf, self.ring_buf = pair_buf, ring_buf
        self.sems, self.number = sems, number

    def turn(self):
        def key(steps):
            first = next((i for i in range(3) if steps[i]), 3)
            return (first, [o == 0 for o in steps])

        return sorted(self.steps, key=key)

    def across(self, steps):
        number = self.steps.index(steps)
        return remote(
            self.term(self.place.index(named(self.order, steps), True)),
            self.pair_buf.at[number],
            self.sems[2].at[self.number, number],
            self.sems[3].at[self.number, number],
            self.place.pair(),
        )

    def fetch(self, steps):
        number = self.steps.index(steps)
        return pltpu.make_async_copy(
            self.term(self.place.index(named(self.order, steps), False)),
            self.own_buf.at[number],
            self.own_sem.at[self.number, number],
        )

    def start(self):
        for steps in self.turn():
            self.across(steps).start()
            if self.own_buf is not None:
                self.fetch(steps).start()

    def hop(self, steps):
        first = min(i for i in range(3) if steps[i])
        there = tuple(o if i == first else 0 for i, o in enumerate(steps))
        number = self.steps.index(steps)
        return remote(
            self.pair_buf.at[number],
            self.ring_buf.at[number],
            self.sems[0].at[self.number, number],
            self.sems[1].at[self.number, number],
            self.place.device(named(self.order, there)),
        )

    def add(self, steps, out=None):
        number = self.steps.index(steps)
        self.across(steps).wait_recv()
        if self.own_buf is None:
            mine = self.term(self.place.index(named(self.order, steps), False))
        else:
            self.fetch(steps).wait()
            mine = self.own_buf.at[number]
        total = mine[...].astype(F32) + self.pair_buf[number].astype(F32)
        for came in self.steps:
            if not any(came):
                continue
            first = min(i for i in range(3) if came[i])
            if tuple(0 if i == first else o for i, o in enumerate(came)) == steps:
                self.hop(came).wait_recv()
                total = total + self.ring_buf[self.steps.index(came)].astype(F32)
        if out is None:
            self.pair_buf[number] = total.astype(BF)
            self.hop(steps).start()
        else:
            out[...] = total

    def finish(self):
        for steps in self.steps:
            self.across(steps).wait_send()
            if any(steps):
                self.hop(steps).wait_send()


def block_swap(x_in, x_out, sem, place):
    s = place.at["x"]
    away = remote(
        x_in.at[1 - s], x_out.at[s], sem.at[0], sem.at[1], place.device({"x": 1, "y": 0, "z": 0})
    )
    return away, pltpu.make_async_copy(x_in.at[s], x_out.at[s], sem.at[2])


def gather_kernel(dp, orders, *refs):
    count = len(orders)
    srcs, x_in = refs[:count], refs[count]
    outs, x_out = refs[count + 1 : 2 * count + 1], refs[2 * count + 1]
    sems, x_sem = refs[2 * count + 2 : -1], refs[-1]
    place = Place(dp)
    place.greet()
    works = [
        Gather(place, dp, orders[a], srcs[a], lambda at, a=a: outs[a].at[at], sems, a)
        for a in range(count)
    ]
    for work in works:
        work.start()
    swap, kept = block_swap(x_in, x_out, x_sem, place)
    swap.start()
    kept.start()
    for i in range(2 * dp - 1):
        for work in works:
            work.forward(work.arrivals()[i])
    for work in works:
        work.finish()
    swap.wait()
    kept.wait()


def gather_sems(dp, count):
    sem = pltpu.SemaphoreType.DMA
    return [sem((count, 2 * dp))] * 4 + [sem((count,))]


def own_gather(dp, shards, blocks, orders):
    count = len(shards)
    anywhere = pl.BlockSpec(memory_space=pl.ANY)
    out = pl.pallas_call(
        functools.partial(gather_kernel, dp, orders),
        in_specs=[anywhere] * (count + 1),
        out_specs=[anywhere] * (count + 1),
        out_shape=[jax.ShapeDtypeStruct((4 * dp, *w.shape), w.dtype) for w in shards]
        + [jax.ShapeDtypeStruct(blocks.shape, blocks.dtype)],
        scratch_shapes=gather_sems(dp, count) + [pltpu.SemaphoreType.DMA((3,))],
        compiler_params=pltpu.CompilerParams(collective_id=0, has_side_effects=True),
    )(*shards, blocks)
    return out[:-1], out[-1]


def scatter_kernel(dp, orders, late, *refs):
    count = len(orders)
    terms, x_in = refs[:count], refs[count]
    outs, x_out = refs[count + 1 : 2 * count + 1], refs[2 * count + 1]
    rest = refs[2 * count + 2 :]
    pair_bufs, ring_bufs = rest[:count], rest[count : 2 * count]
    sems, x_sem = rest[2 * count : -1], rest[-1]
    place = Place(dp)
    place.greet()
    works = [
        Scatter(
            place, dp, orders[a], lambda at, a=a: terms[a].at[at], pair_bufs[a], ring_bufs[a], sems, a
        )
        for a in range(count)
    ]
    swap, kept = block_swap(x_in, x_out, x_sem, place)
    for work in works:
        work.start()
    turns = [work.turn() for work in works]
    for i in range(len(turns[0])):
        if i == late:
            swap.start()
            kept.start()
        for a in range(count):
            works[a].add(turns[a][i], outs[a] if i == len(turns[0]) - 1 else None)
    for work in works:
        work.finish()
    swap.wait()
    kept.wait()


def scatter_sems(dp, count):
    return [pltpu.SemaphoreType.DMA((count, 2 * dp))] * 4


def own_scatter(dp, terms, orders, blocks, late=0):
    count = len(terms)
    anywhere = pl.BlockSpec(memory_space=pl.ANY)
    inside = pl.BlockSpec(memory_space=pltpu.VMEM)
    out = pl.pallas_call(
        functools.partial(scatter_kernel, dp, orders, late),
        in_specs=[inside] * count + [anywhere],
        out_specs=[inside] * count + [anywhere],
        out_shape=[jax.ShapeDtypeStruct(w.shape[1:], F32) for w in terms]
        + [jax.ShapeDtypeStruct(blocks.shape, blocks.dtype)],
        scratch_shapes=[pltpu.VMEM((2 * dp, *w.shape[1:]), BF) for w in terms] * 2
        + scatter_sems(dp, count)
        + [pltpu.SemaphoreType.DMA((3,))],
        compiler_params=pltpu.CompilerParams(
            collective_id=1, has_side_effects=True, vmem_limit_bytes=48 * 2**20
        ),
    )(*terms, blocks)
    return out[:-1], out[-1]


def run_at(plan, point):
    for step in sorted({k[0] for k in plan if k[1] == point}):
        tasks = plan[step, point]

        @pl.when(pl.program_id(0) == step)
        def _(tasks=tasks):
            for task in tasks:
                task()


def gather_plan(place, works, swap, steps, points):
    arrivals = [work.arrivals() for work in works]
    total = steps * points

    def begin():
        place.greet()
        for work in works:
            work.start()
        for copy in swap:
            copy.start()

    def forward(i):
        for work, order in zip(works, arrivals):
            work.forward(order[i])

    def end():
        for work in works:
            work.finish()
        for copy in swap:
            copy.wait()

    plan = {}
    count = len(arrivals[0])
    plan[0, 0] = [begin]
    for i in range(count):
        at = 2 + i * (total - 3) // count
        plan.setdefault(divmod(at, points), []).append(functools.partial(forward, i))
    plan.setdefault(divmod(total, points), []).append(end)
    return plan


def scatter_plan(place, works, outs, swap, steps, points):
    turns = [work.turn() for work in works]
    total = steps * points
    count = len(turns[0])

    def begin():
        place.greet()
        for work in works:
            work.start()
        for copy in swap:
            copy.start()

    def add(i):
        for work, order, out in zip(works, turns, outs):
            work.add(order[i], out if i == count - 1 else None)

    def end():
        for work in works:
            work.finish()
        for copy in swap:
            copy.wait()

    plan = {(0, 0): [begin]}
    for i in range(count):
        at = 1 + i // 2 if i < count // 2 else 6 + (i - count // 2) * (total - 6) // (count - count // 2)
        plan.setdefault(divmod(at, points), []).append(functools.partial(add, i))
    plan.setdefault(divmod(total, points), []).append(end)
    return plan


def dot_nt(a, b):
    return lax.dot_general(a, b, (((1,), (1,)), ((), ())), preferred_element_type=F32)


def dot_nn(a, b):
    return lax.dot_general(a, b, (((1,), (0,)), ((), ())), preferred_element_type=F32)


def causal(s, first_key, first_query):
    keys = first_key + lax.broadcasted_iota(jnp.int32, s.shape, 0)
    rows = first_query + lax.broadcasted_iota(jnp.int32, s.shape, 1)
    return jnp.where(rows >= keys, s, -1e30)


def forward_body(q_ref, kv_ref, o_ref, lse_ref, vt_s, point=lambda i: None):
    groups, chunks, rows, _ = q_ref.shape
    seq = kv_ref.shape[0]
    for h in range(2):
        vt_s[h] = kv_ref[:, h * 128 : (h + 1) * 128].astype(F32).T[DH:].astype(BF)
    for i in range(groups * chunks):
        point(i)
        q = q_ref[i % groups, i // groups].astype(F32) * 0.125
        outs = []
        for h in range(2):
            qh = q[:, h * DH : (h + 1) * DH]
            qp = jnp.concatenate([qh, jnp.zeros_like(qh)], axis=1).astype(BF)
            width = (i + 1) * rows
            s = dot_nt(kv_ref[0:width, h * 128 : (h + 1) * 128], qp)
            tail = causal(s[i * rows :], 0, 0)
            if i > 0:
                head = s[: i * rows]
                top = jnp.maximum(
                    jnp.max(head, axis=0, keepdims=True), jnp.max(tail, axis=0, keepdims=True)
                )
                ph = jnp.exp(head - top)
                pt = jnp.exp(tail - top)
                total = jnp.sum(ph, axis=0, keepdims=True) + jnp.sum(pt, axis=0, keepdims=True)
                o = dot_nn(vt_s[h, :, 0 : i * rows], ph.astype(BF)) + dot_nn(
                    vt_s[h, :, i * rows : width], pt.astype(BF)
                )
            else:
                top = jnp.max(tail, axis=0, keepdims=True)
                pt = jnp.exp(tail - top)
                total = jnp.sum(pt, axis=0, keepdims=True)
                o = dot_nn(vt_s[h, :, 0:width], pt.astype(BF))
            outs.append(o / total)
            lse_ref[h, i * rows : (i + 1) * rows] = (top + jnp.log(total))[0]
        o_ref[i % groups, i // groups] = jnp.concatenate(outs, axis=0).T.astype(BF)


def forward_kernel(q_ref, kv_ref, o_ref, lse_ref, vt_s):
    forward_body(q_ref, kv_ref, o_ref, lse_ref, vt_s)


def forward_gather_kernel(dp, cuts, orders, pairs, *refs):
    q_ref, kv_ref, x_in = refs[:3]
    sources = 1 + max(cut[0] for cut in cuts)
    srcs, refs = refs[3 : 3 + sources], refs[3 + sources :]
    o_ref, lse_ref, x_out = refs[:3]
    outs, refs = refs[3 : 3 + sources], refs[3 + sources :]
    vt_s, x_sem, sems = refs[0], refs[1], refs[2:]
    place = Place(dp)
    works = []
    for number, (a, first, size) in enumerate(cuts):
        cut = pl.ds(first, size)
        works.append(
            Gather(
                place,
                dp,
                orders[number],
                srcs[a].at[:, cut],
                lambda at, a=a, cut=cut: outs[a].at[at, :, cut],
                sems,
                number,
            )
        )
    points = q_ref.shape[0] * q_ref.shape[1]
    plan = gather_plan(place, works, block_swap(x_in, x_out, x_sem, place), pairs, points)
    forward_body(q_ref, kv_ref, o_ref, lse_ref, vt_s, lambda i: run_at(plan, i))
    for point in range(points):
        tasks = plan.get((pairs, point))
        if tasks:

            @pl.when(pl.program_id(0) == pairs - 1)
            def _(tasks=tasks):
                for task in tasks:
                    task()


def forward_specs(q, kv):
    groups, chunks, rows, cols = q.shape
    seq = kv.shape[0]
    pairs = cols // 128
    tok = pl.BlockSpec((groups, chunks, rows, 128), lambda p: (0, 0, 0, p))
    ins = [tok, pl.BlockSpec((seq, 256), lambda p: (0, p))]
    outs = [tok, pl.BlockSpec((None, 2, seq), lambda p: (p, 0, 0))]
    shapes = [jax.ShapeDtypeStruct(q.shape, BF), jax.ShapeDtypeStruct((pairs, 2, seq), F32)]
    scratch = [pltpu.VMEM((2, DH, seq), BF)]
    return pairs, ins, outs, shapes, scratch, cost(8 * pairs * seq * seq * 128)


def attention_forward(q, kv):
    pairs, ins, outs, shapes, scratch, estimate = forward_specs(q, kv)
    return pl.pallas_call(
        forward_kernel,
        grid=(pairs,),
        in_specs=ins,
        out_specs=outs,
        out_shape=shapes,
        scratch_shapes=scratch,
        compiler_params=pltpu.CompilerParams(vmem_limit_bytes=56 * 2**20),
        cost_estimate=estimate,
    )(q, kv)


def attention_forward_gather(dp, q, kv, blocks, shards, cuts, orders):
    pairs, ins, outs, shapes, scratch, estimate = forward_specs(q, kv)
    anywhere = pl.BlockSpec(memory_space=pl.ANY)
    count = len(shards)
    return pl.pallas_call(
        functools.partial(forward_gather_kernel, dp, cuts, orders, pairs),
        grid=(pairs,),
        in_specs=ins + [anywhere] * (1 + count),
        out_specs=outs + [anywhere] * (1 + count),
        out_shape=shapes
        + [jax.ShapeDtypeStruct(blocks.shape, blocks.dtype)]
        + [jax.ShapeDtypeStruct((4 * dp, *w.shape), w.dtype) for w in shards],
        scratch_shapes=scratch + [pltpu.SemaphoreType.DMA((3,))] + gather_sems(dp, len(cuts)),
        compiler_params=pltpu.CompilerParams(
            vmem_limit_bytes=56 * 2**20, collective_id=2, has_side_effects=True
        ),
        cost_estimate=estimate,
    )(q, kv, blocks, *shards)


def backward_body(blk, q_ref, kv_ref, do_ref, o_ref, lse_ref, dq_ref, dkv_ref,
                  kt_s, acc_s, dqt_s, qp_s, dop_s, delta_s, point=lambda i: None):
    groups, chunks, rows, _ = q_ref.shape
    seq = kv_ref.shape[0]
    n = groups * chunks
    for h in range(2):
        kt_s[h] = kv_ref[:, h * 128 : (h + 1) * 128].astype(F32).T[:DH].astype(BF)
    acc_s[...] = jnp.zeros_like(acc_s)
    for i in range(n):
        at = pl.ds(i * rows, rows)
        q = q_ref[i % groups, i // groups].astype(F32) * 0.125
        do = do_ref[i % groups, i // groups].astype(F32)
        o = o_ref[i % groups, i // groups].astype(F32)
        prod = (do * o).T
        zero = jnp.zeros((rows, DH), F32)
        for h in range(2):
            cut = slice(h * DH, (h + 1) * DH)
            qp_s[h, at] = jnp.concatenate([q[:, cut], zero], axis=1).astype(BF)
            dop_s[h, at] = jnp.concatenate([zero, do[:, cut]], axis=1).astype(BF)
            delta_s[h, at] = jnp.sum(prod[cut], axis=0)

    def block(i, j, masked):
        qat = pl.ds(i * blk, blk)
        kat = pl.ds(pl.multiple_of(j * blk, blk), blk)
        for h in range(2):
            kv = kv_ref[kat, h * 128 : (h + 1) * 128]
            qp = qp_s[h, qat]
            dop = dop_s[h, qat]
            s = dot_nt(kv, qp)
            dp = dot_nt(kv, dop)
            if masked:
                s = causal(s, 0, 0)
            p = jnp.exp(s - lse_ref[h : h + 1, qat])
            ds = (p * (dp - delta_s[h : h + 1, qat])).astype(BF)
            acc_s[h, kat] += dot_nn(p.astype(BF), dop) + dot_nn(ds, qp)
            part = dot_nn(kt_s[h, :, kat], ds)
            if masked:
                dqt_s[h * DH : (h + 1) * DH, qat] = part
            else:
                dqt_s[h * DH : (h + 1) * DH, qat] += part

    m = seq // blk

    for i in range(m):
        point(i)
        block(i, i, True)

        def inner(j, _, i=i):
            block(i, j, False)
            return 0

        lax.fori_loop(0, i, inner, 0)
    for i in range(n):
        at = pl.ds(i * rows, rows)
        dq_ref[i % groups, i // groups] = (dqt_s[:, at].T * 0.125).astype(BF)
    for h in range(2):
        dkv_ref[:, h * 128 : (h + 1) * 128] = acc_s[h].astype(BF)


def backward_kernel(blk, *refs):
    backward_body(blk, *refs)


def backward_scatter_kernel(dp, blk, cuts, orders, pairs, *refs):
    ins, x_in, refs = refs[:5], refs[5], refs[6:]
    sources = 1 + max(cut[0] for cut in cuts)
    count = len(cuts)
    terms, refs = refs[:sources], refs[sources:]
    attn_outs, x_out, refs = refs[:2], refs[2], refs[3:]
    outs, refs = refs[:sources], refs[sources:]
    scratch, x_sem, refs = refs[:6], refs[6], refs[7:]
    own_bufs, pair_bufs, ring_bufs = refs[:count], refs[count : 2 * count], refs[2 * count : 3 * count]
    own_sem, sems = refs[3 * count], refs[3 * count + 1 :]
    place = Place(dp)
    works, targets = [], []
    for number, (a, first, size) in enumerate(cuts):
        cut = pl.ds(first, size)
        works.append(
            Scatter(
                place,
                dp,
                orders[number],
                lambda at, a=a, cut=cut: terms[a].at[at, :, cut],
                pair_bufs[number],
                ring_bufs[number],
                sems,
                number,
                (own_bufs[number], own_sem),
            )
        )
        targets.append(outs[a].at[:, cut])
    points = ins[1].shape[0] // blk
    plan = scatter_plan(place, works, targets, block_swap(x_in, x_out, x_sem, place), pairs, points)
    backward_body(blk, *ins, *attn_outs, *scratch, point=lambda i: run_at(plan, i))
    for point in range(points):
        tasks = plan.get((pairs, point))
        if tasks:

            @pl.when(pl.program_id(0) == pairs - 1)
            def _(tasks=tasks):
                for task in tasks:
                    task()


def backward_specs(q, kv):
    groups, chunks, rows, cols = q.shape
    seq = kv.shape[0]
    pairs = cols // 128
    tok = pl.BlockSpec((groups, chunks, rows, 128), lambda p: (0, 0, 0, p))
    wide = pl.BlockSpec((seq, 256), lambda p: (0, p))
    ins = [tok, wide, tok, tok, pl.BlockSpec((None, 2, seq), lambda p: (p, 0, 0))]
    outs = [tok, wide]
    shapes = [jax.ShapeDtypeStruct(q.shape, BF), jax.ShapeDtypeStruct(kv.shape, BF)]
    scratch = [
        pltpu.VMEM((2, DH, seq), BF),
        pltpu.VMEM((2, seq, 128), F32),
        pltpu.VMEM((128, seq), F32),
        pltpu.VMEM((2, seq, 128), BF),
        pltpu.VMEM((2, seq, 128), BF),
        pltpu.VMEM((2, seq), F32),
    ]
    return pairs, ins, outs, shapes, scratch, cost(16 * pairs * seq * seq * 128)


def attention_backward(q, kv, do, o, lse, blk=512):
    pairs, ins, outs, shapes, scratch, estimate = backward_specs(q, kv)
    return pl.pallas_call(
        functools.partial(backward_kernel, blk),
        grid=(pairs,),
        in_specs=ins,
        out_specs=outs,
        out_shape=shapes,
        scratch_shapes=scratch,
        compiler_params=pltpu.CompilerParams(vmem_limit_bytes=56 * 2**20),
        cost_estimate=estimate,
    )(q, kv, do, o, lse)


def attention_backward_scatter(dp, q, kv, do, o, lse, blocks, terms, cuts, orders, blk=512):
    pairs, ins, outs, shapes, scratch, estimate = backward_specs(q, kv)
    anywhere = pl.BlockSpec(memory_space=pl.ANY)
    count = len(cuts)
    bufs = [pltpu.VMEM((2 * dp, terms[a].shape[1], size), BF) for a, _, size in cuts]
    return pl.pallas_call(
        functools.partial(backward_scatter_kernel, dp, blk, cuts, orders, pairs),
        grid=(pairs,),
        in_specs=ins + [anywhere] * (1 + len(terms)),
        out_specs=outs + [anywhere] + [pl.BlockSpec(w.shape[1:], lambda p: (0, 0)) for w in terms],
        out_shape=shapes
        + [jax.ShapeDtypeStruct(blocks.shape, blocks.dtype)]
        + [jax.ShapeDtypeStruct(w.shape[1:], F32) for w in terms],
        scratch_shapes=scratch
        + [pltpu.SemaphoreType.DMA((3,))]
        + bufs * 3
        + [pltpu.SemaphoreType.DMA((count, 2 * dp))]
        + scatter_sems(dp, count),
        compiler_params=pltpu.CompilerParams(
            vmem_limit_bytes=60 * 2**20, collective_id=3, has_side_effects=True
        ),
        cost_estimate=estimate,
    )(q, kv, do, o, lse, blocks, *terms)


HEADS = 16
KVH = 2
LATD = 256
HG = 8
GROUPS = 8
EPSILON = 1e-05
ALL = ("dp", "seq", "grp")


def norm_parts(values, gain):
    inverse = lax.rsqrt(jnp.mean(values * values, axis=-1, keepdims=True) + EPSILON)
    return (values * inverse * gain, inverse)


def norm_back(values, inverse, gain, upstream):
    scaled = upstream * gain
    gain_grad = jnp.sum(upstream * values * inverse, axis=0)
    input_part = inverse * scaled - values * inverse**3 * jnp.mean(
        scaled * values, axis=-1, keepdims=True
    )
    return (input_part, gain_grad)


def dot_tn(a, b):
    return lax.dot_general(a, b, (((0,), (0,)), ((), ())), preferred_element_type=F32)


def swap_sequences(blocks, count):
    if count == 2:
        me = lax.axis_index("seq")
        sent = lax.ppermute(blocks[1 - me], "seq", [(0, 1), (1, 0)])
        kept = blocks[me]
        first = me == 0
        return jnp.stack([jnp.where(first, kept, sent), jnp.where(first, sent, kept)])
    return lax.all_to_all(blocks, "seq", 0, 0, tiled=True)


def swap_group(blocks):
    return lax.all_to_all(blocks, "grp", 0, 0, tiled=True)


def local(
    inputs,
    cotangent,
    group_ids,
    group_scale,
    norm_gain,
    w_query,
    w_latent,
    expansion_weight,
    w_output,
    ffn_gain,
    w_gate,
    w_up,
    w_down,
):
    devices = lax.axis_size("dp") * lax.axis_size("seq") * lax.axis_size("grp")
    groups = lax.axis_size("grp")
    me = lax.axis_index("grp")
    seqs, rows, width = inputs.shape
    count = seqs * rows
    hidden_size = w_gate.shape[1]
    heads = HEADS // groups
    cols = heads * DH
    drows = width // devices

    dp = lax.axis_size("dp")
    ring = groups == 2 and seqs == 2 and dp % 2 == 0
    expand_rows = expansion_weight.reshape(-1, expansion_weight.shape[2])
    gains = jnp.pad(jnp.concatenate([norm_gain, ffn_gain])[None], ((0, 15), (0, 128 - 2 * drows)))
    if ring:
        shards = (w_query, w_latent, expand_rows, gains)
        full, own_inputs = own_gather(dp, shards, inputs, ("xzy",) * 4)
    else:
        shards = (w_query, w_latent, expand_rows, gains, w_output)
        full = [lax.all_gather(w, ALL, axis=0) for w in shards]
        own_inputs = swap_sequences(inputs, seqs)
    ffn_full = lax.all_gather(jnp.concatenate([w_gate, w_up], axis=1), ALL, axis=0, tiled=True)
    down_full = lax.all_gather(w_down, ALL, axis=0, tiled=True)
    query_full = full[0].reshape(width, -1)
    latent_full = full[1].reshape(width, -1)
    expand_full = full[2].reshape(devices, KVH, LATD // devices, -1)
    gain_one = full[3][:, 0, :drows].reshape(width).astype(F32)
    gain_two = full[3][:, 0, drows : 2 * drows].reshape(width).astype(F32)
    gate_full = ffn_full[:, :hidden_size]
    up_full = ffn_full[:, hidden_size:]


    token_rows = own_inputs.astype(F32).reshape(count, width)
    normed, inverse_one = norm_parts(token_rows, gain_one)
    normed_low = normed.astype(BF)
    query_send = jnp.stack(
        [dot_nn(normed_low, query_full[:, j * cols : (j + 1) * cols]).astype(BF) for j in range(groups)]
    ).reshape(groups, seqs, rows, cols)
    latent_state = [
        dot_nn(normed_low, latent_full[:, g * LATD : (g + 1) * LATD]).astype(BF) for g in range(KVH)
    ]
    latent_send = jnp.stack([latent_state[j * heads // HG] for j in range(groups)]).reshape(
        groups, seqs, rows, LATD
    )
    head_queries = swap_group(query_send)
    head_latent = swap_group(latent_send).transpose(1, 0, 2, 3).reshape(-1, LATD)
    expand_local = lax.dynamic_slice(
        expand_full,
        (0, me * heads // HG, 0, me * heads % HG * 2 * DH),
        (devices, 1, LATD // devices, heads * 2 * DH),
    ).reshape(LATD, -1)
    head_pairs = dot_nn(head_latent, expand_local).astype(BF)
    if ring:
        attended, logsum, own_cotangent, output_full = attention_forward_gather(
            dp, head_queries, head_pairs, cotangent, (w_output,), ((0, 0, width),), ("xzy",)
        )
    else:
        attended, logsum = attention_forward(head_queries, head_pairs)
        own_cotangent = swap_sequences(cotangent, seqs)
        output_full = full[4]
    output_full = output_full.reshape(-1, width)
    token_attended = swap_group(attended).reshape(groups, count, cols)
    branch = sum(
        dot_nn(token_attended[j], output_full[j * cols : (j + 1) * cols]) for j in range(groups)
    )
    middle = token_rows + branch
    normed_two, inverse_two = norm_parts(middle, gain_two)
    normed_two_low = normed_two.astype(BF)
    gate_pre = dot_nn(normed_two_low, gate_full)
    upward = dot_nn(normed_two_low, up_full)
    sigmoid = jax.nn.sigmoid(gate_pre)
    activated = gate_pre * sigmoid
    hidden = (activated * upward).astype(BF)
    result = middle + dot_nn(hidden, down_full)
    own_output = result.astype(BF).reshape(seqs, rows, width)

    seq_group = lax.dynamic_index_in_dim(group_ids, lax.axis_index("seq"), 0, keepdims=False)
    chosen = (seq_group == jnp.arange(GROUPS)).astype(F32)
    seq_scale = jnp.sum(chosen * group_scale)
    upstream = own_cotangent.astype(F32).reshape(count, width) * seq_scale
    upstream_low = upstream.astype(BF)
    down_grad = dot_tn(hidden, upstream_low)
    hidden_back = dot_nt(upstream_low, down_full)
    gate_back = (hidden_back * upward * sigmoid * (1.0 + gate_pre * (1.0 - sigmoid))).astype(BF)
    up_back = (hidden_back * activated).astype(BF)
    gate_grad = dot_tn(normed_two_low, gate_back)
    up_grad = dot_tn(normed_two_low, up_back)
    normed_two_back = dot_nt(gate_back, gate_full) + dot_nt(up_back, up_full)
    middle_part, gain_two_grad = norm_back(middle, inverse_two, gain_two, normed_two_back)
    middle_grad = upstream + middle_part
    if ring:
        both = jnp.concatenate([gate_grad.astype(BF), up_grad.astype(BF)], axis=1).reshape(
            devices, drows, -1
        )
        whole = both.shape[2] // width * width
        half = drows // 2
        packed = jnp.concatenate(
            [both[:, :, a : a + width] for a in range(0, whole, width)]
            + [
                jnp.concatenate([both[:, :half, whole:], both[:, half:, whole:]], axis=2),
                down_grad.astype(BF).reshape(devices, -1, width),
            ],
            axis=1,
        )
        share = lax.psum_scatter(packed, ALL, scatter_dimension=0, tiled=True)[0].astype(F32)
        tall = whole // width * drows
        tail = share[tall : tall + half]
        ffn_share = jnp.concatenate(
            [share[a : a + drows] for a in range(0, tall, drows)]
            + [jnp.concatenate([tail[:, : width // 2], tail[:, width // 2 :]], axis=0)],
            axis=1,
        )
        down_share = share[tall + half :]
    else:
        ffn_share = lax.psum_scatter(
            jnp.concatenate([gate_grad.astype(BF), up_grad.astype(BF)], axis=1),
            ALL,
            scatter_dimension=0,
            tiled=True,
        ).astype(F32)
        down_share = lax.psum_scatter(
            down_grad.astype(BF), ALL, scatter_dimension=0, tiled=True
        ).astype(F32)

    branch_low = middle_grad.astype(BF)
    output_grad = jnp.concatenate(
        [dot_tn(token_attended[j], branch_low) for j in range(groups)], axis=0
    )
    back_send = jnp.stack(
        [
            dot_nt(branch_low, output_full[j * cols : (j + 1) * cols]).astype(BF)
            for j in range(groups)
        ]
    ).reshape(groups, seqs, rows, cols)
    head_upstream = swap_group(back_send)
    terms = output_grad.astype(BF).reshape(devices, drows, width)
    attention = (head_queries, head_pairs, head_upstream, attended, logsum)
    if ring:
        query_back, pair_back, output, output_share = attention_backward_scatter(
            dp, *attention, own_output, (terms,), ((0, 0, width),), ("yzx",)
        )
    else:
        query_back, pair_back = attention_backward(*attention)
        output = swap_sequences(own_output, seqs)
        output_share = lax.psum_scatter(terms, ALL, scatter_dimension=0, tiled=True)[0].astype(F32)
    latent_terms = dot_nt(pair_back, expand_local).astype(BF)
    expand_part = dot_tn(head_latent, pair_back)
    expand_grad = lax.dynamic_update_slice(
        jnp.zeros(expand_full.shape, BF),
        expand_part.astype(BF).reshape(devices, 1, LATD // devices, -1),
        (0, me * heads // HG, 0, me * heads % HG * 2 * DH),
    )
    query_token = swap_group(query_back).reshape(groups, count, cols)
    latent_token = swap_group(
        latent_terms.reshape(seqs, groups, rows, LATD).transpose(1, 0, 2, 3)
    ).reshape(KVH, groups // KVH, count, LATD)
    latent_token = jnp.sum(latent_token.astype(F32), axis=1).astype(BF)
    query_grad = jnp.concatenate([dot_tn(normed_low, query_token[j]) for j in range(groups)], axis=1)
    latent_grad = jnp.concatenate([dot_tn(normed_low, latent_token[g]) for g in range(KVH)], axis=1)
    normed_back = sum(
        dot_nt(query_token[j], query_full[:, j * cols : (j + 1) * cols]) for j in range(groups)
    ) + sum(
        dot_nt(latent_token[g], latent_full[:, g * LATD : (g + 1) * LATD]) for g in range(KVH)
    )
    input_part, gain_one_grad = norm_back(token_rows, inverse_one, gain_one, normed_back)
    own_input_grad = (middle_grad + input_part).astype(BF).reshape(seqs, rows, width)
    gain_grads = jnp.concatenate(
        [gain_one_grad.reshape(devices, 1, drows), gain_two_grad.reshape(devices, 1, drows)], axis=2
    ).astype(BF)
    gain_grads = jnp.pad(gain_grads, ((0, 0), (0, 15), (0, 128 - 2 * drows)))
    terms = (
        query_grad.astype(BF).reshape(devices, drows, -1),
        latent_grad.astype(BF).reshape(devices, drows, -1),
        expand_grad.reshape(devices, -1, expand_grad.shape[3]),
        gain_grads,
    )
    if ring:
        sums, input_grad = own_scatter(dp, terms, ("yzx",) * 4, own_input_grad)
    else:
        sums = [
            lax.psum_scatter(w, ALL, scatter_dimension=0, tiled=True)[0].astype(F32) for w in terms
        ]
        input_grad = swap_sequences(own_input_grad, seqs)
    return (
        output,
        input_grad,
        sums[3][0, :drows],
        sums[0],
        sums[1],
        sums[2].reshape(expansion_weight.shape),
        output_share,
        sums[3][0, drows : 2 * drows],
        ffn_share[:, :hidden_size],
        ffn_share[:, hidden_size:],
        down_share,
    )


def solution(mesh):
    def run(*arrays):
        dp, sp = mesh.shape["dp"], mesh.shape["sp"]
        seqs = arrays[0].shape[0] // dp
        grid = Mesh(mesh.devices.reshape(dp, seqs, sp // seqs), ALL)
        tokens = P("dp", ("seq", "grp"), None)
        matrix = P(ALL, None)
        expand = P(None, ALL, None)
        return jax.shard_map(
            local,
            mesh=grid,
            in_specs=(
                tokens,
                tokens,
                P("dp"),
                P(),
                P(ALL),
                matrix,
                matrix,
                expand,
                matrix,
                P(ALL),
                matrix,
                matrix,
                matrix,
            ),
            out_specs=(
                tokens,
                tokens,
                P(ALL),
                matrix,
                matrix,
                expand,
                matrix,
                P(ALL),
                matrix,
                matrix,
                matrix,
            ),
            check_vma=False,
        )(*arrays)

    return run
```

```python
import functools
import jax
import jax.numpy as jnp
from jax import lax
from jax.sharding import Mesh
from jax.sharding import PartitionSpec as P
from jax.experimental import pallas as pl
from jax.experimental.pallas import tpu as pltpu

DH = 64
EPSILON = 1e-05
F32 = jnp.float32
BF = jnp.bfloat16


def cost(flops):
    return pl.CostEstimate(flops=flops, bytes_accessed=2**23, transcendentals=0)


MESH = pl.DeviceIdType.MESH


class Place:

    def __init__(self, dp):
        self.sizes = {"x": 2, "y": 2, "z": dp // 2}
        d = lax.axis_index("dp")
        self.at = {"x": lax.axis_index("seq"), "y": lax.rem(d, 2), "z": lax.div(d, 2)}
        self.core = lax.axis_index("grp")

    def coords(self, offset):
        at = {k: lax.rem(self.at[k] + o, self.sizes[k]) if o else self.at[k] for k, o in offset.items()}
        return at["z"] * 2 + at["y"], at["x"]

    def index(self, offset, other):
        d, s = self.coords(offset)
        core = 1 - self.core if other else self.core
        return (d * 2 + s) * 2 + core

    def device(self, offset):
        return (*self.coords(offset), self.core)

    def pair(self):
        return (*self.coords({"x": 0, "y": 0, "z": 0}), 1 - self.core)

    def greet(self):
        there = [self.pair()]
        for k in "xyz":
            for o in range(1, self.sizes[k]):
                there.append(self.device({"x": 0, "y": 0, "z": 0, k: o}))
        barrier = pltpu.get_barrier_semaphore()
        for device in there:
            pl.semaphore_signal(barrier, inc=1, device_id=device, device_id_type=MESH)
        pl.semaphore_wait(barrier, len(there))


def offsets_of(order, dp):
    sizes = {"x": 2, "y": 2, "z": dp // 2}
    a, b, c = (sizes[k] for k in order)
    return [(i, j, k) for i in range(a) for j in range(b) for k in range(c)]


def named(order, steps):
    return dict(zip(order, steps))


def remote(src, dst, send, recv, there):
    return pltpu.make_async_remote_copy(
        src_ref=src, dst_ref=dst, send_sem=send, recv_sem=recv, device_id=there, device_id_type=MESH
    )


class Gather:

    def __init__(self, place, dp, order, src, out, sems, number):
        self.place, self.order, self.src, self.out = place, order, src, out
        self.steps = offsets_of(order, dp)
        self.sems, self.number = sems, number

    def slot(self, steps, other=False):
        return self.out(self.place.index(named(self.order, steps), other))

    def source(self, steps):
        last = max(i for i in range(3) if steps[i])
        return tuple(0 if i == last else o for i, o in enumerate(steps))

    def hop(self, steps):
        last = max(i for i in range(3) if steps[i])
        source = self.source(steps)
        size = self.place.sizes[self.order[last]]
        back = tuple(size - o if i == last else 0 for i, o in enumerate(steps))
        number = self.steps.index(steps)
        here = self.slot(source)
        src = here if any(source) else self.src
        return remote(
            src,
            here,
            self.sems[0].at[self.number, number],
            self.sems[1].at[self.number, number],
            self.place.device(named(self.order, back)),
        )

    def across(self, steps):
        number = self.steps.index(steps)
        src = self.slot(steps) if any(steps) else self.src
        return remote(
            src,
            self.slot(steps),
            self.sems[2].at[self.number, number],
            self.sems[3].at[self.number, number],
            self.place.pair(),
        )

    def keep(self):
        return pltpu.make_async_copy(self.src, self.slot((0, 0, 0)), self.sems[4].at[self.number])

    def send_from(self, source):
        for steps in self.steps:
            if any(steps) and self.source(steps) == source:
                self.hop(steps).start()
        self.across(source).start()

    def start(self):
        self.send_from((0, 0, 0))
        self.keep().start()

    def arrivals(self):
        return sorted((s for s in self.steps if any(s)), key=lambda s: [o > 0 for o in s][::-1])

    def forward(self, steps):
        number = self.steps.index(steps)
        here = self.slot(steps)
        remote(
            here,
            here,
            self.sems[0].at[self.number, number],
            self.sems[1].at[self.number, number],
            self.place.pair(),
        ).wait_recv()
        self.send_from(steps)

    def finish(self):
        for steps in self.steps:
            number = self.steps.index(steps)
            here = self.slot(steps, True)
            remote(
                here,
                here,
                self.sems[2].at[self.number, number],
                self.sems[3].at[self.number, number],
                self.place.pair(),
            ).wait_recv()
            self.across(steps).wait_send()
            if any(steps):
                self.hop(steps).wait_send()
        self.keep().wait()


class Scatter:

    def __init__(self, place, dp, order, term, pair_buf, ring_buf, sems, number, own=None):
        self.place, self.order, self.term = place, order, term
        self.own_buf, self.own_sem = own if own else (None, None)
        self.steps = offsets_of(order, dp)
        self.pair_buf, self.ring_buf = pair_buf, ring_buf
        self.sems, self.number = sems, number

    def turn(self):
        def key(steps):
            first = next((i for i in range(3) if steps[i]), 3)
            return (first, [o == 0 for o in steps])

        return sorted(self.steps, key=key)

    def across(self, steps):
        number = self.steps.index(steps)
        return remote(
            self.term(self.place.index(named(self.order, steps), True)),
            self.pair_buf.at[number],
            self.sems[2].at[self.number, number],
            self.sems[3].at[self.number, number],
            self.place.pair(),
        )

    def fetch(self, steps):
        number = self.steps.index(steps)
        return pltpu.make_async_copy(
            self.term(self.place.index(named(self.order, steps), False)),
            self.own_buf.at[number],
            self.own_sem.at[self.number, number],
        )

    def start(self):
        for steps in self.turn():
            self.across(steps).start()
            if self.own_buf is not None:
                self.fetch(steps).start()

    def hop(self, steps):
        first = min(i for i in range(3) if steps[i])
        there = tuple(o if i == first else 0 for i, o in enumerate(steps))
        number = self.steps.index(steps)
        return remote(
            self.pair_buf.at[number],
            self.ring_buf.at[number],
            self.sems[0].at[self.number, number],
            self.sems[1].at[self.number, number],
            self.place.device(named(self.order, there)),
        )

    def add(self, steps, out=None):
        number = self.steps.index(steps)
        self.across(steps).wait_recv()
        if self.own_buf is None:
            mine = self.term(self.place.index(named(self.order, steps), False))
        else:
            self.fetch(steps).wait()
            mine = self.own_buf.at[number]
        total = mine[...].astype(F32) + self.pair_buf[number].astype(F32)
        for came in self.steps:
            if not any(came):
                continue
            first = min(i for i in range(3) if came[i])
            if tuple(0 if i == first else o for i, o in enumerate(came)) == steps:
                self.hop(came).wait_recv()
                total = total + self.ring_buf[self.steps.index(came)].astype(F32)
        if out is None:
            self.pair_buf[number] = total.astype(BF)
            self.hop(steps).start()
        else:
            out[...] = total

    def finish(self):
        for steps in self.steps:
            self.across(steps).wait_send()
            if any(steps):
                self.hop(steps).wait_send()


def block_swap(x_in, x_out, sem, place):
    s = place.at["x"]
    away = remote(
        x_in.at[1 - s], x_out.at[s], sem.at[0], sem.at[1], place.device({"x": 1, "y": 0, "z": 0})
    )
    return away, pltpu.make_async_copy(x_in.at[s], x_out.at[s], sem.at[2])


def gather_kernel(dp, orders, *refs):
    count = len(orders)
    srcs, x_in = refs[:count], refs[count]
    outs, x_out = refs[count + 1 : 2 * count + 1], refs[2 * count + 1]
    sems, x_sem = refs[2 * count + 2 : -1], refs[-1]
    place = Place(dp)
    place.greet()
    works = [
        Gather(place, dp, orders[a], srcs[a], lambda at, a=a: outs[a].at[at], sems, a)
        for a in range(count)
    ]
    for work in works:
        work.start()
    swap, kept = block_swap(x_in, x_out, x_sem, place)
    swap.start()
    kept.start()
    for i in range(2 * dp - 1):
        for work in works:
            work.forward(work.arrivals()[i])
    for work in works:
        work.finish()
    swap.wait()
    kept.wait()


def gather_sems(dp, count):
    sem = pltpu.SemaphoreType.DMA
    return [sem((count, 2 * dp))] * 4 + [sem((count,))]


def own_gather(dp, shards, blocks, orders):
    count = len(shards)
    anywhere = pl.BlockSpec(memory_space=pl.ANY)
    out = pl.pallas_call(
        functools.partial(gather_kernel, dp, orders),
        in_specs=[anywhere] * (count + 1),
        out_specs=[anywhere] * (count + 1),
        out_shape=[jax.ShapeDtypeStruct((4 * dp, *w.shape), w.dtype) for w in shards]
        + [jax.ShapeDtypeStruct(blocks.shape, blocks.dtype)],
        scratch_shapes=gather_sems(dp, count) + [pltpu.SemaphoreType.DMA((3,))],
        compiler_params=pltpu.CompilerParams(collective_id=0, has_side_effects=True),
    )(*shards, blocks)
    return out[:-1], out[-1]


def scatter_kernel(dp, orders, late, *refs):
    count = len(orders)
    terms, x_in = refs[:count], refs[count]
    outs, x_out = refs[count + 1 : 2 * count + 1], refs[2 * count + 1]
    rest = refs[2 * count + 2 :]
    pair_bufs, ring_bufs = rest[:count], rest[count : 2 * count]
    sems, x_sem = rest[2 * count : -1], rest[-1]
    place = Place(dp)
    place.greet()
    works = [
        Scatter(
            place, dp, orders[a], lambda at, a=a: terms[a].at[at], pair_bufs[a], ring_bufs[a], sems, a
        )
        for a in range(count)
    ]
    swap, kept = block_swap(x_in, x_out, x_sem, place)
    for work in works:
        work.start()
    turns = [work.turn() for work in works]
    for i in range(len(turns[0])):
        if i == late:
            swap.start()
            kept.start()
        for a in range(count):
            works[a].add(turns[a][i], outs[a] if i == len(turns[0]) - 1 else None)
    for work in works:
        work.finish()
    swap.wait()
    kept.wait()


def scatter_sems(dp, count):
    return [pltpu.SemaphoreType.DMA((count, 2 * dp))] * 4


def own_scatter(dp, terms, orders, blocks, late=0):
    count = len(terms)
    anywhere = pl.BlockSpec(memory_space=pl.ANY)
    inside = pl.BlockSpec(memory_space=pltpu.VMEM)
    out = pl.pallas_call(
        functools.partial(scatter_kernel, dp, orders, late),
        in_specs=[inside] * count + [anywhere],
        out_specs=[inside] * count + [anywhere],
        out_shape=[jax.ShapeDtypeStruct(w.shape[1:], F32) for w in terms]
        + [jax.ShapeDtypeStruct(blocks.shape, blocks.dtype)],
        scratch_shapes=[pltpu.VMEM((2 * dp, *w.shape[1:]), BF) for w in terms] * 2
        + scatter_sems(dp, count)
        + [pltpu.SemaphoreType.DMA((3,))],
        compiler_params=pltpu.CompilerParams(
            collective_id=1, has_side_effects=True, vmem_limit_bytes=48 * 2**20
        ),
    )(*terms, blocks)
    return out[:-1], out[-1]


def run_at(plan, point):
    for step in sorted({k[0] for k in plan if k[1] == point}):
        tasks = plan[step, point]

        @pl.when(pl.program_id(0) == step)
        def _(tasks=tasks):
            for task in tasks:
                task()


def gather_plan(place, works, swap, steps, points):
    arrivals = [work.arrivals() for work in works]
    total = steps * points

    def begin():
        place.greet()
        for work in works:
            work.start()
        for copy in swap:
            copy.start()

    def forward(i):
        for work, order in zip(works, arrivals):
            work.forward(order[i])

    def end():
        for work in works:
            work.finish()
        for copy in swap:
            copy.wait()

    plan = {}
    count = len(arrivals[0])
    plan[0, 0] = [begin]
    for i in range(count):
        at = 2 + i * (total - 3) // count
        plan.setdefault(divmod(at, points), []).append(functools.partial(forward, i))
    plan.setdefault(divmod(total, points), []).append(end)
    return plan


def scatter_plan(place, works, outs, swap, steps, points):
    turns = [work.turn() for work in works]
    total = steps * points
    count = len(turns[0])

    def begin():
        place.greet()
        for work in works:
            work.start()
        for copy in swap:
            copy.start()

    def add(i):
        for work, order, out in zip(works, turns, outs):
            work.add(order[i], out if i == count - 1 else None)

    def end():
        for work in works:
            work.finish()
        for copy in swap:
            copy.wait()

    plan = {(0, 0): [begin]}
    for i in range(count):
        at = 1 + i // 2 if i < count // 2 else 6 + (i - count // 2) * (total - 6) // (count - count // 2)
        plan.setdefault(divmod(at, points), []).append(functools.partial(add, i))
    plan.setdefault(divmod(total, points), []).append(end)
    return plan


def dot_nt(a, b):
    return lax.dot_general(a, b, (((1,), (1,)), ((), ())), preferred_element_type=F32)


def dot_nn(a, b):
    return lax.dot_general(a, b, (((1,), (0,)), ((), ())), preferred_element_type=F32)


def dot_tn(a, b):
    return lax.dot_general(a, b, (((0,), (0,)), ((), ())), preferred_element_type=F32)


def causal(s, first_key, first_query):
    keys = first_key + lax.broadcasted_iota(jnp.int32, s.shape, 0)
    rows = first_query + lax.broadcasted_iota(jnp.int32, s.shape, 1)
    return jnp.where(rows >= keys, s, -1e30)


def forward_body(q_ref, kv_ref, o_ref, lse_ref, vt_s, point=lambda i: None):
    groups, chunks, rows, _ = q_ref.shape
    seq = kv_ref.shape[0]
    for h in range(2):
        vt_s[h] = kv_ref[:, h * 128 : (h + 1) * 128].astype(F32).T[DH:].astype(BF)
    for i in range(groups * chunks):
        point(i)
        q = q_ref[i % groups, i // groups].astype(F32) * 0.125
        outs = []
        for h in range(2):
            qh = q[:, h * DH : (h + 1) * DH]
            qp = jnp.concatenate([qh, jnp.zeros_like(qh)], axis=1).astype(BF)
            width = (i + 1) * rows
            s = dot_nt(kv_ref[0:width, h * 128 : (h + 1) * 128], qp)
            tail = causal(s[i * rows :], 0, 0)
            if i > 0:
                head = s[: i * rows]
                top = jnp.maximum(
                    jnp.max(head, axis=0, keepdims=True), jnp.max(tail, axis=0, keepdims=True)
                )
                ph = jnp.exp(head - top)
                pt = jnp.exp(tail - top)
                total = jnp.sum(ph, axis=0, keepdims=True) + jnp.sum(pt, axis=0, keepdims=True)
                o = dot_nn(vt_s[h, :, 0 : i * rows], ph.astype(BF)) + dot_nn(
                    vt_s[h, :, i * rows : width], pt.astype(BF)
                )
            else:
                top = jnp.max(tail, axis=0, keepdims=True)
                pt = jnp.exp(tail - top)
                total = jnp.sum(pt, axis=0, keepdims=True)
                o = dot_nn(vt_s[h, :, 0:width], pt.astype(BF))
            outs.append(o / total)
            lse_ref[h, i * rows : (i + 1) * rows] = (top + jnp.log(total))[0]
        o_ref[i % groups, i // groups] = jnp.concatenate(outs, axis=0).T.astype(BF)


def forward_kernel(q_ref, kv_ref, o_ref, lse_ref, vt_s):
    forward_body(q_ref, kv_ref, o_ref, lse_ref, vt_s)


def forward_gather_kernel(dp, cuts, orders, pairs, *refs):
    q_ref, kv_ref, x_in = refs[:3]
    sources = 1 + max(cut[0] for cut in cuts)
    srcs, refs = refs[3 : 3 + sources], refs[3 + sources :]
    o_ref, lse_ref, x_out = refs[:3]
    outs, refs = refs[3 : 3 + sources], refs[3 + sources :]
    vt_s, x_sem, sems = refs[0], refs[1], refs[2:]
    place = Place(dp)
    works = []
    for number, (a, first, size) in enumerate(cuts):
        cut = pl.ds(first, size)
        works.append(
            Gather(
                place,
                dp,
                orders[number],
                srcs[a].at[:, cut],
                lambda at, a=a, cut=cut: outs[a].at[at, :, cut],
                sems,
                number,
            )
        )
    points = q_ref.shape[0] * q_ref.shape[1]
    plan = gather_plan(place, works, block_swap(x_in, x_out, x_sem, place), pairs, points)
    forward_body(q_ref, kv_ref, o_ref, lse_ref, vt_s, lambda i: run_at(plan, i))
    for point in range(points):
        tasks = plan.get((pairs, point))
        if tasks:

            @pl.when(pl.program_id(0) == pairs - 1)
            def _(tasks=tasks):
                for task in tasks:
                    task()


def forward_specs(q, kv):
    groups, chunks, rows, cols = q.shape
    seq = kv.shape[0]
    pairs = cols // 128
    tok = pl.BlockSpec((groups, chunks, rows, 128), lambda p: (0, 0, 0, p))
    ins = [tok, pl.BlockSpec((seq, 256), lambda p: (0, p))]
    outs = [tok, pl.BlockSpec((None, 2, seq), lambda p: (p, 0, 0))]
    shapes = [jax.ShapeDtypeStruct(q.shape, BF), jax.ShapeDtypeStruct((pairs, 2, seq), F32)]
    scratch = [pltpu.VMEM((2, DH, seq), BF)]
    return pairs, ins, outs, shapes, scratch, cost(8 * pairs * seq * seq * 128)


def attention_forward(q, kv):
    pairs, ins, outs, shapes, scratch, estimate = forward_specs(q, kv)
    return pl.pallas_call(
        forward_kernel,
        grid=(pairs,),
        in_specs=ins,
        out_specs=outs,
        out_shape=shapes,
        scratch_shapes=scratch,
        compiler_params=pltpu.CompilerParams(vmem_limit_bytes=56 * 2**20),
        cost_estimate=estimate,
    )(q, kv)


def attention_forward_gather(dp, q, kv, blocks, shards, cuts, orders):
    pairs, ins, outs, shapes, scratch, estimate = forward_specs(q, kv)
    anywhere = pl.BlockSpec(memory_space=pl.ANY)
    count = len(shards)
    return pl.pallas_call(
        functools.partial(forward_gather_kernel, dp, cuts, orders, pairs),
        grid=(pairs,),
        in_specs=ins + [anywhere] * (1 + count),
        out_specs=outs + [anywhere] * (1 + count),
        out_shape=shapes
        + [jax.ShapeDtypeStruct(blocks.shape, blocks.dtype)]
        + [jax.ShapeDtypeStruct((4 * dp, *w.shape), w.dtype) for w in shards],
        scratch_shapes=scratch + [pltpu.SemaphoreType.DMA((3,))] + gather_sems(dp, len(cuts)),
        compiler_params=pltpu.CompilerParams(
            vmem_limit_bytes=56 * 2**20, collective_id=2, has_side_effects=True
        ),
        cost_estimate=estimate,
    )(q, kv, blocks, *shards)


def backward_body(blk, q_ref, kv_ref, do_ref, o_ref, lse_ref, dq_ref, dkv_ref,
                  kt_s, acc_s, dqt_s, qp_s, dop_s, delta_s, point=lambda i: None):
    groups, chunks, rows, _ = q_ref.shape
    seq = kv_ref.shape[0]
    n = groups * chunks
    for h in range(2):
        kt_s[h] = kv_ref[:, h * 128 : (h + 1) * 128].astype(F32).T[:DH].astype(BF)
    acc_s[...] = jnp.zeros_like(acc_s)
    for i in range(n):
        at = pl.ds(i * rows, rows)
        q = q_ref[i % groups, i // groups].astype(F32) * 0.125
        do = do_ref[i % groups, i // groups].astype(F32)
        o = o_ref[i % groups, i // groups].astype(F32)
        prod = (do * o).T
        zero = jnp.zeros((rows, DH), F32)
        for h in range(2):
            cut = slice(h * DH, (h + 1) * DH)
            qp_s[h, at] = jnp.concatenate([q[:, cut], zero], axis=1).astype(BF)
            dop_s[h, at] = jnp.concatenate([zero, do[:, cut]], axis=1).astype(BF)
            delta_s[h, at] = jnp.sum(prod[cut], axis=0)

    def block(i, j, masked):
        qat = pl.ds(i * blk, blk)
        kat = pl.ds(pl.multiple_of(j * blk, blk), blk)
        for h in range(2):
            kv = kv_ref[kat, h * 128 : (h + 1) * 128]
            qp = qp_s[h, qat]
            dop = dop_s[h, qat]
            s = dot_nt(kv, qp)
            dp = dot_nt(kv, dop)
            if masked:
                s = causal(s, 0, 0)
            p = jnp.exp(s - lse_ref[h : h + 1, qat])
            ds = (p * (dp - delta_s[h : h + 1, qat])).astype(BF)
            acc_s[h, kat] += dot_nn(p.astype(BF), dop) + dot_nn(ds, qp)
            part = dot_nn(kt_s[h, :, kat], ds)
            if masked:
                dqt_s[h * DH : (h + 1) * DH, qat] = part
            else:
                dqt_s[h * DH : (h + 1) * DH, qat] += part

    m = seq // blk

    for i in range(m):
        point(i)
        block(i, i, True)

        def inner(j, _, i=i):
            block(i, j, False)
            return 0

        lax.fori_loop(0, i, inner, 0)
    for i in range(n):
        at = pl.ds(i * rows, rows)
        dq_ref[i % groups, i // groups] = (dqt_s[:, at].T * 0.125).astype(BF)
    for h in range(2):
        dkv_ref[:, h * 128 : (h + 1) * 128] = acc_s[h].astype(BF)


def backward_kernel(blk, *refs):
    backward_body(blk, *refs)


def backward_scatter_kernel(dp, blk, cuts, orders, pairs, *refs):
    ins, x_in, refs = refs[:5], refs[5], refs[6:]
    sources = 1 + max(cut[0] for cut in cuts)
    count = len(cuts)
    terms, refs = refs[:sources], refs[sources:]
    attn_outs, x_out, refs = refs[:2], refs[2], refs[3:]
    outs, refs = refs[:sources], refs[sources:]
    scratch, x_sem, refs = refs[:6], refs[6], refs[7:]
    own_bufs, pair_bufs, ring_bufs = refs[:count], refs[count : 2 * count], refs[2 * count : 3 * count]
    own_sem, sems = refs[3 * count], refs[3 * count + 1 :]
    place = Place(dp)
    works, targets = [], []
    for number, (a, first, size) in enumerate(cuts):
        cut = pl.ds(first, size)
        works.append(
            Scatter(
                place,
                dp,
                orders[number],
                lambda at, a=a, cut=cut: terms[a].at[at, :, cut],
                pair_bufs[number],
                ring_bufs[number],
                sems,
                number,
                (own_bufs[number], own_sem),
            )
        )
        targets.append(outs[a].at[:, cut])
    points = ins[1].shape[0] // blk
    plan = scatter_plan(place, works, targets, block_swap(x_in, x_out, x_sem, place), pairs, points)
    backward_body(blk, *ins, *attn_outs, *scratch, point=lambda i: run_at(plan, i))
    for point in range(points):
        tasks = plan.get((pairs, point))
        if tasks:

            @pl.when(pl.program_id(0) == pairs - 1)
            def _(tasks=tasks):
                for task in tasks:
                    task()


def backward_specs(q, kv):
    groups, chunks, rows, cols = q.shape
    seq = kv.shape[0]
    pairs = cols // 128
    tok = pl.BlockSpec((groups, chunks, rows, 128), lambda p: (0, 0, 0, p))
    wide = pl.BlockSpec((seq, 256), lambda p: (0, p))
    ins = [tok, wide, tok, tok, pl.BlockSpec((None, 2, seq), lambda p: (p, 0, 0))]
    outs = [tok, wide]
    shapes = [jax.ShapeDtypeStruct(q.shape, BF), jax.ShapeDtypeStruct(kv.shape, BF)]
    scratch = [
        pltpu.VMEM((2, DH, seq), BF),
        pltpu.VMEM((2, seq, 128), F32),
        pltpu.VMEM((128, seq), F32),
        pltpu.VMEM((2, seq, 128), BF),
        pltpu.VMEM((2, seq, 128), BF),
        pltpu.VMEM((2, seq), F32),
    ]
    return pairs, ins, outs, shapes, scratch, cost(16 * pairs * seq * seq * 128)


def attention_backward(q, kv, do, o, lse, blk=512):
    pairs, ins, outs, shapes, scratch, estimate = backward_specs(q, kv)
    return pl.pallas_call(
        functools.partial(backward_kernel, blk),
        grid=(pairs,),
        in_specs=ins,
        out_specs=outs,
        out_shape=shapes,
        scratch_shapes=scratch,
        compiler_params=pltpu.CompilerParams(vmem_limit_bytes=56 * 2**20),
        cost_estimate=estimate,
    )(q, kv, do, o, lse)


def attention_backward_scatter(dp, q, kv, do, o, lse, blocks, terms, cuts, orders, blk=512):
    pairs, ins, outs, shapes, scratch, estimate = backward_specs(q, kv)
    anywhere = pl.BlockSpec(memory_space=pl.ANY)
    count = len(cuts)
    bufs = [pltpu.VMEM((2 * dp, terms[a].shape[1], size), BF) for a, _, size in cuts]
    return pl.pallas_call(
        functools.partial(backward_scatter_kernel, dp, blk, cuts, orders, pairs),
        grid=(pairs,),
        in_specs=ins + [anywhere] * (1 + len(terms)),
        out_specs=outs + [anywhere] + [pl.BlockSpec(w.shape[1:], lambda p: (0, 0)) for w in terms],
        out_shape=shapes
        + [jax.ShapeDtypeStruct(blocks.shape, blocks.dtype)]
        + [jax.ShapeDtypeStruct(w.shape[1:], F32) for w in terms],
        scratch_shapes=scratch
        + [pltpu.SemaphoreType.DMA((3,))]
        + bufs * 3
        + [pltpu.SemaphoreType.DMA((count, 2 * dp))]
        + scatter_sems(dp, count),
        compiler_params=pltpu.CompilerParams(
            vmem_limit_bytes=60 * 2**20, collective_id=3, has_side_effects=True
        ),
        cost_estimate=estimate,
    )(q, kv, do, o, lse, blocks, *terms)


CUT = 256
PART = 512
TALL = 512
DOWN = 8


class BlockSums:

    def __init__(self, dp, stage, pair_buf, ring_buf, send, recv, out_ref):
        self.place = Place(dp)
        self.stage, self.pair_buf, self.ring_buf = stage, pair_buf, ring_buf
        self.send, self.recv, self.out_ref = send, recv, out_ref
        self.total = pair_buf.shape[1]
        self.unit = out_ref.shape[0]

    def order(self):
        return [
            self.place.index({"y": y, "x": x, "z": z}, other)
            for other in (False, True)
            for y in range(2)
            for x in range(2)
            for z in range(self.place.sizes["z"])
        ]

    def pair(self, j):
        return remote(
            self.stage.at[lax.rem(j, 2), pl.ds(self.total, self.total)],
            self.pair_buf.at[j],
            self.send.at[j, 0],
            self.recv.at[j, 0],
            self.place.pair(),
        )

    def hop(self, j, axis, step, first, size, number):
        rows = pl.ds(first, size)
        offset = {"x": 0, "y": 0, "z": 0, axis: step}
        return remote(
            self.pair_buf.at[j, rows],
            self.ring_buf.at[j, rows],
            self.send.at[j, number],
            self.recv.at[j, number],
            self.place.device(offset),
        )

    def hops(self, odd, phase):
        q = self.total // 4
        if phase == 3:
            sizes = range(1, self.place.sizes["z"])
            return [("z", z, z * self.unit, self.unit, 3 + z) for z in sizes]
        if odd:
            return ([("x", 1, q, q, 1), ("x", 1, 3 * q, q, 2)], [("y", 1, 2 * q, q, 3)])[phase - 1]
        return ([("y", 1, 2 * q, 2 * q, 1)], [("x", 1, q, q, 3)])[phase - 1]

    def add(self, j, to, size, came):
        self.pair_buf[j, to : to + size] = (
            self.pair_buf[j, to : to + size].astype(F32) + came.astype(F32)
        ).astype(BF)

    def advance(self, j, odd, phase):
        q = self.total // 4
        if phase == 1:
            self.pair(j).wait_recv()
            self.add(j, 0, self.total, self.stage[lax.rem(j, 2), : self.total])
        else:
            for hop in self.hops(odd, phase - 1):
                self.hop(j, *hop).wait_recv()
        if phase == 2 and odd:
            self.add(j, 0, q, self.ring_buf[j, q : 2 * q])
            self.add(j, 2 * q, q, self.ring_buf[j, 3 * q :])
        elif phase == 2:
            self.add(j, 0, 2 * q, self.ring_buf[j, 2 * q :])
        elif phase == 3:
            first = 2 * q if odd else q
            self.add(j, 0, q, self.ring_buf[j, first : first + q])
        elif phase == 4:
            total = self.pair_buf[j, : self.unit].astype(F32)
            for z in range(1, self.place.sizes["z"]):
                total = total + self.ring_buf[j, z * self.unit : (z + 1) * self.unit].astype(F32)
            wide = total.shape[1]
            self.out_ref[:, pl.ds(pl.multiple_of(j * wide, wide), wide)] = total
        if phase < 4:
            for hop in self.hops(odd, phase):
                self.hop(j, *hop).start()

    def finish(self, blocks):
        for j in range(blocks):
            for phase in range(1, 4):
                for hop in self.hops(j % 2, phase):
                    self.hop(j, *hop).wait_send()


def ffn_kernel(dp, scale_ref, x_ref, att_ref, wo_ref, gain_ref, cot_ref, gu_ref, down_ref,
               res_ref, mid_ref, nb_ref, gu_out, down_out, *refs):
    n2_s, n2t_s, up_s, acc_s, ht_s, back_s, gu_stage, down_stage, gu_sem, down_sem = refs[:10]
    step = pl.program_id(0)
    rows, width = x_ref.shape
    part = min(PART, rows)
    heads, _, cols = att_ref.shape
    blocks = ht_s.shape[0] // CUT
    wide = 2 * CUT
    tall = ht_s.shape[0] // DOWN
    chunks = [pl.ds(a, part) for a in range(0, rows, part)]
    sums = BlockSums(dp, gu_stage, *refs[10:], gu_out) if dp else None

    @pl.when(step == 0)
    def _():
        if dp:
            sums.place.greet()
        gain = gain_ref[...].astype(F32)
        scale = scale_ref[0, 0]
        for at in chunks:
            mid = x_ref[at].astype(F32)
            for j in range(heads):
                mid = mid + dot_nn(att_ref[j, at], wo_ref[j * cols : (j + 1) * cols])
            mid_ref[at] = mid
            inverse = lax.rsqrt(jnp.mean(mid * mid, axis=-1, keepdims=True) + EPSILON)
            low = (mid * inverse * gain).astype(BF)
            n2_s[at] = low
            if dp:
                gu_stage[0, :, :part] = low.T
                unit = gu_out.shape[0]
                for i, shard in enumerate(sums.order()):
                    there = pl.ds(pl.multiple_of(shard * unit, unit), unit)
                    n2t_s[i * unit : (i + 1) * unit, at] = gu_stage[0, there, :part]
            else:
                n2t_s[:, at] = low.T
            up_s[at] = (cot_ref[at].astype(F32) * scale).astype(BF)
        acc_s[...] = jnp.zeros_like(acc_s)
        nb_ref[...] = jnp.zeros_like(nb_ref)

    def gu_copy(j):
        slot = lax.rem(j, 2)
        return pltpu.make_async_copy(
            gu_stage.at[slot],
            gu_out.at[:, pl.ds(pl.multiple_of(j * wide, wide), wide)],
            gu_sem.at[slot],
        )

    def advance(phases):
        for phase in phases:
            j = step - phase
            for odd in range(2):

                @pl.when(
                    jnp.logical_and(
                        jnp.logical_and(step >= phase, step < phase + blocks), lax.rem(j, 2) == odd
                    )
                )
                def _(j=j, odd=odd, phase=phase):
                    sums.advance(j, odd, phase)

    @pl.when(step < blocks)
    def _():
        for at in chunks:
            both = dot_nn(n2_s[at], gu_ref[...])
            gate, up = both[:, :CUT], both[:, CUT:]
            back = dot_nt(up_s[at], down_ref[...])
            sig = 0.5 * jnp.tanh(0.5 * gate) + 0.5
            act = gate * sig
            hidden = (act * up).astype(BF)
            ht_s[pl.ds(pl.multiple_of(step * CUT, CUT), CUT), at] = hidden.T
            back_s[at, :CUT] = (back * up * sig * (1.0 + gate * (1.0 - sig))).astype(BF)
            back_s[at, CUT:] = (back * act).astype(BF)
            acc_s[at] += dot_nn(hidden, down_ref[...])
            nb_ref[at] += dot_nt(back_s[at], gu_ref[...])

    if dp:
        advance((4, 3, 2, 1))

    @pl.when(jnp.logical_and(step >= 2, step < blocks))
    def _():
        if dp:
            sums.pair(step - 2).wait_send()
        else:
            gu_copy(step - 2).wait()

    @pl.when(step < blocks)
    def _():
        for a in range(0, width, TALL):
            gu_stage[lax.rem(step, 2), a : a + TALL] = dot_nn(
                n2t_s[a : a + TALL], back_s[...]
            ).astype(BF)
        if dp:
            sums.pair(step).start()
        else:
            gu_copy(step).start()

    def down_copy(p):
        slot = lax.rem(p, 2)
        there = down_out.at[pl.ds(pl.multiple_of(p * tall, tall), tall)]
        return pltpu.make_async_copy(down_stage.at[slot], there, down_sem.at[slot])

    @pl.when(step >= blocks)
    def _():
        p = step - blocks

        @pl.when(p == 0)
        def _():
            for at in chunks:
                res_ref[at] = (mid_ref[at] + acc_s[at]).astype(BF)

        @pl.when(p >= 2)
        def _():
            down_copy(p - 2).wait()

        grad = dot_nn(ht_s[pl.ds(pl.multiple_of(p * tall, tall), tall)], up_s[...])
        down_stage[lax.rem(p, 2)] = grad.astype(BF)
        down_copy(p).start()

        @pl.when(p == DOWN - 1)
        def _():
            if dp:
                sums.pair(blocks - 2).wait_send()
                sums.pair(blocks - 1).wait_send()
                sums.finish(blocks)
            else:
                gu_copy(blocks - 2).wait()
                gu_copy(blocks - 1).wait()
            down_copy(p - 1).wait()
            down_copy(p).wait()


def feed_forward(dp, scale, x, att, wo, gain, cot, gu, down):
    rows, width = x.shape
    size = down.shape[0]
    blocks, tall = size // CUT, size // DOWN
    once = pl.Buffered(1)

    def whole(w):
        return pl.BlockSpec(w.shape, lambda i: (0,) * len(w.shape), pipeline_mode=once)

    def last(i):
        return jnp.minimum(i, blocks - 1)

    shape = jax.ShapeDtypeStruct
    anywhere = pl.BlockSpec(memory_space=pl.ANY)
    out = [shape((rows, width), BF), shape((rows, width), F32), shape((rows, width), F32)]
    out_specs = [whole(w) for w in out]
    scratch = []
    params = {}
    if dp:
        out.append(shape((width // (4 * dp), 2 * size), F32))
        out_specs.append(whole(out[-1]))
        sem = pltpu.SemaphoreType.DMA((blocks, 3 + dp // 2))
        scratch = [pltpu.VMEM((blocks, width // 2, 2 * CUT), BF)] * 2 + [sem] * 2
        params = {"collective_id": 4, "has_side_effects": True}
    else:
        out.append(shape((width, 2 * size), BF))
        out_specs.append(anywhere)
    out.append(shape((size, width), BF))
    out_specs.append(anywhere)
    return pl.pallas_call(
        functools.partial(ffn_kernel, dp),
        grid=(blocks + DOWN,),
        in_specs=[
            pl.BlockSpec(memory_space=pltpu.SMEM),
            whole(x),
            whole(att),
            whole(wo),
            whole(gain),
            whole(cot),
            pl.BlockSpec((width, 2 * CUT), lambda i: (0, last(i))),
            pl.BlockSpec((CUT, width), lambda i: (last(i), 0)),
        ],
        out_specs=out_specs,
        out_shape=out,
        scratch_shapes=[
            pltpu.VMEM((rows, width), BF),
            pltpu.VMEM((width, rows), BF),
            pltpu.VMEM((rows, width), BF),
            pltpu.VMEM((rows, width), F32),
            pltpu.VMEM((size, rows), BF),
            pltpu.VMEM((rows, 2 * CUT), BF),
            pltpu.VMEM((2, width, 2 * CUT), BF),
            pltpu.VMEM((2, tall, width), BF),
            pltpu.SemaphoreType.DMA((2,)),
            pltpu.SemaphoreType.DMA((2,)),
            *scratch,
        ],
        compiler_params=pltpu.CompilerParams(vmem_limit_bytes=63 * 2**20, **params),
        cost_estimate=cost(18 * rows * width * size),
    )(scale, x, att, wo, gain, cot, gu, down)


def branch_kernel(scale_ref, mid_ref, nb_ref, cot_ref, att_ref, wo_ref, gain_ref,
                  mg_ref, send_ref, og_ref, gg_ref, branch_s):
    step = pl.program_id(0)
    part, width = mid_ref.shape
    heads, rows, cols = att_ref.shape
    mid, nback, gain = mid_ref[...], nb_ref[...], gain_ref[...].astype(F32)
    inverse = lax.rsqrt(jnp.mean(mid * mid, axis=-1, keepdims=True) + EPSILON)
    scaled = nback * gain
    middle_grad = cot_ref[...].astype(F32) * scale_ref[0, 0] + (
        inverse * scaled
        - mid * (inverse * inverse * inverse) * jnp.mean(scaled * mid, axis=-1, keepdims=True)
    )
    gain_part = jnp.sum(nback * mid * inverse, axis=0, keepdims=True)
    mg_ref[...] = middle_grad
    branch = middle_grad.astype(BF)
    branch_s[pl.ds(pl.multiple_of(step * part, part), part)] = branch
    for j in range(heads):
        send_ref[j] = dot_nt(branch, wo_ref[j * cols : (j + 1) * cols]).astype(BF)

    @pl.when(step == 0)
    def _():
        gg_ref[...] = gain_part

    @pl.when(step > 0)
    def _():
        gg_ref[...] += gain_part

    @pl.when(step == rows // part - 1)
    def _():
        for j in range(heads):
            og_ref[j * cols : (j + 1) * cols] = dot_tn(att_ref[j], branch_s[...]).astype(BF)


def branch_back(scale, mid, nback, cot, att, wo, gain):
    rows, width = mid.shape
    heads, _, cols = att.shape
    part = min(256, rows)
    rowwise = pl.BlockSpec((part, width), lambda i: (i, 0))

    def whole(w):
        return pl.BlockSpec(w.shape, lambda i: (0,) * len(w.shape))

    out = [
        jax.ShapeDtypeStruct((rows, width), F32),
        jax.ShapeDtypeStruct((heads, rows, cols), BF),
        jax.ShapeDtypeStruct((width, width), BF),
        jax.ShapeDtypeStruct((1, width), F32),
    ]
    return pl.pallas_call(
        branch_kernel,
        grid=(rows // part,),
        in_specs=[
            pl.BlockSpec(memory_space=pltpu.SMEM),
            rowwise,
            rowwise,
            rowwise,
            whole(att),
            whole(wo),
            whole(gain),
        ],
        out_specs=[
            rowwise,
            pl.BlockSpec((heads, part, cols), lambda i: (0, i, 0)),
            whole(out[2]),
            whole(out[3]),
        ],
        out_shape=out,
        scratch_shapes=[pltpu.VMEM((rows, width), BF)],
        compiler_params=pltpu.CompilerParams(vmem_limit_bytes=48 * 2**20),
        cost_estimate=cost(4 * rows * width * width),
    )(scale, mid, nback, cot, att, wo, gain)


HEADS = 16
KVH = 2
LATD = 256
HG = 8
GROUPS = 8
ALL = ("dp", "seq", "grp")


def norm_parts(values, gain):
    inverse = lax.rsqrt(jnp.mean(values * values, axis=-1, keepdims=True) + EPSILON)
    return (values * inverse * gain, inverse)


def norm_back(values, inverse, gain, upstream):
    scaled = upstream * gain
    gain_grad = jnp.sum(upstream * values * inverse, axis=0)
    input_part = inverse * scaled - values * inverse**3 * jnp.mean(
        scaled * values, axis=-1, keepdims=True
    )
    return (input_part, gain_grad)


def swap_sequences(blocks, count):
    if count == 2:
        me = lax.axis_index("seq")
        sent = lax.ppermute(blocks[1 - me], "seq", [(0, 1), (1, 0)])
        kept = blocks[me]
        first = me == 0
        return jnp.stack([jnp.where(first, kept, sent), jnp.where(first, sent, kept)])
    return lax.all_to_all(blocks, "seq", 0, 0, tiled=True)


def swap_group(blocks):
    return lax.all_to_all(blocks, "grp", 0, 0, tiled=True)


def local(
    inputs,
    cotangent,
    group_ids,
    group_scale,
    norm_gain,
    w_query,
    w_latent,
    expansion_weight,
    w_output,
    ffn_gain,
    w_gate,
    w_up,
    w_down,
):
    devices = lax.axis_size("dp") * lax.axis_size("seq") * lax.axis_size("grp")
    groups = lax.axis_size("grp")
    me = lax.axis_index("grp")
    seqs, rows, width = inputs.shape
    count = seqs * rows
    hidden_size = w_gate.shape[1]
    heads = HEADS // groups
    cols = heads * DH
    drows = width // devices

    dp = lax.axis_size("dp")
    ring = groups == 2 and seqs == 2 and dp % 2 == 0
    expand_rows = expansion_weight.reshape(-1, expansion_weight.shape[2])
    gains = jnp.pad(jnp.concatenate([norm_gain, ffn_gain])[None], ((0, 15), (0, 128 - 2 * drows)))
    if ring:
        shards = (w_query, w_latent, expand_rows, gains)
        full, own_inputs = own_gather(dp, shards, inputs, ("xzy",) * 4)
    else:
        shards = (w_query, w_latent, expand_rows, gains, w_output, w_down)
        full = [lax.all_gather(w, ALL, axis=0) for w in shards]
        own_inputs = swap_sequences(inputs, seqs)
    gate_up = jnp.stack(
        [w_gate.reshape(drows, -1, CUT), w_up.reshape(drows, -1, CUT)], axis=2
    ).reshape(drows, -1)
    gu_full = lax.all_gather(gate_up, ALL, axis=0, tiled=True)
    query_full = full[0].reshape(width, -1)
    latent_full = full[1].reshape(width, -1)
    expand_full = full[2].reshape(devices, KVH, LATD // devices, -1)
    gain_one = full[3][:, 0, :drows].reshape(width).astype(F32)
    gain_two = full[3][:, 0, drows : 2 * drows].reshape(1, width)

    token_rows = own_inputs.astype(F32).reshape(count, width)
    normed, inverse_one = norm_parts(token_rows, gain_one)
    normed_low = normed.astype(BF)
    query_send = jnp.stack(
        [dot_nn(normed_low, query_full[:, j * cols : (j + 1) * cols]).astype(BF) for j in range(groups)]
    ).reshape(groups, seqs, rows, cols)
    latent_state = [
        dot_nn(normed_low, latent_full[:, g * LATD : (g + 1) * LATD]).astype(BF) for g in range(KVH)
    ]
    latent_send = jnp.stack([latent_state[j * heads // HG] for j in range(groups)]).reshape(
        groups, seqs, rows, LATD
    )
    head_queries = swap_group(query_send)
    head_latent = swap_group(latent_send).transpose(1, 0, 2, 3).reshape(-1, LATD)
    expand_local = lax.dynamic_slice(
        expand_full,
        (0, me * heads // HG, 0, me * heads % HG * 2 * DH),
        (devices, 1, LATD // devices, heads * 2 * DH),
    ).reshape(LATD, -1)
    head_pairs = dot_nn(head_latent, expand_local).astype(BF)
    if ring:
        half = width // 2
        attended, logsum, own_cotangent, output_full, down_full = attention_forward_gather(
            dp,
            head_queries,
            head_pairs,
            cotangent,
            (w_output, w_down),
            ((0, 0, width), (1, 0, half), (1, half, half)),
            ("xzy", "zyx", "zxy"),
        )
    else:
        attended, logsum = attention_forward(head_queries, head_pairs)
        own_cotangent = swap_sequences(cotangent, seqs)
        output_full, down_full = full[4:]
    output_full = output_full.reshape(-1, width)
    down_full = down_full.reshape(-1, width)
    token_attended = swap_group(attended).reshape(groups, count, cols)
    seq_group = lax.dynamic_index_in_dim(group_ids, lax.axis_index("seq"), 0, keepdims=False)
    chosen = (seq_group == jnp.arange(GROUPS)).astype(F32)
    seq_scale = jnp.sum(chosen * group_scale).reshape(1, 1)
    x_rows = own_inputs.reshape(count, width)
    cot_rows = own_cotangent.reshape(count, width)
    result, middle, normed_two_back, gu_share, down_grad = feed_forward(
        dp if ring else None,
        seq_scale,
        x_rows,
        token_attended,
        output_full,
        gain_two,
        cot_rows,
        gu_full,
        down_full,
    )
    own_output = result.reshape(seqs, rows, width)
    if not ring:
        gu_share = lax.psum_scatter(gu_share, ALL, scatter_dimension=0, tiled=True).astype(F32)
    gu_share = gu_share.reshape(drows, -1, 2, CUT)
    middle_grad, back_send, output_grad, gain_two_grad = branch_back(
        seq_scale, middle, normed_two_back, cot_rows, token_attended, output_full, gain_two
    )
    head_upstream = swap_group(back_send.reshape(groups, seqs, rows, cols))
    terms = (output_grad.reshape(devices, drows, width), down_grad.reshape(devices, -1, width))
    attention = (head_queries, head_pairs, head_upstream, attended, logsum)
    if ring:
        half = width // 2
        query_back, pair_back, output, output_share, down_share = attention_backward_scatter(
            dp,
            *attention,
            own_output,
            terms,
            ((0, 0, width), (1, 0, half), (1, half, half)),
            ("yzx", "yxz", "xyz"),
        )
    else:
        query_back, pair_back = attention_backward(*attention)
        output = swap_sequences(own_output, seqs)
        output_share, down_share = [
            lax.psum_scatter(w, ALL, scatter_dimension=0, tiled=True)[0].astype(F32) for w in terms
        ]
    latent_terms = dot_nt(pair_back, expand_local).astype(BF)
    expand_part = dot_tn(head_latent, pair_back)
    expand_grad = lax.dynamic_update_slice(
        jnp.zeros(expand_full.shape, BF),
        expand_part.astype(BF).reshape(devices, 1, LATD // devices, -1),
        (0, me * heads // HG, 0, me * heads % HG * 2 * DH),
    )
    query_token = swap_group(query_back).reshape(groups, count, cols)
    latent_token = swap_group(
        latent_terms.reshape(seqs, groups, rows, LATD).transpose(1, 0, 2, 3)
    ).reshape(KVH, groups // KVH, count, LATD)
    latent_token = jnp.sum(latent_token.astype(F32), axis=1).astype(BF)
    query_grad = jnp.concatenate([dot_tn(normed_low, query_token[j]) for j in range(groups)], axis=1)
    latent_grad = jnp.concatenate([dot_tn(normed_low, latent_token[g]) for g in range(KVH)], axis=1)
    normed_back = sum(
        dot_nt(query_token[j], query_full[:, j * cols : (j + 1) * cols]) for j in range(groups)
    ) + sum(
        dot_nt(latent_token[g], latent_full[:, g * LATD : (g + 1) * LATD]) for g in range(KVH)
    )
    input_part, gain_one_grad = norm_back(token_rows, inverse_one, gain_one, normed_back)
    own_input_grad = (middle_grad + input_part).astype(BF).reshape(seqs, rows, width)
    gain_grads = jnp.concatenate(
        [gain_one_grad.reshape(devices, 1, drows), gain_two_grad.reshape(devices, 1, drows)], axis=2
    ).astype(BF)
    gain_grads = jnp.pad(gain_grads, ((0, 0), (0, 15), (0, 128 - 2 * drows)))
    terms = (
        query_grad.astype(BF).reshape(devices, drows, -1),
        latent_grad.astype(BF).reshape(devices, drows, -1),
        expand_grad.reshape(devices, -1, expand_grad.shape[3]),
        gain_grads,
    )
    if ring:
        sums, input_grad = own_scatter(dp, terms, ("yzx",) * 4, own_input_grad)
    else:
        sums = [
            lax.psum_scatter(w, ALL, scatter_dimension=0, tiled=True)[0].astype(F32) for w in terms
        ]
        input_grad = swap_sequences(own_input_grad, seqs)
    return (
        output,
        input_grad,
        sums[3][0, :drows],
        sums[0],
        sums[1],
        sums[2].reshape(expansion_weight.shape),
        output_share,
        sums[3][0, drows : 2 * drows],
        gu_share[:, :, 0].reshape(drows, -1),
        gu_share[:, :, 1].reshape(drows, -1),
        down_share,
    )


def solution(mesh):
    def run(*arrays):
        dp, sp = mesh.shape["dp"], mesh.shape["sp"]
        seqs = arrays[0].shape[0] // dp
        grid = Mesh(mesh.devices.reshape(dp, seqs, sp // seqs), ALL)
        tokens = P("dp", ("seq", "grp"), None)
        matrix = P(ALL, None)
        expand = P(None, ALL, None)
        return jax.shard_map(
            local,
            mesh=grid,
            in_specs=(
                tokens,
                tokens,
                P("dp"),
                P(),
                P(ALL),
                matrix,
                matrix,
                expand,
                matrix,
                P(ALL),
                matrix,
                matrix,
                matrix,
            ),
            out_specs=(
                tokens,
                tokens,
                P(ALL),
                matrix,
                matrix,
                expand,
                matrix,
                P(ALL),
                matrix,
                matrix,
                matrix,
            ),
            check_vma=False,
        )(*arrays)

    return run
```

```python
import functools
import jax
import jax.numpy as jnp
from jax import lax
from jax.sharding import Mesh
from jax.sharding import PartitionSpec as P
from jax.experimental import pallas as pl
from jax.experimental.pallas import tpu as pltpu

DH = 64
KVH = 2
EPSILON = 1e-05
F32 = jnp.float32
BF = jnp.bfloat16


def cost(flops):
    return pl.CostEstimate(flops=flops, bytes_accessed=2**23, transcendentals=0)


MESH = pl.DeviceIdType.MESH


class Place:

    def __init__(self, dp):
        self.sizes = {"x": 2, "y": 2, "z": dp // 2}
        d = lax.axis_index("dp")
        self.at = {"x": lax.axis_index("seq"), "y": lax.rem(d, 2), "z": lax.div(d, 2)}
        self.core = lax.axis_index("grp")

    def coords(self, offset):
        at = {k: lax.rem(self.at[k] + o, self.sizes[k]) if o else self.at[k] for k, o in offset.items()}
        return at["z"] * 2 + at["y"], at["x"]

    def index(self, offset, other):
        d, s = self.coords(offset)
        core = 1 - self.core if other else self.core
        return (d * 2 + s) * 2 + core

    def device(self, offset):
        return (*self.coords(offset), self.core)

    def pair(self):
        return (*self.coords({"x": 0, "y": 0, "z": 0}), 1 - self.core)

    def greet(self):
        there = [self.pair()]
        for k in "xyz":
            for o in range(1, self.sizes[k]):
                there.append(self.device({"x": 0, "y": 0, "z": 0, k: o}))
        barrier = pltpu.get_barrier_semaphore()
        for device in there:
            pl.semaphore_signal(barrier, inc=1, device_id=device, device_id_type=MESH)
        pl.semaphore_wait(barrier, len(there))


def offsets_of(order, dp):
    sizes = {"x": 2, "y": 2, "z": dp // 2}
    a, b, c = (sizes[k] for k in order)
    return [(i, j, k) for i in range(a) for j in range(b) for k in range(c)]


def named(order, steps):
    return dict(zip(order, steps))


def remote(src, dst, send, recv, there):
    return pltpu.make_async_remote_copy(
        src_ref=src, dst_ref=dst, send_sem=send, recv_sem=recv, device_id=there, device_id_type=MESH
    )


class Gather:

    def __init__(self, place, dp, order, src, out, sems, number):
        self.place, self.order, self.src, self.out = place, order, src, out
        self.steps = offsets_of(order, dp)
        self.sems, self.number = sems, number

    def slot(self, steps, other=False):
        return self.out(self.place.index(named(self.order, steps), other))

    def source(self, steps):
        last = max(i for i in range(3) if steps[i])
        return tuple(0 if i == last else o for i, o in enumerate(steps))

    def hop(self, steps):
        last = max(i for i in range(3) if steps[i])
        source = self.source(steps)
        size = self.place.sizes[self.order[last]]
        back = tuple(size - o if i == last else 0 for i, o in enumerate(steps))
        number = self.steps.index(steps)
        here = self.slot(source)
        src = here if any(source) else self.src
        return remote(
            src,
            here,
            self.sems[0].at[self.number, number],
            self.sems[1].at[self.number, number],
            self.place.device(named(self.order, back)),
        )

    def across(self, steps):
        number = self.steps.index(steps)
        src = self.slot(steps) if any(steps) else self.src
        return remote(
            src,
            self.slot(steps),
            self.sems[2].at[self.number, number],
            self.sems[3].at[self.number, number],
            self.place.pair(),
        )

    def keep(self):
        return pltpu.make_async_copy(self.src, self.slot((0, 0, 0)), self.sems[4].at[self.number])

    def send_from(self, source):
        for steps in self.steps:
            if any(steps) and self.source(steps) == source:
                self.hop(steps).start()
        self.across(source).start()

    def start(self):
        self.send_from((0, 0, 0))
        self.keep().start()

    def arrivals(self):
        return sorted((s for s in self.steps if any(s)), key=lambda s: [o > 0 for o in s][::-1])

    def forward(self, steps):
        number = self.steps.index(steps)
        here = self.slot(steps)
        remote(
            here,
            here,
            self.sems[0].at[self.number, number],
            self.sems[1].at[self.number, number],
            self.place.pair(),
        ).wait_recv()
        self.send_from(steps)

    def finish(self):
        for steps in self.steps:
            number = self.steps.index(steps)
            here = self.slot(steps, True)
            remote(
                here,
                here,
                self.sems[2].at[self.number, number],
                self.sems[3].at[self.number, number],
                self.place.pair(),
            ).wait_recv()
            self.across(steps).wait_send()
            if any(steps):
                self.hop(steps).wait_send()
        self.keep().wait()


class Scatter:

    def __init__(self, place, dp, order, term, pair_buf, ring_buf, sems, number, own=None):
        self.place, self.order, self.term = place, order, term
        self.own_buf, self.own_sem = own if own else (None, None)
        self.steps = offsets_of(order, dp)
        self.pair_buf, self.ring_buf = pair_buf, ring_buf
        self.sems, self.number = sems, number

    def turn(self):
        def key(steps):
            first = next((i for i in range(3) if steps[i]), 3)
            return (first, [o == 0 for o in steps])

        return sorted(self.steps, key=key)

    def across(self, steps):
        number = self.steps.index(steps)
        return remote(
            self.term(self.place.index(named(self.order, steps), True)),
            self.pair_buf.at[number],
            self.sems[2].at[self.number, number],
            self.sems[3].at[self.number, number],
            self.place.pair(),
        )

    def fetch(self, steps):
        number = self.steps.index(steps)
        return pltpu.make_async_copy(
            self.term(self.place.index(named(self.order, steps), False)),
            self.own_buf.at[number],
            self.own_sem.at[self.number, number],
        )

    def start(self):
        for steps in self.turn():
            self.across(steps).start()
            if self.own_buf is not None:
                self.fetch(steps).start()

    def hop(self, steps):
        first = min(i for i in range(3) if steps[i])
        there = tuple(o if i == first else 0 for i, o in enumerate(steps))
        number = self.steps.index(steps)
        return remote(
            self.pair_buf.at[number],
            self.ring_buf.at[number],
            self.sems[0].at[self.number, number],
            self.sems[1].at[self.number, number],
            self.place.device(named(self.order, there)),
        )

    def add(self, steps, out=None):
        number = self.steps.index(steps)
        self.across(steps).wait_recv()
        if self.own_buf is None:
            mine = self.term(self.place.index(named(self.order, steps), False))
        else:
            self.fetch(steps).wait()
            mine = self.own_buf.at[number]
        total = mine[...].astype(F32) + self.pair_buf[number].astype(F32)
        for came in self.steps:
            if not any(came):
                continue
            first = min(i for i in range(3) if came[i])
            if tuple(0 if i == first else o for i, o in enumerate(came)) == steps:
                self.hop(came).wait_recv()
                total = total + self.ring_buf[self.steps.index(came)].astype(F32)
        if out is None:
            self.pair_buf[number] = total.astype(BF)
            self.hop(steps).start()
        else:
            out[...] = total

    def finish(self):
        for steps in self.steps:
            self.across(steps).wait_send()
            if any(steps):
                self.hop(steps).wait_send()


def block_swap(x_in, x_out, sem, place):
    s = place.at["x"]
    away = remote(
        x_in.at[1 - s], x_out.at[s], sem.at[0], sem.at[1], place.device({"x": 1, "y": 0, "z": 0})
    )
    return away, pltpu.make_async_copy(x_in.at[s], x_out.at[s], sem.at[2])


def gather_kernel(dp, orders, *refs):
    count = len(orders)
    srcs, x_in = refs[:count], refs[count]
    outs, x_out = refs[count + 1 : 2 * count + 1], refs[2 * count + 1]
    sems, x_sem = refs[2 * count + 2 : -1], refs[-1]
    place = Place(dp)
    place.greet()
    works = [
        Gather(place, dp, orders[a], srcs[a], lambda at, a=a: outs[a].at[at], sems, a)
        for a in range(count)
    ]
    for work in works:
        work.start()
    swap, kept = block_swap(x_in, x_out, x_sem, place)
    swap.start()
    kept.start()
    for i in range(2 * dp - 1):
        for work in works:
            work.forward(work.arrivals()[i])
    for work in works:
        work.finish()
    swap.wait()
    kept.wait()


def gather_sems(dp, count):
    sem = pltpu.SemaphoreType.DMA
    return [sem((count, 2 * dp))] * 4 + [sem((count,))]


def own_gather(dp, shards, blocks, orders):
    count = len(shards)
    anywhere = pl.BlockSpec(memory_space=pl.ANY)
    out = pl.pallas_call(
        functools.partial(gather_kernel, dp, orders),
        in_specs=[anywhere] * (count + 1),
        out_specs=[anywhere] * (count + 1),
        out_shape=[jax.ShapeDtypeStruct((4 * dp, *w.shape), w.dtype) for w in shards]
        + [jax.ShapeDtypeStruct(blocks.shape, blocks.dtype)],
        scratch_shapes=gather_sems(dp, count) + [pltpu.SemaphoreType.DMA((3,))],
        compiler_params=pltpu.CompilerParams(collective_id=0, has_side_effects=True),
    )(*shards, blocks)
    return out[:-1], out[-1]


def scatter_sems(dp, count):
    return [pltpu.SemaphoreType.DMA((count, 2 * dp))] * 4


def run_at(plan, point):
    for step in sorted({k[0] for k in plan if k[1] == point}):
        tasks = plan[step, point]

        @pl.when(pl.program_id(0) == step)
        def _(tasks=tasks):
            for task in tasks:
                task()


def gather_plan(place, works, swap, steps, points):
    arrivals = [work.arrivals() for work in works]
    total = steps * points

    def begin():
        place.greet()
        for work in works:
            work.start()
        for copy in swap:
            copy.start()

    def forward(i):
        for work, order in zip(works, arrivals):
            work.forward(order[i])

    def end():
        for work in works:
            work.finish()
        for copy in swap:
            copy.wait()

    plan = {}
    count = len(arrivals[0])
    plan[0, 0] = [begin]
    for i in range(count):
        at = 2 + i * (total - 3) // count
        plan.setdefault(divmod(at, points), []).append(functools.partial(forward, i))
    plan.setdefault(divmod(total, points), []).append(end)
    return plan


def scatter_plan(place, works, outs, swap, steps, points):
    turns = [work.turn() for work in works]
    total = steps * points
    count = len(turns[0])

    def begin():
        place.greet()
        for work in works:
            work.start()
        for copy in swap:
            copy.start()

    def add(i):
        for work, order, out in zip(works, turns, outs):
            work.add(order[i], out if i == count - 1 else None)

    def end():
        for work in works:
            work.finish()
        for copy in swap:
            copy.wait()

    plan = {(0, 0): [begin]}
    for i in range(count):
        at = 1 + i // 2 if i < count // 2 else 6 + (i - count // 2) * (total - 6) // (count - count // 2)
        plan.setdefault(divmod(at, points), []).append(functools.partial(add, i))
    plan.setdefault(divmod(total, points), []).append(end)
    return plan


def dot_nt(a, b):
    return lax.dot_general(a, b, (((1,), (1,)), ((), ())), preferred_element_type=F32)


def dot_nn(a, b):
    return lax.dot_general(a, b, (((1,), (0,)), ((), ())), preferred_element_type=F32)


def dot_tn(a, b):
    return lax.dot_general(a, b, (((0,), (0,)), ((), ())), preferred_element_type=F32)


def causal(s, first_key, first_query):
    keys = first_key + lax.broadcasted_iota(jnp.int32, s.shape, 0)
    rows = first_query + lax.broadcasted_iota(jnp.int32, s.shape, 1)
    return jnp.where(rows >= keys, s, -1e30)


def forward_body(q_ref, kv_ref, o_ref, lse_ref, vt_s, point=lambda i: None):
    groups, chunks, rows, _ = q_ref.shape
    seq = kv_ref.shape[0]
    for h in range(2):
        vt_s[h] = kv_ref[:, h * 128 : (h + 1) * 128].astype(F32).T[DH:].astype(BF)
    for i in range(groups * chunks):
        point(i)
        q = q_ref[i % groups, i // groups].astype(F32) * 0.125
        outs = []
        for h in range(2):
            qh = q[:, h * DH : (h + 1) * DH]
            qp = jnp.concatenate([qh, jnp.zeros_like(qh)], axis=1).astype(BF)
            width = (i + 1) * rows
            s = dot_nt(kv_ref[0:width, h * 128 : (h + 1) * 128], qp)
            tail = causal(s[i * rows :], 0, 0)
            if i > 0:
                head = s[: i * rows]
                top = jnp.maximum(
                    jnp.max(head, axis=0, keepdims=True), jnp.max(tail, axis=0, keepdims=True)
                )
                ph = jnp.exp(head - top)
                pt = jnp.exp(tail - top)
                total = jnp.sum(ph, axis=0, keepdims=True) + jnp.sum(pt, axis=0, keepdims=True)
                o = dot_nn(vt_s[h, :, 0 : i * rows], ph.astype(BF)) + dot_nn(
                    vt_s[h, :, i * rows : width], pt.astype(BF)
                )
            else:
                top = jnp.max(tail, axis=0, keepdims=True)
                pt = jnp.exp(tail - top)
                total = jnp.sum(pt, axis=0, keepdims=True)
                o = dot_nn(vt_s[h, :, 0:width], pt.astype(BF))
            outs.append(o / total)
            lse_ref[h, i * rows : (i + 1) * rows] = (top + jnp.log(total))[0]
        o_ref[i % groups, i // groups] = jnp.concatenate(outs, axis=0).T.astype(BF)


def forward_kernel(q_ref, kv_ref, o_ref, lse_ref, vt_s):
    forward_body(q_ref, kv_ref, o_ref, lse_ref, vt_s)


def forward_gather_kernel(dp, cuts, orders, pairs, *refs):
    q_ref, kv_ref, x_in = refs[:3]
    sources = 1 + max(cut[0] for cut in cuts)
    srcs, refs = refs[3 : 3 + sources], refs[3 + sources :]
    o_ref, lse_ref, x_out = refs[:3]
    outs, refs = refs[3 : 3 + sources], refs[3 + sources :]
    vt_s, x_sem, sems = refs[0], refs[1], refs[2:]
    place = Place(dp)
    works = []
    for number, (a, first, size) in enumerate(cuts):
        cut = pl.ds(first, size)
        works.append(
            Gather(
                place,
                dp,
                orders[number],
                srcs[a].at[:, cut],
                lambda at, a=a, cut=cut: outs[a].at[at, :, cut],
                sems,
                number,
            )
        )
    points = q_ref.shape[0] * q_ref.shape[1]
    plan = gather_plan(place, works, block_swap(x_in, x_out, x_sem, place), pairs, points)
    forward_body(q_ref, kv_ref, o_ref, lse_ref, vt_s, lambda i: run_at(plan, i))
    for point in range(points):
        tasks = plan.get((pairs, point))
        if tasks:

            @pl.when(pl.program_id(0) == pairs - 1)
            def _(tasks=tasks):
                for task in tasks:
                    task()


def forward_specs(q, kv):
    groups, chunks, rows, cols = q.shape
    seq = kv.shape[0]
    pairs = cols // 128
    tok = pl.BlockSpec((groups, chunks, rows, 128), lambda p: (0, 0, 0, p))
    ins = [tok, pl.BlockSpec((seq, 256), lambda p: (0, p))]
    outs = [tok, pl.BlockSpec((None, 2, seq), lambda p: (p, 0, 0))]
    shapes = [jax.ShapeDtypeStruct(q.shape, BF), jax.ShapeDtypeStruct((pairs, 2, seq), F32)]
    scratch = [pltpu.VMEM((2, DH, seq), BF)]
    return pairs, ins, outs, shapes, scratch, cost(8 * pairs * seq * seq * 128)


def attention_forward(q, kv):
    pairs, ins, outs, shapes, scratch, estimate = forward_specs(q, kv)
    return pl.pallas_call(
        forward_kernel,
        grid=(pairs,),
        in_specs=ins,
        out_specs=outs,
        out_shape=shapes,
        scratch_shapes=scratch,
        compiler_params=pltpu.CompilerParams(vmem_limit_bytes=56 * 2**20),
        cost_estimate=estimate,
    )(q, kv)


def attention_forward_gather(dp, q, kv, blocks, shards, cuts, orders):
    pairs, ins, outs, shapes, scratch, estimate = forward_specs(q, kv)
    anywhere = pl.BlockSpec(memory_space=pl.ANY)
    count = len(shards)
    return pl.pallas_call(
        functools.partial(forward_gather_kernel, dp, cuts, orders, pairs),
        grid=(pairs,),
        in_specs=ins + [anywhere] * (1 + count),
        out_specs=outs + [anywhere] * (1 + count),
        out_shape=shapes
        + [jax.ShapeDtypeStruct(blocks.shape, blocks.dtype)]
        + [jax.ShapeDtypeStruct((4 * dp, *w.shape), w.dtype) for w in shards],
        scratch_shapes=scratch + [pltpu.SemaphoreType.DMA((3,))] + gather_sems(dp, len(cuts)),
        compiler_params=pltpu.CompilerParams(
            vmem_limit_bytes=56 * 2**20, collective_id=2, has_side_effects=True
        ),
        cost_estimate=estimate,
    )(q, kv, blocks, *shards)


def backward_body(blk, q_ref, kv_ref, do_ref, o_ref, lse_ref, dq_ref, dkv_ref,
                  kt_s, acc_s, dqt_s, qp_s, dop_s, delta_s, point=lambda i: None):
    groups, chunks, rows, _ = q_ref.shape
    seq = kv_ref.shape[0]
    n = groups * chunks
    for h in range(2):
        kt_s[h] = kv_ref[:, h * 128 : (h + 1) * 128].astype(F32).T[:DH].astype(BF)
    acc_s[...] = jnp.zeros_like(acc_s)
    for i in range(n):
        at = pl.ds(i * rows, rows)
        q = q_ref[i % groups, i // groups].astype(F32) * 0.125
        do = do_ref[i % groups, i // groups].astype(F32)
        o = o_ref[i % groups, i // groups].astype(F32)
        prod = (do * o).T
        zero = jnp.zeros((rows, DH), F32)
        for h in range(2):
            cut = slice(h * DH, (h + 1) * DH)
            qp_s[h, at] = jnp.concatenate([q[:, cut], zero], axis=1).astype(BF)
            dop_s[h, at] = jnp.concatenate([zero, do[:, cut]], axis=1).astype(BF)
            delta_s[h, at] = jnp.sum(prod[cut], axis=0)

    def block(i, j, masked):
        qat = pl.ds(i * blk, blk)
        kat = pl.ds(pl.multiple_of(j * blk, blk), blk)
        for h in range(2):
            kv = kv_ref[kat, h * 128 : (h + 1) * 128]
            qp = qp_s[h, qat]
            dop = dop_s[h, qat]
            s = dot_nt(kv, qp)
            dp = dot_nt(kv, dop)
            if masked:
                s = causal(s, 0, 0)
            p = jnp.exp(s - lse_ref[h : h + 1, qat])
            ds = (p * (dp - delta_s[h : h + 1, qat])).astype(BF)
            acc_s[h, kat] += dot_nn(p.astype(BF), dop) + dot_nn(ds, qp)
            part = dot_nn(kt_s[h, :, kat], ds)
            if masked:
                dqt_s[h * DH : (h + 1) * DH, qat] = part
            else:
                dqt_s[h * DH : (h + 1) * DH, qat] += part

    m = seq // blk

    for i in range(m):
        point(i)
        block(i, i, True)

        def inner(j, _, i=i):
            block(i, j, False)
            return 0

        lax.fori_loop(0, i, inner, 0)
    for i in range(n):
        at = pl.ds(i * rows, rows)
        dq_ref[i % groups, i // groups] = (dqt_s[:, at].T * 0.125).astype(BF)
    for h in range(2):
        dkv_ref[:, h * 128 : (h + 1) * 128] = acc_s[h].astype(BF)


def backward_kernel(blk, *refs):
    backward_body(blk, *refs)


def backward_scatter_kernel(dp, blk, cuts, orders, pairs, *refs):
    ins, x_in, refs = refs[:5], refs[5], refs[6:]
    sources = 1 + max(cut[0] for cut in cuts)
    count = len(cuts)
    terms, refs = refs[:sources], refs[sources:]
    attn_outs, x_out, refs = refs[:2], refs[2], refs[3:]
    outs, refs = refs[:sources], refs[sources:]
    scratch, x_sem, refs = refs[:6], refs[6], refs[7:]
    own_bufs, pair_bufs, ring_bufs = refs[:count], refs[count : 2 * count], refs[2 * count : 3 * count]
    own_sem, sems = refs[3 * count], refs[3 * count + 1 :]
    place = Place(dp)
    works, targets = [], []
    for number, (a, first, size) in enumerate(cuts):
        cut = pl.ds(first, size)
        works.append(
            Scatter(
                place,
                dp,
                orders[number],
                lambda at, a=a, cut=cut: terms[a].at[at, :, cut],
                pair_bufs[number],
                ring_bufs[number],
                sems,
                number,
                (own_bufs[number], own_sem),
            )
        )
        targets.append(outs[a].at[:, cut])
    points = ins[1].shape[0] // blk
    plan = scatter_plan(place, works, targets, block_swap(x_in, x_out, x_sem, place), pairs, points)
    backward_body(blk, *ins, *attn_outs, *scratch, point=lambda i: run_at(plan, i))
    for point in range(points):
        tasks = plan.get((pairs, point))
        if tasks:

            @pl.when(pl.program_id(0) == pairs - 1)
            def _(tasks=tasks):
                for task in tasks:
                    task()


def backward_specs(q, kv):
    groups, chunks, rows, cols = q.shape
    seq = kv.shape[0]
    pairs = cols // 128
    tok = pl.BlockSpec((groups, chunks, rows, 128), lambda p: (0, 0, 0, p))
    wide = pl.BlockSpec((seq, 256), lambda p: (0, p))
    ins = [tok, wide, tok, tok, pl.BlockSpec((None, 2, seq), lambda p: (p, 0, 0))]
    outs = [tok, wide]
    shapes = [jax.ShapeDtypeStruct(q.shape, BF), jax.ShapeDtypeStruct(kv.shape, BF)]
    scratch = [
        pltpu.VMEM((2, DH, seq), BF),
        pltpu.VMEM((2, seq, 128), F32),
        pltpu.VMEM((128, seq), F32),
        pltpu.VMEM((2, seq, 128), BF),
        pltpu.VMEM((2, seq, 128), BF),
        pltpu.VMEM((2, seq), F32),
    ]
    return pairs, ins, outs, shapes, scratch, cost(16 * pairs * seq * seq * 128)


def attention_backward(q, kv, do, o, lse, blk=512):
    pairs, ins, outs, shapes, scratch, estimate = backward_specs(q, kv)
    return pl.pallas_call(
        functools.partial(backward_kernel, blk),
        grid=(pairs,),
        in_specs=ins,
        out_specs=outs,
        out_shape=shapes,
        scratch_shapes=scratch,
        compiler_params=pltpu.CompilerParams(vmem_limit_bytes=56 * 2**20),
        cost_estimate=estimate,
    )(q, kv, do, o, lse)


def attention_backward_scatter(dp, q, kv, do, o, lse, blocks, terms, cuts, orders, blk=512):
    pairs, ins, outs, shapes, scratch, estimate = backward_specs(q, kv)
    anywhere = pl.BlockSpec(memory_space=pl.ANY)
    count = len(cuts)
    bufs = [pltpu.VMEM((2 * dp, terms[a].shape[1], size), BF) for a, _, size in cuts]
    return pl.pallas_call(
        functools.partial(backward_scatter_kernel, dp, blk, cuts, orders, pairs),
        grid=(pairs,),
        in_specs=ins + [anywhere] * (1 + len(terms)),
        out_specs=outs + [anywhere] + [pl.BlockSpec(w.shape[1:], lambda p: (0, 0)) for w in terms],
        out_shape=shapes
        + [jax.ShapeDtypeStruct(blocks.shape, blocks.dtype)]
        + [jax.ShapeDtypeStruct(w.shape[1:], F32) for w in terms],
        scratch_shapes=scratch
        + [pltpu.SemaphoreType.DMA((3,))]
        + bufs * 3
        + [pltpu.SemaphoreType.DMA((count, 2 * dp))]
        + scatter_sems(dp, count),
        compiler_params=pltpu.CompilerParams(
            vmem_limit_bytes=60 * 2**20, collective_id=3, has_side_effects=True
        ),
        cost_estimate=estimate,
    )(q, kv, do, o, lse, blocks, *terms)


CUT = 256
PART = 512
TALL = 512
DOWN = 8
LAGS = (1, 3, 5, 7)


class BlockSums:

    def __init__(self, dp, stage, pair_buf, ring_buf, send, recv, out_ref):
        self.place = Place(dp)
        self.stage, self.pair_buf, self.ring_buf = stage, pair_buf, ring_buf
        self.send, self.recv, self.out_ref = send, recv, out_ref
        self.total = pair_buf.shape[1]
        self.unit = out_ref.shape[0]

    def order(self):
        return [
            self.place.index({"y": y, "x": x, "z": z}, other)
            for other in (False, True)
            for y in range(2)
            for x in range(2)
            for z in range(self.place.sizes["z"])
        ]

    def pair(self, j):
        return remote(
            self.stage.at[lax.rem(j, self.stage.shape[0]), pl.ds(self.total, self.total)],
            self.pair_buf.at[j],
            self.send.at[j, 0],
            self.recv.at[j, 0],
            self.place.pair(),
        )

    def hop(self, j, axis, step, first, size, number):
        rows = pl.ds(first, size)
        offset = {"x": 0, "y": 0, "z": 0, axis: step}
        return remote(
            self.pair_buf.at[j, rows],
            self.ring_buf.at[j, rows],
            self.send.at[j, number],
            self.recv.at[j, number],
            self.place.device(offset),
        )

    def hops(self, odd, phase):
        q = self.total // 4
        if phase == 3:
            sizes = range(1, self.place.sizes["z"])
            return [("z", z, z * self.unit, self.unit, 3 + z) for z in sizes]
        if odd:
            return ([("x", 1, q, q, 1), ("x", 1, 3 * q, q, 2)], [("y", 1, 2 * q, q, 3)])[phase - 1]
        return ([("y", 1, 2 * q, 2 * q, 1)], [("x", 1, q, q, 3)])[phase - 1]

    def add(self, j, to, size, came):
        self.pair_buf[j, to : to + size] = (
            self.pair_buf[j, to : to + size].astype(F32) + came.astype(F32)
        ).astype(BF)

    def advance(self, j, odd, phase):
        q = self.total // 4
        if phase == 1:
            self.pair(j).wait_recv()
            self.add(j, 0, self.total, self.stage[lax.rem(j, self.stage.shape[0]), : self.total])
        else:
            for hop in self.hops(odd, phase - 1):
                self.hop(j, *hop).wait_recv()
        if phase == 2 and odd:
            self.add(j, 0, q, self.ring_buf[j, q : 2 * q])
            self.add(j, 2 * q, q, self.ring_buf[j, 3 * q :])
        elif phase == 2:
            self.add(j, 0, 2 * q, self.ring_buf[j, 2 * q :])
        elif phase == 3:
            first = 2 * q if odd else q
            self.add(j, 0, q, self.ring_buf[j, first : first + q])
        elif phase == 4:
            total = self.pair_buf[j, : self.unit].astype(F32)
            for z in range(1, self.place.sizes["z"]):
                total = total + self.ring_buf[j, z * self.unit : (z + 1) * self.unit].astype(F32)
            wide = total.shape[1]
            self.out_ref[:, pl.ds(pl.multiple_of(j * wide, wide), wide)] = total
        if phase < 4:
            for hop in self.hops(odd, phase):
                self.hop(j, *hop).start()

    def finish(self, parities):
        for j, odd in enumerate(parities):
            for phase in range(1, 4):
                for hop in self.hops(odd, phase):
                    self.hop(j, *hop).wait_send()


def ffn_kernel(dp, scale_ref, x_ref, att_ref, wo_ref, gain_ref, cot_ref, gu_ref, down_ref,
               res_ref, mid_ref, nb_ref, gu_out, down_out, *refs):
    n2_s, n2t_s, up_s, acc_s, ht_s, back_s, gu_stage, down_stage, gu_sem, down_sem = refs[:10]
    step = pl.program_id(0)
    rows, width = x_ref.shape
    part = min(PART, rows)
    heads, _, cols = att_ref.shape
    blocks = ht_s.shape[0] // CUT
    wide = 2 * CUT
    tall = ht_s.shape[0] // DOWN
    chunks = [pl.ds(a, part) for a in range(0, rows, part)]
    sums = BlockSums(dp, gu_stage, *refs[10:], gu_out) if dp else None

    @pl.when(step == 0)
    def _():
        if dp:
            sums.place.greet()
        gain = gain_ref[...].astype(F32)
        scale = scale_ref[0, 0]
        for at in chunks:
            mid = x_ref[at].astype(F32)
            for j in range(heads):
                mid = mid + dot_nn(att_ref[j, at], wo_ref[j * cols : (j + 1) * cols])
            mid_ref[at] = mid
            inverse = lax.rsqrt(jnp.mean(mid * mid, axis=-1, keepdims=True) + EPSILON)
            low = (mid * inverse * gain).astype(BF)
            n2_s[at] = low
            if dp:
                gu_stage[0, :, :part] = low.T
                unit = gu_out.shape[0]
                for i, shard in enumerate(sums.order()):
                    there = pl.ds(pl.multiple_of(shard * unit, unit), unit)
                    n2t_s[i * unit : (i + 1) * unit, at] = gu_stage[0, there, :part]
            else:
                n2t_s[:, at] = low.T
            up_s[at] = (cot_ref[at].astype(F32) * scale).astype(BF)
        acc_s[...] = jnp.zeros_like(acc_s)
        nb_ref[...] = jnp.zeros_like(nb_ref)

    def gu_copy(j):
        slot = lax.rem(j, 2)
        return pltpu.make_async_copy(
            gu_stage.at[slot],
            gu_out.at[:, pl.ds(pl.multiple_of(j * wide, wide), wide)],
            gu_sem.at[slot],
        )

    def advance(phases):
        for phase in phases:
            lag = LAGS[phase - 1]
            j = step - lag
            for odd in range(2):

                @pl.when(
                    jnp.logical_and(
                        jnp.logical_and(step >= lag, step < lag + blocks), lax.rem(j, 2) == odd
                    )
                )
                def _(j=j, odd=odd, phase=phase):
                    sums.advance(j, odd, phase)

    @pl.when(step < blocks)
    def _():
        for at in chunks:
            both = dot_nn(n2_s[at], gu_ref[...])
            gate, up = both[:, :CUT], both[:, CUT:]
            back = dot_nt(up_s[at], down_ref[...])
            sig = 0.5 * jnp.tanh(0.5 * gate) + 0.5
            act = gate * sig
            hidden = (act * up).astype(BF)
            ht_s[pl.ds(pl.multiple_of(step * CUT, CUT), CUT), at] = hidden.T
            back_s[at, :CUT] = (back * up * sig * (1.0 + gate * (1.0 - sig))).astype(BF)
            back_s[at, CUT:] = (back * act).astype(BF)
            acc_s[at] += dot_nn(hidden, down_ref[...])
            nb_ref[at] += dot_nt(back_s[at], gu_ref[...])

    if dp:
        advance((4, 3, 2, 1))

    @pl.when(jnp.logical_and(step >= 2, step < blocks))
    def _():
        if dp:
            sums.pair(step - 2).wait_send()
        else:
            gu_copy(step - 2).wait()

    @pl.when(step < blocks)
    def _():
        for a in range(0, width, TALL):
            gu_stage[lax.rem(step, 2), a : a + TALL] = dot_nn(
                n2t_s[a : a + TALL], back_s[...]
            ).astype(BF)
        if dp:
            sums.pair(step).start()
        else:
            gu_copy(step).start()

    def down_copy(p):
        slot = lax.rem(p, 2)
        there = down_out.at[pl.ds(pl.multiple_of(p * tall, tall), tall)]
        return pltpu.make_async_copy(down_stage.at[slot], there, down_sem.at[slot])

    @pl.when(step >= blocks)
    def _():
        p = step - blocks

        @pl.when(p == 0)
        def _():
            for at in chunks:
                res_ref[at] = (mid_ref[at] + acc_s[at]).astype(BF)

        @pl.when(p >= 2)
        def _():
            down_copy(p - 2).wait()

        grad = dot_nn(ht_s[pl.ds(pl.multiple_of(p * tall, tall), tall)], up_s[...])
        down_stage[lax.rem(p, 2)] = grad.astype(BF)
        down_copy(p).start()

        @pl.when(p == DOWN - 1)
        def _():
            if dp:
                sums.pair(blocks - 2).wait_send()
                sums.pair(blocks - 1).wait_send()
                sums.finish([j % 2 for j in range(blocks)])
            else:
                gu_copy(blocks - 2).wait()
                gu_copy(blocks - 1).wait()
            down_copy(p - 1).wait()
            down_copy(p).wait()


def feed_forward(dp, scale, x, att, wo, gain, cot, gu, down):
    rows, width = x.shape
    size = down.shape[0]
    blocks, tall = size // CUT, size // DOWN
    once = pl.Buffered(1)

    def whole(w):
        return pl.BlockSpec(w.shape, lambda i: (0,) * len(w.shape), pipeline_mode=once)

    def last(i):
        return jnp.minimum(i, blocks - 1)

    shape = jax.ShapeDtypeStruct
    anywhere = pl.BlockSpec(memory_space=pl.ANY)
    out = [shape((rows, width), BF), shape((rows, width), F32), shape((rows, width), F32)]
    out_specs = [whole(w) for w in out]
    scratch = []
    params = {}
    if dp:
        out.append(shape((width // (4 * dp), 2 * size), F32))
        out_specs.append(whole(out[-1]))
        sem = pltpu.SemaphoreType.DMA((blocks, 3 + dp // 2))
        scratch = [pltpu.VMEM((blocks, width // 2, 2 * CUT), BF)] * 2 + [sem] * 2
        params = {"collective_id": 4, "has_side_effects": True}
    else:
        out.append(shape((width, 2 * size), BF))
        out_specs.append(anywhere)
    out.append(shape((size, width), BF))
    out_specs.append(anywhere)
    return pl.pallas_call(
        functools.partial(ffn_kernel, dp),
        grid=(blocks + DOWN,),
        in_specs=[
            pl.BlockSpec(memory_space=pltpu.SMEM),
            whole(x),
            whole(att),
            whole(wo),
            whole(gain),
            whole(cot),
            pl.BlockSpec((width, 2 * CUT), lambda i: (0, last(i))),
            pl.BlockSpec((CUT, width), lambda i: (last(i), 0)),
        ],
        out_specs=out_specs,
        out_shape=out,
        scratch_shapes=[
            pltpu.VMEM((rows, width), BF),
            pltpu.VMEM((width, rows), BF),
            pltpu.VMEM((rows, width), BF),
            pltpu.VMEM((rows, width), F32),
            pltpu.VMEM((size, rows), BF),
            pltpu.VMEM((rows, 2 * CUT), BF),
            pltpu.VMEM((2, width, 2 * CUT), BF),
            pltpu.VMEM((2, tall, width), BF),
            pltpu.SemaphoreType.DMA((2,)),
            pltpu.SemaphoreType.DMA((2,)),
            *scratch,
        ],
        compiler_params=pltpu.CompilerParams(vmem_limit_bytes=63 * 2**20, **params),
        cost_estimate=cost(18 * rows * width * size),
    )(scale, x, att, wo, gain, cot, gu, down)


def branch_kernel(scale_ref, mid_ref, nb_ref, cot_ref, att_ref, wo_ref, gain_ref,
                  mg_ref, send_ref, og_ref, gg_ref, branch_s):
    step = pl.program_id(0)
    part, width = mid_ref.shape
    heads, rows, cols = att_ref.shape
    mid, nback, gain = mid_ref[...], nb_ref[...], gain_ref[...].astype(F32)
    inverse = lax.rsqrt(jnp.mean(mid * mid, axis=-1, keepdims=True) + EPSILON)
    scaled = nback * gain
    middle_grad = cot_ref[...].astype(F32) * scale_ref[0, 0] + (
        inverse * scaled
        - mid * (inverse * inverse * inverse) * jnp.mean(scaled * mid, axis=-1, keepdims=True)
    )
    gain_part = jnp.sum(nback * mid * inverse, axis=0, keepdims=True)
    mg_ref[...] = middle_grad
    branch = middle_grad.astype(BF)
    branch_s[pl.ds(pl.multiple_of(step * part, part), part)] = branch
    for j in range(heads):
        send_ref[j] = dot_nt(branch, wo_ref[j * cols : (j + 1) * cols]).astype(BF)

    @pl.when(step == 0)
    def _():
        gg_ref[...] = gain_part

    @pl.when(step > 0)
    def _():
        gg_ref[...] += gain_part

    @pl.when(step == rows // part - 1)
    def _():
        for j in range(heads):
            og_ref[j * cols : (j + 1) * cols] = dot_tn(att_ref[j], branch_s[...]).astype(BF)


def branch_back(scale, mid, nback, cot, att, wo, gain):
    rows, width = mid.shape
    heads, _, cols = att.shape
    part = min(256, rows)
    rowwise = pl.BlockSpec((part, width), lambda i: (i, 0))

    def whole(w):
        return pl.BlockSpec(w.shape, lambda i: (0,) * len(w.shape))

    out = [
        jax.ShapeDtypeStruct((rows, width), F32),
        jax.ShapeDtypeStruct((heads, rows, cols), BF),
        jax.ShapeDtypeStruct((width, width), BF),
        jax.ShapeDtypeStruct((1, width), F32),
    ]
    return pl.pallas_call(
        branch_kernel,
        grid=(rows // part,),
        in_specs=[
            pl.BlockSpec(memory_space=pltpu.SMEM),
            rowwise,
            rowwise,
            rowwise,
            whole(att),
            whole(wo),
            whole(gain),
        ],
        out_specs=[
            rowwise,
            pl.BlockSpec((heads, part, cols), lambda i: (0, i, 0)),
            whole(out[2]),
            whole(out[3]),
        ],
        out_shape=out,
        scratch_shapes=[pltpu.VMEM((rows, width), BF)],
        compiler_params=pltpu.CompilerParams(vmem_limit_bytes=48 * 2**20),
        cost_estimate=cost(4 * rows * width * width),
    )(scale, mid, nback, cot, att, wo, gain)


def closing_kernel(dp, *refs):
    dq_in, dkv_in, hl_in, ex_in, x_in, gain_ref, wq_in, wl_in, mg_in, gg_ref = refs[:10]
    ig_out, q_out, e_out, g_out = refs[10:14]
    dq, dkv, hl, ex, x, wq, wl, mg = refs[14:22]
    far_dq, far_lat, lat_send, lat_own, e_s, g_s, n1t, flip, ig = refs[22:31]
    q_stage, q_pair, q_ring, e_stage, e_pair, e_ring, g_stage, g_pair, g_ring = refs[31:40]
    load_sem, far_send, far_recv, x_sem = refs[40:44]
    q_send, q_recv, e_send, e_recv, g_send, g_recv = refs[44:]
    place = Place(dp)
    c, s = place.core, place.at["x"]
    rows, width = x.shape
    cols, lat = dq.shape[1], ex.shape[0]
    part = rows // 2
    unit = q_out.shape[0]

    def at(index, size):
        return pl.ds(pl.multiple_of(index * size, size), size)

    loads = [(ex_in, ex), (dkv_in, dkv), (hl_in, hl), (x_in, x), (dq_in.at[c], dq)]
    loads += [(wq_in, wq), (wl_in, wl), (mg_in, mg)]

    def load(i):
        return pltpu.make_async_copy(*loads[i], load_sem.at[i])

    for i in range(len(loads)):
        load(i).start()
    place.greet()
    far_q = remote(dq_in.at[1 - c], far_dq, far_send.at[0], far_recv.at[0], place.pair())
    far_l = remote(lat_send, far_lat, far_send.at[1], far_recv.at[1], place.pair())
    far_q.start()

    q_sums = BlockSums(dp, q_stage, q_pair, q_ring, q_send, q_recv, q_out)
    e_sums = BlockSums(dp, e_stage, e_pair, e_ring, e_send, e_recv, e_out)
    g_sums = BlockSums(dp, g_stage, g_pair, g_ring, g_send, g_recv, g_out)
    order = q_sums.order()

    load(0).wait()
    load(1).wait()
    for u in range(2):
        lat_send[u * part : (u + 1) * part] = dot_nt(dkv[at(u * 2 + 1 - c, part)], ex[...]).astype(BF)
    far_l.start()
    for u in range(2):
        lat_own[u * part : (u + 1) * part] = dot_nt(dkv[at(u * 2 + c, part)], ex[...]).astype(BF)
    load(3).wait()
    gain = gain_ref[...].astype(F32)

    def inverse_of(values):
        return lax.rsqrt(jnp.mean(values * values, axis=-1, keepdims=True) + EPSILON)

    for u in range(2):
        chunk = slice(u * part, (u + 1) * part)
        values = x[chunk].astype(F32)
        flip[...] = (values * inverse_of(values) * gain).astype(BF).T
        for i, shard in enumerate(order):
            n1t[i * unit : (i + 1) * unit, chunk] = flip[at(shard, unit)]
    for i in (4, 5, 6, 7):
        load(i).wait()
    far_q.wait_recv()
    far_l.wait_recv()

    def back(u):
        chunk = at(u, part)
        normed_back = (
            dot_nt(dq[chunk], wq[:, at(c, cols)])
            + dot_nt(far_dq[chunk], wq[:, at(1 - c, cols)])
            + dot_nt(lat_own[chunk], wl[:, at(c, lat)])
            + dot_nt(far_lat[chunk], wl[:, at(1 - c, lat)])
        )
        values = x[chunk].astype(F32)
        inverse = inverse_of(values)
        scaled = normed_back * gain
        grad = mg[chunk] + (
            inverse * scaled
            - values
            * (inverse * inverse * inverse)
            * jnp.mean(scaled * values, axis=-1, keepdims=True)
        )
        ig[u] = grad.astype(BF)
        return jnp.sum(normed_back * values * inverse, axis=0, keepdims=True)

    gain_part = back(1 - s)
    swap, kept = block_swap(ig, ig_out, x_sem, place)
    swap.start()
    q_stage[c] = dot_nn(n1t[...], dq[...]).astype(BF)
    q_stage[1 - c] = dot_nn(n1t[...], far_dq[...]).astype(BF)
    for j in range(2):
        q_sums.pair(j).start()
    q_stage[2, :, at(c, lat)] = dot_nn(n1t[...], lat_own[...]).astype(BF)
    q_stage[2, :, at(1 - c, lat)] = dot_nn(n1t[...], far_lat[...]).astype(BF)
    q_sums.pair(2).start()
    load(2).wait()
    e_s[...] = dot_tn(hl[...], dkv[...])
    share = e_out.shape[0] // KVH
    for i, shard in enumerate(order):
        piece = e_s[at(shard, share)]
        zero = jnp.zeros_like(piece)
        whole = jnp.concatenate(
            [jnp.where(c == 0, piece, zero), jnp.where(c == 0, zero, piece)], axis=0
        ).astype(BF)
        for j in range(2):
            e_stage[j, i * 2 * share : (i + 1) * 2 * share] = whole[:, j * cols : (j + 1) * cols]
    for j in range(2):
        e_sums.pair(j).start()
    for j in range(3):
        q_sums.advance(j, j % 2, 1)
    gain_part = gain_part + back(s)
    kept.start()
    g_s[...] = jnp.concatenate(
        [gain_part, gg_ref[...], jnp.zeros((14, width), F32)], axis=0
    ).astype(BF)
    for i, shard in enumerate(order):
        g_stage[0, i * 16 : (i + 1) * 16] = g_s[:, at(lax.div(shard * unit, 128), 128)]
    g_sums.pair(0).start()
    for j in range(2):
        e_sums.advance(j, 1 - j, 1)
    g_sums.advance(0, 1, 1)
    for phase in (2, 3, 4):
        for j in range(3):
            q_sums.advance(j, j % 2, phase)
        for j in range(2):
            e_sums.advance(j, 1 - j, phase)
        g_sums.advance(0, 1, phase)
    far_q.wait_send()
    far_l.wait_send()
    for sums, parities in ((q_sums, (0, 1, 0)), (e_sums, (1, 0)), (g_sums, (1,))):
        for j in range(len(parities)):
            sums.pair(j).wait_send()
        sums.finish(parities)
    swap.wait()
    kept.wait()


def closing(dp, dq, dkv, head_latent, expand, x, gain, wq, wl, mg, gain_two_grad):
    rows, width = x.shape
    cols, lat = dq.shape[2], expand.shape[0]
    unit = width // (4 * dp)
    n = 2 * dp
    anywhere = pl.BlockSpec(memory_space=pl.ANY)
    inside = pl.BlockSpec(memory_space=pltpu.VMEM)
    vmem = pltpu.VMEM
    sem = pltpu.SemaphoreType.DMA
    share = lat // (2 * n) * KVH
    bulk = [((rows, cols), BF), (dkv.shape, BF), (head_latent.shape, BF), (expand.shape, BF)]
    bulk += [(x.shape, BF), (wq.shape, BF), (wl.shape, BF), (mg.shape, F32)]
    sums = []
    for blocks, high, wide in ((3, unit, cols), (2, share, cols), (1, 16, 128)):
        sums += [vmem((blocks, 2 * n * high, wide), BF)] + [vmem((blocks, n * high, wide), BF)] * 2
    return pl.pallas_call(
        functools.partial(closing_kernel, dp),
        in_specs=[anywhere] * 5 + [inside] + [anywhere] * 3 + [inside],
        out_specs=[anywhere] + [inside] * 3,
        out_shape=[
            jax.ShapeDtypeStruct((2, rows // 2, width), BF),
            jax.ShapeDtypeStruct((unit, 3 * cols), F32),
            jax.ShapeDtypeStruct((share, 2 * cols), F32),
            jax.ShapeDtypeStruct((16, 128), F32),
        ],
        scratch_shapes=[vmem(*b) for b in bulk]
        + [
            vmem((rows, cols), BF),
            vmem((rows, lat), BF),
            vmem((rows, lat), BF),
            vmem((rows, lat), BF),
            vmem((lat, 2 * cols), F32),
            vmem((16, width), BF),
            vmem((width, rows), BF),
            vmem((width, rows // 2), BF),
            vmem((2, rows // 2, width), BF),
        ]
        + sums
        + [sem((8,)), sem((2,)), sem((2,)), sem((3,))]
        + [sem((blocks, 3 + dp // 2)) for blocks in (3, 3, 2, 2, 1, 1)],
        compiler_params=pltpu.CompilerParams(
            collective_id=1, has_side_effects=True, vmem_limit_bytes=60 * 2**20
        ),
    )(dq, dkv, head_latent, expand, x, gain, wq, wl, mg, gain_two_grad)


HEADS = 16
LATD = 256
HG = 8
GROUPS = 8
ALL = ("dp", "seq", "grp")


def norm_parts(values, gain):
    inverse = lax.rsqrt(jnp.mean(values * values, axis=-1, keepdims=True) + EPSILON)
    return (values * inverse * gain, inverse)


def norm_back(values, inverse, gain, upstream):
    scaled = upstream * gain
    gain_grad = jnp.sum(upstream * values * inverse, axis=0)
    input_part = inverse * scaled - values * inverse**3 * jnp.mean(
        scaled * values, axis=-1, keepdims=True
    )
    return (input_part, gain_grad)


def swap_sequences(blocks, count):
    if count == 2:
        me = lax.axis_index("seq")
        sent = lax.ppermute(blocks[1 - me], "seq", [(0, 1), (1, 0)])
        kept = blocks[me]
        first = me == 0
        return jnp.stack([jnp.where(first, kept, sent), jnp.where(first, sent, kept)])
    return lax.all_to_all(blocks, "seq", 0, 0, tiled=True)


def swap_group(blocks):
    return lax.all_to_all(blocks, "grp", 0, 0, tiled=True)


def local(
    inputs,
    cotangent,
    group_ids,
    group_scale,
    norm_gain,
    w_query,
    w_latent,
    expansion_weight,
    w_output,
    ffn_gain,
    w_gate,
    w_up,
    w_down,
):
    devices = lax.axis_size("dp") * lax.axis_size("seq") * lax.axis_size("grp")
    groups = lax.axis_size("grp")
    me = lax.axis_index("grp")
    seqs, rows, width = inputs.shape
    count = seqs * rows
    hidden_size = w_gate.shape[1]
    heads = HEADS // groups
    cols = heads * DH
    drows = width // devices

    dp = lax.axis_size("dp")
    ring = groups == 2 and seqs == 2 and dp % 2 == 0
    expand_rows = expansion_weight.reshape(-1, expansion_weight.shape[2])
    gains = jnp.pad(jnp.concatenate([norm_gain, ffn_gain])[None], ((0, 15), (0, 128 - 2 * drows)))
    if ring:
        shards = (w_query, w_latent, expand_rows, gains)
        full, own_inputs = own_gather(dp, shards, inputs, ("xzy",) * 4)
    else:
        shards = (w_query, w_latent, expand_rows, gains, w_output)
        full = [lax.all_gather(w, ALL, axis=0) for w in shards]
        own_inputs = swap_sequences(inputs, seqs)
    gate_up = jnp.stack(
        [w_gate.reshape(drows, -1, CUT), w_up.reshape(drows, -1, CUT)], axis=2
    ).reshape(drows, -1)
    gu_full = lax.all_gather(gate_up, ALL, axis=0, tiled=True)
    down_full = lax.all_gather(w_down, ALL, axis=0, tiled=True)
    query_full = full[0].reshape(width, -1)
    latent_full = full[1].reshape(width, -1)
    expand_full = full[2].reshape(devices, KVH, LATD // devices, -1)
    gain_one = full[3][:, 0, :drows].reshape(width).astype(F32)
    gain_two = full[3][:, 0, drows : 2 * drows].reshape(1, width)

    token_rows = own_inputs.astype(F32).reshape(count, width)
    normed, inverse_one = norm_parts(token_rows, gain_one)
    normed_low = normed.astype(BF)
    query_send = jnp.stack(
        [dot_nn(normed_low, query_full[:, j * cols : (j + 1) * cols]).astype(BF) for j in range(groups)]
    ).reshape(groups, seqs, rows, cols)
    latent_state = [
        dot_nn(normed_low, latent_full[:, g * LATD : (g + 1) * LATD]).astype(BF) for g in range(KVH)
    ]
    latent_send = jnp.stack([latent_state[j * heads // HG] for j in range(groups)]).reshape(
        groups, seqs, rows, LATD
    )
    head_queries = swap_group(query_send)
    head_latent = swap_group(latent_send).transpose(1, 0, 2, 3).reshape(-1, LATD)
    expand_local = lax.dynamic_slice(
        expand_full,
        (0, me * heads // HG, 0, me * heads % HG * 2 * DH),
        (devices, 1, LATD // devices, heads * 2 * DH),
    ).reshape(LATD, -1)
    head_pairs = dot_nn(head_latent, expand_local).astype(BF)
    if ring:
        attended, logsum, own_cotangent, output_full = attention_forward_gather(
            dp, head_queries, head_pairs, cotangent, (w_output,), ((0, 0, width),), ("xzy",)
        )
    else:
        attended, logsum = attention_forward(head_queries, head_pairs)
        own_cotangent = swap_sequences(cotangent, seqs)
        output_full = full[4]
    output_full = output_full.reshape(-1, width)
    token_attended = swap_group(attended).reshape(groups, count, cols)
    seq_group = lax.dynamic_index_in_dim(group_ids, lax.axis_index("seq"), 0, keepdims=False)
    chosen = (seq_group == jnp.arange(GROUPS)).astype(F32)
    seq_scale = jnp.sum(chosen * group_scale).reshape(1, 1)
    x_rows = own_inputs.reshape(count, width)
    cot_rows = own_cotangent.reshape(count, width)
    result, middle, normed_two_back, gu_share, down_grad = feed_forward(
        dp if ring else None,
        seq_scale,
        x_rows,
        token_attended,
        output_full,
        gain_two,
        cot_rows,
        gu_full,
        down_full,
    )
    own_output = result.reshape(seqs, rows, width)
    if not ring:
        gu_share = lax.psum_scatter(gu_share, ALL, scatter_dimension=0, tiled=True).astype(F32)
    gu_share = gu_share.reshape(drows, -1, 2, CUT)
    middle_grad, back_send, output_grad, gain_two_grad = branch_back(
        seq_scale, middle, normed_two_back, cot_rows, token_attended, output_full, gain_two
    )
    head_upstream = swap_group(back_send.reshape(groups, seqs, rows, cols))
    terms = (output_grad.reshape(devices, drows, width), down_grad.reshape(devices, -1, width))
    attention = (head_queries, head_pairs, head_upstream, attended, logsum)
    if ring:
        half = width // 2
        query_back, pair_back, output, output_share, down_share = attention_backward_scatter(
            dp,
            *attention,
            own_output,
            terms,
            ((0, 0, width), (1, 0, half), (1, half, half)),
            ("yzx", "yxz", "yzx"),
        )
    else:
        query_back, pair_back = attention_backward(*attention)
        output = swap_sequences(own_output, seqs)
        output_share, down_share = [
            lax.psum_scatter(w, ALL, scatter_dimension=0, tiled=True)[0].astype(F32) for w in terms
        ]
    if ring:
        input_grad, q_share, e_share, g_share = closing(
            dp,
            query_back.reshape(groups, count, cols),
            pair_back,
            head_latent,
            expand_local,
            x_rows,
            gain_one,
            query_full,
            latent_full,
            middle_grad,
            gain_two_grad,
        )
        shard = (lax.axis_index("dp") * 2 + lax.axis_index("seq")) * 2 + me
        own_gains = lax.dynamic_slice(g_share, (0, shard * drows % 128), (2, drows))
        sums = (q_share[:, :width], q_share[:, width:], e_share)
    else:
        latent_terms = dot_nt(pair_back, expand_local).astype(BF)
        expand_part = dot_tn(head_latent, pair_back)
        expand_grad = lax.dynamic_update_slice(
            jnp.zeros(expand_full.shape, BF),
            expand_part.astype(BF).reshape(devices, 1, LATD // devices, -1),
            (0, me * heads // HG, 0, me * heads % HG * 2 * DH),
        )
        query_token = swap_group(query_back).reshape(groups, count, cols)
        latent_token = swap_group(
            latent_terms.reshape(seqs, groups, rows, LATD).transpose(1, 0, 2, 3)
        ).reshape(KVH, groups // KVH, count, LATD)
        latent_token = jnp.sum(latent_token.astype(F32), axis=1).astype(BF)
        query_grad = jnp.concatenate([dot_tn(normed_low, query_token[j]) for j in range(groups)], axis=1)
        latent_grad = jnp.concatenate([dot_tn(normed_low, latent_token[g]) for g in range(KVH)], axis=1)
        normed_back = sum(
            dot_nt(query_token[j], query_full[:, j * cols : (j + 1) * cols]) for j in range(groups)
        ) + sum(
            dot_nt(latent_token[g], latent_full[:, g * LATD : (g + 1) * LATD]) for g in range(KVH)
        )
        input_part, gain_one_grad = norm_back(token_rows, inverse_one, gain_one, normed_back)
        own_input_grad = (middle_grad + input_part).astype(BF).reshape(seqs, rows, width)
        gain_grads = jnp.concatenate(
            [gain_one_grad.reshape(devices, 1, drows), gain_two_grad.reshape(devices, 1, drows)], axis=2
        ).astype(BF)
        gain_grads = jnp.pad(gain_grads, ((0, 0), (0, 15), (0, 128 - 2 * drows)))
        terms = (
            query_grad.astype(BF).reshape(devices, drows, -1),
            latent_grad.astype(BF).reshape(devices, drows, -1),
            expand_grad.reshape(devices, -1, expand_grad.shape[3]),
            gain_grads,
        )
        sums = [
            lax.psum_scatter(w, ALL, scatter_dimension=0, tiled=True)[0].astype(F32) for w in terms
        ]
        own_gains = sums[3][0, : 2 * drows].reshape(2, drows)
        input_grad = swap_sequences(own_input_grad, seqs)
    return (
        output,
        input_grad,
        own_gains[0],
        sums[0],
        sums[1],
        sums[2].reshape(expansion_weight.shape),
        output_share,
        own_gains[1],
        gu_share[:, :, 0].reshape(drows, -1),
        gu_share[:, :, 1].reshape(drows, -1),
        down_share,
    )


def solution(mesh):
    def run(*arrays):
        dp, sp = mesh.shape["dp"], mesh.shape["sp"]
        seqs = arrays[0].shape[0] // dp
        grid = Mesh(mesh.devices.reshape(dp, seqs, sp // seqs), ALL)
        tokens = P("dp", ("seq", "grp"), None)
        matrix = P(ALL, None)
        expand = P(None, ALL, None)
        return jax.shard_map(
            local,
            mesh=grid,
            in_specs=(
                tokens,
                tokens,
                P("dp"),
                P(),
                P(ALL),
                matrix,
                matrix,
                expand,
                matrix,
                P(ALL),
                matrix,
                matrix,
                matrix,
            ),
            out_specs=(
                tokens,
                tokens,
                P(ALL),
                matrix,
                matrix,
                expand,
                matrix,
                P(ALL),
                matrix,
                matrix,
                matrix,
            ),
            check_vma=False,
        )(*arrays)

    return run
```

```python
import functools
import jax
import jax.numpy as jnp
from jax import lax
from jax.sharding import Mesh
from jax.sharding import PartitionSpec as P
from jax.experimental import pallas as pl
from jax.experimental.pallas import tpu as pltpu

DH = 64
KVH = 2
EPSILON = 1e-05
F32 = jnp.float32
BF = jnp.bfloat16


def cost(flops):
    return pl.CostEstimate(flops=flops, bytes_accessed=2**23, transcendentals=0)


MESH = pl.DeviceIdType.MESH


class Place:

    def __init__(self, dp):
        self.sizes = {"x": 2, "y": 2, "z": dp // 2}
        d = lax.axis_index("dp")
        self.at = {"x": lax.axis_index("seq"), "y": lax.rem(d, 2), "z": lax.div(d, 2)}
        self.core = lax.axis_index("grp")

    def coords(self, offset):
        at = {k: lax.rem(self.at[k] + o, self.sizes[k]) if o else self.at[k] for k, o in offset.items()}
        return at["z"] * 2 + at["y"], at["x"]

    def index(self, offset, other):
        d, s = self.coords(offset)
        core = 1 - self.core if other else self.core
        return (d * 2 + s) * 2 + core

    def device(self, offset):
        return (*self.coords(offset), self.core)

    def pair(self):
        return (*self.coords({"x": 0, "y": 0, "z": 0}), 1 - self.core)

    def greet(self):
        there = [self.pair()]
        for k in "xyz":
            for o in range(1, self.sizes[k]):
                there.append(self.device({"x": 0, "y": 0, "z": 0, k: o}))
        barrier = pltpu.get_barrier_semaphore()
        for device in there:
            pl.semaphore_signal(barrier, inc=1, device_id=device, device_id_type=MESH)
        pl.semaphore_wait(barrier, len(there))


def offsets_of(order, dp):
    sizes = {"x": 2, "y": 2, "z": dp // 2}
    a, b, c = (sizes[k] for k in order)
    return [(i, j, k) for i in range(a) for j in range(b) for k in range(c)]


def named(order, steps):
    return dict(zip(order, steps))


def remote(src, dst, send, recv, there):
    return pltpu.make_async_remote_copy(
        src_ref=src, dst_ref=dst, send_sem=send, recv_sem=recv, device_id=there, device_id_type=MESH
    )


class Gather:

    def __init__(self, place, dp, order, src, out, sems, number):
        self.place, self.order, self.src, self.out = place, order, src, out
        self.steps = offsets_of(order, dp)
        self.sems, self.number = sems, number

    def slot(self, steps, other=False):
        return self.out(self.place.index(named(self.order, steps), other))

    def source(self, steps):
        last = max(i for i in range(3) if steps[i])
        return tuple(0 if i == last else o for i, o in enumerate(steps))

    def hop(self, steps):
        last = max(i for i in range(3) if steps[i])
        source = self.source(steps)
        size = self.place.sizes[self.order[last]]
        back = tuple(size - o if i == last else 0 for i, o in enumerate(steps))
        number = self.steps.index(steps)
        here = self.slot(source)
        src = here if any(source) else self.src
        return remote(
            src,
            here,
            self.sems[0].at[self.number, number],
            self.sems[1].at[self.number, number],
            self.place.device(named(self.order, back)),
        )

    def across(self, steps):
        number = self.steps.index(steps)
        src = self.slot(steps) if any(steps) else self.src
        return remote(
            src,
            self.slot(steps),
            self.sems[2].at[self.number, number],
            self.sems[3].at[self.number, number],
            self.place.pair(),
        )

    def keep(self):
        return pltpu.make_async_copy(self.src, self.slot((0, 0, 0)), self.sems[4].at[self.number])

    def send_from(self, source):
        for steps in self.steps:
            if any(steps) and self.source(steps) == source:
                self.hop(steps).start()
        self.across(source).start()

    def start(self):
        self.send_from((0, 0, 0))
        self.keep().start()

    def arrivals(self):
        return sorted((s for s in self.steps if any(s)), key=lambda s: [o > 0 for o in s][::-1])

    def forward(self, steps):
        number = self.steps.index(steps)
        here = self.slot(steps)
        remote(
            here,
            here,
            self.sems[0].at[self.number, number],
            self.sems[1].at[self.number, number],
            self.place.pair(),
        ).wait_recv()
        self.send_from(steps)

    def finish(self):
        for steps in self.steps:
            number = self.steps.index(steps)
            here = self.slot(steps, True)
            remote(
                here,
                here,
                self.sems[2].at[self.number, number],
                self.sems[3].at[self.number, number],
                self.place.pair(),
            ).wait_recv()
            self.across(steps).wait_send()
            if any(steps):
                self.hop(steps).wait_send()
        self.keep().wait()


class Scatter:

    def __init__(self, place, dp, order, term, pair_buf, ring_buf, sems, number, own=None):
        self.place, self.order, self.term = place, order, term
        self.own_buf, self.own_sem = own if own else (None, None)
        self.steps = offsets_of(order, dp)
        self.pair_buf, self.ring_buf = pair_buf, ring_buf
        self.sems, self.number = sems, number

    def turn(self):
        def key(steps):
            first = next((i for i in range(3) if steps[i]), 3)
            return (first, [o == 0 for o in steps])

        return sorted(self.steps, key=key)

    def across(self, steps):
        number = self.steps.index(steps)
        return remote(
            self.term(self.place.index(named(self.order, steps), True)),
            self.pair_buf.at[number],
            self.sems[2].at[self.number, number],
            self.sems[3].at[self.number, number],
            self.place.pair(),
        )

    def fetch(self, steps):
        number = self.steps.index(steps)
        return pltpu.make_async_copy(
            self.term(self.place.index(named(self.order, steps), False)),
            self.own_buf.at[number],
            self.own_sem.at[self.number, number],
        )

    def start(self):
        for steps in self.turn():
            self.across(steps).start()
            if self.own_buf is not None:
                self.fetch(steps).start()

    def hop(self, steps):
        first = min(i for i in range(3) if steps[i])
        there = tuple(o if i == first else 0 for i, o in enumerate(steps))
        number = self.steps.index(steps)
        return remote(
            self.pair_buf.at[number],
            self.ring_buf.at[number],
            self.sems[0].at[self.number, number],
            self.sems[1].at[self.number, number],
            self.place.device(named(self.order, there)),
        )

    def add(self, steps, out=None):
        number = self.steps.index(steps)
        self.across(steps).wait_recv()
        if self.own_buf is None:
            mine = self.term(self.place.index(named(self.order, steps), False))
        else:
            self.fetch(steps).wait()
            mine = self.own_buf.at[number]
        total = mine[...].astype(F32) + self.pair_buf[number].astype(F32)
        for came in self.steps:
            if not any(came):
                continue
            first = min(i for i in range(3) if came[i])
            if tuple(0 if i == first else o for i, o in enumerate(came)) == steps:
                self.hop(came).wait_recv()
                total = total + self.ring_buf[self.steps.index(came)].astype(F32)
        if out is None:
            self.pair_buf[number] = total.astype(BF)
            self.hop(steps).start()
        else:
            out[...] = total

    def finish(self):
        for steps in self.steps:
            self.across(steps).wait_send()
            if any(steps):
                self.hop(steps).wait_send()


def block_swap(x_in, x_out, sem, place):
    s = place.at["x"]
    away = remote(
        x_in.at[1 - s], x_out.at[s], sem.at[0], sem.at[1], place.device({"x": 1, "y": 0, "z": 0})
    )
    return away, pltpu.make_async_copy(x_in.at[s], x_out.at[s], sem.at[2])


def gather_kernel(dp, orders, *refs):
    count = len(orders)
    srcs, x_in = refs[:count], refs[count]
    outs, x_out = refs[count + 1 : 2 * count + 1], refs[2 * count + 1]
    sems, x_sem = refs[2 * count + 2 : -1], refs[-1]
    place = Place(dp)
    place.greet()
    works = [
        Gather(place, dp, orders[a], srcs[a], lambda at, a=a: outs[a].at[at], sems, a)
        for a in range(count)
    ]
    for work in works:
        work.start()
    swap, kept = block_swap(x_in, x_out, x_sem, place)
    swap.start()
    kept.start()
    for i in range(2 * dp - 1):
        for work in works:
            work.forward(work.arrivals()[i])
    for work in works:
        work.finish()
    swap.wait()
    kept.wait()


def gather_sems(dp, count):
    sem = pltpu.SemaphoreType.DMA
    return [sem((count, 2 * dp))] * 4 + [sem((count,))]


def own_gather(dp, shards, blocks, orders):
    count = len(shards)
    anywhere = pl.BlockSpec(memory_space=pl.ANY)
    out = pl.pallas_call(
        functools.partial(gather_kernel, dp, orders),
        in_specs=[anywhere] * (count + 1),
        out_specs=[anywhere] * (count + 1),
        out_shape=[jax.ShapeDtypeStruct((4 * dp, *w.shape), w.dtype) for w in shards]
        + [jax.ShapeDtypeStruct(blocks.shape, blocks.dtype)],
        scratch_shapes=gather_sems(dp, count) + [pltpu.SemaphoreType.DMA((3,))],
        compiler_params=pltpu.CompilerParams(collective_id=0, has_side_effects=True),
    )(*shards, blocks)
    return out[:-1], out[-1]


def scatter_sems(dp, count):
    return [pltpu.SemaphoreType.DMA((count, 2 * dp))] * 4


def run_at(plan, point, when=None):
    for step, at in sorted((k for k in plan if k[0] != "last"), key=str):
        if at != (point if when is None else when):
            continue
        tasks = plan[step, at]

        @pl.when(pl.program_id(0) == step)
        def _(tasks=tasks):
            for task in tasks:
                task()


GATHER_AT = (0, 2, 3, 4, 5, 6, 7, 9, 10, 11, 12, 13, 14, 15, 15)
SCATTER_AT = (1, 1, 1, 1, 2, 2, 2, 2, 6, 7, 8, 9, 10, 11, 13, 16)


def put(plan, number, count, table, steps, points, task):
    at = table[number * len(table) // count] * steps * points // 16
    key = ("last", 0) if at >= steps * points else divmod(at, points)
    plan.setdefault(key, []).append(task)


def gather_plan(place, works, swap, steps, points):
    arrivals = [work.arrivals() for work in works]

    def begin():
        place.greet()
        for work in works:
            work.start()
        for copy in swap:
            copy.start()

    def forward(i):
        for work, order in zip(works, arrivals):
            work.forward(order[i])

    def end():
        for work in works:
            work.finish()
        for copy in swap:
            copy.wait()

    plan = {(0, "first"): [begin]}
    for i in range(len(arrivals[0])):
        put(plan, i, len(arrivals[0]), GATHER_AT, steps, points, functools.partial(forward, i))
    plan.setdefault(("last", 0), []).append(end)
    return plan


def scatter_plan(place, works, outs, swap, steps, points):
    turns = [work.turn() for work in works]
    count = len(turns[0])

    def begin():
        place.greet()
        for work in works:
            work.start()
        for copy in swap:
            copy.start()

    def add(i):
        for work, order, out in zip(works, turns, outs):
            work.add(order[i], out if i == count - 1 else None)

    def end():
        for work in works:
            work.finish()
        for copy in swap:
            copy.wait()

    plan = {(0, 0): [begin]}
    for i in range(count):
        put(plan, i, count, SCATTER_AT, steps, points, functools.partial(add, i))
    plan.setdefault(("last", 0), []).append(end)
    return plan


def dot_nt(a, b):
    return lax.dot_general(a, b, (((1,), (1,)), ((), ())), preferred_element_type=F32)


def dot_nn(a, b):
    return lax.dot_general(a, b, (((1,), (0,)), ((), ())), preferred_element_type=F32)


def dot_tn(a, b):
    return lax.dot_general(a, b, (((0,), (0,)), ((), ())), preferred_element_type=F32)


def causal(s, first_key, first_query):
    keys = first_key + lax.broadcasted_iota(jnp.int32, s.shape, 0)
    rows = first_query + lax.broadcasted_iota(jnp.int32, s.shape, 1)
    return jnp.where(rows >= keys, s, -1e30)


def forward_body(q_ref, kv_ref, o_ref, lse_ref, vt_s, point=lambda i: None):
    groups, chunks, rows, _ = q_ref.shape
    seq = kv_ref.shape[0]
    for h in range(2):
        vt_s[h] = kv_ref[:, h * 128 : (h + 1) * 128].astype(F32).T[DH:].astype(BF)
    for i in range(groups * chunks):
        point(i)
        q = q_ref[i % groups, i // groups].astype(F32) * 0.125
        outs = []
        for h in range(2):
            qh = q[:, h * DH : (h + 1) * DH]
            qp = jnp.concatenate([qh, jnp.zeros_like(qh)], axis=1).astype(BF)
            width = (i + 1) * rows
            s = dot_nt(kv_ref[0:width, h * 128 : (h + 1) * 128], qp)
            tail = causal(s[i * rows :], 0, 0)
            if i > 0:
                head = s[: i * rows]
                top = jnp.maximum(
                    jnp.max(head, axis=0, keepdims=True), jnp.max(tail, axis=0, keepdims=True)
                )
                ph = jnp.exp(head - top)
                pt = jnp.exp(tail - top)
                total = jnp.sum(ph, axis=0, keepdims=True) + jnp.sum(pt, axis=0, keepdims=True)
                o = dot_nn(vt_s[h, :, 0 : i * rows], ph.astype(BF)) + dot_nn(
                    vt_s[h, :, i * rows : width], pt.astype(BF)
                )
            else:
                top = jnp.max(tail, axis=0, keepdims=True)
                pt = jnp.exp(tail - top)
                total = jnp.sum(pt, axis=0, keepdims=True)
                o = dot_nn(vt_s[h, :, 0:width], pt.astype(BF))
            outs.append(o / total)
            lse_ref[h, i * rows : (i + 1) * rows] = (top + jnp.log(total))[0]
        o_ref[i % groups, i // groups] = jnp.concatenate(outs, axis=0).T.astype(BF)


def forward_kernel(q_ref, kv_ref, o_ref, lse_ref, vt_s):
    forward_body(q_ref, kv_ref, o_ref, lse_ref, vt_s)


def forward_gather_kernel(dp, cuts, orders, pairs, *refs):
    x_ref, gain_ref, wq_ref, wl_ref, ex_ref, x_in = refs[:6]
    sources = 1 + max(cut[0] for cut in cuts)
    srcs, refs = refs[6 : 6 + sources], refs[6 + sources :]
    o_ref, lse_ref, q_out, kv_out, hl_out, x_out = refs[:6]
    outs, refs = refs[6 : 6 + sources], refs[6 + sources :]
    vt_s, x_sem, low_s, q_send, lat_send, q_s, kv_s, hl_s, far_send, far_recv, save_sem = refs[:11]
    sems = refs[11:]
    place = Place(dp)
    c = place.core
    works = []
    for number, (a, first, size) in enumerate(cuts):
        cut = pl.ds(first, size)
        works.append(
            Gather(
                place,
                dp,
                orders[number],
                srcs[a].at[:, cut],
                lambda at, a=a, cut=cut: outs[a].at[at, :, cut],
                sems,
                number,
            )
        )
    groups, chunks, rows, cols = q_s.shape
    lat = hl_s.shape[1]
    points = groups * chunks
    plan = gather_plan(place, works, block_swap(x_in, x_out, x_sem, place), pairs, points)
    run_at(plan, 0, "first")

    def at(index, size):
        return pl.ds(pl.multiple_of(index * size, size), size)

    def far_q():
        return remote(q_send, q_s.at[c], far_send.at[0], far_recv.at[0], place.pair())

    def far_l(u):
        return remote(
            lat_send.at[u],
            hl_s.at[at(u * groups + c, rows)],
            far_send.at[1 + u],
            far_recv.at[1 + u],
            place.pair(),
        )

    def saves():
        return [
            pltpu.make_async_copy(src, dst, save_sem.at[i])
            for i, (src, dst) in enumerate(((q_s, q_out), (kv_s, kv_out), (hl_s, hl_out)))
        ]

    @pl.when(pl.program_id(0) == 0)
    def _():
        gain = gain_ref[...].astype(F32)
        for u in range(chunks):
            chunk = slice(u * rows, (u + 1) * rows)
            values = x_ref[chunk].astype(F32)
            inverse = lax.rsqrt(jnp.mean(values * values, axis=-1, keepdims=True) + EPSILON)
            low_s[chunk] = (values * inverse * gain).astype(BF)
            lat_send[u] = dot_nn(low_s[chunk], wl_ref[:, at(1 - c, lat)]).astype(BF)
            far_l(u).start()
        for u in range(chunks):
            chunk = slice(u * rows, (u + 1) * rows)
            q_send[u] = dot_nn(low_s[chunk], wq_ref[:, at(1 - c, cols)]).astype(BF)
        far_q().start()
        for u in range(chunks):
            chunk = slice(u * rows, (u + 1) * rows)
            hl_s[at(u * groups + c, rows)] = dot_nn(low_s[chunk], wl_ref[:, at(c, lat)]).astype(BF)
            q_s[c, u] = dot_nn(low_s[chunk], wq_ref[:, at(c, cols)]).astype(BF)
        for u in range(chunks):
            far_l(u).wait_recv()
        for k in range(groups * chunks):
            chunk = slice(k * rows, (k + 1) * rows)
            kv_s[chunk] = dot_nn(hl_s[chunk], ex_ref[...]).astype(BF)
        far_q().wait_recv()
        for save in saves():
            save.start()

    pid = pl.program_id(0)
    forward_body(
        q_s.at[:, :, :, at(pid, 128)],
        kv_s.at[:, at(pid, 256)],
        o_ref,
        lse_ref,
        vt_s,
        lambda i: run_at(plan, i),
    )

    @pl.when(pid == pairs - 1)
    def _():
        far_q().wait_send()
        for u in range(chunks):
            far_l(u).wait_send()
        for save in saves():
            save.wait()
        for task in plan["last", 0]:
            task()


def forward_specs(q, kv):
    groups, chunks, rows, cols = q.shape
    seq = kv.shape[0]
    pairs = cols // 128
    tok = pl.BlockSpec((groups, chunks, rows, 128), lambda p: (0, 0, 0, p))
    ins = [tok, pl.BlockSpec((seq, 256), lambda p: (0, p))]
    outs = [tok, pl.BlockSpec((None, 2, seq), lambda p: (p, 0, 0))]
    shapes = [jax.ShapeDtypeStruct(q.shape, BF), jax.ShapeDtypeStruct((pairs, 2, seq), F32)]
    scratch = [pltpu.VMEM((2, DH, seq), BF)]
    return pairs, ins, outs, shapes, scratch, cost(8 * pairs * seq * seq * 128)


def attention_forward(q, kv):
    pairs, ins, outs, shapes, scratch, estimate = forward_specs(q, kv)
    return pl.pallas_call(
        forward_kernel,
        grid=(pairs,),
        in_specs=ins,
        out_specs=outs,
        out_shape=shapes,
        scratch_shapes=scratch,
        compiler_params=pltpu.CompilerParams(vmem_limit_bytes=56 * 2**20),
        cost_estimate=estimate,
    )(q, kv)


def attention_forward_gather(dp, x, gain, wq, wl, expand, blocks, shards, cuts, orders):
    rows, width = blocks.shape[1], x.shape[1]
    cols, lat = width // 2, expand.shape[0]
    seq = 4 * rows
    q = jax.ShapeDtypeStruct((2, 2, rows, cols), BF)
    kv = jax.ShapeDtypeStruct((seq, 2 * cols), BF)
    hl = jax.ShapeDtypeStruct((seq, lat), BF)
    pairs, _, outs, shapes, scratch, estimate = forward_specs(q, kv)
    anywhere = pl.BlockSpec(memory_space=pl.ANY)
    count = len(shards)
    sem = pltpu.SemaphoreType.DMA

    def whole(w):
        return pl.BlockSpec(w.shape, lambda p: (0, 0), pipeline_mode=pl.Buffered(1))

    return pl.pallas_call(
        functools.partial(forward_gather_kernel, dp, cuts, orders, pairs),
        grid=(pairs,),
        in_specs=[whole(w) for w in (x, gain, wq, wl, expand)] + [anywhere] * (1 + count),
        out_specs=outs + [anywhere] * (4 + count),
        out_shape=shapes
        + [q, kv, hl]
        + [jax.ShapeDtypeStruct(blocks.shape, blocks.dtype)]
        + [jax.ShapeDtypeStruct((4 * dp, *w.shape), w.dtype) for w in shards],
        scratch_shapes=scratch
        + [
            sem((3,)),
            pltpu.VMEM(x.shape, BF),
            pltpu.VMEM((2, rows, cols), BF),
            pltpu.VMEM((2, rows, lat), BF),
            pltpu.VMEM(q.shape, BF),
            pltpu.VMEM(kv.shape, BF),
            pltpu.VMEM(hl.shape, BF),
            sem((3,)),
            sem((3,)),
            sem((3,)),
        ]
        + gather_sems(dp, len(cuts)),
        compiler_params=pltpu.CompilerParams(
            vmem_limit_bytes=60 * 2**20, collective_id=2, has_side_effects=True
        ),
        cost_estimate=estimate,
    )(x, gain, wq, wl, expand, blocks, *shards)


def backward_body(blk, q_ref, kv_ref, do_ref, o_ref, lse_ref, dq_ref, dkv_ref,
                  kt_s, acc_s, dqt_s, qp_s, dop_s, delta_s, point=lambda i: None):
    groups, chunks, rows, _ = q_ref.shape
    seq = kv_ref.shape[0]
    n = groups * chunks
    for h in range(2):
        kt_s[h] = kv_ref[:, h * 128 : (h + 1) * 128].astype(F32).T[:DH].astype(BF)
    acc_s[...] = jnp.zeros_like(acc_s)
    for i in range(n):
        at = pl.ds(i * rows, rows)
        q = q_ref[i % groups, i // groups].astype(F32) * 0.125
        do = do_ref[i % groups, i // groups].astype(F32)
        o = o_ref[i % groups, i // groups].astype(F32)
        prod = (do * o).T
        zero = jnp.zeros((rows, DH), F32)
        for h in range(2):
            cut = slice(h * DH, (h + 1) * DH)
            qp_s[h, at] = jnp.concatenate([q[:, cut], zero], axis=1).astype(BF)
            dop_s[h, at] = jnp.concatenate([zero, do[:, cut]], axis=1).astype(BF)
            delta_s[h, at] = jnp.sum(prod[cut], axis=0)

    def block(i, j, masked):
        qat = pl.ds(i * blk, blk)
        kat = pl.ds(pl.multiple_of(j * blk, blk), blk)
        for h in range(2):
            kv = kv_ref[kat, h * 128 : (h + 1) * 128]
            qp = qp_s[h, qat]
            dop = dop_s[h, qat]
            s = dot_nt(kv, qp)
            dp = dot_nt(kv, dop)
            if masked:
                s = causal(s, 0, 0)
            p = jnp.exp(s - lse_ref[h : h + 1, qat])
            ds = (p * (dp - delta_s[h : h + 1, qat])).astype(BF)
            acc_s[h, kat] += dot_nn(p.astype(BF), dop) + dot_nn(ds, qp)
            part = dot_nn(kt_s[h, :, kat], ds)
            if masked:
                dqt_s[h * DH : (h + 1) * DH, qat] = part
            else:
                dqt_s[h * DH : (h + 1) * DH, qat] += part

    m = seq // blk

    for i in range(m):
        point(i)
        block(i, i, True)

        def inner(j, _, i=i):
            block(i, j, False)
            return 0

        lax.fori_loop(0, i, inner, 0)
    for i in range(n):
        at = pl.ds(i * rows, rows)
        dq_ref[i % groups, i // groups] = (dqt_s[:, at].T * 0.125).astype(BF)
    for h in range(2):
        dkv_ref[:, h * 128 : (h + 1) * 128] = acc_s[h].astype(BF)


def backward_kernel(blk, *refs):
    backward_body(blk, *refs)


def backward_scatter_kernel(dp, blk, cuts, orders, pairs, *refs):
    ins, x_in, refs = refs[:5], refs[5], refs[6:]
    sources = 1 + max(cut[0] for cut in cuts)
    count = len(cuts)
    terms, refs = refs[:sources], refs[sources:]
    attn_outs, x_out, refs = refs[:2], refs[2], refs[3:]
    outs, refs = refs[:sources], refs[sources:]
    scratch, x_sem, refs = refs[:6], refs[6], refs[7:]
    own_bufs, pair_bufs, ring_bufs = refs[:count], refs[count : 2 * count], refs[2 * count : 3 * count]
    own_sem, sems = refs[3 * count], refs[3 * count + 1 :]
    place = Place(dp)
    works, targets = [], []
    for number, (a, first, size) in enumerate(cuts):
        cut = pl.ds(first, size)
        works.append(
            Scatter(
                place,
                dp,
                orders[number],
                lambda at, a=a, cut=cut: terms[a].at[at, :, cut],
                pair_bufs[number],
                ring_bufs[number],
                sems,
                number,
                (own_bufs[number], own_sem),
            )
        )
        targets.append(outs[a].at[:, cut])
    points = ins[1].shape[0] // blk
    plan = scatter_plan(place, works, targets, block_swap(x_in, x_out, x_sem, place), pairs, points)
    backward_body(blk, *ins, *attn_outs, *scratch, point=lambda i: run_at(plan, i))

    @pl.when(pl.program_id(0) == pairs - 1)
    def _():
        for task in plan["last", 0]:
            task()


def backward_specs(q, kv):
    groups, chunks, rows, cols = q.shape
    seq = kv.shape[0]
    pairs = cols // 128
    tok = pl.BlockSpec((groups, chunks, rows, 128), lambda p: (0, 0, 0, p))
    wide = pl.BlockSpec((seq, 256), lambda p: (0, p))
    ins = [tok, wide, tok, tok, pl.BlockSpec((None, 2, seq), lambda p: (p, 0, 0))]
    outs = [tok, wide]
    shapes = [jax.ShapeDtypeStruct(q.shape, BF), jax.ShapeDtypeStruct(kv.shape, BF)]
    scratch = [
        pltpu.VMEM((2, DH, seq), BF),
        pltpu.VMEM((2, seq, 128), F32),
        pltpu.VMEM((128, seq), F32),
        pltpu.VMEM((2, seq, 128), BF),
        pltpu.VMEM((2, seq, 128), BF),
        pltpu.VMEM((2, seq), F32),
    ]
    return pairs, ins, outs, shapes, scratch, cost(16 * pairs * seq * seq * 128)


def attention_backward(q, kv, do, o, lse, blk=512):
    pairs, ins, outs, shapes, scratch, estimate = backward_specs(q, kv)
    return pl.pallas_call(
        functools.partial(backward_kernel, blk),
        grid=(pairs,),
        in_specs=ins,
        out_specs=outs,
        out_shape=shapes,
        scratch_shapes=scratch,
        compiler_params=pltpu.CompilerParams(vmem_limit_bytes=56 * 2**20),
        cost_estimate=estimate,
    )(q, kv, do, o, lse)


def attention_backward_scatter(dp, q, kv, do, o, lse, blocks, terms, cuts, orders, blk=512):
    pairs, ins, outs, shapes, scratch, estimate = backward_specs(q, kv)
    anywhere = pl.BlockSpec(memory_space=pl.ANY)
    count = len(cuts)
    bufs = [pltpu.VMEM((2 * dp, terms[a].shape[1], size), BF) for a, _, size in cuts]
    return pl.pallas_call(
        functools.partial(backward_scatter_kernel, dp, blk, cuts, orders, pairs),
        grid=(pairs,),
        in_specs=ins + [anywhere] * (1 + len(terms)),
        out_specs=outs + [anywhere] + [pl.BlockSpec(w.shape[1:], lambda p: (0, 0)) for w in terms],
        out_shape=shapes
        + [jax.ShapeDtypeStruct(blocks.shape, blocks.dtype)]
        + [jax.ShapeDtypeStruct(w.shape[1:], F32) for w in terms],
        scratch_shapes=scratch
        + [pltpu.SemaphoreType.DMA((3,))]
        + bufs * 3
        + [pltpu.SemaphoreType.DMA((count, 2 * dp))]
        + scatter_sems(dp, count),
        compiler_params=pltpu.CompilerParams(
            vmem_limit_bytes=60 * 2**20, collective_id=3, has_side_effects=True
        ),
        cost_estimate=estimate,
    )(q, kv, do, o, lse, blocks, *terms)


CUT = 256
PART = 512
TALL = 512
DOWN = 8
LAGS = (1, 3, 5, 7)


class BlockSums:

    def __init__(self, dp, stage, pair_buf, ring_buf, send, recv, out_ref, last_ref=None):
        self.last_ref = last_ref
        self.place = Place(dp)
        self.stage, self.pair_buf, self.ring_buf = stage, pair_buf, ring_buf
        self.send, self.recv, self.out_ref = send, recv, out_ref
        self.total = pair_buf.shape[1]
        self.unit = out_ref.shape[0]

    def order(self):
        return [
            self.place.index({"y": y, "x": x, "z": z}, other)
            for other in (False, True)
            for y in range(2)
            for x in range(2)
            for z in range(self.place.sizes["z"])
        ]

    def pair(self, j):
        return remote(
            self.stage.at[lax.rem(j, self.stage.shape[0]), pl.ds(self.total, self.total)],
            self.pair_buf.at[j],
            self.send.at[j, 0],
            self.recv.at[j, 0],
            self.place.pair(),
        )

    def hop(self, j, axis, step, first, size, number):
        rows = pl.ds(first, size)
        offset = {"x": 0, "y": 0, "z": 0, axis: step}
        return remote(
            self.pair_buf.at[j, rows],
            self.ring_buf.at[j, rows],
            self.send.at[j, number],
            self.recv.at[j, number],
            self.place.device(offset),
        )

    def hops(self, odd, phase):
        q = self.total // 4
        if phase == 3:
            sizes = range(1, self.place.sizes["z"])
            return [("z", z, z * self.unit, self.unit, 3 + z) for z in sizes]
        if odd:
            return ([("x", 1, q, q, 1), ("x", 1, 3 * q, q, 2)], [("y", 1, 2 * q, q, 3)])[phase - 1]
        return ([("y", 1, 2 * q, 2 * q, 1)], [("x", 1, q, q, 3)])[phase - 1]

    def add(self, j, to, size, came):
        self.pair_buf[j, to : to + size] = (
            self.pair_buf[j, to : to + size].astype(F32) + came.astype(F32)
        ).astype(BF)

    def advance(self, j, odd, phase):
        q = self.total // 4
        if phase == 1:
            self.pair(j).wait_recv()
            self.add(j, 0, self.total, self.stage[lax.rem(j, self.stage.shape[0]), : self.total])
        else:
            for hop in self.hops(odd, phase - 1):
                self.hop(j, *hop).wait_recv()
        if phase == 2 and odd:
            self.add(j, 0, q, self.ring_buf[j, q : 2 * q])
            self.add(j, 2 * q, q, self.ring_buf[j, 3 * q :])
        elif phase == 2:
            self.add(j, 0, 2 * q, self.ring_buf[j, 2 * q :])
        elif phase == 3:
            first = 2 * q if odd else q
            self.add(j, 0, q, self.ring_buf[j, first : first + q])
        elif phase == 4:
            total = self.pair_buf[j, : self.unit].astype(F32)
            for z in range(1, self.place.sizes["z"]):
                total = total + self.ring_buf[j, z * self.unit : (z + 1) * self.unit].astype(F32)
            wide = total.shape[1]
            if self.last_ref is not None and j == self.pair_buf.shape[0] - 1:
                self.last_ref[...] = total
            else:
                self.out_ref[:, pl.ds(pl.multiple_of(j * wide, wide), wide)] = total
        if phase < 4:
            for hop in self.hops(odd, phase):
                self.hop(j, *hop).start()

    def finish(self, parities):
        for j, odd in enumerate(parities):
            for phase in range(1, 4):
                for hop in self.hops(odd, phase):
                    self.hop(j, *hop).wait_send()


def ffn_kernel(dp, scale_ref, x_ref, att_ref, wo_ref, gain_ref, cot_ref, gu_ref, down_ref,
               res_ref, nb_ref, gu_out, down_out, *refs):
    if dp:
        gg_ref, heads_out, og_out, refs = refs[0], refs[1], refs[2], refs[3:]
        mid_ref, out_sem, far_sem, refs = refs[0], refs[1], refs[2], refs[3:]
    else:
        mid_ref, refs = refs[0], refs[1:]
    n2_s, n2t_s, up_s, acc_s, ht_s, back_s, gu_stage, down_stage, gu_sem, down_sem = refs[:10]
    step = pl.program_id(0)
    rows, width = x_ref.shape
    part = min(PART, rows)
    heads, _, cols = att_ref.shape
    blocks = ht_s.shape[0] // CUT
    wide = 2 * CUT
    tall = ht_s.shape[0] // DOWN
    chunks = [pl.ds(a, part) for a in range(0, rows, part)]
    sums = BlockSums(dp, gu_stage, *refs[10:], gu_out) if dp else None

    @pl.when(step == 0)
    def _():
        if dp:
            sums.place.greet()
        gain = gain_ref[...].astype(F32)
        scale = scale_ref[0, 0]
        for at in chunks:
            mid = x_ref[at].astype(F32)
            for j in range(heads):
                mid = mid + dot_nn(att_ref[j, at], wo_ref[j * cols : (j + 1) * cols])
            mid_ref[at] = mid
            inverse = lax.rsqrt(jnp.mean(mid * mid, axis=-1, keepdims=True) + EPSILON)
            low = (mid * inverse * gain).astype(BF)
            n2_s[at] = low
            if dp:
                gu_stage[0, :, :part] = low.T
                unit = gu_out.shape[0]
                for i, shard in enumerate(sums.order()):
                    there = pl.ds(pl.multiple_of(shard * unit, unit), unit)
                    n2t_s[i * unit : (i + 1) * unit, at] = gu_stage[0, there, :part]
            else:
                n2t_s[:, at] = low.T
            up_s[at] = (cot_ref[at].astype(F32) * scale).astype(BF)
        acc_s[...] = jnp.zeros_like(acc_s)
        nb_ref[...] = jnp.zeros_like(nb_ref)

    def gu_copy(j):
        slot = lax.rem(j, 2)
        return pltpu.make_async_copy(
            gu_stage.at[slot],
            gu_out.at[:, pl.ds(pl.multiple_of(j * wide, wide), wide)],
            gu_sem.at[slot],
        )

    def advance(phases):
        for phase in phases:
            lag = LAGS[phase - 1]
            j = step - lag
            for odd in range(2):

                @pl.when(
                    jnp.logical_and(
                        jnp.logical_and(step >= lag, step < lag + blocks), lax.rem(j, 2) == odd
                    )
                )
                def _(j=j, odd=odd, phase=phase):
                    sums.advance(j, odd, phase)

    @pl.when(step < blocks)
    def _():
        for at in chunks:
            both = dot_nn(n2_s[at], gu_ref[...])
            gate, up = both[:, :CUT], both[:, CUT:]
            back = dot_nt(up_s[at], down_ref[...])
            sig = 0.5 * jnp.tanh(0.5 * gate) + 0.5
            act = gate * sig
            hidden = (act * up).astype(BF)
            ht_s[pl.ds(pl.multiple_of(step * CUT, CUT), CUT), at] = hidden.T
            back_s[at, :CUT] = (back * up * sig * (1.0 + gate * (1.0 - sig))).astype(BF)
            back_s[at, CUT:] = (back * act).astype(BF)
            acc_s[at] += dot_nn(hidden, down_ref[...])
            nb_ref[at] += dot_nt(back_s[at], gu_ref[...])

    if dp:
        advance((4, 3, 2, 1))

    @pl.when(jnp.logical_and(step >= 2, step < blocks))
    def _():
        if dp:
            sums.pair(step - 2).wait_send()
        else:
            gu_copy(step - 2).wait()

    @pl.when(step < blocks)
    def _():
        for a in range(0, width, TALL):
            gu_stage[lax.rem(step, 2), a : a + TALL] = dot_nn(
                n2t_s[a : a + TALL], back_s[...]
            ).astype(BF)
        if dp:
            sums.pair(step).start()
        else:
            gu_copy(step).start()

    def down_copy(p):
        slot = lax.rem(p, 2)
        there = down_out.at[pl.ds(pl.multiple_of(p * tall, tall), tall)]
        return pltpu.make_async_copy(down_stage.at[slot], there, down_sem.at[slot])

    @pl.when(jnp.logical_and(step >= blocks, step < blocks + DOWN))
    def _():
        p = step - blocks

        @pl.when(p == 0)
        def _():
            for at in chunks:
                res_ref[at] = (mid_ref[at] + acc_s[at]).astype(BF)

        @pl.when(p >= 2)
        def _():
            down_copy(p - 2).wait()

        grad = dot_nn(ht_s[pl.ds(pl.multiple_of(p * tall, tall), tall)], up_s[...])
        down_stage[lax.rem(p, 2)] = grad.astype(BF)
        down_copy(p).start()

        @pl.when(p == DOWN - 1)
        def _():
            if dp:
                sums.pair(blocks - 2).wait_send()
                sums.pair(blocks - 1).wait_send()
            else:
                gu_copy(blocks - 2).wait()
                gu_copy(blocks - 1).wait()
            down_copy(p - 1).wait()
            down_copy(p).wait()

    if not dp:
        return
    place = sums.place
    c = place.core
    ends = [
        remote(gu_stage.at[1 - c], heads_out.at[c], far_sem.at[0], far_sem.at[1], place.pair()),
        pltpu.make_async_copy(gu_stage.at[c], heads_out.at[c], out_sem.at[0]),
        pltpu.make_async_copy(n2t_s, og_out, out_sem.at[1]),
    ]
    for q, at in enumerate(chunks):

        @pl.when(step == blocks + DOWN + q)
        def _(q=q, at=at):
            mid, nback, gain = mid_ref[at], nb_ref[at], gain_ref[...].astype(F32)
            inverse = lax.rsqrt(jnp.mean(mid * mid, axis=-1, keepdims=True) + EPSILON)
            scaled = nback * gain
            middle_grad = cot_ref[at].astype(F32) * scale_ref[0, 0] + (
                inverse * scaled
                - mid
                * (inverse * inverse * inverse)
                * jnp.mean(scaled * mid, axis=-1, keepdims=True)
            )
            gain_part = jnp.sum(nback * mid * inverse, axis=0, keepdims=True)
            gg_ref[...] = gain_part if q == 0 else gg_ref[...] + gain_part
            nb_ref[at] = middle_grad
            branch = middle_grad.astype(BF)
            n2_s[at] = branch
            for j in range(heads):
                gu_stage[j, at] = dot_nt(branch, wo_ref[j * cols : (j + 1) * cols]).astype(BF)
            if q == len(chunks) - 1:
                ends[0].start()
                ends[1].start()

    @pl.when(step == blocks + DOWN + len(chunks))
    def _():
        for j in range(heads):
            n2t_s[j * cols : (j + 1) * cols] = dot_tn(att_ref[j], n2_s[...]).astype(BF)
        ends[2].start()
        sums.finish([j % 2 for j in range(blocks)])
        for end in ends:
            end.wait()


def feed_forward(dp, scale, x, att, wo, gain, cot, gu, down):
    rows, width = x.shape
    size = down.shape[0]
    blocks, tall = size // CUT, size // DOWN
    once = pl.Buffered(1)

    def whole(w):
        return pl.BlockSpec(w.shape, lambda i: (0,) * len(w.shape), pipeline_mode=once)

    def last(i):
        return jnp.minimum(i, blocks - 1)

    shape = jax.ShapeDtypeStruct
    anywhere = pl.BlockSpec(memory_space=pl.ANY)
    out = [shape((rows, width), BF), shape((rows, width), F32)]
    out_specs = [whole(w) for w in out]
    first, scratch = [], []
    params = {}
    steps = blocks + DOWN
    sem = pltpu.SemaphoreType.DMA
    if dp:
        out += [shape((width // (4 * dp), 2 * size), F32), shape((size, width), BF)]
        out += [shape((1, width), F32), shape(att.shape, BF), shape((width, width), BF)]
        out_specs += [whole(out[2]), anywhere, whole(out[4]), anywhere, anywhere]
        first = [pltpu.VMEM((rows, width), F32), sem((2,)), sem((2,))]
        sems = sem((blocks, 3 + dp // 2))
        scratch = [pltpu.VMEM((blocks, width // 2, 2 * CUT), BF)] * 2 + [sems] * 2
        params = {"collective_id": 4, "has_side_effects": True}
        steps += rows // min(PART, rows) + 1
    else:
        out += [shape((width, 2 * size), BF), shape((size, width), BF), shape((rows, width), F32)]
        out_specs += [anywhere, anywhere, whole(out[4])]
    return pl.pallas_call(
        functools.partial(ffn_kernel, dp),
        grid=(steps,),
        in_specs=[
            pl.BlockSpec(memory_space=pltpu.SMEM),
            whole(x),
            whole(att),
            whole(wo),
            whole(gain),
            whole(cot),
            pl.BlockSpec((width, 2 * CUT), lambda i: (0, last(i))),
            pl.BlockSpec((CUT, width), lambda i: (last(i), 0)),
        ],
        out_specs=out_specs,
        out_shape=out,
        scratch_shapes=[
            *first,
            pltpu.VMEM((rows, width), BF),
            pltpu.VMEM((width, rows), BF),
            pltpu.VMEM((rows, width), BF),
            pltpu.VMEM((rows, width), F32),
            pltpu.VMEM((size, rows), BF),
            pltpu.VMEM((rows, 2 * CUT), BF),
            pltpu.VMEM((2, width, 2 * CUT), BF),
            pltpu.VMEM((2, tall, width), BF),
            pltpu.SemaphoreType.DMA((2,)),
            pltpu.SemaphoreType.DMA((2,)),
            *scratch,
        ],
        compiler_params=pltpu.CompilerParams(vmem_limit_bytes=63 * 2**20, **params),
        cost_estimate=cost(18 * rows * width * size),
    )(scale, x, att, wo, gain, cot, gu, down)


def branch_kernel(scale_ref, mid_ref, nb_ref, cot_ref, att_ref, wo_ref, gain_ref,
                  mg_ref, send_ref, og_ref, gg_ref, branch_s):
    step = pl.program_id(0)
    part, width = mid_ref.shape
    heads, rows, cols = att_ref.shape
    mid, nback, gain = mid_ref[...], nb_ref[...], gain_ref[...].astype(F32)
    inverse = lax.rsqrt(jnp.mean(mid * mid, axis=-1, keepdims=True) + EPSILON)
    scaled = nback * gain
    middle_grad = cot_ref[...].astype(F32) * scale_ref[0, 0] + (
        inverse * scaled
        - mid * (inverse * inverse * inverse) * jnp.mean(scaled * mid, axis=-1, keepdims=True)
    )
    gain_part = jnp.sum(nback * mid * inverse, axis=0, keepdims=True)
    mg_ref[...] = middle_grad
    branch = middle_grad.astype(BF)
    branch_s[pl.ds(pl.multiple_of(step * part, part), part)] = branch
    for j in range(heads):
        send_ref[j] = dot_nt(branch, wo_ref[j * cols : (j + 1) * cols]).astype(BF)

    @pl.when(step == 0)
    def _():
        gg_ref[...] = gain_part

    @pl.when(step > 0)
    def _():
        gg_ref[...] += gain_part

    @pl.when(step == rows // part - 1)
    def _():
        for j in range(heads):
            og_ref[j * cols : (j + 1) * cols] = dot_tn(att_ref[j], branch_s[...]).astype(BF)


def branch_back(scale, mid, nback, cot, att, wo, gain):
    rows, width = mid.shape
    heads, _, cols = att.shape
    part = min(256, rows)
    rowwise = pl.BlockSpec((part, width), lambda i: (i, 0))

    def whole(w):
        return pl.BlockSpec(w.shape, lambda i: (0,) * len(w.shape))

    out = [
        jax.ShapeDtypeStruct((rows, width), F32),
        jax.ShapeDtypeStruct((heads, rows, cols), BF),
        jax.ShapeDtypeStruct((width, width), BF),
        jax.ShapeDtypeStruct((1, width), F32),
    ]
    return pl.pallas_call(
        branch_kernel,
        grid=(rows // part,),
        in_specs=[
            pl.BlockSpec(memory_space=pltpu.SMEM),
            rowwise,
            rowwise,
            rowwise,
            whole(att),
            whole(wo),
            whole(gain),
        ],
        out_specs=[
            rowwise,
            pl.BlockSpec((heads, part, cols), lambda i: (0, i, 0)),
            whole(out[2]),
            whole(out[3]),
        ],
        out_shape=out,
        scratch_shapes=[pltpu.VMEM((rows, width), BF)],
        compiler_params=pltpu.CompilerParams(vmem_limit_bytes=48 * 2**20),
        cost_estimate=cost(4 * rows * width * width),
    )(scale, mid, nback, cot, att, wo, gain)


def closing_kernel(dp, *refs):
    dq_in, dkv_in, hl_in, ex_in, x_in, gain_ref, wq_in, wl_in, mg_in, gg_ref = refs[:10]
    ig_out, q_out, l_out, e_out, g_out = refs[10:15]
    refs = refs[:14] + refs[15:]
    dq, dkv, hl, ex, x, wq, wl, mg = refs[14:22]
    far_dq, far_lat, lat_send, lat_own, e_s, g_s, n1t, flip, ig = refs[22:31]
    q_stage, q_pair, q_ring, e_stage, e_pair, e_ring, g_stage, g_pair, g_ring = refs[31:40]
    load_sem, far_send, far_recv, x_sem = refs[40:44]
    q_send, q_recv, e_send, e_recv, g_send, g_recv = refs[44:]
    place = Place(dp)
    c, s = place.core, place.at["x"]
    rows, width = x.shape
    cols, lat = dq.shape[1], ex.shape[0]
    part = rows // 2
    unit = q_out.shape[0]

    def at(index, size):
        return pl.ds(pl.multiple_of(index * size, size), size)

    loads = [(ex_in, ex), (dkv_in, dkv), (hl_in, hl), (x_in, x), (dq_in.at[c], dq)]
    loads += [(wq_in, wq), (wl_in, wl), (mg_in, mg)]

    def load(i):
        return pltpu.make_async_copy(*loads[i], load_sem.at[i])

    for i in range(len(loads)):
        load(i).start()
    place.greet()
    far_q = remote(dq_in.at[1 - c], far_dq, far_send.at[0], far_recv.at[0], place.pair())
    far_l = remote(lat_send, far_lat, far_send.at[1], far_recv.at[1], place.pair())
    far_q.start()

    q_sums = BlockSums(dp, q_stage, q_pair, q_ring, q_send, q_recv, q_out, l_out)
    e_sums = BlockSums(dp, e_stage, e_pair, e_ring, e_send, e_recv, e_out)
    g_sums = BlockSums(dp, g_stage, g_pair, g_ring, g_send, g_recv, g_out)
    order = q_sums.order()

    load(0).wait()
    load(1).wait()
    for u in range(2):
        lat_send[u * part : (u + 1) * part] = dot_nt(dkv[at(u * 2 + 1 - c, part)], ex[...]).astype(BF)
    far_l.start()
    for u in range(2):
        lat_own[u * part : (u + 1) * part] = dot_nt(dkv[at(u * 2 + c, part)], ex[...]).astype(BF)
    load(3).wait()
    gain = gain_ref[...].astype(F32)

    def inverse_of(values):
        return lax.rsqrt(jnp.mean(values * values, axis=-1, keepdims=True) + EPSILON)

    for u in range(2):
        chunk = slice(u * part, (u + 1) * part)
        values = x[chunk].astype(F32)
        flip[...] = (values * inverse_of(values) * gain).astype(BF).T
        for i, shard in enumerate(order):
            n1t[i * unit : (i + 1) * unit, chunk] = flip[at(shard, unit)]
    for i in (4, 5, 6, 7):
        load(i).wait()
    far_q.wait_recv()
    far_l.wait_recv()

    def back(u):
        chunk = at(u, part)
        normed_back = (
            dot_nt(dq[chunk], wq[:, at(c, cols)])
            + dot_nt(far_dq[chunk], wq[:, at(1 - c, cols)])
            + dot_nt(lat_own[chunk], wl[:, at(c, lat)])
            + dot_nt(far_lat[chunk], wl[:, at(1 - c, lat)])
        )
        values = x[chunk].astype(F32)
        inverse = inverse_of(values)
        scaled = normed_back * gain
        grad = mg[chunk] + (
            inverse * scaled
            - values
            * (inverse * inverse * inverse)
            * jnp.mean(scaled * values, axis=-1, keepdims=True)
        )
        ig[u] = grad.astype(BF)
        return jnp.sum(normed_back * values * inverse, axis=0, keepdims=True)

    gain_part = back(1 - s)
    swap, kept = block_swap(ig, ig_out, x_sem, place)
    swap.start()
    q_stage[c] = dot_nn(n1t[...], dq[...]).astype(BF)
    q_stage[1 - c] = dot_nn(n1t[...], far_dq[...]).astype(BF)
    for j in range(2):
        q_sums.pair(j).start()
    q_stage[2, :, at(c, lat)] = dot_nn(n1t[...], lat_own[...]).astype(BF)
    q_stage[2, :, at(1 - c, lat)] = dot_nn(n1t[...], far_lat[...]).astype(BF)
    q_sums.pair(2).start()
    load(2).wait()
    e_s[...] = dot_tn(hl[...], dkv[...])
    share = e_out.shape[0] // KVH
    for i, shard in enumerate(order):
        piece = e_s[at(shard, share)]
        zero = jnp.zeros_like(piece)
        whole = jnp.concatenate(
            [jnp.where(c == 0, piece, zero), jnp.where(c == 0, zero, piece)], axis=0
        ).astype(BF)
        for j in range(2):
            e_stage[j, i * 2 * share : (i + 1) * 2 * share] = whole[:, j * cols : (j + 1) * cols]
    for j in range(2):
        e_sums.pair(j).start()
    for j in range(3):
        q_sums.advance(j, j % 2, 1)
    gain_part = gain_part + back(s)
    kept.start()
    g_s[...] = jnp.concatenate(
        [gain_part, gg_ref[...], jnp.zeros((14, width), F32)], axis=0
    ).astype(BF)
    for i, shard in enumerate(order):
        g_stage[0, i * 16 : (i + 1) * 16] = g_s[:, at(lax.div(shard * unit, 128), 128)]
    g_sums.pair(0).start()
    for j in range(2):
        e_sums.advance(j, 1 - j, 1)
    g_sums.advance(0, 1, 1)
    for phase in (2, 3, 4):
        for j in range(3):
            q_sums.advance(j, j % 2, phase)
        for j in range(2):
            e_sums.advance(j, 1 - j, phase)
        g_sums.advance(0, 1, phase)
    far_q.wait_send()
    far_l.wait_send()
    for sums, parities in ((q_sums, (0, 1, 0)), (e_sums, (1, 0)), (g_sums, (1,))):
        for j in range(len(parities)):
            sums.pair(j).wait_send()
        sums.finish(parities)
    swap.wait()
    kept.wait()


def closing(dp, dq, dkv, head_latent, expand, x, gain, wq, wl, mg, gain_two_grad):
    rows, width = x.shape
    cols, lat = dq.shape[2], expand.shape[0]
    unit = width // (4 * dp)
    n = 2 * dp
    anywhere = pl.BlockSpec(memory_space=pl.ANY)
    inside = pl.BlockSpec(memory_space=pltpu.VMEM)
    vmem = pltpu.VMEM
    sem = pltpu.SemaphoreType.DMA
    share = lat // (2 * n) * KVH
    bulk = [((rows, cols), BF), (dkv.shape, BF), (head_latent.shape, BF), (expand.shape, BF)]
    bulk += [(x.shape, BF), (wq.shape, BF), (wl.shape, BF), (mg.shape, F32)]
    sums = []
    for blocks, high, wide in ((3, unit, cols), (2, share, cols), (1, 16, 128)):
        sums += [vmem((blocks, 2 * n * high, wide), BF)] + [vmem((blocks, n * high, wide), BF)] * 2
    return pl.pallas_call(
        functools.partial(closing_kernel, dp),
        in_specs=[anywhere] * 5 + [inside] + [anywhere] * 3 + [inside],
        out_specs=[anywhere] + [inside] * 4,
        out_shape=[
            jax.ShapeDtypeStruct((2, rows // 2, width), BF),
            jax.ShapeDtypeStruct((unit, 2 * cols), F32),
            jax.ShapeDtypeStruct((unit, cols), F32),
            jax.ShapeDtypeStruct((share, 2 * cols), F32),
            jax.ShapeDtypeStruct((16, 128), F32),
        ],
        scratch_shapes=[vmem(*b) for b in bulk]
        + [
            vmem((rows, cols), BF),
            vmem((rows, lat), BF),
            vmem((rows, lat), BF),
            vmem((rows, lat), BF),
            vmem((lat, 2 * cols), F32),
            vmem((16, width), BF),
            vmem((width, rows), BF),
            vmem((width, rows // 2), BF),
            vmem((2, rows // 2, width), BF),
        ]
        + sums
        + [sem((8,)), sem((2,)), sem((2,)), sem((3,))]
        + [sem((blocks, 3 + dp // 2)) for blocks in (3, 3, 2, 2, 1, 1)],
        compiler_params=pltpu.CompilerParams(
            collective_id=1, has_side_effects=True, vmem_limit_bytes=60 * 2**20
        ),
    )(dq, dkv, head_latent, expand, x, gain, wq, wl, mg, gain_two_grad)


HEADS = 16
LATD = 256
HG = 8
GROUPS = 8
ALL = ("dp", "seq", "grp")


def norm_parts(values, gain):
    inverse = lax.rsqrt(jnp.mean(values * values, axis=-1, keepdims=True) + EPSILON)
    return (values * inverse * gain, inverse)


def norm_back(values, inverse, gain, upstream):
    scaled = upstream * gain
    gain_grad = jnp.sum(upstream * values * inverse, axis=0)
    input_part = inverse * scaled - values * inverse**3 * jnp.mean(
        scaled * values, axis=-1, keepdims=True
    )
    return (input_part, gain_grad)


def swap_sequences(blocks, count):
    if count == 2:
        me = lax.axis_index("seq")
        sent = lax.ppermute(blocks[1 - me], "seq", [(0, 1), (1, 0)])
        kept = blocks[me]
        first = me == 0
        return jnp.stack([jnp.where(first, kept, sent), jnp.where(first, sent, kept)])
    return lax.all_to_all(blocks, "seq", 0, 0, tiled=True)


def swap_group(blocks):
    return lax.all_to_all(blocks, "grp", 0, 0, tiled=True)


def local(
    inputs,
    cotangent,
    group_ids,
    group_scale,
    norm_gain,
    w_query,
    w_latent,
    expansion_weight,
    w_output,
    ffn_gain,
    w_gate,
    w_up,
    w_down,
):
    devices = lax.axis_size("dp") * lax.axis_size("seq") * lax.axis_size("grp")
    groups = lax.axis_size("grp")
    me = lax.axis_index("grp")
    seqs, rows, width = inputs.shape
    count = seqs * rows
    hidden_size = w_gate.shape[1]
    heads = HEADS // groups
    cols = heads * DH
    drows = width // devices

    dp = lax.axis_size("dp")
    ring = groups == 2 and seqs == 2 and dp % 2 == 0
    expand_rows = expansion_weight.reshape(-1, expansion_weight.shape[2])
    gains = jnp.pad(jnp.concatenate([norm_gain, ffn_gain])[None], ((0, 15), (0, 128 - 2 * drows)))
    if ring:
        shards = (w_query, w_latent, expand_rows, gains)
        full, own_inputs = own_gather(dp, shards, inputs, ("xzy",) * 4)
    else:
        shards = (w_query, w_latent, expand_rows, gains, w_output)
        full = [lax.all_gather(w, ALL, axis=0) for w in shards]
        own_inputs = swap_sequences(inputs, seqs)
    gate_up = jnp.stack(
        [w_gate.reshape(drows, -1, CUT), w_up.reshape(drows, -1, CUT)], axis=2
    ).reshape(drows, -1)
    gu_full = lax.all_gather(gate_up, ALL, axis=0, tiled=True)
    query_full = full[0].reshape(width, -1)
    latent_full = full[1].reshape(width, -1)
    expand_full = full[2].reshape(devices, KVH, LATD // devices, -1)
    gain_one = full[3][:, 0, :drows].reshape(width).astype(F32)
    gain_two = full[3][:, 0, drows : 2 * drows].reshape(1, width)

    expand_local = lax.dynamic_slice(
        expand_full,
        (0, me * heads // HG, 0, me * heads % HG * 2 * DH),
        (devices, 1, LATD // devices, heads * 2 * DH),
    ).reshape(LATD, -1)
    if ring:
        half = width // 2
        (
            attended,
            logsum,
            head_queries,
            head_pairs,
            head_latent,
            own_cotangent,
            output_full,
            down_full,
        ) = attention_forward_gather(
            dp,
            own_inputs.reshape(count, width),
            gain_one.reshape(1, width),
            query_full,
            latent_full,
            expand_local,
            cotangent,
            (w_output, w_down),
            ((0, 0, width), (1, 0, half), (1, half, half)),
            ("xzy", "xzy", "zyx"),
        )
        down_full = down_full.reshape(-1, width)
    else:
        token_rows = own_inputs.astype(F32).reshape(count, width)
        normed, inverse_one = norm_parts(token_rows, gain_one)
        normed_low = normed.astype(BF)
        query_send = jnp.stack(
            [dot_nn(normed_low, query_full[:, j * cols : (j + 1) * cols]).astype(BF) for j in range(groups)]
        ).reshape(groups, seqs, rows, cols)
        latent_state = [
            dot_nn(normed_low, latent_full[:, g * LATD : (g + 1) * LATD]).astype(BF) for g in range(KVH)
        ]
        latent_send = jnp.stack([latent_state[j * heads // HG] for j in range(groups)]).reshape(
            groups, seqs, rows, LATD
        )
        head_queries = swap_group(query_send)
        head_latent = swap_group(latent_send).transpose(1, 0, 2, 3).reshape(-1, LATD)
        head_pairs = dot_nn(head_latent, expand_local).astype(BF)
        attended, logsum = attention_forward(head_queries, head_pairs)
        own_cotangent = swap_sequences(cotangent, seqs)
        output_full = full[4]
        down_full = lax.all_gather(w_down, ALL, axis=0, tiled=True)
    output_full = output_full.reshape(-1, width)
    token_attended = swap_group(attended).reshape(groups, count, cols)
    seq_group = lax.dynamic_index_in_dim(group_ids, lax.axis_index("seq"), 0, keepdims=False)
    chosen = (seq_group == jnp.arange(GROUPS)).astype(F32)
    seq_scale = jnp.sum(chosen * group_scale).reshape(1, 1)
    x_rows = own_inputs.reshape(count, width)
    cot_rows = own_cotangent.reshape(count, width)
    result, normed_two_back, gu_share, down_grad, *rest = feed_forward(
        dp if ring else None,
        seq_scale,
        x_rows,
        token_attended,
        output_full,
        gain_two,
        cot_rows,
        gu_full,
        down_full,
    )
    own_output = result.reshape(seqs, rows, width)
    if ring:
        middle_grad = normed_two_back
        gain_two_grad, head_upstream, output_grad = rest
        head_upstream = head_upstream.reshape(groups, seqs, rows, cols)
    else:
        gu_share = lax.psum_scatter(gu_share, ALL, scatter_dimension=0, tiled=True).astype(F32)
        middle_grad, back_send, output_grad, gain_two_grad = branch_back(
            seq_scale, *rest, normed_two_back, cot_rows, token_attended, output_full, gain_two
        )
        head_upstream = swap_group(back_send.reshape(groups, seqs, rows, cols))
    gu_share = gu_share.reshape(drows, -1, 2, CUT)
    terms = (output_grad.reshape(devices, drows, width), down_grad.reshape(devices, -1, width))
    attention = (head_queries, head_pairs, head_upstream, attended, logsum)
    if ring:
        half = width // 2
        query_back, pair_back, output, output_share, down_share = attention_backward_scatter(
            dp,
            *attention,
            own_output,
            terms,
            ((0, 0, width), (1, 0, half), (1, half, half)),
            ("yzx", "yxz", "yzx"),
        )
    else:
        query_back, pair_back = attention_backward(*attention)
        output = swap_sequences(own_output, seqs)
        output_share, down_share = [
            lax.psum_scatter(w, ALL, scatter_dimension=0, tiled=True)[0].astype(F32) for w in terms
        ]
    if ring:
        input_grad, q_share, l_share, e_share, g_share = closing(
            dp,
            query_back.reshape(groups, count, cols),
            pair_back,
            head_latent,
            expand_local,
            x_rows,
            gain_one,
            query_full,
            latent_full,
            middle_grad,
            gain_two_grad,
        )
        shard = (lax.axis_index("dp") * 2 + lax.axis_index("seq")) * 2 + me
        own_gains = lax.dynamic_slice(g_share, (0, shard * drows % 128), (2, drows))
        sums = (q_share, l_share, e_share)
    else:
        latent_terms = dot_nt(pair_back, expand_local).astype(BF)
        expand_part = dot_tn(head_latent, pair_back)
        expand_grad = lax.dynamic_update_slice(
            jnp.zeros(expand_full.shape, BF),
            expand_part.astype(BF).reshape(devices, 1, LATD // devices, -1),
            (0, me * heads // HG, 0, me * heads % HG * 2 * DH),
        )
        query_token = swap_group(query_back).reshape(groups, count, cols)
        latent_token = swap_group(
            latent_terms.reshape(seqs, groups, rows, LATD).transpose(1, 0, 2, 3)
        ).reshape(KVH, groups // KVH, count, LATD)
        latent_token = jnp.sum(latent_token.astype(F32), axis=1).astype(BF)
        query_grad = jnp.concatenate([dot_tn(normed_low, query_token[j]) for j in range(groups)], axis=1)
        latent_grad = jnp.concatenate([dot_tn(normed_low, latent_token[g]) for g in range(KVH)], axis=1)
        normed_back = sum(
            dot_nt(query_token[j], query_full[:, j * cols : (j + 1) * cols]) for j in range(groups)
        ) + sum(
            dot_nt(latent_token[g], latent_full[:, g * LATD : (g + 1) * LATD]) for g in range(KVH)
        )
        input_part, gain_one_grad = norm_back(token_rows, inverse_one, gain_one, normed_back)
        own_input_grad = (middle_grad + input_part).astype(BF).reshape(seqs, rows, width)
        gain_grads = jnp.concatenate(
            [gain_one_grad.reshape(devices, 1, drows), gain_two_grad.reshape(devices, 1, drows)], axis=2
        ).astype(BF)
        gain_grads = jnp.pad(gain_grads, ((0, 0), (0, 15), (0, 128 - 2 * drows)))
        terms = (
            query_grad.astype(BF).reshape(devices, drows, -1),
            latent_grad.astype(BF).reshape(devices, drows, -1),
            expand_grad.reshape(devices, -1, expand_grad.shape[3]),
            gain_grads,
        )
        sums = [
            lax.psum_scatter(w, ALL, scatter_dimension=0, tiled=True)[0].astype(F32) for w in terms
        ]
        own_gains = sums[3][0, : 2 * drows].reshape(2, drows)
        input_grad = swap_sequences(own_input_grad, seqs)
    return (
        output,
        input_grad,
        own_gains[0],
        sums[0],
        sums[1],
        sums[2].reshape(expansion_weight.shape),
        output_share,
        own_gains[1],
        gu_share[:, :, 0].reshape(drows, -1),
        gu_share[:, :, 1].reshape(drows, -1),
        down_share,
    )


def solution(mesh):
    def run(*arrays):
        dp, sp = mesh.shape["dp"], mesh.shape["sp"]
        seqs = arrays[0].shape[0] // dp
        grid = Mesh(mesh.devices.reshape(dp, seqs, sp // seqs), ALL)
        tokens = P("dp", ("seq", "grp"), None)
        matrix = P(ALL, None)
        expand = P(None, ALL, None)
        return jax.shard_map(
            local,
            mesh=grid,
            in_specs=(
                tokens,
                tokens,
                P("dp"),
                P(),
                P(ALL),
                matrix,
                matrix,
                expand,
                matrix,
                P(ALL),
                matrix,
                matrix,
                matrix,
            ),
            out_specs=(
                tokens,
                tokens,
                P(ALL),
                matrix,
                matrix,
                expand,
                matrix,
                P(ALL),
                matrix,
                matrix,
                matrix,
            ),
            check_vma=False,
        )(*arrays)

    return run
```

```python
import functools
import jax
import jax.numpy as jnp
from jax import lax
from jax.sharding import Mesh
from jax.sharding import PartitionSpec as P
from jax.experimental import pallas as pl
from jax.experimental.pallas import tpu as pltpu

DH = 64
KVH = 2
EPSILON = 1e-05
F32 = jnp.float32
BF = jnp.bfloat16


def cost(flops):
    return pl.CostEstimate(flops=flops, bytes_accessed=2**23, transcendentals=0)


MESH = pl.DeviceIdType.MESH


class Place:

    def __init__(self, dp):
        self.sizes = {"x": 2, "y": 2, "z": dp // 2}
        d = lax.axis_index("dp")
        self.at = {"x": lax.axis_index("seq"), "y": lax.rem(d, 2), "z": lax.div(d, 2)}
        self.core = lax.axis_index("grp")

    def coords(self, offset):
        at = {k: lax.rem(self.at[k] + o, self.sizes[k]) if o else self.at[k] for k, o in offset.items()}
        return at["z"] * 2 + at["y"], at["x"]

    def index(self, offset, other):
        d, s = self.coords(offset)
        core = 1 - self.core if other else self.core
        return (d * 2 + s) * 2 + core

    def device(self, offset):
        return (*self.coords(offset), self.core)

    def pair(self):
        return (*self.coords({"x": 0, "y": 0, "z": 0}), 1 - self.core)

    def greet(self):
        there = [self.pair()]
        for k in "xyz":
            for o in range(1, self.sizes[k]):
                there.append(self.device({"x": 0, "y": 0, "z": 0, k: o}))
        barrier = pltpu.get_barrier_semaphore()
        for device in there:
            pl.semaphore_signal(barrier, inc=1, device_id=device, device_id_type=MESH)
        pl.semaphore_wait(barrier, len(there))


def offsets_of(order, dp):
    sizes = {"x": 2, "y": 2, "z": dp // 2}
    a, b, c = (sizes[k] for k in order)
    return [(i, j, k) for i in range(a) for j in range(b) for k in range(c)]


def named(order, steps):
    return dict(zip(order, steps))


def remote(src, dst, send, recv, there):
    return pltpu.make_async_remote_copy(
        src_ref=src, dst_ref=dst, send_sem=send, recv_sem=recv, device_id=there, device_id_type=MESH
    )


class Gather:

    def __init__(self, place, dp, order, src, out, sems, number):
        self.place, self.order, self.src, self.out = place, order, src, out
        self.steps = offsets_of(order, dp)
        self.sems, self.number = sems, number

    def slot(self, steps, other=False):
        return self.out(self.place.index(named(self.order, steps), other))

    def source(self, steps):
        last = max(i for i in range(3) if steps[i])
        return tuple(0 if i == last else o for i, o in enumerate(steps))

    def hop(self, steps):
        last = max(i for i in range(3) if steps[i])
        source = self.source(steps)
        size = self.place.sizes[self.order[last]]
        back = tuple(size - o if i == last else 0 for i, o in enumerate(steps))
        number = self.steps.index(steps)
        here = self.slot(source)
        src = here if any(source) else self.src
        return remote(
            src,
            here,
            self.sems[0].at[self.number, number],
            self.sems[1].at[self.number, number],
            self.place.device(named(self.order, back)),
        )

    def across(self, steps):
        number = self.steps.index(steps)
        src = self.slot(steps) if any(steps) else self.src
        return remote(
            src,
            self.slot(steps),
            self.sems[2].at[self.number, number],
            self.sems[3].at[self.number, number],
            self.place.pair(),
        )

    def keep(self):
        return pltpu.make_async_copy(self.src, self.slot((0, 0, 0)), self.sems[4].at[self.number])

    def send_from(self, source):
        for steps in self.steps:
            if any(steps) and self.source(steps) == source:
                self.hop(steps).start()
        self.across(source).start()

    def start(self):
        self.send_from((0, 0, 0))
        self.keep().start()

    def arrivals(self):
        return sorted((s for s in self.steps if any(s)), key=lambda s: [o > 0 for o in s][::-1])

    def forward(self, steps):
        number = self.steps.index(steps)
        here = self.slot(steps)
        remote(
            here,
            here,
            self.sems[0].at[self.number, number],
            self.sems[1].at[self.number, number],
            self.place.pair(),
        ).wait_recv()
        self.send_from(steps)

    def finish(self):
        for steps in self.steps:
            number = self.steps.index(steps)
            here = self.slot(steps, True)
            remote(
                here,
                here,
                self.sems[2].at[self.number, number],
                self.sems[3].at[self.number, number],
                self.place.pair(),
            ).wait_recv()
            self.across(steps).wait_send()
            if any(steps):
                self.hop(steps).wait_send()
        self.keep().wait()


class Scatter:

    def __init__(self, place, dp, order, term, pair_buf, ring_buf, sems, number, own=None):
        self.place, self.order, self.term = place, order, term
        self.own_buf, self.own_sem = own if own else (None, None)
        self.steps = offsets_of(order, dp)
        self.pair_buf, self.ring_buf = pair_buf, ring_buf
        self.sems, self.number = sems, number

    def turn(self):
        def key(steps):
            first = next((i for i in range(3) if steps[i]), 3)
            return (first, [o == 0 for o in steps])

        return sorted(self.steps, key=key)

    def across(self, steps):
        number = self.steps.index(steps)
        return remote(
            self.term(self.place.index(named(self.order, steps), True)),
            self.pair_buf.at[number],
            self.sems[2].at[self.number, number],
            self.sems[3].at[self.number, number],
            self.place.pair(),
        )

    def fetch(self, steps):
        number = self.steps.index(steps)
        return pltpu.make_async_copy(
            self.term(self.place.index(named(self.order, steps), False)),
            self.own_buf.at[number],
            self.own_sem.at[self.number, number],
        )

    def start(self):
        for steps in self.turn():
            self.across(steps).start()
            if self.own_buf is not None:
                self.fetch(steps).start()

    def hop(self, steps):
        first = min(i for i in range(3) if steps[i])
        there = tuple(o if i == first else 0 for i, o in enumerate(steps))
        number = self.steps.index(steps)
        return remote(
            self.pair_buf.at[number],
            self.ring_buf.at[number],
            self.sems[0].at[self.number, number],
            self.sems[1].at[self.number, number],
            self.place.device(named(self.order, there)),
        )

    def add(self, steps, out=None):
        number = self.steps.index(steps)
        self.across(steps).wait_recv()
        if self.own_buf is None:
            mine = self.term(self.place.index(named(self.order, steps), False))
        else:
            self.fetch(steps).wait()
            mine = self.own_buf.at[number]
        total = mine[...].astype(F32) + self.pair_buf[number].astype(F32)
        for came in self.steps:
            if not any(came):
                continue
            first = min(i for i in range(3) if came[i])
            if tuple(0 if i == first else o for i, o in enumerate(came)) == steps:
                self.hop(came).wait_recv()
                total = total + self.ring_buf[self.steps.index(came)].astype(F32)
        if out is None:
            self.pair_buf[number] = total.astype(BF)
            self.hop(steps).start()
        else:
            out[...] = total

    def finish(self):
        for steps in self.steps:
            self.across(steps).wait_send()
            if any(steps):
                self.hop(steps).wait_send()


def block_swap(x_in, x_out, sem, place):
    s = place.at["x"]
    away = remote(
        x_in.at[1 - s], x_out.at[s], sem.at[0], sem.at[1], place.device({"x": 1, "y": 0, "z": 0})
    )
    return away, pltpu.make_async_copy(x_in.at[s], x_out.at[s], sem.at[2])


def gather_kernel(dp, orders, *refs):
    count = len(orders)
    srcs, x_in = refs[:count], refs[count]
    outs, x_out = refs[count + 1 : 2 * count + 1], refs[2 * count + 1]
    sems, x_sem = refs[2 * count + 2 : -1], refs[-1]
    place = Place(dp)
    place.greet()
    works = [
        Gather(place, dp, orders[a], srcs[a], lambda at, a=a: outs[a].at[at], sems, a)
        for a in range(count)
    ]
    for work in works:
        work.start()
    swap, kept = block_swap(x_in, x_out, x_sem, place)
    swap.start()
    kept.start()
    for i in range(2 * dp - 1):
        for work in works:
            work.forward(work.arrivals()[i])
    for work in works:
        work.finish()
    swap.wait()
    kept.wait()


def gather_sems(dp, count):
    sem = pltpu.SemaphoreType.DMA
    return [sem((count, 2 * dp))] * 4 + [sem((count,))]


def own_gather(dp, shards, blocks, orders):
    count = len(shards)
    anywhere = pl.BlockSpec(memory_space=pl.ANY)
    out = pl.pallas_call(
        functools.partial(gather_kernel, dp, orders),
        in_specs=[anywhere] * (count + 1),
        out_specs=[anywhere] * (count + 1),
        out_shape=[jax.ShapeDtypeStruct((4 * dp, *w.shape), w.dtype) for w in shards]
        + [jax.ShapeDtypeStruct(blocks.shape, blocks.dtype)],
        scratch_shapes=gather_sems(dp, count) + [pltpu.SemaphoreType.DMA((3,))],
        compiler_params=pltpu.CompilerParams(collective_id=0, has_side_effects=True),
    )(*shards, blocks)
    return out[:-1], out[-1]


def scatter_sems(dp, count):
    return [pltpu.SemaphoreType.DMA((count, 2 * dp))] * 4


def run_at(plan, point, when=None):
    for step, at in sorted((k for k in plan if k[0] != "last"), key=str):
        if at != (point if when is None else when):
            continue
        tasks = plan[step, at]

        @pl.when(pl.program_id(0) == step)
        def _(tasks=tasks):
            for task in tasks:
                task()


GATHER_AT = (0, 2, 3, 4, 5, 6, 7, 9, 10, 11, 12, 13, 14, 15, 15)
SCATTER_AT = (1, 1, 1, 1, 2, 2, 2, 2, 6, 7, 8, 9, 10, 11, 13, 16)


def put(plan, number, count, table, steps, points, task):
    at = table[number * len(table) // count] * steps * points // 16
    key = ("last", 0) if at >= steps * points else divmod(at, points)
    plan.setdefault(key, []).append(task)


def gather_plan(place, works, swap, steps, points):
    arrivals = [work.arrivals() for work in works]

    def begin():
        place.greet()
        for work in works:
            work.start()
        for copy in swap:
            copy.start()

    def forward(i):
        for work, order in zip(works, arrivals):
            work.forward(order[i])

    def end():
        for work in works:
            work.finish()
        for copy in swap:
            copy.wait()

    plan = {(0, "first"): [begin]}
    for i in range(len(arrivals[0])):
        put(plan, i, len(arrivals[0]), GATHER_AT, steps, points, functools.partial(forward, i))
    plan.setdefault(("last", 0), []).append(end)
    return plan


def scatter_plan(place, works, outs, swap, steps, points):
    turns = [work.turn() for work in works]
    count = len(turns[0])

    def begin():
        place.greet()
        for work in works:
            work.start()
        for copy in swap:
            copy.start()

    def add(i):
        for work, order, out in zip(works, turns, outs):
            work.add(order[i], out if i == count - 1 else None)

    def end():
        for work in works:
            work.finish()
        for copy in swap:
            copy.wait()

    plan = {(0, 0): [begin]}
    for i in range(count):
        put(plan, i, count, SCATTER_AT, steps, points, functools.partial(add, i))
    plan.setdefault(("last", 0), []).append(end)
    return plan


def dot_nt(a, b):
    return lax.dot_general(a, b, (((1,), (1,)), ((), ())), preferred_element_type=F32)


def dot_nn(a, b):
    return lax.dot_general(a, b, (((1,), (0,)), ((), ())), preferred_element_type=F32)


def dot_tn(a, b):
    return lax.dot_general(a, b, (((0,), (0,)), ((), ())), preferred_element_type=F32)


def causal(s, first_key, first_query):
    keys = first_key + lax.broadcasted_iota(jnp.int32, s.shape, 0)
    rows = first_query + lax.broadcasted_iota(jnp.int32, s.shape, 1)
    return jnp.where(rows >= keys, s, -1e30)


def forward_body(q_ref, kv_ref, o_ref, lse_ref, vt_s, point=lambda i: None):
    groups, chunks, rows, _ = q_ref.shape
    seq = kv_ref.shape[0]
    for h in range(2):
        vt_s[h] = kv_ref[:, h * 128 : (h + 1) * 128].astype(F32).T[DH:].astype(BF)
    for i in range(groups * chunks):
        point(i)
        q = q_ref[i % groups, i // groups].astype(F32) * 0.125
        outs = []
        for h in range(2):
            qh = q[:, h * DH : (h + 1) * DH]
            qp = jnp.concatenate([qh, jnp.zeros_like(qh)], axis=1).astype(BF)
            width = (i + 1) * rows
            s = dot_nt(kv_ref[0:width, h * 128 : (h + 1) * 128], qp)
            tail = causal(s[i * rows :], 0, 0)
            if i > 0:
                head = s[: i * rows]
                top = jnp.maximum(
                    jnp.max(head, axis=0, keepdims=True), jnp.max(tail, axis=0, keepdims=True)
                )
                ph = jnp.exp(head - top)
                pt = jnp.exp(tail - top)
                total = jnp.sum(ph, axis=0, keepdims=True) + jnp.sum(pt, axis=0, keepdims=True)
                o = dot_nn(vt_s[h, :, 0 : i * rows], ph.astype(BF)) + dot_nn(
                    vt_s[h, :, i * rows : width], pt.astype(BF)
                )
            else:
                top = jnp.max(tail, axis=0, keepdims=True)
                pt = jnp.exp(tail - top)
                total = jnp.sum(pt, axis=0, keepdims=True)
                o = dot_nn(vt_s[h, :, 0:width], pt.astype(BF))
            outs.append(o / total)
            lse_ref[h, i * rows : (i + 1) * rows] = (top + jnp.log(total))[0]
        o_ref[i % groups, i // groups] = jnp.concatenate(outs, axis=0).T.astype(BF)


def forward_kernel(q_ref, kv_ref, o_ref, lse_ref, vt_s):
    forward_body(q_ref, kv_ref, o_ref, lse_ref, vt_s)


def forward_gather_kernel(dp, cuts, orders, pairs, *refs):
    x_ref, gain_ref, wq_ref, wl_ref, ex_ref, x_in = refs[:6]
    sources = 1 + max(cut[0] for cut in cuts)
    srcs, refs = refs[6 : 6 + sources], refs[6 + sources :]
    lse_ref, o_out, token_out, q_out, kv_out, hl_out, x_out = refs[:7]
    outs, refs = refs[7 : 7 + sources], refs[7 + sources :]
    vt_s, x_sem, low_s, q_send, lat_send, q_s, kv_s, hl_s, o_s = refs[:9]
    far_send, far_recv, save_sem = refs[9:12]
    sems = refs[12:]
    place = Place(dp)
    c = place.core
    works = []
    for number, (a, first, size) in enumerate(cuts):
        cut = pl.ds(first, size)
        works.append(
            Gather(
                place,
                dp,
                orders[number],
                srcs[a].at[:, cut],
                lambda at, a=a, cut=cut: outs[a].at[at, :, cut],
                sems,
                number,
            )
        )
    groups, chunks, rows, cols = q_s.shape
    lat = hl_s.shape[1]
    points = groups * chunks
    plan = gather_plan(place, works, block_swap(x_in, x_out, x_sem, place), pairs, points)
    run_at(plan, 0, "first")

    def at(index, size):
        return pl.ds(pl.multiple_of(index * size, size), size)

    def far_q():
        return remote(q_send, q_s.at[c], far_send.at[0], far_recv.at[0], place.pair())

    def far_l(u):
        return remote(
            lat_send.at[u],
            hl_s.at[at(u * groups + c, rows)],
            far_send.at[1 + u],
            far_recv.at[1 + u],
            place.pair(),
        )

    def saves():
        return [
            pltpu.make_async_copy(src, dst, save_sem.at[i])
            for i, (src, dst) in enumerate(((q_s, q_out), (kv_s, kv_out), (hl_s, hl_out)))
        ]

    def hand_over():
        return [
            remote(o_s.at[1 - c], token_out.at[c], far_send.at[3], far_recv.at[3], place.pair()),
            pltpu.make_async_copy(o_s.at[c], token_out.at[c], save_sem.at[3]),
            pltpu.make_async_copy(o_s, o_out, save_sem.at[4]),
        ]

    @pl.when(pl.program_id(0) == 0)
    def _():
        gain = gain_ref[...].astype(F32)
        for u in range(chunks):
            chunk = slice(u * rows, (u + 1) * rows)
            values = x_ref[chunk].astype(F32)
            inverse = lax.rsqrt(jnp.mean(values * values, axis=-1, keepdims=True) + EPSILON)
            low_s[chunk] = (values * inverse * gain).astype(BF)
            lat_send[u] = dot_nn(low_s[chunk], wl_ref[:, at(1 - c, lat)]).astype(BF)
            far_l(u).start()
        for u in range(chunks):
            chunk = slice(u * rows, (u + 1) * rows)
            q_send[u] = dot_nn(low_s[chunk], wq_ref[:, at(1 - c, cols)]).astype(BF)
        far_q().start()
        for u in range(chunks):
            chunk = slice(u * rows, (u + 1) * rows)
            hl_s[at(u * groups + c, rows)] = dot_nn(low_s[chunk], wl_ref[:, at(c, lat)]).astype(BF)
            q_s[c, u] = dot_nn(low_s[chunk], wq_ref[:, at(c, cols)]).astype(BF)
        for u in range(chunks):
            far_l(u).wait_recv()
        for k in range(groups * chunks):
            chunk = slice(k * rows, (k + 1) * rows)
            kv_s[chunk] = dot_nn(hl_s[chunk], ex_ref[...]).astype(BF)
        far_q().wait_recv()
        for save in saves():
            save.start()

    pid = pl.program_id(0)
    forward_body(
        q_s.at[:, :, :, at(pid, 128)],
        kv_s.at[:, at(pid, 256)],
        o_s.at[:, :, :, at(pid, 128)],
        lse_ref,
        vt_s,
        lambda i: run_at(plan, i),
    )

    @pl.when(pid == pairs - 1)
    def _():
        for copy in hand_over():
            copy.start()
        far_q().wait_send()
        for u in range(chunks):
            far_l(u).wait_send()
        for copy in saves() + hand_over():
            copy.wait()
        for task in plan["last", 0]:
            task()


def forward_specs(q, kv):
    groups, chunks, rows, cols = q.shape
    seq = kv.shape[0]
    pairs = cols // 128
    tok = pl.BlockSpec((groups, chunks, rows, 128), lambda p: (0, 0, 0, p))
    ins = [tok, pl.BlockSpec((seq, 256), lambda p: (0, p))]
    outs = [tok, pl.BlockSpec((None, 2, seq), lambda p: (p, 0, 0))]
    shapes = [jax.ShapeDtypeStruct(q.shape, BF), jax.ShapeDtypeStruct((pairs, 2, seq), F32)]
    scratch = [pltpu.VMEM((2, DH, seq), BF)]
    return pairs, ins, outs, shapes, scratch, cost(8 * pairs * seq * seq * 128)


def attention_forward(q, kv):
    pairs, ins, outs, shapes, scratch, estimate = forward_specs(q, kv)
    return pl.pallas_call(
        forward_kernel,
        grid=(pairs,),
        in_specs=ins,
        out_specs=outs,
        out_shape=shapes,
        scratch_shapes=scratch,
        compiler_params=pltpu.CompilerParams(vmem_limit_bytes=56 * 2**20),
        cost_estimate=estimate,
    )(q, kv)


def attention_forward_gather(dp, x, gain, wq, wl, expand, blocks, shards, cuts, orders):
    rows, width = blocks.shape[1], x.shape[1]
    cols, lat = width // 2, expand.shape[0]
    seq = 4 * rows
    q = jax.ShapeDtypeStruct((2, 2, rows, cols), BF)
    kv = jax.ShapeDtypeStruct((seq, 2 * cols), BF)
    hl = jax.ShapeDtypeStruct((seq, lat), BF)
    pairs, _, outs, shapes, scratch, estimate = forward_specs(q, kv)
    anywhere = pl.BlockSpec(memory_space=pl.ANY)
    count = len(shards)
    sem = pltpu.SemaphoreType.DMA

    def whole(w):
        return pl.BlockSpec(w.shape, lambda p: (0, 0), pipeline_mode=pl.Buffered(1))

    return pl.pallas_call(
        functools.partial(forward_gather_kernel, dp, cuts, orders, pairs),
        grid=(pairs,),
        in_specs=[whole(w) for w in (x, gain, wq, wl, expand)] + [anywhere] * (1 + count),
        out_specs=outs[1:] + [anywhere] * (6 + count),
        out_shape=shapes[1:]
        + [q, q, q, kv, hl]
        + [jax.ShapeDtypeStruct(blocks.shape, blocks.dtype)]
        + [jax.ShapeDtypeStruct((4 * dp, *w.shape), w.dtype) for w in shards],
        scratch_shapes=scratch
        + [
            sem((3,)),
            pltpu.VMEM(x.shape, BF),
            pltpu.VMEM((2, rows, cols), BF),
            pltpu.VMEM((2, rows, lat), BF),
            pltpu.VMEM(q.shape, BF),
            pltpu.VMEM(kv.shape, BF),
            pltpu.VMEM(hl.shape, BF),
            pltpu.VMEM(q.shape, BF),
            sem((4,)),
            sem((4,)),
            sem((5,)),
        ]
        + gather_sems(dp, len(cuts)),
        compiler_params=pltpu.CompilerParams(
            vmem_limit_bytes=60 * 2**20, collective_id=2, has_side_effects=True
        ),
        cost_estimate=estimate,
    )(x, gain, wq, wl, expand, blocks, *shards)


def backward_body(blk, q_ref, kv_ref, do_ref, o_ref, lse_ref, dq_ref, dkv_ref,
                  kt_s, acc_s, dqt_s, qp_s, dop_s, delta_s, point=lambda i: None):
    groups, chunks, rows, _ = q_ref.shape
    seq = kv_ref.shape[0]
    n = groups * chunks
    for h in range(2):
        kt_s[h] = kv_ref[:, h * 128 : (h + 1) * 128].astype(F32).T[:DH].astype(BF)
    acc_s[...] = jnp.zeros_like(acc_s)
    for i in range(n):
        at = pl.ds(i * rows, rows)
        q = q_ref[i % groups, i // groups].astype(F32) * 0.125
        do = do_ref[i % groups, i // groups].astype(F32)
        o = o_ref[i % groups, i // groups].astype(F32)
        prod = (do * o).T
        zero = jnp.zeros((rows, DH), F32)
        for h in range(2):
            cut = slice(h * DH, (h + 1) * DH)
            qp_s[h, at] = jnp.concatenate([q[:, cut], zero], axis=1).astype(BF)
            dop_s[h, at] = jnp.concatenate([zero, do[:, cut]], axis=1).astype(BF)
            delta_s[h, at] = jnp.sum(prod[cut], axis=0)

    def block(i, j, masked):
        qat = pl.ds(i * blk, blk)
        kat = pl.ds(pl.multiple_of(j * blk, blk), blk)
        for h in range(2):
            kv = kv_ref[kat, h * 128 : (h + 1) * 128]
            qp = qp_s[h, qat]
            dop = dop_s[h, qat]
            s = dot_nt(kv, qp)
            dp = dot_nt(kv, dop)
            if masked:
                s = causal(s, 0, 0)
            p = jnp.exp(s - lse_ref[h : h + 1, qat])
            ds = (p * (dp - delta_s[h : h + 1, qat])).astype(BF)
            acc_s[h, kat] += dot_nn(p.astype(BF), dop) + dot_nn(ds, qp)
            part = dot_nn(kt_s[h, :, kat], ds)
            if masked:
                dqt_s[h * DH : (h + 1) * DH, qat] = part
            else:
                dqt_s[h * DH : (h + 1) * DH, qat] += part

    m = seq // blk

    for i in range(m):
        point(i)
        block(i, i, True)

        def inner(j, _, i=i):
            block(i, j, False)
            return 0

        lax.fori_loop(0, i, inner, 0)
    for i in range(n):
        at = pl.ds(i * rows, rows)
        dq_ref[i % groups, i // groups] = (dqt_s[:, at].T * 0.125).astype(BF)
    for h in range(2):
        dkv_ref[:, h * 128 : (h + 1) * 128] = acc_s[h].astype(BF)


def backward_kernel(blk, *refs):
    backward_body(blk, *refs)


def backward_scatter_kernel(dp, blk, cuts, orders, pairs, *refs):
    ins, x_in, refs = refs[:5], refs[5], refs[6:]
    sources = 1 + max(cut[0] for cut in cuts)
    count = len(cuts)
    terms, refs = refs[:sources], refs[sources:]
    attn_outs, x_out, refs = refs[:2], refs[2], refs[3:]
    outs, refs = refs[:sources], refs[sources:]
    scratch, x_sem, refs = refs[:6], refs[6], refs[7:]
    own_bufs, pair_bufs, ring_bufs = refs[:count], refs[count : 2 * count], refs[2 * count : 3 * count]
    own_sem, sems = refs[3 * count], refs[3 * count + 1 :]
    place = Place(dp)
    works, targets = [], []
    for number, (a, first, size) in enumerate(cuts):
        cut = pl.ds(first, size)
        works.append(
            Scatter(
                place,
                dp,
                orders[number],
                lambda at, a=a, cut=cut: terms[a].at[at, :, cut],
                pair_bufs[number],
                ring_bufs[number],
                sems,
                number,
                (own_bufs[number], own_sem),
            )
        )
        targets.append(outs[a].at[:, cut])
    points = ins[1].shape[0] // blk
    plan = scatter_plan(place, works, targets, block_swap(x_in, x_out, x_sem, place), pairs, points)
    backward_body(blk, *ins, *attn_outs, *scratch, point=lambda i: run_at(plan, i))

    @pl.when(pl.program_id(0) == pairs - 1)
    def _():
        for task in plan["last", 0]:
            task()


def backward_specs(q, kv):
    groups, chunks, rows, cols = q.shape
    seq = kv.shape[0]
    pairs = cols // 128
    tok = pl.BlockSpec((groups, chunks, rows, 128), lambda p: (0, 0, 0, p))
    wide = pl.BlockSpec((seq, 256), lambda p: (0, p))
    ins = [tok, wide, tok, tok, pl.BlockSpec((None, 2, seq), lambda p: (p, 0, 0))]
    outs = [tok, wide]
    shapes = [jax.ShapeDtypeStruct(q.shape, BF), jax.ShapeDtypeStruct(kv.shape, BF)]
    scratch = [
        pltpu.VMEM((2, DH, seq), BF),
        pltpu.VMEM((2, seq, 128), F32),
        pltpu.VMEM((128, seq), F32),
        pltpu.VMEM((2, seq, 128), BF),
        pltpu.VMEM((2, seq, 128), BF),
        pltpu.VMEM((2, seq), F32),
    ]
    return pairs, ins, outs, shapes, scratch, cost(16 * pairs * seq * seq * 128)


def attention_backward(q, kv, do, o, lse, blk=512):
    pairs, ins, outs, shapes, scratch, estimate = backward_specs(q, kv)
    return pl.pallas_call(
        functools.partial(backward_kernel, blk),
        grid=(pairs,),
        in_specs=ins,
        out_specs=outs,
        out_shape=shapes,
        scratch_shapes=scratch,
        compiler_params=pltpu.CompilerParams(vmem_limit_bytes=56 * 2**20),
        cost_estimate=estimate,
    )(q, kv, do, o, lse)


def attention_backward_scatter(dp, q, kv, do, o, lse, blocks, terms, cuts, orders, blk=512):
    pairs, ins, outs, shapes, scratch, estimate = backward_specs(q, kv)
    anywhere = pl.BlockSpec(memory_space=pl.ANY)
    count = len(cuts)
    bufs = [pltpu.VMEM((2 * dp, terms[a].shape[1], size), BF) for a, _, size in cuts]
    return pl.pallas_call(
        functools.partial(backward_scatter_kernel, dp, blk, cuts, orders, pairs),
        grid=(pairs,),
        in_specs=ins + [anywhere] * (1 + len(terms)),
        out_specs=outs + [anywhere] + [pl.BlockSpec(w.shape[1:], lambda p: (0, 0)) for w in terms],
        out_shape=shapes
        + [jax.ShapeDtypeStruct(blocks.shape, blocks.dtype)]
        + [jax.ShapeDtypeStruct(w.shape[1:], F32) for w in terms],
        scratch_shapes=scratch
        + [pltpu.SemaphoreType.DMA((3,))]
        + bufs * 3
        + [pltpu.SemaphoreType.DMA((count, 2 * dp))]
        + scatter_sems(dp, count),
        compiler_params=pltpu.CompilerParams(
            vmem_limit_bytes=60 * 2**20, collective_id=3, has_side_effects=True
        ),
        cost_estimate=estimate,
    )(q, kv, do, o, lse, blocks, *terms)


CUT = 256
PART = 512
TALL = 512
DOWN = 8
LAGS = (1, 3, 5, 7)


class BlockSums:

    def __init__(self, dp, stage, pair_buf, ring_buf, send, recv, out_ref, last_ref=None):
        self.last_ref = last_ref
        self.place = Place(dp)
        self.stage, self.pair_buf, self.ring_buf = stage, pair_buf, ring_buf
        self.send, self.recv, self.out_ref = send, recv, out_ref
        self.total = pair_buf.shape[1]
        self.unit = out_ref.shape[0]

    def order(self):
        return [
            self.place.index({"y": y, "x": x, "z": z}, other)
            for other in (False, True)
            for y in range(2)
            for x in range(2)
            for z in range(self.place.sizes["z"])
        ]

    def pair(self, j):
        return remote(
            self.stage.at[lax.rem(j, self.stage.shape[0]), pl.ds(self.total, self.total)],
            self.pair_buf.at[j],
            self.send.at[j, 0],
            self.recv.at[j, 0],
            self.place.pair(),
        )

    def hop(self, j, axis, step, first, size, number):
        rows = pl.ds(first, size)
        offset = {"x": 0, "y": 0, "z": 0, axis: step}
        return remote(
            self.pair_buf.at[j, rows],
            self.ring_buf.at[j, rows],
            self.send.at[j, number],
            self.recv.at[j, number],
            self.place.device(offset),
        )

    def hops(self, way, phase):
        q, unit = self.total // 4, self.unit
        sizes = range(1, self.place.sizes["z"])
        if way == 2:
            far = [("z", z, z * unit, unit, 1 + 2 * z) for z in sizes]
            far += [("z", z, q + z * unit, unit, 2 + 2 * z) for z in sizes]
            return ([("y", 1, 2 * q, 2 * q, 1)], far, [("x", 1, q, unit, 2)])[phase - 1]
        if phase == 3:
            return [("z", z, z * unit, unit, 3 + z) for z in sizes]
        if way:
            return ([("x", 1, q, q, 1), ("x", 1, 3 * q, q, 2)], [("y", 1, 2 * q, q, 3)])[phase - 1]
        return ([("y", 1, 2 * q, 2 * q, 1)], [("x", 1, q, q, 3)])[phase - 1]

    def add(self, j, to, size, came):
        self.pair_buf[j, to : to + size] = (
            self.pair_buf[j, to : to + size].astype(F32) + came.astype(F32)
        ).astype(BF)

    def advance(self, j, way, phase):
        q, unit = self.total // 4, self.unit
        sizes = range(1, self.place.sizes["z"])
        if phase == 1:
            self.pair(j).wait_recv()
            self.add(j, 0, self.total, self.stage[lax.rem(j, self.stage.shape[0]), : self.total])
        else:
            for hop in self.hops(way, phase - 1):
                self.hop(j, *hop).wait_recv()
        if phase == 2 and way == 1:
            self.add(j, 0, q, self.ring_buf[j, q : 2 * q])
            self.add(j, 2 * q, q, self.ring_buf[j, 3 * q :])
        elif phase == 2:
            self.add(j, 0, 2 * q, self.ring_buf[j, 2 * q :])
        elif phase == 3 and way == 2:
            for first in (0, q):
                total = self.pair_buf[j, first : first + unit].astype(F32)
                for z in sizes:
                    came = slice(first + z * unit, first + (z + 1) * unit)
                    total = total + self.ring_buf[j, came].astype(F32)
                self.pair_buf[j, first : first + unit] = total.astype(BF)
        elif phase == 3:
            first = 2 * q if way else q
            self.add(j, 0, q, self.ring_buf[j, first : first + q])
        elif phase == 4:
            total = self.pair_buf[j, :unit].astype(F32)
            for first in (q,) if way == 2 else [z * unit for z in sizes]:
                total = total + self.ring_buf[j, first : first + unit].astype(F32)
            wide = total.shape[1]
            if self.last_ref is not None and j == self.pair_buf.shape[0] - 1:
                self.last_ref[...] = total
            else:
                self.out_ref[:, pl.ds(pl.multiple_of(j * wide, wide), wide)] = total
        if phase < 4:
            for hop in self.hops(way, phase):
                self.hop(j, *hop).start()

    def finish(self, parities):
        for j, odd in enumerate(parities):
            for phase in range(1, 4):
                for hop in self.hops(odd, phase):
                    self.hop(j, *hop).wait_send()


def ffn_kernel(dp, scale_ref, x_ref, att_ref, wo_ref, gain_ref, cot_ref, gu_ref, down_ref,
               res_ref, nb_ref, gu_out, down_out, *refs):
    if dp:
        gg_ref, heads_out, og_out, refs = refs[0], refs[1], refs[2], refs[3:]
        mid_ref, out_sem, far_sem, refs = refs[0], refs[1], refs[2], refs[3:]
    else:
        mid_ref, refs = refs[0], refs[1:]
    n2_s, n2t_s, up_s, acc_s, ht_s, back_s, gu_stage, down_stage, gu_sem, down_sem = refs[:10]
    step = pl.program_id(0)
    rows, width = x_ref.shape
    part = min(PART, rows)
    heads, _, cols = att_ref.shape
    blocks = ht_s.shape[0] // CUT
    wide = 2 * CUT
    tall = ht_s.shape[0] // DOWN
    chunks = [pl.ds(a, part) for a in range(0, rows, part)]
    sums = BlockSums(dp, gu_stage, *refs[10:], gu_out) if dp else None

    @pl.when(step == 0)
    def _():
        if dp:
            sums.place.greet()
        gain = gain_ref[...].astype(F32)
        scale = scale_ref[0, 0]
        for at in chunks:
            mid = x_ref[at].astype(F32)
            for j in range(heads):
                mid = mid + dot_nn(att_ref[j, at], wo_ref[j * cols : (j + 1) * cols])
            mid_ref[at] = mid
            inverse = lax.rsqrt(jnp.mean(mid * mid, axis=-1, keepdims=True) + EPSILON)
            low = (mid * inverse * gain).astype(BF)
            n2_s[at] = low
            if dp:
                gu_stage[0, :, :part] = low.T
                unit = gu_out.shape[0]
                for i, shard in enumerate(sums.order()):
                    there = pl.ds(pl.multiple_of(shard * unit, unit), unit)
                    n2t_s[i * unit : (i + 1) * unit, at] = gu_stage[0, there, :part]
            else:
                n2t_s[:, at] = low.T
            up_s[at] = (cot_ref[at].astype(F32) * scale).astype(BF)
        acc_s[...] = jnp.zeros_like(acc_s)
        nb_ref[...] = jnp.zeros_like(nb_ref)

    def gu_copy(j):
        slot = lax.rem(j, 2)
        return pltpu.make_async_copy(
            gu_stage.at[slot],
            gu_out.at[:, pl.ds(pl.multiple_of(j * wide, wide), wide)],
            gu_sem.at[slot],
        )

    def advance(phases):
        for phase in phases:
            lag = LAGS[phase - 1]
            j = step - lag
            for odd in range(2):

                @pl.when(
                    jnp.logical_and(
                        jnp.logical_and(step >= lag, step < lag + blocks), lax.rem(j, 2) == odd
                    )
                )
                def _(j=j, odd=odd, phase=phase):
                    sums.advance(j, odd, phase)

    @pl.when(step < blocks)
    def _():
        for at in chunks:
            both = dot_nn(n2_s[at], gu_ref[...])
            gate, up = both[:, :CUT], both[:, CUT:]
            back = dot_nt(up_s[at], down_ref[...])
            sig = 0.5 * jnp.tanh(0.5 * gate) + 0.5
            act = gate * sig
            hidden = (act * up).astype(BF)
            ht_s[pl.ds(pl.multiple_of(step * CUT, CUT), CUT), at] = hidden.T
            back_s[at, :CUT] = (back * up * sig * (1.0 + gate * (1.0 - sig))).astype(BF)
            back_s[at, CUT:] = (back * act).astype(BF)
            acc_s[at] += dot_nn(hidden, down_ref[...])
            nb_ref[at] += dot_nt(back_s[at], gu_ref[...])

    if dp:
        advance((4, 3, 2, 1))

    @pl.when(jnp.logical_and(step >= 2, step < blocks))
    def _():
        if dp:
            sums.pair(step - 2).wait_send()
        else:
            gu_copy(step - 2).wait()

    @pl.when(step < blocks)
    def _():
        for a in range(0, width, TALL):
            gu_stage[lax.rem(step, 2), a : a + TALL] = dot_nn(
                n2t_s[a : a + TALL], back_s[...]
            ).astype(BF)
        if dp:
            sums.pair(step).start()
        else:
            gu_copy(step).start()

    def down_copy(p):
        slot = lax.rem(p, 2)
        there = down_out.at[pl.ds(pl.multiple_of(p * tall, tall), tall)]
        return pltpu.make_async_copy(down_stage.at[slot], there, down_sem.at[slot])

    @pl.when(jnp.logical_and(step >= blocks, step < blocks + DOWN))
    def _():
        p = step - blocks

        @pl.when(p == 0)
        def _():
            for at in chunks:
                res_ref[at] = (mid_ref[at] + acc_s[at]).astype(BF)

        @pl.when(p >= 2)
        def _():
            down_copy(p - 2).wait()

        grad = dot_nn(ht_s[pl.ds(pl.multiple_of(p * tall, tall), tall)], up_s[...])
        down_stage[lax.rem(p, 2)] = grad.astype(BF)
        down_copy(p).start()

        @pl.when(p == DOWN - 1)
        def _():
            if dp:
                sums.pair(blocks - 2).wait_send()
                sums.pair(blocks - 1).wait_send()
            else:
                gu_copy(blocks - 2).wait()
                gu_copy(blocks - 1).wait()
            down_copy(p - 1).wait()
            down_copy(p).wait()

    if not dp:
        return
    place = sums.place
    c = place.core
    ends = [
        remote(gu_stage.at[1 - c], heads_out.at[c], far_sem.at[0], far_sem.at[1], place.pair()),
        pltpu.make_async_copy(gu_stage.at[c], heads_out.at[c], out_sem.at[0]),
        pltpu.make_async_copy(n2t_s, og_out, out_sem.at[1]),
    ]
    for q, at in enumerate(chunks):

        @pl.when(step == blocks + DOWN + q)
        def _(q=q, at=at):
            mid, nback, gain = mid_ref[at], nb_ref[at], gain_ref[...].astype(F32)
            inverse = lax.rsqrt(jnp.mean(mid * mid, axis=-1, keepdims=True) + EPSILON)
            scaled = nback * gain
            middle_grad = cot_ref[at].astype(F32) * scale_ref[0, 0] + (
                inverse * scaled
                - mid
                * (inverse * inverse * inverse)
                * jnp.mean(scaled * mid, axis=-1, keepdims=True)
            )
            gain_part = jnp.sum(nback * mid * inverse, axis=0, keepdims=True)
            gg_ref[...] = gain_part if q == 0 else gg_ref[...] + gain_part
            nb_ref[at] = middle_grad
            branch = middle_grad.astype(BF)
            n2_s[at] = branch
            for j in range(heads):
                gu_stage[j, at] = dot_nt(branch, wo_ref[j * cols : (j + 1) * cols]).astype(BF)
            if q == len(chunks) - 1:
                ends[0].start()
                ends[1].start()

    @pl.when(step == blocks + DOWN + len(chunks))
    def _():
        for j in range(heads):
            n2t_s[j * cols : (j + 1) * cols] = dot_tn(att_ref[j], n2_s[...]).astype(BF)
        ends[2].start()
        sums.finish([j % 2 for j in range(blocks)])
        for end in ends:
            end.wait()


def feed_forward(dp, scale, x, att, gain, cot, wide, down):
    rows, width = x.shape
    size = down.shape[0]
    blocks, tall = size // CUT, size // DOWN
    once = pl.Buffered(1)

    def whole(w):
        return pl.BlockSpec(w.shape, lambda i: (0,) * len(w.shape), pipeline_mode=once)

    def last(i):
        return jnp.minimum(i, blocks - 1)

    shape = jax.ShapeDtypeStruct
    anywhere = pl.BlockSpec(memory_space=pl.ANY)
    out = [shape((rows, width), BF), shape((rows, width), F32)]
    out_specs = [whole(w) for w in out]
    first, scratch = [], []
    params = {}
    steps = blocks + DOWN
    sem = pltpu.SemaphoreType.DMA
    if dp:
        out += [shape((width // (4 * dp), 2 * size), F32), shape((size, width), BF)]
        out += [shape((1, width), F32), shape(att.shape, BF), shape((width, width), BF)]
        out_specs += [whole(out[2]), anywhere, whole(out[4]), anywhere, anywhere]
        first = [pltpu.VMEM((rows, width), F32), sem((2,)), sem((2,))]
        sems = sem((blocks, dp + 1))
        scratch = [pltpu.VMEM((blocks, width // 2, 2 * CUT), BF)] * 2 + [sems] * 2
        params = {"collective_id": 4, "has_side_effects": True}
        steps += rows // min(PART, rows) + 1
    else:
        out += [shape((width, 2 * size), BF), shape((size, width), BF), shape((rows, width), F32)]
        out_specs += [anywhere, anywhere, whole(out[4])]
    return pl.pallas_call(
        functools.partial(ffn_kernel, dp),
        grid=(steps,),
        in_specs=[
            pl.BlockSpec(memory_space=pltpu.SMEM),
            whole(x),
            whole(att),
            pl.BlockSpec((width, width), lambda i: (0, 0), pipeline_mode=once),
            whole(gain),
            whole(cot),
            pl.BlockSpec((width, 2 * CUT), lambda i: (0, last(i) + width // (2 * CUT))),
            pl.BlockSpec((CUT, width), lambda i: (last(i), 0)),
        ],
        out_specs=out_specs,
        out_shape=out,
        scratch_shapes=[
            *first,
            pltpu.VMEM((rows, width), BF),
            pltpu.VMEM((width, rows), BF),
            pltpu.VMEM((rows, width), BF),
            pltpu.VMEM((rows, width), F32),
            pltpu.VMEM((size, rows), BF),
            pltpu.VMEM((rows, 2 * CUT), BF),
            pltpu.VMEM((2, width, 2 * CUT), BF),
            pltpu.VMEM((2, tall, width), BF),
            pltpu.SemaphoreType.DMA((2,)),
            pltpu.SemaphoreType.DMA((2,)),
            *scratch,
        ],
        compiler_params=pltpu.CompilerParams(vmem_limit_bytes=63 * 2**20, **params),
        cost_estimate=cost(18 * rows * width * size),
    )(scale, x, att, wide, gain, cot, wide, down)


def branch_kernel(scale_ref, mid_ref, nb_ref, cot_ref, att_ref, wo_ref, gain_ref,
                  mg_ref, send_ref, og_ref, gg_ref, branch_s):
    step = pl.program_id(0)
    part, width = mid_ref.shape
    heads, rows, cols = att_ref.shape
    mid, nback, gain = mid_ref[...], nb_ref[...], gain_ref[...].astype(F32)
    inverse = lax.rsqrt(jnp.mean(mid * mid, axis=-1, keepdims=True) + EPSILON)
    scaled = nback * gain
    middle_grad = cot_ref[...].astype(F32) * scale_ref[0, 0] + (
        inverse * scaled
        - mid * (inverse * inverse * inverse) * jnp.mean(scaled * mid, axis=-1, keepdims=True)
    )
    gain_part = jnp.sum(nback * mid * inverse, axis=0, keepdims=True)
    mg_ref[...] = middle_grad
    branch = middle_grad.astype(BF)
    branch_s[pl.ds(pl.multiple_of(step * part, part), part)] = branch
    for j in range(heads):
        send_ref[j] = dot_nt(branch, wo_ref[j * cols : (j + 1) * cols]).astype(BF)

    @pl.when(step == 0)
    def _():
        gg_ref[...] = gain_part

    @pl.when(step > 0)
    def _():
        gg_ref[...] += gain_part

    @pl.when(step == rows // part - 1)
    def _():
        for j in range(heads):
            og_ref[j * cols : (j + 1) * cols] = dot_tn(att_ref[j], branch_s[...]).astype(BF)


def branch_back(scale, mid, nback, cot, att, wo, gain):
    rows, width = mid.shape
    heads, _, cols = att.shape
    part = min(256, rows)
    rowwise = pl.BlockSpec((part, width), lambda i: (i, 0))

    def whole(w):
        return pl.BlockSpec(w.shape, lambda i: (0,) * len(w.shape))

    out = [
        jax.ShapeDtypeStruct((rows, width), F32),
        jax.ShapeDtypeStruct((heads, rows, cols), BF),
        jax.ShapeDtypeStruct((width, width), BF),
        jax.ShapeDtypeStruct((1, width), F32),
    ]
    return pl.pallas_call(
        branch_kernel,
        grid=(rows // part,),
        in_specs=[
            pl.BlockSpec(memory_space=pltpu.SMEM),
            rowwise,
            rowwise,
            rowwise,
            whole(att),
            whole(wo),
            whole(gain),
        ],
        out_specs=[
            rowwise,
            pl.BlockSpec((heads, part, cols), lambda i: (0, i, 0)),
            whole(out[2]),
            whole(out[3]),
        ],
        out_shape=out,
        scratch_shapes=[pltpu.VMEM((rows, width), BF)],
        compiler_params=pltpu.CompilerParams(vmem_limit_bytes=48 * 2**20),
        cost_estimate=cost(4 * rows * width * width),
    )(scale, mid, nback, cot, att, wo, gain)


Q_WAYS = (2, 2, 0)


def closing_kernel(dp, *refs):
    dq_in, dkv_in, hl_in, ex_in, x_in, gain_ref, wq_in, wl_in, mg_in, gg_ref = refs[:10]
    ig_out, q_out, l_out, e_out, g_out = refs[10:15]
    refs = refs[:14] + refs[15:]
    dq, dkv, hl, ex, x, wq, wl, mg = refs[14:22]
    far_dq, far_lat, lat_send, lat_own, e_s, g_s, n1t, flip, ig = refs[22:31]
    q_stage, q_pair, q_ring, e_stage, e_pair, e_ring, g_stage, g_pair, g_ring = refs[31:40]
    load_sem, far_send, far_recv, x_sem = refs[40:44]
    q_send, q_recv, e_send, e_recv, g_send, g_recv = refs[44:]
    place = Place(dp)
    c, s = place.core, place.at["x"]
    rows, width = x.shape
    cols, lat = dq.shape[1], ex.shape[0]
    part = rows // 2
    unit = q_out.shape[0]

    def at(index, size):
        return pl.ds(pl.multiple_of(index * size, size), size)

    loads = [(ex_in, ex), (dkv_in, dkv), (hl_in, hl), (x_in, x), (dq_in.at[c], dq)]
    loads += [(wq_in, wq), (wl_in, wl), (mg_in, mg)]

    def load(i):
        return pltpu.make_async_copy(*loads[i], load_sem.at[i])

    for i in (3, 4, 0, 1, 5, 6, 7, 2):
        load(i).start()
    place.greet()
    far_q = remote(dq_in.at[1 - c], far_dq, far_send.at[0], far_recv.at[0], place.pair())
    far_l = remote(lat_send, far_lat, far_send.at[1], far_recv.at[1], place.pair())
    far_q.start()

    q_sums = BlockSums(dp, q_stage, q_pair, q_ring, q_send, q_recv, q_out, l_out)
    e_sums = BlockSums(dp, e_stage, e_pair, e_ring, e_send, e_recv, e_out)
    g_sums = BlockSums(dp, g_stage, g_pair, g_ring, g_send, g_recv, g_out)
    order = q_sums.order()

    load(3).wait()
    gain = gain_ref[...].astype(F32)

    def inverse_of(values):
        return lax.rsqrt(jnp.mean(values * values, axis=-1, keepdims=True) + EPSILON)

    for u in range(2):
        chunk = slice(u * part, (u + 1) * part)
        values = x[chunk].astype(F32)
        flip[...] = (values * inverse_of(values) * gain).astype(BF).T
        for i, shard in enumerate(order):
            n1t[i * unit : (i + 1) * unit, chunk] = flip[at(shard, unit)]
    load(4).wait()
    q_stage[c] = dot_nn(n1t[...], dq[...]).astype(BF)
    load(0).wait()
    load(1).wait()
    for u in range(2):
        lat_send[u * part : (u + 1) * part] = dot_nt(dkv[at(u * 2 + 1 - c, part)], ex[...]).astype(BF)
    far_l.start()
    for u in range(2):
        lat_own[u * part : (u + 1) * part] = dot_nt(dkv[at(u * 2 + c, part)], ex[...]).astype(BF)
    far_q.wait_recv()
    q_stage[1 - c] = dot_nn(n1t[...], far_dq[...]).astype(BF)
    for j in range(2):
        q_sums.pair(j).start()
    for i in (5, 6, 7):
        load(i).wait()
    far_l.wait_recv()

    def back(u):
        chunk = at(u, part)
        normed_back = (
            dot_nt(dq[chunk], wq[:, at(c, cols)])
            + dot_nt(far_dq[chunk], wq[:, at(1 - c, cols)])
            + dot_nt(lat_own[chunk], wl[:, at(c, lat)])
            + dot_nt(far_lat[chunk], wl[:, at(1 - c, lat)])
        )
        values = x[chunk].astype(F32)
        inverse = inverse_of(values)
        scaled = normed_back * gain
        grad = mg[chunk] + (
            inverse * scaled
            - values
            * (inverse * inverse * inverse)
            * jnp.mean(scaled * values, axis=-1, keepdims=True)
        )
        ig[u] = grad.astype(BF)
        return jnp.sum(normed_back * values * inverse, axis=0, keepdims=True)

    gain_part = back(1 - s)
    swap, kept = block_swap(ig, ig_out, x_sem, place)
    swap.start()
    for j in range(2):
        q_sums.advance(j, 2, 1)
    q_stage[2, :, at(c, lat)] = dot_nn(n1t[...], lat_own[...]).astype(BF)
    q_stage[2, :, at(1 - c, lat)] = dot_nn(n1t[...], far_lat[...]).astype(BF)
    q_sums.pair(2).start()
    load(2).wait()
    e_s[...] = dot_tn(hl[...], dkv[...])
    share = e_out.shape[0] // KVH
    for i, shard in enumerate(order):
        piece = e_s[at(shard, share)]
        zero = jnp.zeros_like(piece)
        whole = jnp.concatenate(
            [jnp.where(c == 0, piece, zero), jnp.where(c == 0, zero, piece)], axis=0
        ).astype(BF)
        for j in range(2):
            e_stage[j, i * 2 * share : (i + 1) * 2 * share] = whole[:, j * cols : (j + 1) * cols]
    for j in range(2):
        e_sums.pair(j).start()
    q_sums.advance(2, 0, 1)
    gain_part = gain_part + back(s)
    kept.start()
    g_s[...] = jnp.concatenate(
        [gain_part, gg_ref[...], jnp.zeros((14, width), F32)], axis=0
    ).astype(BF)
    for i, shard in enumerate(order):
        g_stage[0, i * 16 : (i + 1) * 16] = g_s[:, at(lax.div(shard * unit, 128), 128)]
    g_sums.pair(0).start()
    for j in range(2):
        e_sums.advance(j, 2, 1)
    g_sums.advance(0, 2, 1)
    for phase in (2, 3, 4):
        for j in range(3):
            q_sums.advance(j, Q_WAYS[j], phase)
        for j in range(2):
            e_sums.advance(j, 2, phase)
        g_sums.advance(0, 2, phase)
    far_q.wait_send()
    far_l.wait_send()
    for sums, parities in ((q_sums, Q_WAYS), (e_sums, (2, 2)), (g_sums, (2,))):
        for j in range(len(parities)):
            sums.pair(j).wait_send()
        sums.finish(parities)
    swap.wait()
    kept.wait()


def closing(dp, dq, dkv, head_latent, expand, x, gain, wq, wl, mg, gain_two_grad):
    rows, width = x.shape
    cols, lat = dq.shape[2], expand.shape[0]
    unit = width // (4 * dp)
    n = 2 * dp
    anywhere = pl.BlockSpec(memory_space=pl.ANY)
    inside = pl.BlockSpec(memory_space=pltpu.VMEM)
    vmem = pltpu.VMEM
    sem = pltpu.SemaphoreType.DMA
    share = lat // (2 * n) * KVH
    bulk = [((rows, cols), BF), (dkv.shape, BF), (head_latent.shape, BF), (expand.shape, BF)]
    bulk += [(x.shape, BF), (wq.shape, BF), (wl.shape, BF), (mg.shape, F32)]
    sums = []
    for blocks, high, wide in ((3, unit, cols), (2, share, cols), (1, 16, 128)):
        sums += [vmem((blocks, 2 * n * high, wide), BF)] + [vmem((blocks, n * high, wide), BF)] * 2
    return pl.pallas_call(
        functools.partial(closing_kernel, dp),
        in_specs=[anywhere] * 5 + [inside] + [anywhere] * 3 + [inside],
        out_specs=[anywhere] + [inside] * 4,
        out_shape=[
            jax.ShapeDtypeStruct((2, rows // 2, width), BF),
            jax.ShapeDtypeStruct((unit, 2 * cols), F32),
            jax.ShapeDtypeStruct((unit, cols), F32),
            jax.ShapeDtypeStruct((share, 2 * cols), F32),
            jax.ShapeDtypeStruct((16, 128), F32),
        ],
        scratch_shapes=[vmem(*b) for b in bulk]
        + [
            vmem((rows, cols), BF),
            vmem((rows, lat), BF),
            vmem((rows, lat), BF),
            vmem((rows, lat), BF),
            vmem((lat, 2 * cols), F32),
            vmem((16, width), BF),
            vmem((width, rows), BF),
            vmem((width, rows // 2), BF),
            vmem((2, rows // 2, width), BF),
        ]
        + sums
        + [sem((8,)), sem((2,)), sem((2,)), sem((3,))]
        + [sem((blocks, dp + 1)) for blocks in (3, 3, 2, 2, 1, 1)],
        compiler_params=pltpu.CompilerParams(
            collective_id=1, has_side_effects=True, vmem_limit_bytes=60 * 2**20
        ),
    )(dq, dkv, head_latent, expand, x, gain, wq, wl, mg, gain_two_grad)


HEADS = 16
LATD = 256
HG = 8
GROUPS = 8
ALL = ("dp", "seq", "grp")


def norm_parts(values, gain):
    inverse = lax.rsqrt(jnp.mean(values * values, axis=-1, keepdims=True) + EPSILON)
    return (values * inverse * gain, inverse)


def norm_back(values, inverse, gain, upstream):
    scaled = upstream * gain
    gain_grad = jnp.sum(upstream * values * inverse, axis=0)
    input_part = inverse * scaled - values * inverse**3 * jnp.mean(
        scaled * values, axis=-1, keepdims=True
    )
    return (input_part, gain_grad)


def swap_sequences(blocks, count):
    if count == 2:
        me = lax.axis_index("seq")
        sent = lax.ppermute(blocks[1 - me], "seq", [(0, 1), (1, 0)])
        kept = blocks[me]
        first = me == 0
        return jnp.stack([jnp.where(first, kept, sent), jnp.where(first, sent, kept)])
    return lax.all_to_all(blocks, "seq", 0, 0, tiled=True)


def swap_group(blocks):
    return lax.all_to_all(blocks, "grp", 0, 0, tiled=True)


def local(
    inputs,
    cotangent,
    group_ids,
    group_scale,
    norm_gain,
    w_query,
    w_latent,
    expansion_weight,
    w_output,
    ffn_gain,
    w_gate,
    w_up,
    w_down,
):
    devices = lax.axis_size("dp") * lax.axis_size("seq") * lax.axis_size("grp")
    groups = lax.axis_size("grp")
    me = lax.axis_index("grp")
    seqs, rows, width = inputs.shape
    count = seqs * rows
    hidden_size = w_gate.shape[1]
    heads = HEADS // groups
    cols = heads * DH
    drows = width // devices

    dp = lax.axis_size("dp")
    ring = groups == 2 and seqs == 2 and dp % 2 == 0
    expand_rows = expansion_weight.reshape(-1, expansion_weight.shape[2])
    gains = jnp.pad(jnp.concatenate([norm_gain, ffn_gain])[None], ((0, 15), (0, 128 - 2 * drows)))
    if ring:
        shards = (w_query, w_latent, expand_rows, gains)
        full, own_inputs = own_gather(dp, shards, inputs, ("xzy",) * 4)
    else:
        shards = (w_query, w_latent, expand_rows, gains)
        full = [lax.all_gather(w, ALL, axis=0) for w in shards]
        own_inputs = swap_sequences(inputs, seqs)
    gate_up = jnp.stack(
        [w_gate.reshape(drows, -1, CUT), w_up.reshape(drows, -1, CUT)], axis=2
    ).reshape(drows, -1)
    wide_full = lax.all_gather(
        jnp.concatenate([w_output, gate_up], axis=1), ALL, axis=0, tiled=True
    )
    query_full = full[0].reshape(width, -1)
    latent_full = full[1].reshape(width, -1)
    expand_full = full[2].reshape(devices, KVH, LATD // devices, -1)
    gain_one = full[3][:, 0, :drows].reshape(width).astype(F32)
    gain_two = full[3][:, 0, drows : 2 * drows].reshape(1, width)

    expand_local = lax.dynamic_slice(
        expand_full,
        (0, me * heads // HG, 0, me * heads % HG * 2 * DH),
        (devices, 1, LATD // devices, heads * 2 * DH),
    ).reshape(LATD, -1)
    if ring:
        half = width // 2
        (
            logsum,
            attended,
            token_attended,
            head_queries,
            head_pairs,
            head_latent,
            own_cotangent,
            down_full,
        ) = attention_forward_gather(
            dp,
            own_inputs.reshape(count, width),
            gain_one.reshape(1, width),
            query_full,
            latent_full,
            expand_local,
            cotangent,
            (w_down,),
            ((0, 0, half), (0, half, half)),
            ("xzy", "zxy"),
        )
        down_full = down_full.reshape(-1, width)
    else:
        token_rows = own_inputs.astype(F32).reshape(count, width)
        normed, inverse_one = norm_parts(token_rows, gain_one)
        normed_low = normed.astype(BF)
        query_send = jnp.stack(
            [dot_nn(normed_low, query_full[:, j * cols : (j + 1) * cols]).astype(BF) for j in range(groups)]
        ).reshape(groups, seqs, rows, cols)
        latent_state = [
            dot_nn(normed_low, latent_full[:, g * LATD : (g + 1) * LATD]).astype(BF) for g in range(KVH)
        ]
        latent_send = jnp.stack([latent_state[j * heads // HG] for j in range(groups)]).reshape(
            groups, seqs, rows, LATD
        )
        head_queries = swap_group(query_send)
        head_latent = swap_group(latent_send).transpose(1, 0, 2, 3).reshape(-1, LATD)
        head_pairs = dot_nn(head_latent, expand_local).astype(BF)
        attended, logsum = attention_forward(head_queries, head_pairs)
        token_attended = swap_group(attended)
        own_cotangent = swap_sequences(cotangent, seqs)
        down_full = lax.all_gather(w_down, ALL, axis=0, tiled=True)
    token_attended = token_attended.reshape(groups, count, cols)
    seq_group = lax.dynamic_index_in_dim(group_ids, lax.axis_index("seq"), 0, keepdims=False)
    chosen = (seq_group == jnp.arange(GROUPS)).astype(F32)
    seq_scale = jnp.sum(chosen * group_scale).reshape(1, 1)
    x_rows = own_inputs.reshape(count, width)
    cot_rows = own_cotangent.reshape(count, width)
    result, normed_two_back, gu_share, down_grad, *rest = feed_forward(
        dp if ring else None,
        seq_scale,
        x_rows,
        token_attended,
        gain_two,
        cot_rows,
        wide_full,
        down_full,
    )
    own_output = result.reshape(seqs, rows, width)
    if ring:
        middle_grad = normed_two_back
        gain_two_grad, head_upstream, output_grad = rest
        head_upstream = head_upstream.reshape(groups, seqs, rows, cols)
    else:
        gu_share = lax.psum_scatter(gu_share, ALL, scatter_dimension=0, tiled=True).astype(F32)
        middle_grad, back_send, output_grad, gain_two_grad = branch_back(
            seq_scale, *rest, normed_two_back, cot_rows, token_attended, wide_full[:, :width], gain_two
        )
        head_upstream = swap_group(back_send.reshape(groups, seqs, rows, cols))
    gu_share = gu_share.reshape(drows, -1, 2, CUT)
    terms = (output_grad.reshape(devices, drows, width), down_grad.reshape(devices, -1, width))
    attention = (head_queries, head_pairs, head_upstream, attended, logsum)
    if ring:
        half = width // 2
        query_back, pair_back, output, output_share, down_share = attention_backward_scatter(
            dp,
            *attention,
            own_output,
            terms,
            ((0, 0, width), (1, 0, half), (1, half, half)),
            ("yzx", "yxz", "yzx"),
        )
    else:
        query_back, pair_back = attention_backward(*attention)
        output = swap_sequences(own_output, seqs)
        output_share, down_share = [
            lax.psum_scatter(w, ALL, scatter_dimension=0, tiled=True)[0].astype(F32) for w in terms
        ]
    if ring:
        input_grad, q_share, l_share, e_share, g_share = closing(
            dp,
            query_back.reshape(groups, count, cols),
            pair_back,
            head_latent,
            expand_local,
            x_rows,
            gain_one,
            query_full,
            latent_full,
            middle_grad,
            gain_two_grad,
        )
        shard = (lax.axis_index("dp") * 2 + lax.axis_index("seq")) * 2 + me
        own_gains = lax.dynamic_slice(g_share, (0, shard * drows % 128), (2, drows))
        sums = (q_share, l_share, e_share)
    else:
        latent_terms = dot_nt(pair_back, expand_local).astype(BF)
        expand_part = dot_tn(head_latent, pair_back)
        expand_grad = lax.dynamic_update_slice(
            jnp.zeros(expand_full.shape, BF),
            expand_part.astype(BF).reshape(devices, 1, LATD // devices, -1),
            (0, me * heads // HG, 0, me * heads % HG * 2 * DH),
        )
        query_token = swap_group(query_back).reshape(groups, count, cols)
        latent_token = swap_group(
            latent_terms.reshape(seqs, groups, rows, LATD).transpose(1, 0, 2, 3)
        ).reshape(KVH, groups // KVH, count, LATD)
        latent_token = jnp.sum(latent_token.astype(F32), axis=1).astype(BF)
        query_grad = jnp.concatenate([dot_tn(normed_low, query_token[j]) for j in range(groups)], axis=1)
        latent_grad = jnp.concatenate([dot_tn(normed_low, latent_token[g]) for g in range(KVH)], axis=1)
        normed_back = sum(
            dot_nt(query_token[j], query_full[:, j * cols : (j + 1) * cols]) for j in range(groups)
        ) + sum(
            dot_nt(latent_token[g], latent_full[:, g * LATD : (g + 1) * LATD]) for g in range(KVH)
        )
        input_part, gain_one_grad = norm_back(token_rows, inverse_one, gain_one, normed_back)
        own_input_grad = (middle_grad + input_part).astype(BF).reshape(seqs, rows, width)
        gain_grads = jnp.concatenate(
            [gain_one_grad.reshape(devices, 1, drows), gain_two_grad.reshape(devices, 1, drows)], axis=2
        ).astype(BF)
        gain_grads = jnp.pad(gain_grads, ((0, 0), (0, 15), (0, 128 - 2 * drows)))
        terms = (
            query_grad.astype(BF).reshape(devices, drows, -1),
            latent_grad.astype(BF).reshape(devices, drows, -1),
            expand_grad.reshape(devices, -1, expand_grad.shape[3]),
            gain_grads,
        )
        sums = [
            lax.psum_scatter(w, ALL, scatter_dimension=0, tiled=True)[0].astype(F32) for w in terms
        ]
        own_gains = sums[3][0, : 2 * drows].reshape(2, drows)
        input_grad = swap_sequences(own_input_grad, seqs)
    return (
        output,
        input_grad,
        own_gains[0],
        sums[0],
        sums[1],
        sums[2].reshape(expansion_weight.shape),
        output_share,
        own_gains[1],
        gu_share[:, :, 0].reshape(drows, -1),
        gu_share[:, :, 1].reshape(drows, -1),
        down_share,
    )


def solution(mesh):
    def run(*arrays):
        dp, sp = mesh.shape["dp"], mesh.shape["sp"]
        seqs = arrays[0].shape[0] // dp
        grid = Mesh(mesh.devices.reshape(dp, seqs, sp // seqs), ALL)
        tokens = P("dp", ("seq", "grp"), None)
        matrix = P(ALL, None)
        expand = P(None, ALL, None)
        return jax.shard_map(
            local,
            mesh=grid,
            in_specs=(
                tokens,
                tokens,
                P("dp"),
                P(),
                P(ALL),
                matrix,
                matrix,
                expand,
                matrix,
                P(ALL),
                matrix,
                matrix,
                matrix,
            ),
            out_specs=(
                tokens,
                tokens,
                P(ALL),
                matrix,
                matrix,
                expand,
                matrix,
                P(ALL),
                matrix,
                matrix,
                matrix,
            ),
            check_vma=False,
        )(*arrays)

    return run
```

```python
import functools
import jax
import jax.numpy as jnp
from jax import lax
from jax.sharding import Mesh
from jax.sharding import PartitionSpec as P
from jax.experimental import pallas as pl
from jax.experimental.pallas import tpu as pltpu

DH = 64
KVH = 2
EPSILON = 1e-05
F32 = jnp.float32
BF = jnp.bfloat16


def cost(flops):
    return pl.CostEstimate(flops=flops, bytes_accessed=2**23, transcendentals=0)


MESH = pl.DeviceIdType.MESH


class Place:

    def __init__(self, dp):
        self.sizes = {"x": 2, "y": 2, "z": dp // 2}
        d = lax.axis_index("dp")
        self.at = {"x": lax.axis_index("seq"), "y": lax.rem(d, 2), "z": lax.div(d, 2)}
        self.core = lax.axis_index("grp")

    def coords(self, offset):
        at = {k: lax.rem(self.at[k] + o, self.sizes[k]) if o else self.at[k] for k, o in offset.items()}
        return at["z"] * 2 + at["y"], at["x"]

    def index(self, offset, other):
        d, s = self.coords(offset)
        core = 1 - self.core if other else self.core
        return (d * 2 + s) * 2 + core

    def device(self, offset):
        return (*self.coords(offset), self.core)

    def pair(self):
        return (*self.coords({"x": 0, "y": 0, "z": 0}), 1 - self.core)

    def greet(self):
        there = [self.pair()]
        for k in "xyz":
            for o in range(1, self.sizes[k]):
                there.append(self.device({"x": 0, "y": 0, "z": 0, k: o}))
        barrier = pltpu.get_barrier_semaphore()
        for device in there:
            pl.semaphore_signal(barrier, inc=1, device_id=device, device_id_type=MESH)
        pl.semaphore_wait(barrier, len(there))


def offsets_of(order, dp):
    sizes = {"x": 2, "y": 2, "z": dp // 2}
    a, b, c = (sizes[k] for k in order)
    return [(i, j, k) for i in range(a) for j in range(b) for k in range(c)]


def named(order, steps):
    return dict(zip(order, steps))


def remote(src, dst, send, recv, there):
    return pltpu.make_async_remote_copy(
        src_ref=src, dst_ref=dst, send_sem=send, recv_sem=recv, device_id=there, device_id_type=MESH
    )


class Gather:

    def __init__(self, place, dp, order, src, out, sems, number):
        self.place, self.order, self.src, self.out = place, order, src, out
        self.steps = offsets_of(order, dp)
        self.sems, self.number = sems, number

    def slot(self, steps, other=False):
        return self.out(self.place.index(named(self.order, steps), other))

    def source(self, steps):
        last = max(i for i in range(3) if steps[i])
        return tuple(0 if i == last else o for i, o in enumerate(steps))

    def hop(self, steps):
        last = max(i for i in range(3) if steps[i])
        source = self.source(steps)
        size = self.place.sizes[self.order[last]]
        back = tuple(size - o if i == last else 0 for i, o in enumerate(steps))
        number = self.steps.index(steps)
        here = self.slot(source)
        src = here if any(source) else self.src
        return remote(
            src,
            here,
            self.sems[0].at[self.number, number],
            self.sems[1].at[self.number, number],
            self.place.device(named(self.order, back)),
        )

    def across(self, steps):
        number = self.steps.index(steps)
        src = self.slot(steps) if any(steps) else self.src
        return remote(
            src,
            self.slot(steps),
            self.sems[2].at[self.number, number],
            self.sems[3].at[self.number, number],
            self.place.pair(),
        )

    def keep(self):
        return pltpu.make_async_copy(self.src, self.slot((0, 0, 0)), self.sems[4].at[self.number])

    def send_from(self, source):
        for steps in self.steps:
            if any(steps) and self.source(steps) == source:
                self.hop(steps).start()
        self.across(source).start()

    def start(self):
        self.send_from((0, 0, 0))
        self.keep().start()

    def arrivals(self):
        return sorted((s for s in self.steps if any(s)), key=lambda s: [o > 0 for o in s][::-1])

    def forward(self, steps):
        number = self.steps.index(steps)
        here = self.slot(steps)
        remote(
            here,
            here,
            self.sems[0].at[self.number, number],
            self.sems[1].at[self.number, number],
            self.place.pair(),
        ).wait_recv()
        self.send_from(steps)

    def finish(self):
        for steps in self.steps:
            number = self.steps.index(steps)
            here = self.slot(steps, True)
            remote(
                here,
                here,
                self.sems[2].at[self.number, number],
                self.sems[3].at[self.number, number],
                self.place.pair(),
            ).wait_recv()
            self.across(steps).wait_send()
            if any(steps):
                self.hop(steps).wait_send()
        self.keep().wait()


class Scatter:

    def __init__(self, place, dp, order, term, pair_buf, ring_buf, sems, number, own=None):
        self.place, self.order, self.term = place, order, term
        self.own_buf, self.own_sem = own if own else (None, None)
        self.steps = offsets_of(order, dp)
        self.pair_buf, self.ring_buf = pair_buf, ring_buf
        self.sems, self.number = sems, number

    def turn(self):
        def key(steps):
            first = next((i for i in range(3) if steps[i]), 3)
            return (first, [o == 0 for o in steps])

        return sorted(self.steps, key=key)

    def across(self, steps):
        number = self.steps.index(steps)
        return remote(
            self.term(self.place.index(named(self.order, steps), True)),
            self.pair_buf.at[number],
            self.sems[2].at[self.number, number],
            self.sems[3].at[self.number, number],
            self.place.pair(),
        )

    def fetch(self, steps):
        number = self.steps.index(steps)
        return pltpu.make_async_copy(
            self.term(self.place.index(named(self.order, steps), False)),
            self.own_buf.at[number],
            self.own_sem.at[self.number, number],
        )

    def start(self):
        for steps in self.turn():
            self.across(steps).start()
            if self.own_buf is not None:
                self.fetch(steps).start()

    def hop(self, steps):
        first = min(i for i in range(3) if steps[i])
        there = tuple(o if i == first else 0 for i, o in enumerate(steps))
        number = self.steps.index(steps)
        return remote(
            self.pair_buf.at[number],
            self.ring_buf.at[number],
            self.sems[0].at[self.number, number],
            self.sems[1].at[self.number, number],
            self.place.device(named(self.order, there)),
        )

    def add(self, steps, out=None):
        number = self.steps.index(steps)
        self.across(steps).wait_recv()
        if self.own_buf is None:
            mine = self.term(self.place.index(named(self.order, steps), False))
        else:
            self.fetch(steps).wait()
            mine = self.own_buf.at[number]
        total = mine[...].astype(F32) + self.pair_buf[number].astype(F32)
        for came in self.steps:
            if not any(came):
                continue
            first = min(i for i in range(3) if came[i])
            if tuple(0 if i == first else o for i, o in enumerate(came)) == steps:
                self.hop(came).wait_recv()
                total = total + self.ring_buf[self.steps.index(came)].astype(F32)
        if out is None:
            self.pair_buf[number] = total.astype(BF)
            self.hop(steps).start()
        else:
            out[...] = total

    def finish(self):
        for steps in self.steps:
            self.across(steps).wait_send()
            if any(steps):
                self.hop(steps).wait_send()


def block_swap(x_in, x_out, sem, place):
    s = place.at["x"]
    away = remote(
        x_in.at[1 - s], x_out.at[s], sem.at[0], sem.at[1], place.device({"x": 1, "y": 0, "z": 0})
    )
    return away, pltpu.make_async_copy(x_in.at[s], x_out.at[s], sem.at[2])


def gather_kernel(dp, orders, *refs):
    count = len(orders)
    srcs, x_in = refs[:count], refs[count]
    outs, x_out = refs[count + 1 : 2 * count + 1], refs[2 * count + 1]
    sems, x_sem = refs[2 * count + 2 : -1], refs[-1]
    place = Place(dp)
    place.greet()
    works = [
        Gather(place, dp, orders[a], srcs[a], lambda at, a=a: outs[a].at[at], sems, a)
        for a in range(count)
    ]
    for work in works:
        work.start()
    swap, kept = block_swap(x_in, x_out, x_sem, place)
    swap.start()
    kept.start()
    for i in range(2 * dp - 1):
        for work in works:
            work.forward(work.arrivals()[i])
    for work in works:
        work.finish()
    swap.wait()
    kept.wait()


def gather_sems(dp, count):
    sem = pltpu.SemaphoreType.DMA
    return [sem((count, 2 * dp))] * 4 + [sem((count,))]


def own_gather(dp, shards, blocks, orders):
    count = len(shards)
    anywhere = pl.BlockSpec(memory_space=pl.ANY)
    out = pl.pallas_call(
        functools.partial(gather_kernel, dp, orders),
        in_specs=[anywhere] * (count + 1),
        out_specs=[anywhere] * (count + 1),
        out_shape=[jax.ShapeDtypeStruct((4 * dp, *w.shape), w.dtype) for w in shards]
        + [jax.ShapeDtypeStruct(blocks.shape, blocks.dtype)],
        scratch_shapes=gather_sems(dp, count) + [pltpu.SemaphoreType.DMA((3,))],
        compiler_params=pltpu.CompilerParams(collective_id=0, has_side_effects=True),
    )(*shards, blocks)
    return out[:-1], out[-1]


def scatter_sems(dp, count):
    return [pltpu.SemaphoreType.DMA((count, 2 * dp))] * 4


def run_at(plan, point, when=None):
    for step, at in sorted((k for k in plan if k[0] != "last"), key=str):
        if at != (point if when is None else when):
            continue
        tasks = plan[step, at]

        @pl.when(pl.program_id(0) == step)
        def _(tasks=tasks):
            for task in tasks:
                task()


GATHER_AT = (0, 2, 3, 4, 5, 6, 7, 9, 10, 11, 12, 13, 14, 15, 15)
SCATTER_AT = (1, 1, 1, 1, 2, 2, 2, 2, 6, 7, 8, 9, 10, 11, 13, 16)


def put(plan, number, count, table, steps, points, task):
    at = table[number * len(table) // count] * steps * points // 16
    key = ("last", 0) if at >= steps * points else divmod(at, points)
    plan.setdefault(key, []).append(task)


def gather_plan(place, works, swap, steps, points):
    arrivals = [work.arrivals() for work in works]

    def begin():
        place.greet()
        for work in works:
            work.start()
        for copy in swap:
            copy.start()

    def forward(i):
        for work, order in zip(works, arrivals):
            work.forward(order[i])

    def end():
        for work in works:
            work.finish()
        for copy in swap:
            copy.wait()

    plan = {(0, "first"): [begin]}
    for i in range(len(arrivals[0])):
        put(plan, i, len(arrivals[0]), GATHER_AT, steps, points, functools.partial(forward, i))
    plan.setdefault(("last", 0), []).append(end)
    return plan


def scatter_plan(place, works, outs, swap, steps, points):
    turns = [work.turn() for work in works]
    count = len(turns[0])

    def begin():
        place.greet()
        for work in works:
            work.start()
        for copy in swap:
            copy.start()

    def add(i):
        for work, order, out in zip(works, turns, outs):
            work.add(order[i], out if i == count - 1 else None)

    def end():
        for work in works:
            work.finish()
        for copy in swap:
            copy.wait()

    plan = {(0, 0): [begin]}
    for i in range(count):
        put(plan, i, count, SCATTER_AT, steps, points, functools.partial(add, i))
    plan.setdefault(("last", 0), []).append(end)
    return plan


def dot_nt(a, b):
    return lax.dot_general(a, b, (((1,), (1,)), ((), ())), preferred_element_type=F32)


def dot_nn(a, b):
    return lax.dot_general(a, b, (((1,), (0,)), ((), ())), preferred_element_type=F32)


def dot_tn(a, b):
    return lax.dot_general(a, b, (((0,), (0,)), ((), ())), preferred_element_type=F32)


def causal(s, first_key, first_query):
    keys = first_key + lax.broadcasted_iota(jnp.int32, s.shape, 0)
    rows = first_query + lax.broadcasted_iota(jnp.int32, s.shape, 1)
    return jnp.where(rows >= keys, s, -1e30)


def forward_body(q_ref, kv_ref, o_ref, lse_ref, vt_s, point=lambda i: None):
    groups, chunks, rows, _ = q_ref.shape
    seq = kv_ref.shape[0]
    for h in range(2):
        vt_s[h] = kv_ref[:, h * 128 : (h + 1) * 128].astype(F32).T[DH:].astype(BF)
    for i in range(groups * chunks):
        point(i)
        q = q_ref[i % groups, i // groups].astype(F32) * 0.125
        outs = []
        for h in range(2):
            qh = q[:, h * DH : (h + 1) * DH]
            qp = jnp.concatenate([qh, jnp.zeros_like(qh)], axis=1).astype(BF)
            width = (i + 1) * rows
            s = dot_nt(kv_ref[0:width, h * 128 : (h + 1) * 128], qp)
            tail = causal(s[i * rows :], 0, 0)
            if i > 0:
                head = s[: i * rows]
                top = jnp.maximum(
                    jnp.max(head, axis=0, keepdims=True), jnp.max(tail, axis=0, keepdims=True)
                )
                ph = jnp.exp(head - top)
                pt = jnp.exp(tail - top)
                total = jnp.sum(ph, axis=0, keepdims=True) + jnp.sum(pt, axis=0, keepdims=True)
                o = dot_nn(vt_s[h, :, 0 : i * rows], ph.astype(BF)) + dot_nn(
                    vt_s[h, :, i * rows : width], pt.astype(BF)
                )
            else:
                top = jnp.max(tail, axis=0, keepdims=True)
                pt = jnp.exp(tail - top)
                total = jnp.sum(pt, axis=0, keepdims=True)
                o = dot_nn(vt_s[h, :, 0:width], pt.astype(BF))
            outs.append(o / total)
            lse_ref[h, i * rows : (i + 1) * rows] = (top + jnp.log(total))[0]
        o_ref[i % groups, i // groups] = jnp.concatenate(outs, axis=0).T.astype(BF)


def forward_kernel(q_ref, kv_ref, o_ref, lse_ref, vt_s):
    forward_body(q_ref, kv_ref, o_ref, lse_ref, vt_s)


def forward_gather_kernel(dp, cuts, orders, pairs, *refs):
    x_ref, tiles_ref, wq_ref, wl_ref, shards_ref, x_in = refs[:6]
    sources = 1 + max(cut[0] for cut in cuts)
    srcs, refs = refs[6 : 6 + sources], refs[6 + sources :]
    lse_ref, gain_ref, o_out, token_out, q_out, kv_out, hl_out, ex_out, x_out = refs[:9]
    outs, refs = refs[9 : 9 + sources], refs[9 + sources :]
    vt_s, x_sem, low_s, q_send, lat_send, q_s, kv_s, hl_s, o_s, ex_s = refs[:10]
    far_send, far_recv, save_sem = refs[10:13]
    sems = refs[13:]
    place = Place(dp)
    c = place.core
    works = []
    for number, (a, first, size) in enumerate(cuts):
        cut = pl.ds(first, size)
        works.append(
            Gather(
                place,
                dp,
                orders[number],
                srcs[a].at[:, cut],
                lambda at, a=a, cut=cut: outs[a].at[at, :, cut],
                sems,
                number,
            )
        )
    groups, chunks, rows, cols = q_s.shape
    lat = hl_s.shape[1]
    points = groups * chunks
    plan = gather_plan(place, works, block_swap(x_in, x_out, x_sem, place), pairs, points)
    run_at(plan, 0, "first")

    def at(index, size):
        return pl.ds(pl.multiple_of(index * size, size), size)

    def far_q():
        return remote(q_send, q_s.at[c], far_send.at[0], far_recv.at[0], place.pair())

    def far_l(u):
        return remote(
            lat_send.at[u],
            hl_s.at[at(u * groups + c, rows)],
            far_send.at[1 + u],
            far_recv.at[1 + u],
            place.pair(),
        )

    def saves():
        return [
            pltpu.make_async_copy(src, dst, save_sem.at[i])
            for i, (src, dst) in enumerate(
                ((q_s, q_out), (kv_s, kv_out), (hl_s, hl_out), (ex_s, ex_out))
            )
        ]

    def hand_over():
        return [
            remote(o_s.at[1 - c], token_out.at[c], far_send.at[3], far_recv.at[3], place.pair()),
            pltpu.make_async_copy(o_s.at[c], token_out.at[c], save_sem.at[4]),
            pltpu.make_async_copy(o_s, o_out, save_sem.at[5]),
        ]

    @pl.when(pl.program_id(0) == 0)
    def _():
        count = 128 * tiles_ref.shape[0] // gain_ref.shape[1]
        for t in range(gain_ref.shape[1] // 128):
            total = tiles_ref[t * count].astype(F32)
            for i in range(1, count):
                total = total + tiles_ref[t * count + i].astype(F32)
            gain_ref[:, t * 128 : (t + 1) * 128] = total[:8]
        share = shards_ref.shape[1] // KVH
        for i in range(0, shards_ref.shape[0], KVH):
            pieces = []
            for k in range(KVH):
                both = shards_ref[i + k].astype(F32)
                pieces.append(jnp.where(c == 0, both[:share], both[share:]))
            ex_s[i * share : (i + KVH) * share] = jnp.concatenate(pieces, axis=0).astype(BF)
        gain = gain_ref[0:1]
        for u in range(chunks):
            chunk = slice(u * rows, (u + 1) * rows)
            values = x_ref[chunk].astype(F32)
            inverse = lax.rsqrt(jnp.mean(values * values, axis=-1, keepdims=True) + EPSILON)
            low_s[chunk] = (values * inverse * gain).astype(BF)
            lat_send[u] = dot_nn(low_s[chunk], wl_ref[:, at(1 - c, lat)]).astype(BF)
            far_l(u).start()
        for u in range(chunks):
            chunk = slice(u * rows, (u + 1) * rows)
            q_send[u] = dot_nn(low_s[chunk], wq_ref[:, at(1 - c, cols)]).astype(BF)
        far_q().start()
        for u in range(chunks):
            chunk = slice(u * rows, (u + 1) * rows)
            hl_s[at(u * groups + c, rows)] = dot_nn(low_s[chunk], wl_ref[:, at(c, lat)]).astype(BF)
            q_s[c, u] = dot_nn(low_s[chunk], wq_ref[:, at(c, cols)]).astype(BF)
        for u in range(chunks):
            far_l(u).wait_recv()
        for k in range(groups * chunks):
            chunk = slice(k * rows, (k + 1) * rows)
            kv_s[chunk] = dot_nn(hl_s[chunk], ex_s[...]).astype(BF)
        far_q().wait_recv()
        for save in saves():
            save.start()

    pid = pl.program_id(0)
    forward_body(
        q_s.at[:, :, :, at(pid, 128)],
        kv_s.at[:, at(pid, 256)],
        o_s.at[:, :, :, at(pid, 128)],
        lse_ref,
        vt_s,
        lambda i: run_at(plan, i),
    )

    @pl.when(pid == pairs - 1)
    def _():
        for copy in hand_over():
            copy.start()
        far_q().wait_send()
        for u in range(chunks):
            far_l(u).wait_send()
        for copy in saves() + hand_over():
            copy.wait()
        for task in plan["last", 0]:
            task()


def forward_specs(q, kv):
    groups, chunks, rows, cols = q.shape
    seq = kv.shape[0]
    pairs = cols // 128
    tok = pl.BlockSpec((groups, chunks, rows, 128), lambda p: (0, 0, 0, p))
    ins = [tok, pl.BlockSpec((seq, 256), lambda p: (0, p))]
    outs = [tok, pl.BlockSpec((None, 2, seq), lambda p: (p, 0, 0))]
    shapes = [jax.ShapeDtypeStruct(q.shape, BF), jax.ShapeDtypeStruct((pairs, 2, seq), F32)]
    scratch = [pltpu.VMEM((2, DH, seq), BF)]
    return pairs, ins, outs, shapes, scratch, cost(8 * pairs * seq * seq * 128)


def attention_forward(q, kv):
    pairs, ins, outs, shapes, scratch, estimate = forward_specs(q, kv)
    return pl.pallas_call(
        forward_kernel,
        grid=(pairs,),
        in_specs=ins,
        out_specs=outs,
        out_shape=shapes,
        scratch_shapes=scratch,
        compiler_params=pltpu.CompilerParams(vmem_limit_bytes=56 * 2**20),
        cost_estimate=estimate,
    )(q, kv)


def attention_forward_gather(dp, x, tiles, wq, wl, expand, blocks, shards, cuts, orders):
    rows, width = blocks.shape[1], x.shape[1]
    cols, lat = width // 2, expand.shape[0] * expand.shape[1] // KVH
    seq = 4 * rows
    q = jax.ShapeDtypeStruct((2, 2, rows, cols), BF)
    kv = jax.ShapeDtypeStruct((seq, 2 * cols), BF)
    hl = jax.ShapeDtypeStruct((seq, lat), BF)
    ex = jax.ShapeDtypeStruct((lat, 2 * cols), BF)
    gains = jax.ShapeDtypeStruct((8, width), F32)
    pairs, _, outs, shapes, scratch, estimate = forward_specs(q, kv)
    anywhere = pl.BlockSpec(memory_space=pl.ANY)
    count = len(shards)
    sem = pltpu.SemaphoreType.DMA

    def whole(w):
        return pl.BlockSpec(w.shape, lambda p: (0,) * len(w.shape), pipeline_mode=pl.Buffered(1))

    return pl.pallas_call(
        functools.partial(forward_gather_kernel, dp, cuts, orders, pairs),
        grid=(pairs,),
        in_specs=[whole(w) for w in (x, tiles, wq, wl, expand)] + [anywhere] * (1 + count),
        out_specs=outs[1:] + [whole(gains)] + [anywhere] * (7 + count),
        out_shape=shapes[1:]
        + [gains, q, q, q, kv, hl, ex]
        + [jax.ShapeDtypeStruct(blocks.shape, blocks.dtype)]
        + [jax.ShapeDtypeStruct((4 * dp, *w.shape), w.dtype) for w in shards],
        scratch_shapes=scratch
        + [
            sem((3,)),
            pltpu.VMEM(x.shape, BF),
            pltpu.VMEM((2, rows, cols), BF),
            pltpu.VMEM((2, rows, lat), BF),
            pltpu.VMEM(q.shape, BF),
            pltpu.VMEM(kv.shape, BF),
            pltpu.VMEM(hl.shape, BF),
            pltpu.VMEM(q.shape, BF),
            pltpu.VMEM(ex.shape, BF),
            sem((4,)),
            sem((4,)),
            sem((6,)),
        ]
        + gather_sems(dp, len(cuts)),
        compiler_params=pltpu.CompilerParams(
            vmem_limit_bytes=60 * 2**20, collective_id=2, has_side_effects=True
        ),
        cost_estimate=estimate,
    )(x, tiles, wq, wl, expand, blocks, *shards)


def backward_body(blk, q_ref, kv_ref, do_ref, o_ref, lse_ref, dq_ref, dkv_ref,
                  kt_s, acc_s, dqt_s, qp_s, dop_s, delta_s, point=lambda i: None):
    groups, chunks, rows, _ = q_ref.shape
    seq = kv_ref.shape[0]
    n = groups * chunks
    for h in range(2):
        kt_s[h] = kv_ref[:, h * 128 : (h + 1) * 128].astype(F32).T[:DH].astype(BF)
    acc_s[...] = jnp.zeros_like(acc_s)
    for i in range(n):
        at = pl.ds(i * rows, rows)
        q = q_ref[i % groups, i // groups].astype(F32) * 0.125
        do = do_ref[i % groups, i // groups].astype(F32)
        o = o_ref[i % groups, i // groups].astype(F32)
        prod = (do * o).T
        zero = jnp.zeros((rows, DH), F32)
        for h in range(2):
            cut = slice(h * DH, (h + 1) * DH)
            qp_s[h, at] = jnp.concatenate([q[:, cut], zero], axis=1).astype(BF)
            dop_s[h, at] = jnp.concatenate([zero, do[:, cut]], axis=1).astype(BF)
            delta_s[h, at] = jnp.sum(prod[cut], axis=0)

    def block(i, j, masked):
        qat = pl.ds(i * blk, blk)
        kat = pl.ds(pl.multiple_of(j * blk, blk), blk)
        for h in range(2):
            kv = kv_ref[kat, h * 128 : (h + 1) * 128]
            qp = qp_s[h, qat]
            dop = dop_s[h, qat]
            s = dot_nt(kv, qp)
            dp = dot_nt(kv, dop)
            if masked:
                s = causal(s, 0, 0)
            p = jnp.exp(s - lse_ref[h : h + 1, qat])
            ds = (p * (dp - delta_s[h : h + 1, qat])).astype(BF)
            acc_s[h, kat] += dot_nn(p.astype(BF), dop) + dot_nn(ds, qp)
            part = dot_nn(kt_s[h, :, kat], ds)
            if masked:
                dqt_s[h * DH : (h + 1) * DH, qat] = part
            else:
                dqt_s[h * DH : (h + 1) * DH, qat] += part

    m = seq // blk

    for i in range(m):
        point(i)
        block(i, i, True)

        def inner(j, _, i=i):
            block(i, j, False)
            return 0

        lax.fori_loop(0, i, inner, 0)
    for i in range(n):
        at = pl.ds(i * rows, rows)
        dq_ref[i % groups, i // groups] = (dqt_s[:, at].T * 0.125).astype(BF)
    for h in range(2):
        dkv_ref[:, h * 128 : (h + 1) * 128] = acc_s[h].astype(BF)


def backward_kernel(blk, *refs):
    backward_body(blk, *refs)


def backward_scatter_kernel(dp, blk, cuts, orders, pairs, *refs):
    ins, x_in, refs = refs[:5], refs[5], refs[6:]
    sources = 1 + max(cut[0] for cut in cuts)
    count = len(cuts)
    terms, refs = refs[:sources], refs[sources:]
    attn_outs, x_out, refs = refs[:2], refs[2], refs[3:]
    outs, refs = refs[:sources], refs[sources:]
    scratch, x_sem, refs = refs[:6], refs[6], refs[7:]
    own_bufs, pair_bufs, ring_bufs = refs[:count], refs[count : 2 * count], refs[2 * count : 3 * count]
    own_sem, sems = refs[3 * count], refs[3 * count + 1 :]
    place = Place(dp)
    works, targets = [], []
    for number, (a, first, size) in enumerate(cuts):
        cut = pl.ds(first, size)
        works.append(
            Scatter(
                place,
                dp,
                orders[number],
                lambda at, a=a, cut=cut: terms[a].at[at, :, cut],
                pair_bufs[number],
                ring_bufs[number],
                sems,
                number,
                (own_bufs[number], own_sem),
            )
        )
        targets.append(outs[a].at[:, cut])
    points = ins[1].shape[0] // blk
    plan = scatter_plan(place, works, targets, block_swap(x_in, x_out, x_sem, place), pairs, points)
    backward_body(blk, *ins, *attn_outs, *scratch, point=lambda i: run_at(plan, i))

    @pl.when(pl.program_id(0) == pairs - 1)
    def _():
        for task in plan["last", 0]:
            task()


def backward_specs(q, kv):
    groups, chunks, rows, cols = q.shape
    seq = kv.shape[0]
    pairs = cols // 128
    tok = pl.BlockSpec((groups, chunks, rows, 128), lambda p: (0, 0, 0, p))
    wide = pl.BlockSpec((seq, 256), lambda p: (0, p))
    ins = [tok, wide, tok, tok, pl.BlockSpec((None, 2, seq), lambda p: (p, 0, 0))]
    outs = [tok, wide]
    shapes = [jax.ShapeDtypeStruct(q.shape, BF), jax.ShapeDtypeStruct(kv.shape, BF)]
    scratch = [
        pltpu.VMEM((2, DH, seq), BF),
        pltpu.VMEM((2, seq, 128), F32),
        pltpu.VMEM((128, seq), F32),
        pltpu.VMEM((2, seq, 128), BF),
        pltpu.VMEM((2, seq, 128), BF),
        pltpu.VMEM((2, seq), F32),
    ]
    return pairs, ins, outs, shapes, scratch, cost(16 * pairs * seq * seq * 128)


def attention_backward(q, kv, do, o, lse, blk=512):
    pairs, ins, outs, shapes, scratch, estimate = backward_specs(q, kv)
    return pl.pallas_call(
        functools.partial(backward_kernel, blk),
        grid=(pairs,),
        in_specs=ins,
        out_specs=outs,
        out_shape=shapes,
        scratch_shapes=scratch,
        compiler_params=pltpu.CompilerParams(vmem_limit_bytes=56 * 2**20),
        cost_estimate=estimate,
    )(q, kv, do, o, lse)


def attention_backward_scatter(dp, q, kv, do, o, lse, blocks, terms, cuts, orders, blk=512):
    pairs, ins, outs, shapes, scratch, estimate = backward_specs(q, kv)
    anywhere = pl.BlockSpec(memory_space=pl.ANY)
    count = len(cuts)
    bufs = [pltpu.VMEM((2 * dp, terms[a].shape[1], size), BF) for a, _, size in cuts]
    return pl.pallas_call(
        functools.partial(backward_scatter_kernel, dp, blk, cuts, orders, pairs),
        grid=(pairs,),
        in_specs=ins + [anywhere] * (1 + len(terms)),
        out_specs=outs + [anywhere] + [pl.BlockSpec(w.shape[1:], lambda p: (0, 0)) for w in terms],
        out_shape=shapes
        + [jax.ShapeDtypeStruct(blocks.shape, blocks.dtype)]
        + [jax.ShapeDtypeStruct(w.shape[1:], F32) for w in terms],
        scratch_shapes=scratch
        + [pltpu.SemaphoreType.DMA((3,))]
        + bufs * 3
        + [pltpu.SemaphoreType.DMA((count, 2 * dp))]
        + scatter_sems(dp, count),
        compiler_params=pltpu.CompilerParams(
            vmem_limit_bytes=60 * 2**20, collective_id=3, has_side_effects=True
        ),
        cost_estimate=estimate,
    )(q, kv, do, o, lse, blocks, *terms)


CUT = 256
PART = 512
TALL = 512
DOWN = 8
LAGS = (1, 3, 6, 9)


class BlockSums:

    def __init__(self, dp, stage, pair_buf, ring_buf, send, recv, out_ref, last_ref=None):
        self.last_ref = last_ref
        self.place = Place(dp)
        self.stage, self.pair_buf, self.ring_buf = stage, pair_buf, ring_buf
        self.send, self.recv, self.out_ref = send, recv, out_ref
        self.total = pair_buf.shape[1]
        self.unit = out_ref.shape[0]

    def order(self):
        return [
            self.place.index({"y": y, "x": x, "z": z}, other)
            for other in (False, True)
            for y in range(2)
            for x in range(2)
            for z in range(self.place.sizes["z"])
        ]

    def pair(self, j):
        return remote(
            self.stage.at[lax.rem(j, self.stage.shape[0]), pl.ds(self.total, self.total)],
            self.pair_buf.at[j],
            self.send.at[j, 0],
            self.recv.at[j, 0],
            self.place.pair(),
        )

    def hop(self, j, axis, step, first, size, number):
        rows = pl.ds(first, size)
        offset = {"x": 0, "y": 0, "z": 0, axis: step}
        return remote(
            self.pair_buf.at[j, rows],
            self.ring_buf.at[j, rows],
            self.send.at[j, number],
            self.recv.at[j, number],
            self.place.device(offset),
        )

    def hops(self, way, phase):
        q, unit = self.total // 4, self.unit
        sizes = range(1, self.place.sizes["z"])
        if way == 2:
            far = [("z", z, z * unit, unit, 1 + 2 * z) for z in sizes]
            far += [("z", z, q + z * unit, unit, 2 + 2 * z) for z in sizes]
            return ([("y", 1, 2 * q, 2 * q, 1)], far, [("x", 1, q, unit, 2)])[phase - 1]
        if phase == 3:
            return [("z", z, z * unit, unit, 3 + z) for z in sizes]
        if way:
            return ([("x", 1, q, q, 1), ("x", 1, 3 * q, q, 2)], [("y", 1, 2 * q, q, 3)])[phase - 1]
        return ([("y", 1, 2 * q, 2 * q, 1)], [("x", 1, q, q, 3)])[phase - 1]

    def add(self, j, to, size, came):
        self.pair_buf[j, to : to + size] = (
            self.pair_buf[j, to : to + size].astype(F32) + came.astype(F32)
        ).astype(BF)

    def advance(self, j, way, phase):
        q, unit = self.total // 4, self.unit
        sizes = range(1, self.place.sizes["z"])
        if phase == 1:
            self.pair(j).wait_recv()
            self.add(j, 0, self.total, self.stage[lax.rem(j, self.stage.shape[0]), : self.total])
        else:
            for hop in self.hops(way, phase - 1):
                self.hop(j, *hop).wait_recv()
        if phase == 2 and way == 1:
            self.add(j, 0, q, self.ring_buf[j, q : 2 * q])
            self.add(j, 2 * q, q, self.ring_buf[j, 3 * q :])
        elif phase == 2:
            self.add(j, 0, 2 * q, self.ring_buf[j, 2 * q :])
        elif phase == 3 and way == 2:
            for first in (0, q):
                total = self.pair_buf[j, first : first + unit].astype(F32)
                for z in sizes:
                    came = slice(first + z * unit, first + (z + 1) * unit)
                    total = total + self.ring_buf[j, came].astype(F32)
                self.pair_buf[j, first : first + unit] = total.astype(BF)
        elif phase == 3:
            first = 2 * q if way else q
            self.add(j, 0, q, self.ring_buf[j, first : first + q])
        elif phase == 4:
            total = self.pair_buf[j, :unit].astype(F32)
            for first in (q,) if way == 2 else [z * unit for z in sizes]:
                total = total + self.ring_buf[j, first : first + unit].astype(F32)
            wide = total.shape[1]
            if self.last_ref is not None and j == self.pair_buf.shape[0] - 1:
                self.last_ref[...] = total
            else:
                self.out_ref[:, pl.ds(pl.multiple_of(j * wide, wide), wide)] = total
        if phase < 4:
            for hop in self.hops(way, phase):
                self.hop(j, *hop).start()

    def finish(self, parities):
        for j, odd in enumerate(parities):
            for phase in range(1, 4):
                for hop in self.hops(odd, phase):
                    self.hop(j, *hop).wait_send()


def ffn_kernel(dp, scale_ref, x_ref, att_ref, wo_ref, gain_ref, cot_ref, gu_ref, down_ref,
               res_ref, nb_ref, gu_out, down_out, *refs):
    if dp:
        gg_ref, heads_out, og_out, refs = refs[0], refs[1], refs[2], refs[3:]
        mid_ref, out_sem, far_sem, refs = refs[0], refs[1], refs[2], refs[3:]
    else:
        mid_ref, refs = refs[0], refs[1:]
    n2_s, n2t_s, up_s, acc_s, ht_s, back_s, gu_stage, down_stage, gu_sem, down_sem = refs[:10]
    step = pl.program_id(0)
    rows, width = x_ref.shape
    part = min(PART, rows)
    heads, _, cols = att_ref.shape
    blocks = ht_s.shape[0] // CUT
    wide = 2 * CUT
    tall = ht_s.shape[0] // DOWN
    chunks = [pl.ds(a, part) for a in range(0, rows, part)]
    sums = BlockSums(dp, gu_stage, *refs[10:], gu_out) if dp else None

    @pl.when(step == 0)
    def _():
        if dp:
            sums.place.greet()
        gain = (gain_ref[1:2] if dp else gain_ref[...]).astype(F32)
        scale = scale_ref[0, 0]
        for at in chunks:
            mid = x_ref[at].astype(F32)
            for j in range(heads):
                mid = mid + dot_nn(att_ref[j, at], wo_ref[j * cols : (j + 1) * cols])
            mid_ref[at] = mid
            inverse = lax.rsqrt(jnp.mean(mid * mid, axis=-1, keepdims=True) + EPSILON)
            low = (mid * inverse * gain).astype(BF)
            n2_s[at] = low
            if dp:
                gu_stage[0, :, :part] = low.T
                unit = gu_out.shape[0]
                for i, shard in enumerate(sums.order()):
                    there = pl.ds(pl.multiple_of(shard * unit, unit), unit)
                    n2t_s[i * unit : (i + 1) * unit, at] = gu_stage[0, there, :part]
            else:
                n2t_s[:, at] = low.T
            up_s[at] = (cot_ref[at].astype(F32) * scale).astype(BF)
        acc_s[...] = jnp.zeros_like(acc_s)
        nb_ref[...] = jnp.zeros_like(nb_ref)

    def gu_copy(j):
        slot = lax.rem(j, 2)
        return pltpu.make_async_copy(
            gu_stage.at[slot],
            gu_out.at[:, pl.ds(pl.multiple_of(j * wide, wide), wide)],
            gu_sem.at[slot],
        )

    def advance(phases):
        for phase in phases:
            lag = LAGS[phase - 1]
            j = step - lag
            for odd in range(2):

                @pl.when(
                    jnp.logical_and(
                        jnp.logical_and(step >= lag, step < lag + blocks), lax.rem(j, 2) == odd
                    )
                )
                def _(j=j, odd=odd, phase=phase):
                    sums.advance(j, odd, phase)

    @pl.when(step < blocks)
    def _():
        for at in chunks:
            both = dot_nn(n2_s[at], gu_ref[...])
            gate, up = both[:, :CUT], both[:, CUT:]
            back = dot_nt(up_s[at], down_ref[...])
            sig = 0.5 * jnp.tanh(0.5 * gate) + 0.5
            act = gate * sig
            hidden = (act * up).astype(BF)
            ht_s[pl.ds(pl.multiple_of(step * CUT, CUT), CUT), at] = hidden.T
            back_s[at, :CUT] = (back * up * sig * (1.0 + gate * (1.0 - sig))).astype(BF)
            back_s[at, CUT:] = (back * act).astype(BF)
            acc_s[at] += dot_nn(hidden, down_ref[...])
            nb_ref[at] += dot_nt(back_s[at], gu_ref[...])

    if dp:
        advance((4, 3, 2, 1))

    @pl.when(jnp.logical_and(step >= 2, step < blocks))
    def _():
        if dp:
            sums.pair(step - 2).wait_send()
        else:
            gu_copy(step - 2).wait()

    @pl.when(step < blocks)
    def _():
        for a in range(0, width, TALL):
            gu_stage[lax.rem(step, 2), a : a + TALL] = dot_nn(
                n2t_s[a : a + TALL], back_s[...]
            ).astype(BF)
        if dp:
            sums.pair(step).start()
        else:
            gu_copy(step).start()

    def down_copy(p):
        slot = lax.rem(p, 2)
        there = down_out.at[pl.ds(pl.multiple_of(p * tall, tall), tall)]
        return pltpu.make_async_copy(down_stage.at[slot], there, down_sem.at[slot])

    @pl.when(jnp.logical_and(step >= blocks, step < blocks + DOWN))
    def _():
        p = step - blocks

        @pl.when(p == 0)
        def _():
            for at in chunks:
                res_ref[at] = (mid_ref[at] + acc_s[at]).astype(BF)

        @pl.when(p >= 2)
        def _():
            down_copy(p - 2).wait()

        grad = dot_nn(ht_s[pl.ds(pl.multiple_of(p * tall, tall), tall)], up_s[...])
        down_stage[lax.rem(p, 2)] = grad.astype(BF)
        down_copy(p).start()

        @pl.when(p == DOWN - 1)
        def _():
            if dp:
                sums.pair(blocks - 2).wait_send()
                sums.pair(blocks - 1).wait_send()
            else:
                gu_copy(blocks - 2).wait()
                gu_copy(blocks - 1).wait()
            down_copy(p - 1).wait()
            down_copy(p).wait()

    if not dp:
        return
    place = sums.place
    c = place.core
    ends = [
        remote(gu_stage.at[1 - c], heads_out.at[c], far_sem.at[0], far_sem.at[1], place.pair()),
        pltpu.make_async_copy(gu_stage.at[c], heads_out.at[c], out_sem.at[0]),
        pltpu.make_async_copy(n2t_s, og_out, out_sem.at[1]),
    ]
    for q, at in enumerate(chunks):

        @pl.when(step == blocks + DOWN + q)
        def _(q=q, at=at):
            mid, nback, gain = mid_ref[at], nb_ref[at], gain_ref[1:2]
            inverse = lax.rsqrt(jnp.mean(mid * mid, axis=-1, keepdims=True) + EPSILON)
            scaled = nback * gain
            middle_grad = cot_ref[at].astype(F32) * scale_ref[0, 0] + (
                inverse * scaled
                - mid
                * (inverse * inverse * inverse)
                * jnp.mean(scaled * mid, axis=-1, keepdims=True)
            )
            gain_part = jnp.sum(nback * mid * inverse, axis=0, keepdims=True)
            gg_ref[...] = gain_part if q == 0 else gg_ref[...] + gain_part
            nb_ref[at] = middle_grad
            branch = middle_grad.astype(BF)
            n2_s[at] = branch
            for j in range(heads):
                gu_stage[j, at] = dot_nt(branch, wo_ref[j * cols : (j + 1) * cols]).astype(BF)
            if q == len(chunks) - 1:
                ends[0].start()
                ends[1].start()

    @pl.when(step == blocks + DOWN + len(chunks))
    def _():
        for j in range(heads):
            n2t_s[j * cols : (j + 1) * cols] = dot_tn(att_ref[j], n2_s[...]).astype(BF)
        ends[2].start()
        sums.finish([j % 2 for j in range(blocks)])
        for end in ends:
            end.wait()


def feed_forward(dp, scale, x, att, gain, cot, wide, down):
    rows, width = x.shape
    size = down.shape[0]
    blocks, tall = size // CUT, size // DOWN
    once = pl.Buffered(1)

    def whole(w):
        return pl.BlockSpec(w.shape, lambda i: (0,) * len(w.shape), pipeline_mode=once)

    def last(i):
        return jnp.minimum(i, blocks - 1)

    shape = jax.ShapeDtypeStruct
    anywhere = pl.BlockSpec(memory_space=pl.ANY)
    out = [shape((rows, width), BF), shape((rows, width), F32)]
    out_specs = [whole(w) for w in out]
    first, scratch = [], []
    params = {}
    steps = blocks + DOWN
    sem = pltpu.SemaphoreType.DMA
    if dp:
        out += [shape((width // (4 * dp), 2 * size), F32), shape((size, width), BF)]
        out += [shape((1, width), F32), shape(att.shape, BF), shape((width, width), BF)]
        out_specs += [whole(out[2]), anywhere, whole(out[4]), anywhere, anywhere]
        first = [pltpu.VMEM((rows, width), F32), sem((2,)), sem((2,))]
        sems = sem((blocks, dp + 1))
        scratch = [pltpu.VMEM((blocks, width // 2, 2 * CUT), BF)] * 2 + [sems] * 2
        params = {"collective_id": 4, "has_side_effects": True}
        steps += rows // min(PART, rows) + 1
    else:
        out += [shape((width, 2 * size), BF), shape((size, width), BF), shape((rows, width), F32)]
        out_specs += [anywhere, anywhere, whole(out[4])]
    return pl.pallas_call(
        functools.partial(ffn_kernel, dp),
        grid=(steps,),
        in_specs=[
            pl.BlockSpec(memory_space=pltpu.SMEM),
            whole(x),
            whole(att),
            pl.BlockSpec((width, width), lambda i: (0, 0), pipeline_mode=once),
            whole(gain),
            whole(cot),
            pl.BlockSpec((width, 2 * CUT), lambda i: (0, last(i) + width // (2 * CUT))),
            pl.BlockSpec((CUT, width), lambda i: (last(i), 0)),
        ],
        out_specs=out_specs,
        out_shape=out,
        scratch_shapes=[
            *first,
            pltpu.VMEM((rows, width), BF),
            pltpu.VMEM((width, rows), BF),
            pltpu.VMEM((rows, width), BF),
            pltpu.VMEM((rows, width), F32),
            pltpu.VMEM((size, rows), BF),
            pltpu.VMEM((rows, 2 * CUT), BF),
            pltpu.VMEM((2, width, 2 * CUT), BF),
            pltpu.VMEM((2, tall, width), BF),
            pltpu.SemaphoreType.DMA((2,)),
            pltpu.SemaphoreType.DMA((2,)),
            *scratch,
        ],
        compiler_params=pltpu.CompilerParams(vmem_limit_bytes=63 * 2**20, **params),
        cost_estimate=cost(18 * rows * width * size),
    )(scale, x, att, wide, gain, cot, wide, down)


def branch_kernel(scale_ref, mid_ref, nb_ref, cot_ref, att_ref, wo_ref, gain_ref,
                  mg_ref, send_ref, og_ref, gg_ref, branch_s):
    step = pl.program_id(0)
    part, width = mid_ref.shape
    heads, rows, cols = att_ref.shape
    mid, nback, gain = mid_ref[...], nb_ref[...], gain_ref[...].astype(F32)
    inverse = lax.rsqrt(jnp.mean(mid * mid, axis=-1, keepdims=True) + EPSILON)
    scaled = nback * gain
    middle_grad = cot_ref[...].astype(F32) * scale_ref[0, 0] + (
        inverse * scaled
        - mid * (inverse * inverse * inverse) * jnp.mean(scaled * mid, axis=-1, keepdims=True)
    )
    gain_part = jnp.sum(nback * mid * inverse, axis=0, keepdims=True)
    mg_ref[...] = middle_grad
    branch = middle_grad.astype(BF)
    branch_s[pl.ds(pl.multiple_of(step * part, part), part)] = branch
    for j in range(heads):
        send_ref[j] = dot_nt(branch, wo_ref[j * cols : (j + 1) * cols]).astype(BF)

    @pl.when(step == 0)
    def _():
        gg_ref[...] = gain_part

    @pl.when(step > 0)
    def _():
        gg_ref[...] += gain_part

    @pl.when(step == rows // part - 1)
    def _():
        for j in range(heads):
            og_ref[j * cols : (j + 1) * cols] = dot_tn(att_ref[j], branch_s[...]).astype(BF)


def branch_back(scale, mid, nback, cot, att, wo, gain):
    rows, width = mid.shape
    heads, _, cols = att.shape
    part = min(256, rows)
    rowwise = pl.BlockSpec((part, width), lambda i: (i, 0))

    def whole(w):
        return pl.BlockSpec(w.shape, lambda i: (0,) * len(w.shape))

    out = [
        jax.ShapeDtypeStruct((rows, width), F32),
        jax.ShapeDtypeStruct((heads, rows, cols), BF),
        jax.ShapeDtypeStruct((width, width), BF),
        jax.ShapeDtypeStruct((1, width), F32),
    ]
    return pl.pallas_call(
        branch_kernel,
        grid=(rows // part,),
        in_specs=[
            pl.BlockSpec(memory_space=pltpu.SMEM),
            rowwise,
            rowwise,
            rowwise,
            whole(att),
            whole(wo),
            whole(gain),
        ],
        out_specs=[
            rowwise,
            pl.BlockSpec((heads, part, cols), lambda i: (0, i, 0)),
            whole(out[2]),
            whole(out[3]),
        ],
        out_shape=out,
        scratch_shapes=[pltpu.VMEM((rows, width), BF)],
        compiler_params=pltpu.CompilerParams(vmem_limit_bytes=48 * 2**20),
        cost_estimate=cost(4 * rows * width * width),
    )(scale, mid, nback, cot, att, wo, gain)


Q_WAYS = (2, 2, 0)


def closing_kernel(dp, *refs):
    dq_in, dkv_in, hl_in, ex_in, x_in, gain_ref, wq_in, wl_in, mg_in, gg_ref = refs[:10]
    ig_out, q_out, l_out, e_out, g_out = refs[10:15]
    refs = refs[:14] + refs[15:]
    dq, dkv, hl, ex, x, wq, wl, mg = refs[14:22]
    far_dq, far_lat, lat_send, lat_own, e_s, g_s, n1t, flip, ig = refs[22:31]
    q_stage, q_pair, q_ring, e_stage, e_pair, e_ring, g_stage, g_pair, g_ring = refs[31:40]
    load_sem, far_send, far_recv, x_sem = refs[40:44]
    q_send, q_recv, e_send, e_recv, g_send, g_recv = refs[44:]
    place = Place(dp)
    c, s = place.core, place.at["x"]
    rows, width = x.shape
    cols, lat = dq.shape[1], ex.shape[0]
    part = rows // 2
    unit = q_out.shape[0]

    def at(index, size):
        return pl.ds(pl.multiple_of(index * size, size), size)

    loads = [(ex_in, ex), (dkv_in, dkv), (hl_in, hl), (x_in, x), (dq_in.at[c], dq)]
    loads += [(wq_in, wq), (wl_in, wl), (mg_in, mg)]

    def load(i):
        return pltpu.make_async_copy(*loads[i], load_sem.at[i])

    for i in (3, 4, 0, 1, 5, 6, 7, 2):
        load(i).start()
    place.greet()
    far_q = remote(dq_in.at[1 - c], far_dq, far_send.at[0], far_recv.at[0], place.pair())
    far_l = remote(lat_send, far_lat, far_send.at[1], far_recv.at[1], place.pair())
    far_q.start()

    q_sums = BlockSums(dp, q_stage, q_pair, q_ring, q_send, q_recv, q_out, l_out)
    e_sums = BlockSums(dp, e_stage, e_pair, e_ring, e_send, e_recv, e_out)
    g_sums = BlockSums(dp, g_stage, g_pair, g_ring, g_send, g_recv, g_out)
    order = q_sums.order()

    load(3).wait()
    gain = gain_ref[0:1]

    def inverse_of(values):
        return lax.rsqrt(jnp.mean(values * values, axis=-1, keepdims=True) + EPSILON)

    for u in range(2):
        chunk = slice(u * part, (u + 1) * part)
        values = x[chunk].astype(F32)
        flip[...] = (values * inverse_of(values) * gain).astype(BF).T
        for i, shard in enumerate(order):
            n1t[i * unit : (i + 1) * unit, chunk] = flip[at(shard, unit)]
    load(4).wait()
    q_stage[c] = dot_nn(n1t[...], dq[...]).astype(BF)
    load(0).wait()
    load(1).wait()
    for u in range(2):
        lat_send[u * part : (u + 1) * part] = dot_nt(dkv[at(u * 2 + 1 - c, part)], ex[...]).astype(BF)
    far_l.start()
    for u in range(2):
        lat_own[u * part : (u + 1) * part] = dot_nt(dkv[at(u * 2 + c, part)], ex[...]).astype(BF)
    far_q.wait_recv()
    q_stage[1 - c] = dot_nn(n1t[...], far_dq[...]).astype(BF)
    for j in range(2):
        q_sums.pair(j).start()
    for i in (5, 6, 7):
        load(i).wait()
    far_l.wait_recv()

    def back(u):
        chunk = at(u, part)
        normed_back = (
            dot_nt(dq[chunk], wq[:, at(c, cols)])
            + dot_nt(far_dq[chunk], wq[:, at(1 - c, cols)])
            + dot_nt(lat_own[chunk], wl[:, at(c, lat)])
            + dot_nt(far_lat[chunk], wl[:, at(1 - c, lat)])
        )
        values = x[chunk].astype(F32)
        inverse = inverse_of(values)
        scaled = normed_back * gain
        grad = mg[chunk] + (
            inverse * scaled
            - values
            * (inverse * inverse * inverse)
            * jnp.mean(scaled * values, axis=-1, keepdims=True)
        )
        ig[u] = grad.astype(BF)
        return jnp.sum(normed_back * values * inverse, axis=0, keepdims=True)

    gain_part = back(1 - s)
    swap, kept = block_swap(ig, ig_out, x_sem, place)
    swap.start()
    for j in range(2):
        q_sums.advance(j, 2, 1)
    q_stage[2, :, at(c, lat)] = dot_nn(n1t[...], lat_own[...]).astype(BF)
    q_stage[2, :, at(1 - c, lat)] = dot_nn(n1t[...], far_lat[...]).astype(BF)
    q_sums.pair(2).start()
    load(2).wait()
    e_s[...] = dot_tn(hl[...], dkv[...])
    share = e_out.shape[0] // KVH
    for i, shard in enumerate(order):
        piece = e_s[at(shard, share)]
        zero = jnp.zeros_like(piece)
        whole = jnp.concatenate(
            [jnp.where(c == 0, piece, zero), jnp.where(c == 0, zero, piece)], axis=0
        ).astype(BF)
        for j in range(2):
            e_stage[j, i * 2 * share : (i + 1) * 2 * share] = whole[:, j * cols : (j + 1) * cols]
    for j in range(2):
        e_sums.pair(j).start()
    q_sums.advance(2, 0, 1)
    gain_part = gain_part + back(s)
    kept.start()
    g_s[...] = jnp.concatenate(
        [gain_part, gg_ref[...], jnp.zeros((14, width), F32)], axis=0
    ).astype(BF)
    for i, shard in enumerate(order):
        g_stage[0, i * 16 : (i + 1) * 16] = g_s[:, at(lax.div(shard * unit, 128), 128)]
    g_sums.pair(0).start()
    for j in range(2):
        e_sums.advance(j, 2, 1)
    g_sums.advance(0, 2, 1)
    for phase in (2, 3, 4):
        for j in range(3):
            q_sums.advance(j, Q_WAYS[j], phase)
        for j in range(2):
            e_sums.advance(j, 2, phase)
        g_sums.advance(0, 2, phase)
    far_q.wait_send()
    far_l.wait_send()
    for sums, parities in ((q_sums, Q_WAYS), (e_sums, (2, 2)), (g_sums, (2,))):
        for j in range(len(parities)):
            sums.pair(j).wait_send()
        sums.finish(parities)
    swap.wait()
    kept.wait()


def closing(dp, dq, dkv, head_latent, expand, x, gain, wq, wl, mg, gain_two_grad):
    rows, width = x.shape
    cols, lat = dq.shape[2], expand.shape[0]
    unit = width // (4 * dp)
    n = 2 * dp
    anywhere = pl.BlockSpec(memory_space=pl.ANY)
    inside = pl.BlockSpec(memory_space=pltpu.VMEM)
    vmem = pltpu.VMEM
    sem = pltpu.SemaphoreType.DMA
    share = lat // (2 * n) * KVH
    bulk = [((rows, cols), BF), (dkv.shape, BF), (head_latent.shape, BF), (expand.shape, BF)]
    bulk += [(x.shape, BF), (wq.shape, BF), (wl.shape, BF), (mg.shape, F32)]
    sums = []
    for blocks, high, wide in ((3, unit, cols), (2, share, cols), (1, 16, 128)):
        sums += [vmem((blocks, 2 * n * high, wide), BF)] + [vmem((blocks, n * high, wide), BF)] * 2
    return pl.pallas_call(
        functools.partial(closing_kernel, dp),
        in_specs=[anywhere] * 5 + [inside] + [anywhere] * 3 + [inside],
        out_specs=[anywhere] + [inside] * 4,
        out_shape=[
            jax.ShapeDtypeStruct((2, rows // 2, width), BF),
            jax.ShapeDtypeStruct((unit, 2 * cols), F32),
            jax.ShapeDtypeStruct((unit, cols), F32),
            jax.ShapeDtypeStruct((share, 2 * cols), F32),
            jax.ShapeDtypeStruct((16, 128), F32),
        ],
        scratch_shapes=[vmem(*b) for b in bulk]
        + [
            vmem((rows, cols), BF),
            vmem((rows, lat), BF),
            vmem((rows, lat), BF),
            vmem((rows, lat), BF),
            vmem((lat, 2 * cols), F32),
            vmem((16, width), BF),
            vmem((width, rows), BF),
            vmem((width, rows // 2), BF),
            vmem((2, rows // 2, width), BF),
        ]
        + sums
        + [sem((8,)), sem((2,)), sem((2,)), sem((3,))]
        + [sem((blocks, dp + 1)) for blocks in (3, 3, 2, 2, 1, 1)],
        compiler_params=pltpu.CompilerParams(
            collective_id=1, has_side_effects=True, vmem_limit_bytes=60 * 2**20
        ),
    )(dq, dkv, head_latent, expand, x, gain, wq, wl, mg, gain_two_grad)


HEADS = 16
LATD = 256
HG = 8
GROUPS = 8
ALL = ("dp", "seq", "grp")


def norm_parts(values, gain):
    inverse = lax.rsqrt(jnp.mean(values * values, axis=-1, keepdims=True) + EPSILON)
    return (values * inverse * gain, inverse)


def norm_back(values, inverse, gain, upstream):
    scaled = upstream * gain
    gain_grad = jnp.sum(upstream * values * inverse, axis=0)
    input_part = inverse * scaled - values * inverse**3 * jnp.mean(
        scaled * values, axis=-1, keepdims=True
    )
    return (input_part, gain_grad)


def swap_sequences(blocks, count):
    if count == 2:
        me = lax.axis_index("seq")
        sent = lax.ppermute(blocks[1 - me], "seq", [(0, 1), (1, 0)])
        kept = blocks[me]
        first = me == 0
        return jnp.stack([jnp.where(first, kept, sent), jnp.where(first, sent, kept)])
    return lax.all_to_all(blocks, "seq", 0, 0, tiled=True)


def swap_group(blocks):
    return lax.all_to_all(blocks, "grp", 0, 0, tiled=True)


def local(
    inputs,
    cotangent,
    group_ids,
    group_scale,
    norm_gain,
    w_query,
    w_latent,
    expansion_weight,
    w_output,
    ffn_gain,
    w_gate,
    w_up,
    w_down,
):
    devices = lax.axis_size("dp") * lax.axis_size("seq") * lax.axis_size("grp")
    groups = lax.axis_size("grp")
    me = lax.axis_index("grp")
    seqs, rows, width = inputs.shape
    count = seqs * rows
    hidden_size = w_gate.shape[1]
    heads = HEADS // groups
    cols = heads * DH
    drows = width // devices

    dp = lax.axis_size("dp")
    ring = groups == 2 and seqs == 2 and dp % 2 == 0
    expand_rows = expansion_weight.reshape(-1, expansion_weight.shape[2])
    shard = (lax.axis_index("dp") * seqs + lax.axis_index("seq")) * groups + me
    both_gains = jnp.stack([norm_gain, ffn_gain])
    gains = lax.dynamic_update_slice(jnp.zeros((16, 128), BF), both_gains, (0, shard * drows % 128))
    if ring:
        shards = (w_query, w_latent, expand_rows, gains)
        full, own_inputs = own_gather(dp, shards, inputs, ("xzy",) * 4)
    else:
        shards = (w_query, w_latent, expand_rows)
        full = [lax.all_gather(w, ALL, axis=0) for w in shards]
        own_inputs = swap_sequences(inputs, seqs)
    gate_up = jnp.stack(
        [w_gate.reshape(drows, -1, CUT), w_up.reshape(drows, -1, CUT)], axis=2
    ).reshape(drows, -1)
    wide_full = lax.all_gather(
        jnp.concatenate([w_output, gate_up], axis=1), ALL, axis=0, tiled=True
    )
    query_full = full[0].reshape(width, -1)
    latent_full = full[1].reshape(width, -1)
    expand_full = full[2].reshape(devices, KVH, LATD // devices, -1)
    if ring:
        half = width // 2
        (
            logsum,
            gain_rows,
            attended,
            token_attended,
            head_queries,
            head_pairs,
            head_latent,
            expand_local,
            own_cotangent,
            down_full,
        ) = attention_forward_gather(
            dp,
            own_inputs.reshape(count, width),
            full[3],
            query_full,
            latent_full,
            full[2],
            cotangent,
            (w_down,),
            ((0, 0, half), (0, half, half)),
            ("xzy", "zxy"),
        )
        down_full = down_full.reshape(-1, width)
        gain_one = gain_two = gain_rows
    else:
        gain_one, gain_two = [
            lax.all_gather(w, ALL, axis=0, tiled=True).reshape(1, width) for w in (norm_gain, ffn_gain)
        ]
        expand_local = lax.dynamic_slice(
            expand_full,
            (0, me * heads // HG, 0, me * heads % HG * 2 * DH),
            (devices, 1, LATD // devices, heads * 2 * DH),
        ).reshape(LATD, -1)
        token_rows = own_inputs.astype(F32).reshape(count, width)
        normed, inverse_one = norm_parts(token_rows, gain_one)
        normed_low = normed.astype(BF)
        query_send = jnp.stack(
            [dot_nn(normed_low, query_full[:, j * cols : (j + 1) * cols]).astype(BF) for j in range(groups)]
        ).reshape(groups, seqs, rows, cols)
        latent_state = [
            dot_nn(normed_low, latent_full[:, g * LATD : (g + 1) * LATD]).astype(BF) for g in range(KVH)
        ]
        latent_send = jnp.stack([latent_state[j * heads // HG] for j in range(groups)]).reshape(
            groups, seqs, rows, LATD
        )
        head_queries = swap_group(query_send)
        head_latent = swap_group(latent_send).transpose(1, 0, 2, 3).reshape(-1, LATD)
        head_pairs = dot_nn(head_latent, expand_local).astype(BF)
        attended, logsum = attention_forward(head_queries, head_pairs)
        token_attended = swap_group(attended)
        own_cotangent = swap_sequences(cotangent, seqs)
        down_full = lax.all_gather(w_down, ALL, axis=0, tiled=True)
    token_attended = token_attended.reshape(groups, count, cols)
    seq_group = lax.dynamic_index_in_dim(group_ids, lax.axis_index("seq"), 0, keepdims=False)
    chosen = (seq_group == jnp.arange(GROUPS)).astype(F32)
    seq_scale = jnp.sum(chosen * group_scale).reshape(1, 1)
    x_rows = own_inputs.reshape(count, width)
    cot_rows = own_cotangent.reshape(count, width)
    result, normed_two_back, gu_share, down_grad, *rest = feed_forward(
        dp if ring else None,
        seq_scale,
        x_rows,
        token_attended,
        gain_two,
        cot_rows,
        wide_full,
        down_full,
    )
    own_output = result.reshape(seqs, rows, width)
    if ring:
        middle_grad = normed_two_back
        gain_two_grad, head_upstream, output_grad = rest
        head_upstream = head_upstream.reshape(groups, seqs, rows, cols)
    else:
        gu_share = lax.psum_scatter(gu_share, ALL, scatter_dimension=0, tiled=True).astype(F32)
        middle_grad, back_send, output_grad, gain_two_grad = branch_back(
            seq_scale, *rest, normed_two_back, cot_rows, token_attended, wide_full[:, :width], gain_two
        )
        head_upstream = swap_group(back_send.reshape(groups, seqs, rows, cols))
    gu_share = gu_share.reshape(drows, -1, 2, CUT)
    terms = (output_grad.reshape(devices, drows, width), down_grad.reshape(devices, -1, width))
    attention = (head_queries, head_pairs, head_upstream, attended, logsum)
    if ring:
        half = width // 2
        query_back, pair_back, output, output_share, down_share = attention_backward_scatter(
            dp,
            *attention,
            own_output,
            terms,
            ((0, 0, width), (1, 0, half), (1, half, half)),
            ("yzx", "yxz", "yzx"),
        )
    else:
        query_back, pair_back = attention_backward(*attention)
        output = swap_sequences(own_output, seqs)
        output_share, down_share = [
            lax.psum_scatter(w, ALL, scatter_dimension=0, tiled=True)[0].astype(F32) for w in terms
        ]
    if ring:
        input_grad, q_share, l_share, e_share, g_share = closing(
            dp,
            query_back.reshape(groups, count, cols),
            pair_back,
            head_latent,
            expand_local,
            x_rows,
            gain_one,
            query_full,
            latent_full,
            middle_grad,
            gain_two_grad,
        )
        own_gains = lax.dynamic_slice(g_share, (0, shard * drows % 128), (2, drows))
        sums = (q_share, l_share, e_share)
    else:
        latent_terms = dot_nt(pair_back, expand_local).astype(BF)
        expand_part = dot_tn(head_latent, pair_back)
        expand_grad = lax.dynamic_update_slice(
            jnp.zeros(expand_full.shape, BF),
            expand_part.astype(BF).reshape(devices, 1, LATD // devices, -1),
            (0, me * heads // HG, 0, me * heads % HG * 2 * DH),
        )
        query_token = swap_group(query_back).reshape(groups, count, cols)
        latent_token = swap_group(
            latent_terms.reshape(seqs, groups, rows, LATD).transpose(1, 0, 2, 3)
        ).reshape(KVH, groups // KVH, count, LATD)
        latent_token = jnp.sum(latent_token.astype(F32), axis=1).astype(BF)
        query_grad = jnp.concatenate([dot_tn(normed_low, query_token[j]) for j in range(groups)], axis=1)
        latent_grad = jnp.concatenate([dot_tn(normed_low, latent_token[g]) for g in range(KVH)], axis=1)
        normed_back = sum(
            dot_nt(query_token[j], query_full[:, j * cols : (j + 1) * cols]) for j in range(groups)
        ) + sum(
            dot_nt(latent_token[g], latent_full[:, g * LATD : (g + 1) * LATD]) for g in range(KVH)
        )
        input_part, gain_one_grad = norm_back(token_rows, inverse_one, gain_one, normed_back)
        own_input_grad = (middle_grad + input_part).astype(BF).reshape(seqs, rows, width)
        gain_grads = jnp.concatenate(
            [gain_one_grad.reshape(devices, 1, drows), gain_two_grad.reshape(devices, 1, drows)], axis=2
        ).astype(BF)
        gain_grads = jnp.pad(gain_grads, ((0, 0), (0, 15), (0, 128 - 2 * drows)))
        terms = (
            query_grad.astype(BF).reshape(devices, drows, -1),
            latent_grad.astype(BF).reshape(devices, drows, -1),
            expand_grad.reshape(devices, -1, expand_grad.shape[3]),
            gain_grads,
        )
        sums = [
            lax.psum_scatter(w, ALL, scatter_dimension=0, tiled=True)[0].astype(F32) for w in terms
        ]
        own_gains = sums[3][0, : 2 * drows].reshape(2, drows)
        input_grad = swap_sequences(own_input_grad, seqs)
    return (
        output,
        input_grad,
        own_gains[0],
        sums[0],
        sums[1],
        sums[2].reshape(expansion_weight.shape),
        output_share,
        own_gains[1],
        gu_share[:, :, 0].reshape(drows, -1),
        gu_share[:, :, 1].reshape(drows, -1),
        down_share,
    )


def solution(mesh):
    def run(*arrays):
        dp, sp = mesh.shape["dp"], mesh.shape["sp"]
        seqs = arrays[0].shape[0] // dp
        grid = Mesh(mesh.devices.reshape(dp, seqs, sp // seqs), ALL)
        tokens = P("dp", ("seq", "grp"), None)
        matrix = P(ALL, None)
        expand = P(None, ALL, None)
        return jax.shard_map(
            local,
            mesh=grid,
            in_specs=(
                tokens,
                tokens,
                P("dp"),
                P(),
                P(ALL),
                matrix,
                matrix,
                expand,
                matrix,
                P(ALL),
                matrix,
                matrix,
                matrix,
            ),
            out_specs=(
                tokens,
                tokens,
                P(ALL),
                matrix,
                matrix,
                expand,
                matrix,
                P(ALL),
                matrix,
                matrix,
                matrix,
            ),
            check_vma=False,
        )(*arrays)

    return run
```

```python
import functools
import jax
import jax.numpy as jnp
from jax import lax
from jax.sharding import Mesh
from jax.sharding import PartitionSpec as P
from jax.experimental import pallas as pl
from jax.experimental.pallas import tpu as pltpu

DH = 64
KVH = 2
EPSILON = 1e-05
F32 = jnp.float32
BF = jnp.bfloat16


def cost(flops):
    return pl.CostEstimate(flops=flops, bytes_accessed=2**23, transcendentals=0)


MESH = pl.DeviceIdType.MESH


class Place:

    def __init__(self, dp):
        self.sizes = {"x": 2, "y": 2, "z": dp // 2}
        d = lax.axis_index("dp")
        self.at = {"x": lax.axis_index("seq"), "y": lax.rem(d, 2), "z": lax.div(d, 2)}
        self.core = lax.axis_index("grp")

    def coords(self, offset):
        at = {k: lax.rem(self.at[k] + o, self.sizes[k]) if o else self.at[k] for k, o in offset.items()}
        return at["z"] * 2 + at["y"], at["x"]

    def index(self, offset, other):
        d, s = self.coords(offset)
        core = 1 - self.core if other else self.core
        return (d * 2 + s) * 2 + core

    def device(self, offset):
        return (*self.coords(offset), self.core)

    def pair(self):
        return (*self.coords({"x": 0, "y": 0, "z": 0}), 1 - self.core)

    def greet(self):
        there = [self.pair()]
        for k in "xyz":
            for o in range(1, self.sizes[k]):
                there.append(self.device({"x": 0, "y": 0, "z": 0, k: o}))
        barrier = pltpu.get_barrier_semaphore()
        for device in there:
            pl.semaphore_signal(barrier, inc=1, device_id=device, device_id_type=MESH)
        pl.semaphore_wait(barrier, len(there))


def offsets_of(order, dp):
    sizes = {"x": 2, "y": 2, "z": dp // 2}
    a, b, c = (sizes[k] for k in order)
    return [(i, j, k) for i in range(a) for j in range(b) for k in range(c)]


def named(order, steps):
    return dict(zip(order, steps))


def remote(src, dst, send, recv, there):
    return pltpu.make_async_remote_copy(
        src_ref=src, dst_ref=dst, send_sem=send, recv_sem=recv, device_id=there, device_id_type=MESH
    )


class Gather:

    def __init__(self, place, dp, order, src, out, sems, number):
        self.place, self.order, self.src, self.out = place, order, src, out
        self.steps = offsets_of(order, dp)
        self.sems, self.number = sems, number

    def slot(self, steps, other=False):
        return self.out(self.place.index(named(self.order, steps), other))

    def source(self, steps):
        last = max(i for i in range(3) if steps[i])
        return tuple(0 if i == last else o for i, o in enumerate(steps))

    def hop(self, steps):
        last = max(i for i in range(3) if steps[i])
        source = self.source(steps)
        size = self.place.sizes[self.order[last]]
        back = tuple(size - o if i == last else 0 for i, o in enumerate(steps))
        number = self.steps.index(steps)
        here = self.slot(source)
        src = here if any(source) else self.src
        return remote(
            src,
            here,
            self.sems[0].at[self.number, number],
            self.sems[1].at[self.number, number],
            self.place.device(named(self.order, back)),
        )

    def across(self, steps):
        number = self.steps.index(steps)
        src = self.slot(steps) if any(steps) else self.src
        return remote(
            src,
            self.slot(steps),
            self.sems[2].at[self.number, number],
            self.sems[3].at[self.number, number],
            self.place.pair(),
        )

    def keep(self):
        return pltpu.make_async_copy(self.src, self.slot((0, 0, 0)), self.sems[4].at[self.number])

    def send_from(self, source):
        for steps in self.steps:
            if any(steps) and self.source(steps) == source:
                self.hop(steps).start()
        self.across(source).start()

    def start(self):
        self.send_from((0, 0, 0))
        self.keep().start()

    def arrivals(self):
        return sorted((s for s in self.steps if any(s)), key=lambda s: [o > 0 for o in s][::-1])

    def forward(self, steps):
        number = self.steps.index(steps)
        here = self.slot(steps)
        remote(
            here,
            here,
            self.sems[0].at[self.number, number],
            self.sems[1].at[self.number, number],
            self.place.pair(),
        ).wait_recv()
        self.send_from(steps)

    def finish(self):
        for steps in self.steps:
            number = self.steps.index(steps)
            here = self.slot(steps, True)
            remote(
                here,
                here,
                self.sems[2].at[self.number, number],
                self.sems[3].at[self.number, number],
                self.place.pair(),
            ).wait_recv()
            self.across(steps).wait_send()
            if any(steps):
                self.hop(steps).wait_send()
        self.keep().wait()


class Scatter:

    def __init__(self, place, dp, order, term, pair_buf, ring_buf, sems, number, own=None):
        self.place, self.order, self.term = place, order, term
        self.own_buf, self.own_sem = own if own else (None, None)
        self.steps = offsets_of(order, dp)
        self.pair_buf, self.ring_buf = pair_buf, ring_buf
        self.sems, self.number = sems, number

    def turn(self):
        def key(steps):
            first = next((i for i in range(3) if steps[i]), 3)
            return (first, [o == 0 for o in steps])

        return sorted(self.steps, key=key)

    def across(self, steps):
        number = self.steps.index(steps)
        return remote(
            self.term(self.place.index(named(self.order, steps), True)),
            self.pair_buf.at[number],
            self.sems[2].at[self.number, number],
            self.sems[3].at[self.number, number],
            self.place.pair(),
        )

    def fetch(self, steps):
        number = self.steps.index(steps)
        return pltpu.make_async_copy(
            self.term(self.place.index(named(self.order, steps), False)),
            self.own_buf.at[number],
            self.own_sem.at[self.number, number],
        )

    def start(self):
        for steps in self.turn():
            self.across(steps).start()
            if self.own_buf is not None:
                self.fetch(steps).start()

    def hop(self, steps):
        first = min(i for i in range(3) if steps[i])
        there = tuple(o if i == first else 0 for i, o in enumerate(steps))
        number = self.steps.index(steps)
        return remote(
            self.pair_buf.at[number],
            self.ring_buf.at[number],
            self.sems[0].at[self.number, number],
            self.sems[1].at[self.number, number],
            self.place.device(named(self.order, there)),
        )

    def add(self, steps, out=None):
        number = self.steps.index(steps)
        self.across(steps).wait_recv()
        if self.own_buf is None:
            mine = self.term(self.place.index(named(self.order, steps), False))
        else:
            self.fetch(steps).wait()
            mine = self.own_buf.at[number]
        total = mine[...].astype(F32) + self.pair_buf[number].astype(F32)
        for came in self.steps:
            if not any(came):
                continue
            first = min(i for i in range(3) if came[i])
            if tuple(0 if i == first else o for i, o in enumerate(came)) == steps:
                self.hop(came).wait_recv()
                total = total + self.ring_buf[self.steps.index(came)].astype(F32)
        if out is None:
            self.pair_buf[number] = total.astype(BF)
            self.hop(steps).start()
        else:
            out[...] = total

    def finish(self):
        for steps in self.steps:
            self.across(steps).wait_send()
            if any(steps):
                self.hop(steps).wait_send()


def block_swap(x_in, x_out, sem, place):
    s = place.at["x"]
    away = remote(
        x_in.at[1 - s], x_out.at[s], sem.at[0], sem.at[1], place.device({"x": 1, "y": 0, "z": 0})
    )
    return away, pltpu.make_async_copy(x_in.at[s], x_out.at[s], sem.at[2])


def gather_kernel(dp, orders, *refs):
    count = len(orders)
    srcs, x_in = refs[:count], refs[count]
    outs, x_out = refs[count + 1 : 2 * count + 1], refs[2 * count + 1]
    sems, x_sem = refs[2 * count + 2 : -1], refs[-1]
    place = Place(dp)
    place.greet()
    works = [
        Gather(place, dp, orders[a], srcs[a], lambda at, a=a: outs[a].at[at], sems, a)
        for a in range(count)
    ]
    for work in works:
        work.start()
    swap, kept = block_swap(x_in, x_out, x_sem, place)
    swap.start()
    kept.start()
    for i in range(2 * dp - 1):
        for work in works:
            work.forward(work.arrivals()[i])
    for work in works:
        work.finish()
    swap.wait()
    kept.wait()


def gather_sems(dp, count):
    sem = pltpu.SemaphoreType.DMA
    return [sem((count, 2 * dp))] * 4 + [sem((count,))]


def own_gather(dp, shards, blocks, orders):
    count = len(shards)
    anywhere = pl.BlockSpec(memory_space=pl.ANY)
    out = pl.pallas_call(
        functools.partial(gather_kernel, dp, orders),
        in_specs=[anywhere] * (count + 1),
        out_specs=[anywhere] * (count + 1),
        out_shape=[jax.ShapeDtypeStruct((4 * dp, *w.shape), w.dtype) for w in shards]
        + [jax.ShapeDtypeStruct(blocks.shape, blocks.dtype)],
        scratch_shapes=gather_sems(dp, count) + [pltpu.SemaphoreType.DMA((3,))],
        compiler_params=pltpu.CompilerParams(collective_id=0, has_side_effects=True),
    )(*shards, blocks)
    return out[:-1], out[-1]


def scatter_sems(dp, count):
    return [pltpu.SemaphoreType.DMA((count, 2 * dp))] * 4


def run_at(plan, point, when=None):
    for step, at in sorted((k for k in plan if k[0] != "last"), key=str):
        if at != (point if when is None else when):
            continue
        tasks = plan[step, at]

        @pl.when(pl.program_id(0) == step)
        def _(tasks=tasks):
            for task in tasks:
                task()


GATHER_AT = (0, 2, 3, 4, 5, 6, 7, 9, 10, 11, 12, 13, 14, 15, 15)
SCATTER_AT = (1, 1, 1, 1, 2, 2, 2, 2, 6, 7, 8, 9, 10, 11, 13, 16)


def put(plan, number, count, table, steps, points, task):
    at = table[number * len(table) // count] * steps * points // 16
    key = ("last", 0) if at >= steps * points else divmod(at, points)
    plan.setdefault(key, []).append(task)


def gather_plan(place, works, swap, steps, points):
    arrivals = [work.arrivals() for work in works]

    def begin():
        place.greet()
        for work in works:
            work.start()
        for copy in swap:
            copy.start()

    def forward(i):
        for work, order in zip(works, arrivals):
            work.forward(order[i])

    def end():
        for work in works:
            work.finish()
        for copy in swap:
            copy.wait()

    plan = {(0, "first"): [begin]}
    for i in range(len(arrivals[0])):
        put(plan, i, len(arrivals[0]), GATHER_AT, steps, points, functools.partial(forward, i))
    plan.setdefault(("last", 0), []).append(end)
    return plan


def scatter_plan(place, works, outs, swap, steps, points):
    turns = [work.turn() for work in works]
    count = len(turns[0])

    def begin():
        place.greet()
        for work in works:
            work.start()
        for copy in swap:
            copy.start()

    def add(i):
        for work, order, out in zip(works, turns, outs):
            work.add(order[i], out if i == count - 1 else None)

    def end():
        for work in works:
            work.finish()
        for copy in swap:
            copy.wait()

    plan = {(0, 0): [begin]}
    for i in range(count):
        put(plan, i, count, SCATTER_AT, steps, points, functools.partial(add, i))
    plan.setdefault(("last", 0), []).append(end)
    return plan


def dot_nt(a, b):
    return lax.dot_general(a, b, (((1,), (1,)), ((), ())), preferred_element_type=F32)


def dot_nn(a, b):
    return lax.dot_general(a, b, (((1,), (0,)), ((), ())), preferred_element_type=F32)


def dot_tn(a, b):
    return lax.dot_general(a, b, (((0,), (0,)), ((), ())), preferred_element_type=F32)


def causal(s, first_key, first_query):
    keys = first_key + lax.broadcasted_iota(jnp.int32, s.shape, 0)
    rows = first_query + lax.broadcasted_iota(jnp.int32, s.shape, 1)
    return jnp.where(rows >= keys, s, -1e30)


def forward_body(q_ref, kv_ref, o_ref, lse_ref, vt_s, point=lambda i: None):
    groups, chunks, rows, _ = q_ref.shape
    seq = kv_ref.shape[0]
    for h in range(2):
        vt_s[h] = kv_ref[:, h * 128 : (h + 1) * 128].astype(F32).T[DH:].astype(BF)
    for i in range(groups * chunks):
        point(i)
        q = q_ref[i % groups, i // groups].astype(F32) * 0.125
        outs = []
        for h in range(2):
            qh = q[:, h * DH : (h + 1) * DH]
            qp = jnp.concatenate([qh, jnp.zeros_like(qh)], axis=1).astype(BF)
            width = (i + 1) * rows
            s = dot_nt(kv_ref[0:width, h * 128 : (h + 1) * 128], qp)
            tail = causal(s[i * rows :], 0, 0)
            if i > 0:
                head = s[: i * rows]
                top = jnp.maximum(
                    jnp.max(head, axis=0, keepdims=True), jnp.max(tail, axis=0, keepdims=True)
                )
                ph = jnp.exp(head - top)
                pt = jnp.exp(tail - top)
                total = jnp.sum(ph, axis=0, keepdims=True) + jnp.sum(pt, axis=0, keepdims=True)
                o = dot_nn(vt_s[h, :, 0 : i * rows], ph.astype(BF)) + dot_nn(
                    vt_s[h, :, i * rows : width], pt.astype(BF)
                )
            else:
                top = jnp.max(tail, axis=0, keepdims=True)
                pt = jnp.exp(tail - top)
                total = jnp.sum(pt, axis=0, keepdims=True)
                o = dot_nn(vt_s[h, :, 0:width], pt.astype(BF))
            outs.append(o / total)
            lse_ref[h, i * rows : (i + 1) * rows] = (top + jnp.log(total))[0]
        o_ref[i % groups, i // groups] = jnp.concatenate(outs, axis=0).T.astype(BF)


def forward_kernel(q_ref, kv_ref, o_ref, lse_ref, vt_s):
    forward_body(q_ref, kv_ref, o_ref, lse_ref, vt_s)


def forward_gather_kernel(dp, cuts, orders, pairs, *refs):
    x_ref, tiles_ref, wq_ref, wl_ref, shards_ref, x_in = refs[:6]
    sources = 1 + max(cut[0] for cut in cuts)
    srcs, refs = refs[6 : 6 + sources], refs[6 + sources :]
    lse_ref, gain_ref, o_out, token_out, q_out, kv_out, hl_out, ex_out, x_out = refs[:9]
    outs, refs = refs[9 : 9 + sources], refs[9 + sources :]
    vt_s, x_sem, low_s, q_send, lat_send, q_s, kv_s, hl_s, o_s, ex_s = refs[:10]
    far_send, far_recv, save_sem = refs[10:13]
    sems = refs[13:]
    place = Place(dp)
    c = place.core
    works = []
    for number, (a, first, size) in enumerate(cuts):
        cut = pl.ds(first, size)
        works.append(
            Gather(
                place,
                dp,
                orders[number],
                srcs[a].at[:, cut],
                lambda at, a=a, cut=cut: outs[a].at[at, :, cut],
                sems,
                number,
            )
        )
    groups, chunks, rows, cols = q_s.shape
    lat = hl_s.shape[1]
    points = groups * chunks
    plan = gather_plan(place, works, block_swap(x_in, x_out, x_sem, place), pairs, points)
    run_at(plan, 0, "first")

    def at(index, size):
        return pl.ds(pl.multiple_of(index * size, size), size)

    def far_q():
        return remote(q_send, q_s.at[c], far_send.at[0], far_recv.at[0], place.pair())

    def far_l(u):
        return remote(
            lat_send.at[u],
            hl_s.at[at(u * groups + c, rows)],
            far_send.at[1 + u],
            far_recv.at[1 + u],
            place.pair(),
        )

    def saves():
        return [
            pltpu.make_async_copy(src, dst, save_sem.at[i])
            for i, (src, dst) in enumerate(
                ((q_s, q_out), (kv_s, kv_out), (hl_s, hl_out), (ex_s, ex_out))
            )
        ]

    def hand_over():
        return [
            remote(o_s.at[1 - c], token_out.at[c], far_send.at[3], far_recv.at[3], place.pair()),
            pltpu.make_async_copy(o_s.at[c], token_out.at[c], save_sem.at[4]),
            pltpu.make_async_copy(o_s, o_out, save_sem.at[5]),
        ]

    @pl.when(pl.program_id(0) == 0)
    def _():
        count = 128 * tiles_ref.shape[0] // gain_ref.shape[1]
        for t in range(gain_ref.shape[1] // 128):
            total = tiles_ref[t * count].astype(F32)
            for i in range(1, count):
                total = total + tiles_ref[t * count + i].astype(F32)
            gain_ref[:, t * 128 : (t + 1) * 128] = total[:8]
        share = shards_ref.shape[1] // KVH
        for i in range(0, shards_ref.shape[0], KVH):
            pieces = []
            for k in range(KVH):
                both = shards_ref[i + k].astype(F32)
                pieces.append(jnp.where(c == 0, both[:share], both[share:]))
            ex_s[i * share : (i + KVH) * share] = jnp.concatenate(pieces, axis=0).astype(BF)
        gain = gain_ref[0:1]
        for u in range(chunks):
            chunk = slice(u * rows, (u + 1) * rows)
            values = x_ref[chunk].astype(F32)
            inverse = lax.rsqrt(jnp.mean(values * values, axis=-1, keepdims=True) + EPSILON)
            low_s[chunk] = (values * inverse * gain).astype(BF)
            lat_send[u] = dot_nn(low_s[chunk], wl_ref[:, at(1 - c, lat)]).astype(BF)
            far_l(u).start()
        for u in range(chunks):
            chunk = slice(u * rows, (u + 1) * rows)
            q_send[u] = dot_nn(low_s[chunk], wq_ref[:, at(1 - c, cols)]).astype(BF)
        far_q().start()
        for u in range(chunks):
            chunk = slice(u * rows, (u + 1) * rows)
            hl_s[at(u * groups + c, rows)] = dot_nn(low_s[chunk], wl_ref[:, at(c, lat)]).astype(BF)
            q_s[c, u] = dot_nn(low_s[chunk], wq_ref[:, at(c, cols)]).astype(BF)
        for u in range(chunks):
            far_l(u).wait_recv()
        for k in range(groups * chunks):
            chunk = slice(k * rows, (k + 1) * rows)
            kv_s[chunk] = dot_nn(hl_s[chunk], ex_s[...]).astype(BF)
        far_q().wait_recv()
        for save in saves():
            save.start()

    pid = pl.program_id(0)
    forward_body(
        q_s.at[:, :, :, at(pid, 128)],
        kv_s.at[:, at(pid, 256)],
        o_s.at[:, :, :, at(pid, 128)],
        lse_ref,
        vt_s,
        lambda i: run_at(plan, i),
    )

    @pl.when(pid == pairs - 1)
    def _():
        for copy in hand_over():
            copy.start()
        far_q().wait_send()
        for u in range(chunks):
            far_l(u).wait_send()
        for copy in saves() + hand_over():
            copy.wait()
        for task in plan["last", 0]:
            task()


def forward_specs(q, kv):
    groups, chunks, rows, cols = q.shape
    seq = kv.shape[0]
    pairs = cols // 128
    tok = pl.BlockSpec((groups, chunks, rows, 128), lambda p: (0, 0, 0, p))
    ins = [tok, pl.BlockSpec((seq, 256), lambda p: (0, p))]
    outs = [tok, pl.BlockSpec((None, 2, seq), lambda p: (p, 0, 0))]
    shapes = [jax.ShapeDtypeStruct(q.shape, BF), jax.ShapeDtypeStruct((pairs, 2, seq), F32)]
    scratch = [pltpu.VMEM((2, DH, seq), BF)]
    return pairs, ins, outs, shapes, scratch, cost(8 * pairs * seq * seq * 128)


def attention_forward(q, kv):
    pairs, ins, outs, shapes, scratch, estimate = forward_specs(q, kv)
    return pl.pallas_call(
        forward_kernel,
        grid=(pairs,),
        in_specs=ins,
        out_specs=outs,
        out_shape=shapes,
        scratch_shapes=scratch,
        compiler_params=pltpu.CompilerParams(vmem_limit_bytes=56 * 2**20),
        cost_estimate=estimate,
    )(q, kv)


def attention_forward_gather(dp, x, tiles, wq, wl, expand, blocks, shards, cuts, orders):
    rows, width = blocks.shape[1], x.shape[1]
    cols, lat = width // 2, expand.shape[0] * expand.shape[1] // KVH
    seq = 4 * rows
    q = jax.ShapeDtypeStruct((2, 2, rows, cols), BF)
    kv = jax.ShapeDtypeStruct((seq, 2 * cols), BF)
    hl = jax.ShapeDtypeStruct((seq, lat), BF)
    ex = jax.ShapeDtypeStruct((lat, 2 * cols), BF)
    gains = jax.ShapeDtypeStruct((8, width), F32)
    pairs, _, outs, shapes, scratch, estimate = forward_specs(q, kv)
    anywhere = pl.BlockSpec(memory_space=pl.ANY)
    count = len(shards)
    sem = pltpu.SemaphoreType.DMA

    def whole(w):
        return pl.BlockSpec(w.shape, lambda p: (0,) * len(w.shape), pipeline_mode=pl.Buffered(1))

    return pl.pallas_call(
        functools.partial(forward_gather_kernel, dp, cuts, orders, pairs),
        grid=(pairs,),
        in_specs=[whole(w) for w in (x, tiles, wq, wl, expand)] + [anywhere] * (1 + count),
        out_specs=outs[1:] + [whole(gains)] + [anywhere] * (7 + count),
        out_shape=shapes[1:]
        + [gains, q, q, q, kv, hl, ex]
        + [jax.ShapeDtypeStruct(blocks.shape, blocks.dtype)]
        + [jax.ShapeDtypeStruct((4 * dp, *w.shape), w.dtype) for w in shards],
        scratch_shapes=scratch
        + [
            sem((3,)),
            pltpu.VMEM(x.shape, BF),
            pltpu.VMEM((2, rows, cols), BF),
            pltpu.VMEM((2, rows, lat), BF),
            pltpu.VMEM(q.shape, BF),
            pltpu.VMEM(kv.shape, BF),
            pltpu.VMEM(hl.shape, BF),
            pltpu.VMEM(q.shape, BF),
            pltpu.VMEM(ex.shape, BF),
            sem((4,)),
            sem((4,)),
            sem((6,)),
        ]
        + gather_sems(dp, len(cuts)),
        compiler_params=pltpu.CompilerParams(
            vmem_limit_bytes=60 * 2**20, collective_id=2, has_side_effects=True
        ),
        cost_estimate=estimate,
    )(x, tiles, wq, wl, expand, blocks, *shards)


def backward_body(blk, q_ref, kv_ref, do_ref, o_ref, lse_ref, dq_ref, dkv_ref,
                  kt_s, acc_s, dqt_s, qp_s, dop_s, delta_s, point=lambda i: None):
    groups, chunks, rows, _ = q_ref.shape
    seq = kv_ref.shape[0]
    n = groups * chunks
    for h in range(2):
        kt_s[h] = kv_ref[:, h * 128 : (h + 1) * 128].astype(F32).T[:DH].astype(BF)
    acc_s[...] = jnp.zeros_like(acc_s)
    for i in range(n):
        at = pl.ds(i * rows, rows)
        q = q_ref[i % groups, i // groups].astype(F32) * 0.125
        do = do_ref[i % groups, i // groups].astype(F32)
        o = o_ref[i % groups, i // groups].astype(F32)
        prod = (do * o).T
        zero = jnp.zeros((rows, DH), F32)
        for h in range(2):
            cut = slice(h * DH, (h + 1) * DH)
            qp_s[h, at] = jnp.concatenate([q[:, cut], zero], axis=1).astype(BF)
            dop_s[h, at] = jnp.concatenate([zero, do[:, cut]], axis=1).astype(BF)
            delta_s[h, at] = jnp.sum(prod[cut], axis=0)

    def block(i, j, masked):
        qat = pl.ds(i * blk, blk)
        kat = pl.ds(pl.multiple_of(j * blk, blk), blk)
        for h in range(2):
            kv = kv_ref[kat, h * 128 : (h + 1) * 128]
            qp = qp_s[h, qat]
            dop = dop_s[h, qat]
            s = dot_nt(kv, qp)
            dp = dot_nt(kv, dop)
            if masked:
                s = causal(s, 0, 0)
            p = jnp.exp(s - lse_ref[h : h + 1, qat])
            ds = (p * (dp - delta_s[h : h + 1, qat])).astype(BF)
            acc_s[h, kat] += dot_nn(p.astype(BF), dop) + dot_nn(ds, qp)
            part = dot_nn(kt_s[h, :, kat], ds)
            if masked:
                dqt_s[h * DH : (h + 1) * DH, qat] = part
            else:
                dqt_s[h * DH : (h + 1) * DH, qat] += part

    m = seq // blk

    for i in range(m):
        point(i)
        block(i, i, True)

        def inner(j, _, i=i):
            block(i, j, False)
            return 0

        lax.fori_loop(0, i, inner, 0)
    for i in range(n):
        at = pl.ds(i * rows, rows)
        dq_ref[i % groups, i // groups] = (dqt_s[:, at].T * 0.125).astype(BF)
    for h in range(2):
        dkv_ref[:, h * 128 : (h + 1) * 128] = acc_s[h].astype(BF)


def backward_kernel(blk, *refs):
    backward_body(blk, *refs)


def backward_scatter_kernel(dp, blk, cuts, orders, pairs, *refs):
    ins, x_in, refs = refs[:5], refs[5], refs[6:]
    sources = 1 + max(cut[0] for cut in cuts)
    count = len(cuts)
    terms, refs = refs[:sources], refs[sources:]
    attn_outs, x_out, refs = refs[:2], refs[2], refs[3:]
    outs, refs = refs[:sources], refs[sources:]
    scratch, x_sem, refs = refs[:6], refs[6], refs[7:]
    own_bufs, pair_bufs, ring_bufs = refs[:count], refs[count : 2 * count], refs[2 * count : 3 * count]
    own_sem, sems = refs[3 * count], refs[3 * count + 1 :]
    place = Place(dp)
    works, targets = [], []
    for number, (a, first, size) in enumerate(cuts):
        cut = pl.ds(first, size)
        works.append(
            Scatter(
                place,
                dp,
                orders[number],
                lambda at, a=a, cut=cut: terms[a].at[at, :, cut],
                pair_bufs[number],
                ring_bufs[number],
                sems,
                number,
                (own_bufs[number], own_sem),
            )
        )
        targets.append(outs[a].at[:, cut])
    points = ins[1].shape[0] // blk
    plan = scatter_plan(place, works, targets, block_swap(x_in, x_out, x_sem, place), pairs, points)
    backward_body(blk, *ins, *attn_outs, *scratch, point=lambda i: run_at(plan, i))

    @pl.when(pl.program_id(0) == pairs - 1)
    def _():
        for task in plan["last", 0]:
            task()


def backward_specs(q, kv):
    groups, chunks, rows, cols = q.shape
    seq = kv.shape[0]
    pairs = cols // 128
    tok = pl.BlockSpec((groups, chunks, rows, 128), lambda p: (0, 0, 0, p))
    wide = pl.BlockSpec((seq, 256), lambda p: (0, p))
    ins = [tok, wide, tok, tok, pl.BlockSpec((None, 2, seq), lambda p: (p, 0, 0))]
    outs = [tok, wide]
    shapes = [jax.ShapeDtypeStruct(q.shape, BF), jax.ShapeDtypeStruct(kv.shape, BF)]
    scratch = [
        pltpu.VMEM((2, DH, seq), BF),
        pltpu.VMEM((2, seq, 128), F32),
        pltpu.VMEM((128, seq), F32),
        pltpu.VMEM((2, seq, 128), BF),
        pltpu.VMEM((2, seq, 128), BF),
        pltpu.VMEM((2, seq), F32),
    ]
    return pairs, ins, outs, shapes, scratch, cost(16 * pairs * seq * seq * 128)


def attention_backward(q, kv, do, o, lse, blk=512):
    pairs, ins, outs, shapes, scratch, estimate = backward_specs(q, kv)
    return pl.pallas_call(
        functools.partial(backward_kernel, blk),
        grid=(pairs,),
        in_specs=ins,
        out_specs=outs,
        out_shape=shapes,
        scratch_shapes=scratch,
        compiler_params=pltpu.CompilerParams(vmem_limit_bytes=56 * 2**20),
        cost_estimate=estimate,
    )(q, kv, do, o, lse)


def attention_backward_scatter(dp, q, kv, do, o, lse, blocks, terms, cuts, orders, blk=512):
    pairs, ins, outs, shapes, scratch, estimate = backward_specs(q, kv)
    anywhere = pl.BlockSpec(memory_space=pl.ANY)
    count = len(cuts)
    bufs = [pltpu.VMEM((2 * dp, terms[a].shape[1], size), BF) for a, _, size in cuts]
    return pl.pallas_call(
        functools.partial(backward_scatter_kernel, dp, blk, cuts, orders, pairs),
        grid=(pairs,),
        in_specs=ins + [anywhere] * (1 + len(terms)),
        out_specs=outs + [anywhere] + [pl.BlockSpec(w.shape[1:], lambda p: (0, 0)) for w in terms],
        out_shape=shapes
        + [jax.ShapeDtypeStruct(blocks.shape, blocks.dtype)]
        + [jax.ShapeDtypeStruct(w.shape[1:], F32) for w in terms],
        scratch_shapes=scratch
        + [pltpu.SemaphoreType.DMA((3,))]
        + bufs * 3
        + [pltpu.SemaphoreType.DMA((count, 2 * dp))]
        + scatter_sems(dp, count),
        compiler_params=pltpu.CompilerParams(
            vmem_limit_bytes=60 * 2**20, collective_id=3, has_side_effects=True
        ),
        cost_estimate=estimate,
    )(q, kv, do, o, lse, blocks, *terms)


CUT = 256
PART = 512
TALL = 512
DOWN = 8
LAGS = (1, 3, 6, 9)


class BlockSums:

    def __init__(self, dp, stage, pair_buf, ring_buf, send, recv, out_ref, last_ref=None):
        self.last_ref = last_ref
        self.place = Place(dp)
        self.stage, self.pair_buf, self.ring_buf = stage, pair_buf, ring_buf
        self.send, self.recv, self.out_ref = send, recv, out_ref
        self.total = pair_buf.shape[1]
        self.unit = out_ref.shape[0]

    def order(self):
        return [
            self.place.index({"y": y, "x": x, "z": z}, other)
            for other in (False, True)
            for y in range(2)
            for x in range(2)
            for z in range(self.place.sizes["z"])
        ]

    def pair(self, j):
        return remote(
            self.stage.at[lax.rem(j, self.stage.shape[0]), pl.ds(self.total, self.total)],
            self.pair_buf.at[j],
            self.send.at[j, 0],
            self.recv.at[j, 0],
            self.place.pair(),
        )

    def hop(self, j, axis, step, first, size, number):
        rows = pl.ds(first, size)
        offset = {"x": 0, "y": 0, "z": 0, axis: step}
        return remote(
            self.pair_buf.at[j, rows],
            self.ring_buf.at[j, rows],
            self.send.at[j, number],
            self.recv.at[j, number],
            self.place.device(offset),
        )

    def hops(self, way, phase):
        q, unit = self.total // 4, self.unit
        sizes = range(1, self.place.sizes["z"])
        if way == 2:
            far = [("z", z, z * unit, unit, 1 + 2 * z) for z in sizes]
            far += [("z", z, q + z * unit, unit, 2 + 2 * z) for z in sizes]
            return ([("y", 1, 2 * q, 2 * q, 1)], far, [("x", 1, q, unit, 2)])[phase - 1]
        if phase == 3:
            return [("z", z, z * unit, unit, 3 + z) for z in sizes]
        if way:
            return ([("x", 1, q, q, 1), ("x", 1, 3 * q, q, 2)], [("y", 1, 2 * q, q, 3)])[phase - 1]
        return ([("y", 1, 2 * q, 2 * q, 1)], [("x", 1, q, q, 3)])[phase - 1]

    def add(self, j, to, size, came):
        self.pair_buf[j, to : to + size] = (
            self.pair_buf[j, to : to + size].astype(F32) + came.astype(F32)
        ).astype(BF)

    def advance(self, j, way, phase):
        q, unit = self.total // 4, self.unit
        sizes = range(1, self.place.sizes["z"])
        if phase == 1:
            self.pair(j).wait_recv()
            self.add(j, 0, self.total, self.stage[lax.rem(j, self.stage.shape[0]), : self.total])
        else:
            for hop in self.hops(way, phase - 1):
                self.hop(j, *hop).wait_recv()
        if phase == 2 and way == 1:
            self.add(j, 0, q, self.ring_buf[j, q : 2 * q])
            self.add(j, 2 * q, q, self.ring_buf[j, 3 * q :])
        elif phase == 2:
            self.add(j, 0, 2 * q, self.ring_buf[j, 2 * q :])
        elif phase == 3 and way == 2:
            for first in (0, q):
                total = self.pair_buf[j, first : first + unit].astype(F32)
                for z in sizes:
                    came = slice(first + z * unit, first + (z + 1) * unit)
                    total = total + self.ring_buf[j, came].astype(F32)
                self.pair_buf[j, first : first + unit] = total.astype(BF)
        elif phase == 3:
            first = 2 * q if way else q
            self.add(j, 0, q, self.ring_buf[j, first : first + q])
        elif phase == 4:
            total = self.pair_buf[j, :unit].astype(F32)
            for first in (q,) if way == 2 else [z * unit for z in sizes]:
                total = total + self.ring_buf[j, first : first + unit].astype(F32)
            wide = total.shape[1]
            if self.last_ref is not None and j == self.pair_buf.shape[0] - 1:
                self.last_ref[...] = total
            else:
                self.out_ref[:, pl.ds(pl.multiple_of(j * wide, wide), wide)] = total
        if phase < 4:
            for hop in self.hops(way, phase):
                self.hop(j, *hop).start()

    def finish(self, parities):
        for j, odd in enumerate(parities):
            for phase in range(1, 4):
                for hop in self.hops(odd, phase):
                    self.hop(j, *hop).wait_send()


def ffn_kernel(dp, scale_ref, x_ref, att_ref, wo_ref, gain_ref, cot_ref, gu_ref, down_ref,
               res_ref, nb_ref, gu_out, down_out, *refs):
    if dp:
        gg_ref, heads_out, og_out, refs = refs[0], refs[1], refs[2], refs[3:]
        mid_ref, out_sem, far_sem, refs = refs[0], refs[1], refs[2], refs[3:]
    else:
        mid_ref, refs = refs[0], refs[1:]
    n2_s, n2t_s, up_s, acc_s, ht_s, back_s, gu_stage, down_stage, gu_sem, down_sem = refs[:10]
    step = pl.program_id(0)
    rows, width = x_ref.shape
    part = min(PART, rows)
    heads, _, cols = att_ref.shape
    blocks = ht_s.shape[0] // CUT
    wide = 2 * CUT
    tall = ht_s.shape[0] // DOWN
    chunks = [pl.ds(a, part) for a in range(0, rows, part)]
    sums = BlockSums(dp, gu_stage, *refs[10:], gu_out) if dp else None

    @pl.when(step == 0)
    def _():
        if dp:
            sums.place.greet()
        gain = (gain_ref[1:2] if dp else gain_ref[...]).astype(F32)
        scale = scale_ref[0, 0]
        for at in chunks:
            mid = x_ref[at].astype(F32)
            for j in range(heads):
                mid = mid + dot_nn(att_ref[j, at], wo_ref[j * cols : (j + 1) * cols])
            mid_ref[at] = mid
            inverse = lax.rsqrt(jnp.mean(mid * mid, axis=-1, keepdims=True) + EPSILON)
            low = (mid * inverse * gain).astype(BF)
            n2_s[at] = low
            if dp:
                gu_stage[0, :, :part] = low.T
                unit = gu_out.shape[0]
                for i, shard in enumerate(sums.order()):
                    there = pl.ds(pl.multiple_of(shard * unit, unit), unit)
                    n2t_s[i * unit : (i + 1) * unit, at] = gu_stage[0, there, :part]
            else:
                n2t_s[:, at] = low.T
            up_s[at] = (cot_ref[at].astype(F32) * scale).astype(BF)
        acc_s[...] = jnp.zeros_like(acc_s)
        nb_ref[...] = jnp.zeros_like(nb_ref)

    def gu_copy(j):
        slot = lax.rem(j, 2)
        return pltpu.make_async_copy(
            gu_stage.at[slot],
            gu_out.at[:, pl.ds(pl.multiple_of(j * wide, wide), wide)],
            gu_sem.at[slot],
        )

    def advance(phases):
        for phase in phases:
            lag = LAGS[phase - 1]
            j = step - lag
            for odd in range(2):

                @pl.when(
                    jnp.logical_and(
                        jnp.logical_and(step >= lag, step < lag + blocks), lax.rem(j, 2) == odd
                    )
                )
                def _(j=j, odd=odd, phase=phase):
                    sums.advance(j, odd, phase)

    @pl.when(step < blocks)
    def _():
        for at in chunks:
            both = dot_nn(n2_s[at], gu_ref[...])
            gate, up = both[:, :CUT], both[:, CUT:]
            back = dot_nt(up_s[at], down_ref[...])
            sig = 0.5 * jnp.tanh(0.5 * gate) + 0.5
            act = gate * sig
            hidden = (act * up).astype(BF)
            ht_s[pl.ds(pl.multiple_of(step * CUT, CUT), CUT), at] = hidden.T
            back_s[at, :CUT] = (back * up * sig * (1.0 + gate * (1.0 - sig))).astype(BF)
            back_s[at, CUT:] = (back * act).astype(BF)
            acc_s[at] += dot_nn(hidden, down_ref[...])
            nb_ref[at] += dot_nt(back_s[at], gu_ref[...])

    if dp:
        advance((4, 3, 2, 1))

    @pl.when(jnp.logical_and(step >= 2, step < blocks))
    def _():
        if dp:
            sums.pair(step - 2).wait_send()
        else:
            gu_copy(step - 2).wait()

    @pl.when(step < blocks)
    def _():
        for a in range(0, width, TALL):
            gu_stage[lax.rem(step, 2), a : a + TALL] = dot_nn(
                n2t_s[a : a + TALL], back_s[...]
            ).astype(BF)
        if dp:
            sums.pair(step).start()
        else:
            gu_copy(step).start()

    def down_copy(p):
        slot = lax.rem(p, 2)
        there = down_out.at[pl.ds(pl.multiple_of(p * tall, tall), tall)]
        return pltpu.make_async_copy(down_stage.at[slot], there, down_sem.at[slot])

    @pl.when(jnp.logical_and(step >= blocks, step < blocks + DOWN))
    def _():
        p = step - blocks

        @pl.when(p == 0)
        def _():
            for at in chunks:
                res_ref[at] = (mid_ref[at] + acc_s[at]).astype(BF)

        @pl.when(p >= 2)
        def _():
            down_copy(p - 2).wait()

        grad = dot_nn(ht_s[pl.ds(pl.multiple_of(p * tall, tall), tall)], up_s[...])
        down_stage[lax.rem(p, 2)] = grad.astype(BF)
        down_copy(p).start()

        @pl.when(p == DOWN - 1)
        def _():
            if dp:
                sums.pair(blocks - 2).wait_send()
                sums.pair(blocks - 1).wait_send()
            else:
                gu_copy(blocks - 2).wait()
                gu_copy(blocks - 1).wait()
            down_copy(p - 1).wait()
            down_copy(p).wait()

    if not dp:
        return
    place = sums.place
    c = place.core
    ends = [
        remote(gu_stage.at[1 - c], heads_out.at[c], far_sem.at[0], far_sem.at[1], place.pair()),
        pltpu.make_async_copy(gu_stage.at[c], heads_out.at[c], out_sem.at[0]),
        pltpu.make_async_copy(n2t_s, og_out, out_sem.at[1]),
    ]
    for q, at in enumerate(chunks):

        @pl.when(step == blocks + DOWN + q)
        def _(q=q, at=at):
            mid, nback, gain = mid_ref[at], nb_ref[at], gain_ref[1:2]
            inverse = lax.rsqrt(jnp.mean(mid * mid, axis=-1, keepdims=True) + EPSILON)
            scaled = nback * gain
            middle_grad = cot_ref[at].astype(F32) * scale_ref[0, 0] + (
                inverse * scaled
                - mid
                * (inverse * inverse * inverse)
                * jnp.mean(scaled * mid, axis=-1, keepdims=True)
            )
            gain_part = jnp.sum(nback * mid * inverse, axis=0, keepdims=True)
            gg_ref[...] = gain_part if q == 0 else gg_ref[...] + gain_part
            nb_ref[at] = middle_grad
            branch = middle_grad.astype(BF)
            n2_s[at] = branch
            for j in range(heads):
                gu_stage[j, at] = dot_nt(branch, wo_ref[j * cols : (j + 1) * cols]).astype(BF)
            if q == len(chunks) - 1:
                ends[0].start()
                ends[1].start()

    @pl.when(step == blocks + DOWN + len(chunks))
    def _():
        for j in range(heads):
            n2t_s[j * cols : (j + 1) * cols] = dot_tn(att_ref[j], n2_s[...]).astype(BF)
        ends[2].start()
        sums.finish([j % 2 for j in range(blocks)])
        for end in ends:
            end.wait()


def feed_forward(dp, scale, x, att, gain, cot, wide, down):
    rows, width = x.shape
    size = down.shape[0]
    blocks, tall = size // CUT, size // DOWN
    once = pl.Buffered(1)

    def whole(w):
        return pl.BlockSpec(w.shape, lambda i: (0,) * len(w.shape), pipeline_mode=once)

    def last(i):
        return jnp.minimum(i, blocks - 1)

    shape = jax.ShapeDtypeStruct
    anywhere = pl.BlockSpec(memory_space=pl.ANY)
    out = [shape((rows, width), BF), shape((rows, width), F32)]
    out_specs = [whole(w) for w in out]
    first, scratch = [], []
    params = {}
    steps = blocks + DOWN
    sem = pltpu.SemaphoreType.DMA
    if dp:
        out += [shape((width // (4 * dp), 2 * size), F32), shape((size, width), BF)]
        out += [shape((1, width), F32), shape(att.shape, BF), shape((width, width), BF)]
        out_specs += [whole(out[2]), anywhere, whole(out[4]), anywhere, anywhere]
        first = [pltpu.VMEM((rows, width), F32), sem((2,)), sem((2,))]
        sems = sem((blocks, dp + 1))
        scratch = [pltpu.VMEM((blocks, width // 2, 2 * CUT), BF)] * 2 + [sems] * 2
        params = {"collective_id": 4, "has_side_effects": True}
        steps += rows // min(PART, rows) + 1
    else:
        out += [shape((width, 2 * size), BF), shape((size, width), BF), shape((rows, width), F32)]
        out_specs += [anywhere, anywhere, whole(out[4])]
    return pl.pallas_call(
        functools.partial(ffn_kernel, dp),
        grid=(steps,),
        in_specs=[
            pl.BlockSpec(memory_space=pltpu.SMEM),
            whole(x),
            whole(att),
            pl.BlockSpec((width, width), lambda i: (0, 0), pipeline_mode=once),
            whole(gain),
            whole(cot),
            pl.BlockSpec((width, 2 * CUT), lambda i: (0, last(i) + width // (2 * CUT))),
            pl.BlockSpec((CUT, width), lambda i: (last(i), 0)),
        ],
        out_specs=out_specs,
        out_shape=out,
        scratch_shapes=[
            *first,
            pltpu.VMEM((rows, width), BF),
            pltpu.VMEM((width, rows), BF),
            pltpu.VMEM((rows, width), BF),
            pltpu.VMEM((rows, width), F32),
            pltpu.VMEM((size, rows), BF),
            pltpu.VMEM((rows, 2 * CUT), BF),
            pltpu.VMEM((2, width, 2 * CUT), BF),
            pltpu.VMEM((2, tall, width), BF),
            pltpu.SemaphoreType.DMA((2,)),
            pltpu.SemaphoreType.DMA((2,)),
            *scratch,
        ],
        compiler_params=pltpu.CompilerParams(vmem_limit_bytes=63 * 2**20, **params),
        cost_estimate=cost(18 * rows * width * size),
    )(scale, x, att, wide, gain, cot, wide, down)


def branch_kernel(scale_ref, mid_ref, nb_ref, cot_ref, att_ref, wo_ref, gain_ref,
                  mg_ref, send_ref, og_ref, gg_ref, branch_s):
    step = pl.program_id(0)
    part, width = mid_ref.shape
    heads, rows, cols = att_ref.shape
    mid, nback, gain = mid_ref[...], nb_ref[...], gain_ref[...].astype(F32)
    inverse = lax.rsqrt(jnp.mean(mid * mid, axis=-1, keepdims=True) + EPSILON)
    scaled = nback * gain
    middle_grad = cot_ref[...].astype(F32) * scale_ref[0, 0] + (
        inverse * scaled
        - mid * (inverse * inverse * inverse) * jnp.mean(scaled * mid, axis=-1, keepdims=True)
    )
    gain_part = jnp.sum(nback * mid * inverse, axis=0, keepdims=True)
    mg_ref[...] = middle_grad
    branch = middle_grad.astype(BF)
    branch_s[pl.ds(pl.multiple_of(step * part, part), part)] = branch
    for j in range(heads):
        send_ref[j] = dot_nt(branch, wo_ref[j * cols : (j + 1) * cols]).astype(BF)

    @pl.when(step == 0)
    def _():
        gg_ref[...] = gain_part

    @pl.when(step > 0)
    def _():
        gg_ref[...] += gain_part

    @pl.when(step == rows // part - 1)
    def _():
        for j in range(heads):
            og_ref[j * cols : (j + 1) * cols] = dot_tn(att_ref[j], branch_s[...]).astype(BF)


def branch_back(scale, mid, nback, cot, att, wo, gain):
    rows, width = mid.shape
    heads, _, cols = att.shape
    part = min(256, rows)
    rowwise = pl.BlockSpec((part, width), lambda i: (i, 0))

    def whole(w):
        return pl.BlockSpec(w.shape, lambda i: (0,) * len(w.shape))

    out = [
        jax.ShapeDtypeStruct((rows, width), F32),
        jax.ShapeDtypeStruct((heads, rows, cols), BF),
        jax.ShapeDtypeStruct((width, width), BF),
        jax.ShapeDtypeStruct((1, width), F32),
    ]
    return pl.pallas_call(
        branch_kernel,
        grid=(rows // part,),
        in_specs=[
            pl.BlockSpec(memory_space=pltpu.SMEM),
            rowwise,
            rowwise,
            rowwise,
            whole(att),
            whole(wo),
            whole(gain),
        ],
        out_specs=[
            rowwise,
            pl.BlockSpec((heads, part, cols), lambda i: (0, i, 0)),
            whole(out[2]),
            whole(out[3]),
        ],
        out_shape=out,
        scratch_shapes=[pltpu.VMEM((rows, width), BF)],
        compiler_params=pltpu.CompilerParams(vmem_limit_bytes=48 * 2**20),
        cost_estimate=cost(4 * rows * width * width),
    )(scale, mid, nback, cot, att, wo, gain)


Q_WAYS = (2, 2, 0)


def closing_kernel(dp, *refs):
    dq_in, dkv_in, hl_in, ex_in, x_in, gain_ref, wq_in, wl_in, mg_in, gg_ref = refs[:10]
    ig_out, q_out, l_out, e_out, g_out = refs[10:15]
    refs = refs[:14] + refs[15:]
    dq, dkv, hl, ex, x, wq, wl, mg = refs[14:22]
    far_dq, far_lat, lat_send, lat_own, e_s, g_s, n1t, flip, ig = refs[22:31]
    q_stage, q_pair, q_ring, e_stage, e_pair, e_ring, g_stage, g_pair, g_ring = refs[31:40]
    load_sem, far_send, far_recv, x_sem = refs[40:44]
    q_send, q_recv, e_send, e_recv, g_send, g_recv = refs[44:]
    place = Place(dp)
    c, s = place.core, place.at["x"]
    rows, width = x.shape
    cols, lat = dq.shape[1], ex.shape[0]
    part = rows // 2
    unit = q_out.shape[0]

    def at(index, size):
        return pl.ds(pl.multiple_of(index * size, size), size)

    loads = [(ex_in, ex), (dkv_in, dkv), (hl_in, hl), (x_in, x), (dq_in.at[c], dq)]
    loads += [(wq_in, wq), (wl_in, wl), (mg_in, mg)]

    def load(i):
        return pltpu.make_async_copy(*loads[i], load_sem.at[i])

    for i in (3, 4, 0, 1, 5, 6, 7, 2):
        load(i).start()
    place.greet()
    far_q = remote(dq_in.at[1 - c], far_dq, far_send.at[0], far_recv.at[0], place.pair())
    far_l = remote(lat_send, far_lat, far_send.at[1], far_recv.at[1], place.pair())
    far_q.start()

    q_sums = BlockSums(dp, q_stage, q_pair, q_ring, q_send, q_recv, q_out, l_out)
    e_sums = BlockSums(dp, e_stage, e_pair, e_ring, e_send, e_recv, e_out)
    g_sums = BlockSums(dp, g_stage, g_pair, g_ring, g_send, g_recv, g_out)
    order = q_sums.order()

    load(3).wait()
    gain = gain_ref[0:1]

    def inverse_of(values):
        return lax.rsqrt(jnp.mean(values * values, axis=-1, keepdims=True) + EPSILON)

    for u in range(2):
        chunk = slice(u * part, (u + 1) * part)
        values = x[chunk].astype(F32)
        flip[...] = (values * inverse_of(values) * gain).astype(BF).T
        for i, shard in enumerate(order):
            n1t[i * unit : (i + 1) * unit, chunk] = flip[at(shard, unit)]
    load(4).wait()
    q_stage[c] = dot_nn(n1t[...], dq[...]).astype(BF)
    load(0).wait()
    load(1).wait()
    for u in range(2):
        lat_send[u * part : (u + 1) * part] = dot_nt(dkv[at(u * 2 + 1 - c, part)], ex[...]).astype(BF)
    far_l.start()
    for u in range(2):
        lat_own[u * part : (u + 1) * part] = dot_nt(dkv[at(u * 2 + c, part)], ex[...]).astype(BF)
    far_q.wait_recv()
    q_stage[1 - c] = dot_nn(n1t[...], far_dq[...]).astype(BF)
    for j in range(2):
        q_sums.pair(j).start()
    for i in (5, 6, 7):
        load(i).wait()
    far_l.wait_recv()

    def back(u):
        chunk = at(u, part)
        normed_back = (
            dot_nt(dq[chunk], wq[:, at(c, cols)])
            + dot_nt(far_dq[chunk], wq[:, at(1 - c, cols)])
            + dot_nt(lat_own[chunk], wl[:, at(c, lat)])
            + dot_nt(far_lat[chunk], wl[:, at(1 - c, lat)])
        )
        values = x[chunk].astype(F32)
        inverse = inverse_of(values)
        scaled = normed_back * gain
        grad = mg[chunk] + (
            inverse * scaled
            - values
            * (inverse * inverse * inverse)
            * jnp.mean(scaled * values, axis=-1, keepdims=True)
        )
        ig[u] = grad.astype(BF)
        return jnp.sum(normed_back * values * inverse, axis=0, keepdims=True)

    gain_part = back(1 - s)
    swap, kept = block_swap(ig, ig_out, x_sem, place)
    swap.start()
    for j in range(2):
        q_sums.advance(j, 2, 1)
    q_stage[2, :, at(c, lat)] = dot_nn(n1t[...], lat_own[...]).astype(BF)
    q_stage[2, :, at(1 - c, lat)] = dot_nn(n1t[...], far_lat[...]).astype(BF)
    q_sums.pair(2).start()
    load(2).wait()
    e_s[...] = dot_tn(hl[...], dkv[...])
    share = e_out.shape[0] // KVH
    for i, shard in enumerate(order):
        piece = e_s[at(shard, share)]
        zero = jnp.zeros_like(piece)
        whole = jnp.concatenate(
            [jnp.where(c == 0, piece, zero), jnp.where(c == 0, zero, piece)], axis=0
        ).astype(BF)
        for j in range(2):
            e_stage[j, i * 2 * share : (i + 1) * 2 * share] = whole[:, j * cols : (j + 1) * cols]
    for j in range(2):
        e_sums.pair(j).start()
    q_sums.advance(2, 0, 1)
    gain_part = gain_part + back(s)
    kept.start()
    g_s[...] = jnp.concatenate(
        [gain_part, gg_ref[...], jnp.zeros((14, width), F32)], axis=0
    ).astype(BF)
    for i, shard in enumerate(order):
        g_stage[0, i * 16 : (i + 1) * 16] = g_s[:, at(lax.div(shard * unit, 128), 128)]
    g_sums.pair(0).start()
    for j in range(2):
        e_sums.advance(j, 2, 1)
    g_sums.advance(0, 2, 1)
    for phase in (2, 3, 4):
        for j in range(3):
            q_sums.advance(j, Q_WAYS[j], phase)
        for j in range(2):
            e_sums.advance(j, 2, phase)
        g_sums.advance(0, 2, phase)
    far_q.wait_send()
    far_l.wait_send()
    for sums, parities in ((q_sums, Q_WAYS), (e_sums, (2, 2)), (g_sums, (2,))):
        for j in range(len(parities)):
            sums.pair(j).wait_send()
        sums.finish(parities)
    swap.wait()
    kept.wait()


def closing(dp, dq, dkv, head_latent, expand, x, gain, wq, wl, mg, gain_two_grad):
    rows, width = x.shape
    cols, lat = dq.shape[2], expand.shape[0]
    unit = width // (4 * dp)
    n = 2 * dp
    anywhere = pl.BlockSpec(memory_space=pl.ANY)
    inside = pl.BlockSpec(memory_space=pltpu.VMEM)
    vmem = pltpu.VMEM
    sem = pltpu.SemaphoreType.DMA
    share = lat // (2 * n) * KVH
    bulk = [((rows, cols), BF), (dkv.shape, BF), (head_latent.shape, BF), (expand.shape, BF)]
    bulk += [(x.shape, BF), (wq.shape, BF), (wl.shape, BF), (mg.shape, F32)]
    sums = []
    for blocks, high, wide in ((3, unit, cols), (2, share, cols), (1, 16, 128)):
        sums += [vmem((blocks, 2 * n * high, wide), BF)] + [vmem((blocks, n * high, wide), BF)] * 2
    return pl.pallas_call(
        functools.partial(closing_kernel, dp),
        in_specs=[anywhere] * 5 + [inside] + [anywhere] * 3 + [inside],
        out_specs=[anywhere] + [inside] * 4,
        out_shape=[
            jax.ShapeDtypeStruct((2, rows // 2, width), BF),
            jax.ShapeDtypeStruct((unit, 2 * cols), F32),
            jax.ShapeDtypeStruct((unit, cols), F32),
            jax.ShapeDtypeStruct((share, 2 * cols), F32),
            jax.ShapeDtypeStruct((16, 128), F32),
        ],
        scratch_shapes=[vmem(*b) for b in bulk]
        + [
            vmem((rows, cols), BF),
            vmem((rows, lat), BF),
            vmem((rows, lat), BF),
            vmem((rows, lat), BF),
            vmem((lat, 2 * cols), F32),
            vmem((16, width), BF),
            vmem((width, rows), BF),
            vmem((width, rows // 2), BF),
            vmem((2, rows // 2, width), BF),
        ]
        + sums
        + [sem((8,)), sem((2,)), sem((2,)), sem((3,))]
        + [sem((blocks, dp + 1)) for blocks in (3, 3, 2, 2, 1, 1)],
        compiler_params=pltpu.CompilerParams(
            collective_id=1, has_side_effects=True, vmem_limit_bytes=60 * 2**20
        ),
    )(dq, dkv, head_latent, expand, x, gain, wq, wl, mg, gain_two_grad)


HEADS = 16
LATD = 256
HG = 8
GROUPS = 8
ALL = ("dp", "seq", "grp")


def norm_parts(values, gain):
    inverse = lax.rsqrt(jnp.mean(values * values, axis=-1, keepdims=True) + EPSILON)
    return (values * inverse * gain, inverse)


def norm_back(values, inverse, gain, upstream):
    scaled = upstream * gain
    gain_grad = jnp.sum(upstream * values * inverse, axis=0)
    input_part = inverse * scaled - values * inverse**3 * jnp.mean(
        scaled * values, axis=-1, keepdims=True
    )
    return (input_part, gain_grad)


def swap_sequences(blocks, count):
    if count == 2:
        me = lax.axis_index("seq")
        sent = lax.ppermute(blocks[1 - me], "seq", [(0, 1), (1, 0)])
        kept = blocks[me]
        first = me == 0
        return jnp.stack([jnp.where(first, kept, sent), jnp.where(first, sent, kept)])
    return lax.all_to_all(blocks, "seq", 0, 0, tiled=True)


def swap_group(blocks):
    return lax.all_to_all(blocks, "grp", 0, 0, tiled=True)


def local(
    inputs,
    cotangent,
    group_ids,
    group_scale,
    norm_gain,
    w_query,
    w_latent,
    expansion_weight,
    w_output,
    ffn_gain,
    w_gate,
    w_up,
    w_down,
):
    devices = lax.axis_size("dp") * lax.axis_size("seq") * lax.axis_size("grp")
    groups = lax.axis_size("grp")
    me = lax.axis_index("grp")
    seqs, rows, width = inputs.shape
    count = seqs * rows
    hidden_size = w_gate.shape[1]
    heads = HEADS // groups
    cols = heads * DH
    drows = width // devices

    dp = lax.axis_size("dp")
    ring = groups == 2 and seqs == 2 and dp % 2 == 0
    expand_rows = expansion_weight.reshape(-1, expansion_weight.shape[2])
    shard = (lax.axis_index("dp") * seqs + lax.axis_index("seq")) * groups + me
    both_gains = jnp.stack([norm_gain, ffn_gain])
    gains = lax.dynamic_update_slice(jnp.zeros((16, 128), BF), both_gains, (0, shard * drows % 128))
    if ring:
        shards = (w_query, w_latent, expand_rows, gains)
        full, own_inputs = own_gather(dp, shards, inputs, ("xzy",) * 4)
    else:
        shards = (w_query, w_latent, expand_rows)
        full = [lax.all_gather(w, ALL, axis=0) for w in shards]
        own_inputs = swap_sequences(inputs, seqs)
    gate_up = jnp.stack(
        [w_gate.reshape(drows, -1, CUT), w_up.reshape(drows, -1, CUT)], axis=2
    ).reshape(drows, -1)
    wide_full = lax.all_gather(
        jnp.concatenate([w_output, gate_up], axis=1), ALL, axis=0, tiled=True
    )
    query_full = full[0].reshape(width, -1)
    latent_full = full[1].reshape(width, -1)
    expand_full = full[2].reshape(devices, KVH, LATD // devices, -1)
    if ring:
        half = width // 2
        (
            logsum,
            gain_rows,
            attended,
            token_attended,
            head_queries,
            head_pairs,
            head_latent,
            expand_local,
            own_cotangent,
            down_full,
        ) = attention_forward_gather(
            dp,
            own_inputs.reshape(count, width),
            full[3],
            query_full,
            latent_full,
            full[2],
            cotangent,
            (w_down,),
            ((0, 0, half), (0, half, half)),
            ("yzx", "xzy"),
        )
        down_full = down_full.reshape(-1, width)
        gain_one = gain_two = gain_rows
    else:
        gain_one, gain_two = [
            lax.all_gather(w, ALL, axis=0, tiled=True).reshape(1, width) for w in (norm_gain, ffn_gain)
        ]
        expand_local = lax.dynamic_slice(
            expand_full,
            (0, me * heads // HG, 0, me * heads % HG * 2 * DH),
            (devices, 1, LATD // devices, heads * 2 * DH),
        ).reshape(LATD, -1)
        token_rows = own_inputs.astype(F32).reshape(count, width)
        normed, inverse_one = norm_parts(token_rows, gain_one)
        normed_low = normed.astype(BF)
        query_send = jnp.stack(
            [dot_nn(normed_low, query_full[:, j * cols : (j + 1) * cols]).astype(BF) for j in range(groups)]
        ).reshape(groups, seqs, rows, cols)
        latent_state = [
            dot_nn(normed_low, latent_full[:, g * LATD : (g + 1) * LATD]).astype(BF) for g in range(KVH)
        ]
        latent_send = jnp.stack([latent_state[j * heads // HG] for j in range(groups)]).reshape(
            groups, seqs, rows, LATD
        )
        head_queries = swap_group(query_send)
        head_latent = swap_group(latent_send).transpose(1, 0, 2, 3).reshape(-1, LATD)
        head_pairs = dot_nn(head_latent, expand_local).astype(BF)
        attended, logsum = attention_forward(head_queries, head_pairs)
        token_attended = swap_group(attended)
        own_cotangent = swap_sequences(cotangent, seqs)
        down_full = lax.all_gather(w_down, ALL, axis=0, tiled=True)
    token_attended = token_attended.reshape(groups, count, cols)
    seq_group = lax.dynamic_index_in_dim(group_ids, lax.axis_index("seq"), 0, keepdims=False)
    chosen = (seq_group == jnp.arange(GROUPS)).astype(F32)
    seq_scale = jnp.sum(chosen * group_scale).reshape(1, 1)
    x_rows = own_inputs.reshape(count, width)
    cot_rows = own_cotangent.reshape(count, width)
    result, normed_two_back, gu_share, down_grad, *rest = feed_forward(
        dp if ring else None,
        seq_scale,
        x_rows,
        token_attended,
        gain_two,
        cot_rows,
        wide_full,
        down_full,
    )
    own_output = result.reshape(seqs, rows, width)
    if ring:
        middle_grad = normed_two_back
        gain_two_grad, head_upstream, output_grad = rest
        head_upstream = head_upstream.reshape(groups, seqs, rows, cols)
    else:
        gu_share = lax.psum_scatter(gu_share, ALL, scatter_dimension=0, tiled=True).astype(F32)
        middle_grad, back_send, output_grad, gain_two_grad = branch_back(
            seq_scale, *rest, normed_two_back, cot_rows, token_attended, wide_full[:, :width], gain_two
        )
        head_upstream = swap_group(back_send.reshape(groups, seqs, rows, cols))
    gu_share = gu_share.reshape(drows, -1, 2, CUT)
    terms = (output_grad.reshape(devices, drows, width), down_grad.reshape(devices, -1, width))
    attention = (head_queries, head_pairs, head_upstream, attended, logsum)
    if ring:
        half = width // 2
        query_back, pair_back, output, output_share, down_share = attention_backward_scatter(
            dp,
            *attention,
            own_output,
            terms,
            ((0, 0, width), (1, 0, half), (1, half, half)),
            ("yzx", "yxz", "yzx"),
        )
    else:
        query_back, pair_back = attention_backward(*attention)
        output = swap_sequences(own_output, seqs)
        output_share, down_share = [
            lax.psum_scatter(w, ALL, scatter_dimension=0, tiled=True)[0].astype(F32) for w in terms
        ]
    if ring:
        input_grad, q_share, l_share, e_share, g_share = closing(
            dp,
            query_back.reshape(groups, count, cols),
            pair_back,
            head_latent,
            expand_local,
            x_rows,
            gain_one,
            query_full,
            latent_full,
            middle_grad,
            gain_two_grad,
        )
        own_gains = lax.dynamic_slice(g_share, (0, shard * drows % 128), (2, drows))
        sums = (q_share, l_share, e_share)
    else:
        latent_terms = dot_nt(pair_back, expand_local).astype(BF)
        expand_part = dot_tn(head_latent, pair_back)
        expand_grad = lax.dynamic_update_slice(
            jnp.zeros(expand_full.shape, BF),
            expand_part.astype(BF).reshape(devices, 1, LATD // devices, -1),
            (0, me * heads // HG, 0, me * heads % HG * 2 * DH),
        )
        query_token = swap_group(query_back).reshape(groups, count, cols)
        latent_token = swap_group(
            latent_terms.reshape(seqs, groups, rows, LATD).transpose(1, 0, 2, 3)
        ).reshape(KVH, groups // KVH, count, LATD)
        latent_token = jnp.sum(latent_token.astype(F32), axis=1).astype(BF)
        query_grad = jnp.concatenate([dot_tn(normed_low, query_token[j]) for j in range(groups)], axis=1)
        latent_grad = jnp.concatenate([dot_tn(normed_low, latent_token[g]) for g in range(KVH)], axis=1)
        normed_back = sum(
            dot_nt(query_token[j], query_full[:, j * cols : (j + 1) * cols]) for j in range(groups)
        ) + sum(
            dot_nt(latent_token[g], latent_full[:, g * LATD : (g + 1) * LATD]) for g in range(KVH)
        )
        input_part, gain_one_grad = norm_back(token_rows, inverse_one, gain_one, normed_back)
        own_input_grad = (middle_grad + input_part).astype(BF).reshape(seqs, rows, width)
        gain_grads = jnp.concatenate(
            [gain_one_grad.reshape(devices, 1, drows), gain_two_grad.reshape(devices, 1, drows)], axis=2
        ).astype(BF)
        gain_grads = jnp.pad(gain_grads, ((0, 0), (0, 15), (0, 128 - 2 * drows)))
        terms = (
            query_grad.astype(BF).reshape(devices, drows, -1),
            latent_grad.astype(BF).reshape(devices, drows, -1),
            expand_grad.reshape(devices, -1, expand_grad.shape[3]),
            gain_grads,
        )
        sums = [
            lax.psum_scatter(w, ALL, scatter_dimension=0, tiled=True)[0].astype(F32) for w in terms
        ]
        own_gains = sums[3][0, : 2 * drows].reshape(2, drows)
        input_grad = swap_sequences(own_input_grad, seqs)
    return (
        output,
        input_grad,
        own_gains[0],
        sums[0],
        sums[1],
        sums[2].reshape(expansion_weight.shape),
        output_share,
        own_gains[1],
        gu_share[:, :, 0].reshape(drows, -1),
        gu_share[:, :, 1].reshape(drows, -1),
        down_share,
    )


def solution(mesh):
    def run(*arrays):
        dp, sp = mesh.shape["dp"], mesh.shape["sp"]
        seqs = arrays[0].shape[0] // dp
        grid = Mesh(mesh.devices.reshape(dp, seqs, sp // seqs), ALL)
        tokens = P("dp", ("seq", "grp"), None)
        matrix = P(ALL, None)
        expand = P(None, ALL, None)
        return jax.shard_map(
            local,
            mesh=grid,
            in_specs=(
                tokens,
                tokens,
                P("dp"),
                P(),
                P(ALL),
                matrix,
                matrix,
                expand,
                matrix,
                P(ALL),
                matrix,
                matrix,
                matrix,
            ),
            out_specs=(
                tokens,
                tokens,
                P(ALL),
                matrix,
                matrix,
                expand,
                matrix,
                P(ALL),
                matrix,
                matrix,
                matrix,
            ),
            check_vma=False,
        )(*arrays)

    return run
```
